32 devices in a mesh: batch: 16 (over z, y, core), seq: 2 (over x).
Axes of the slice: x: 2, y: 2, z: 4, core: 2. Of those that a mesh axis runs over, the one named last changes fastest.
Arguments:
- tokens: bfloat16 [24576, 768], P(('batch', 'seq')), may hold values from -6 to 6
- lengths: int32 [16, 3], P('batch'), may hold values from 16 to 1504, as said below
- labels: int32 [48], replicated, may hold values from 0 to 47, as said below
- attention_gain: bfloat16 [768], P('batch'), may hold values from 0.5 to 1.5
- query_weight: bfloat16 [768, 768], P('batch'), may hold values from -0.02734375 to 0.02734375
- key_weight: bfloat16 [768, 768], P('batch'), may hold values from -0.21875 to 0.21875
- value_weight: bfloat16 [768, 768], P('batch'), may hold values from -0.21875 to 0.21875
- attention_out: bfloat16 [768, 768], P('batch'), may hold values from -0.875 to 0.875
- position_bias: bfloat16 [32, 12], P('batch'), may hold values from -4 to 4
- feed_gain: bfloat16 [768], P('batch'), may hold values from 0.5 to 1.5
- feed_inner: bfloat16 [768, 3072], P('batch'), may hold values from -0.21875 to 0.21875
- feed_outer: bfloat16 [3072, 768], P('batch'), may hold values from -0.109375 to 0.109375
- encoder_gain: bfloat16 [768], P('batch'), may hold values from 0.5 to 1.5
- start_token: bfloat16 [768], P('batch'), may hold values from -6 to 6
- self_gain: bfloat16 [768], P('batch'), may hold values from 0.5 to 1.5
- self_value: bfloat16 [768, 768], P('batch'), may hold values from -0.21875 to 0.21875
- self_out: bfloat16 [768, 768], P('batch'), may hold values from -0.21875 to 0.21875
- cross_gain: bfloat16 [768], P('batch'), may hold values from 0.5 to 1.5
- cross_query: bfloat16 [768, 768], P('batch'), may hold values from -0.02734375 to 0.02734375
- cross_key: bfloat16 [768, 768], P('batch'), may hold values from -0.21875 to 0.21875
- cross_value: bfloat16 [768, 768], P('batch'), may hold values from -0.21875 to 0.21875
- cross_out: bfloat16 [768, 768], P('batch'), may hold values from -0.875 to 0.875
- second_gain: bfloat16 [768], P('batch'), may hold values from 0.5 to 1.5
- second_inner: bfloat16 [768, 3072], P('batch'), may hold values from -0.21875 to 0.21875
- second_outer: bfloat16 [3072, 768], P('batch'), may hold values from -0.109375 to 0.109375
- final_gain: bfloat16 [768], P('batch'), may hold values from 0.5 to 1.5
- pooler_weight: bfloat16 [768, 768], P('batch'), may hold values from -0.21875 to 0.21875
Outputs:
- contrastive_loss: float32 [1], replicated
- embeddings: float32 [48, 768], P('batch')
- grad_tokens: float32 [24576, 768], P(('batch', 'seq'))
- grad_attention_gain: float32 [768], P('batch')
- grad_query_weight: float32 [768, 768], P('batch')
- grad_key_weight: float32 [768, 768], P('batch')
- grad_value_weight: float32 [768, 768], P('batch')
- grad_attention_out: float32 [768, 768], P('batch')
- grad_position_bias: float32 [32, 12], P('batch')
- grad_feed_gain: float32 [768], P('batch')
- grad_feed_inner: float32 [768, 3072], P('batch')
- grad_feed_outer: float32 [3072, 768], P('batch')
- grad_encoder_gain: float32 [768], P('batch')
- grad_start_token: float32 [768], P('batch')
- grad_self_gain: float32 [768], P('batch')
- grad_self_value: float32 [768, 768], P('batch')
- grad_self_out: float32 [768, 768], P('batch')
- grad_cross_gain: float32 [768], P('batch')
- grad_cross_query: float32 [768, 768], P('batch')
- grad_cross_key: float32 [768, 768], P('batch')
- grad_cross_value: float32 [768, 768], P('batch')
- grad_cross_out: float32 [768, 768], P('batch')
- grad_second_gain: float32 [768], P('batch')
- grad_second_inner: float32 [768, 3072], P('batch')
- grad_second_outer: float32 [3072, 768], P('batch')
- grad_final_gain: float32 [768], P('batch')
- grad_pooler_weight: float32 [768, 768], P('batch')
The draws below stay inside these ranges and needn't reach their ends.
Inputs may be any that keep to these rules, and one draw needn't show every extreme that they name: `lengths`: each row lists the 3 sequences of one group in order: one query, one document, one query; each query has 16 to 128 tokens and every row sums to 1536. labels[i] is never i.
All inputs are finite; a program needn't handle non-finite values.
Results may differ from the reference program's by a relative error of at most 0.033.
Values may be sent and summed in bfloat16 or wider, within the bound.
A program may use at most 320 MiB of HBM per device.

```python
import jax
import jax.numpy as jnp
from jax import lax

D = 768
HEADS = 12
HEAD = 64
FF = 3072
BUCKETS = 32
PACK = 1536
SIDE = 1
SHORT_MIN = 16
SHORT_MAX = 128
SEQS = 3
GROUPS = 16
ALL_SEQS = 48
TOKENS = 24576


def draw_lengths(key, part):
    key = jax.random.fold_in(key, 11)
    queries = jax.random.randint(key, (GROUPS, 2 * SIDE), SHORT_MIN, SHORT_MAX + 1).astype(jnp.int32)
    document = PACK - jnp.sum(queries, axis=1, keepdims=True).astype(jnp.int32)
    return jnp.concatenate([queries[:, :SIDE], document, queries[:, SIDE:]], axis=1).astype(jnp.int32)


def draw_labels(key, part):
    key = jax.random.fold_in(key, 23)
    places = jnp.arange(ALL_SEQS, dtype=jnp.int32)
    stride = jax.random.randint(key, (ALL_SEQS,), 1, ALL_SEQS).astype(jnp.int32)
    return ((places + stride) % ALL_SEQS).astype(jnp.int32)


def block_scale(key, dims, split, smallest, largest):
    loudness, own = 1.0, jax.random.fold_in(key, 6)
    for axis_at, blocks in split:
        heights = jnp.exp(jax.random.uniform(jax.random.fold_in(own, axis_at), (blocks,), jnp.float32, smallest / len(split), largest / len(split)))
        loudness = loudness * jnp.repeat(heights, dims[axis_at] // blocks).reshape([-1 if axis == axis_at else 1 for axis in range(len(dims))])
    return loudness


def bell_draw(stream_key, dims, width, limit, split=(), kind=jnp.bfloat16):
    array = jax.random.normal(stream_key, dims, jnp.float32) * width
    if len(split) > 0:
        array = block_scale(stream_key, dims, split, -0.22, 0.18) * array
    return jnp.clip(array, min=-limit, max=limit).astype(kind)


def setup_inputs(seed: int = 0) -> dict:
    keys = jax.random.split(jax.random.key(seed), 28)
    tokens = bell_draw(keys[0], (TOKENS, D), 1.0, 6.0, ((0, 32),))
    lengths = draw_lengths(jax.random.fold_in(keys[27], 71), 0)
    labels = draw_labels(jax.random.fold_in(keys[27], 71), 0)
    attention_gain = jnp.clip(1.0 + 0.1 * jax.random.normal(keys[3], (D,), jnp.float32), 0.5, 1.5).astype(jnp.bfloat16)
    query_weight = bell_draw(keys[4], (D, D), (D * HEAD) ** -0.5, 0.02734375, ((0, 16),))
    key_weight = bell_draw(keys[5], (D, D), D ** -0.5, 0.21875, ((0, 16),))
    value_weight = bell_draw(keys[6], (D, D), D ** -0.5, 0.21875, ((0, 16),))
    attention_out = bell_draw(keys[7], (D, D), (D // 16) ** -0.5, 0.875, ((0, 16),))
    position_bias = bell_draw(keys[8], (BUCKETS, HEADS), 1.0, 4.0, ((0, 16),))
    feed_gain = jnp.clip(1.0 + 0.1 * jax.random.normal(keys[9], (D,), jnp.float32), 0.5, 1.5).astype(jnp.bfloat16)
    feed_inner = bell_draw(keys[10], (D, FF), D ** -0.5, 0.21875, ((0, 16),))
    feed_outer = bell_draw(keys[11], (FF, D), FF ** -0.5, 0.109375, ((0, 16),))
    encoder_gain = jnp.clip(1.0 + 0.1 * jax.random.normal(keys[12], (D,), jnp.float32), 0.5, 1.5).astype(jnp.bfloat16)
    start_token = bell_draw(keys[13], (D,), 1.0, 6.0, ((0, 16),))
    self_gain = jnp.clip(1.0 + 0.1 * jax.random.normal(keys[14], (D,), jnp.float32), 0.5, 1.5).astype(jnp.bfloat16)
    self_value = bell_draw(keys[15], (D, D), D ** -0.5, 0.21875, ((0, 16),))
    self_out = bell_draw(keys[16], (D, D), D ** -0.5, 0.21875, ((0, 16),))
    cross_gain = jnp.clip(1.0 + 0.1 * jax.random.normal(keys[17], (D,), jnp.float32), 0.5, 1.5).astype(jnp.bfloat16)
    cross_query = bell_draw(keys[18], (D, D), (D * HEAD) ** -0.5, 0.02734375, ((0, 16),))
    cross_key = bell_draw(keys[19], (D, D), D ** -0.5, 0.21875, ((0, 16),))
    cross_value = bell_draw(keys[20], (D, D), D ** -0.5, 0.21875, ((0, 16),))
    cross_out = bell_draw(keys[21], (D, D), (D // 16) ** -0.5, 0.875, ((0, 16),))
    second_gain = jnp.clip(1.0 + 0.1 * jax.random.normal(keys[22], (D,), jnp.float32), 0.5, 1.5).astype(jnp.bfloat16)
    second_inner = bell_draw(keys[23], (D, FF), D ** -0.5, 0.21875, ((0, 16),))
    second_outer = bell_draw(keys[24], (FF, D), FF ** -0.5, 0.109375, ((0, 16),))
    final_gain = jnp.clip(1.0 + 0.1 * jax.random.normal(keys[25], (D,), jnp.float32), 0.5, 1.5).astype(jnp.bfloat16)
    pooler_weight = bell_draw(keys[26], (D, D), D ** -0.5, 0.21875, ((0, 16),))
    return {"tokens": tokens, "lengths": lengths, "labels": labels, "attention_gain": attention_gain, "query_weight": query_weight, "key_weight": key_weight, "value_weight": value_weight, "attention_out": attention_out, "position_bias": position_bias, "feed_gain": feed_gain, "feed_inner": feed_inner, "feed_outer": feed_outer, "encoder_gain": encoder_gain, "start_token": start_token, "self_gain": self_gain, "self_value": self_value, "self_out": self_out, "cross_gain": cross_gain, "cross_query": cross_query, "cross_key": cross_key, "cross_value": cross_value, "cross_out": cross_out, "second_gain": second_gain, "second_inner": second_inner, "second_outer": second_outer, "final_gain": final_gain, "pooler_weight": pooler_weight}


@jax.custom_vjp
def low(v):
    return lax.optimization_barrier(v.astype(jnp.bfloat16)).astype(jnp.float32)

@jax.custom_vjp
def low_back(v):
    return v

def low_keep(v):
    return (low(v), None)

def low_pass(kept, grad):
    return (grad,)

def back_keep(v):
    return (v, None)

def back_low(kept, grad):
    return (low(grad),)
low.defvjp(low_keep, low_pass)
low_back.defvjp(back_keep, back_low)
eps_norm = 1e-06
masked_score = -1000000000.0
logit_scale = 20.0
bucket_limits = (12, 16, 23, 32, 46, 64, 91)
highest = lax.Precision.HIGHEST

def low_both(values):
    return low(low_back(values))

def matmul(left_side, right_side):
    return jnp.dot(left_side, right_side, precision=highest)

def rms_norm(values, gain_vector):
    return values * lax.rsqrt(lax.optimization_barrier(jnp.mean(values * values, axis=-1, keepdims=True)) + eps_norm) * gain_vector

def unit_length(values):
    return values * lax.rsqrt(lax.optimization_barrier(jnp.sum(values * values, axis=-1, keepdims=True)) + eps_norm)

def bucket_of(offsets):
    upper_half = jnp.where(offsets > 0, 16, 0).astype(jnp.int32)
    distance = jnp.abs(offsets).astype(jnp.int32)
    far_bucket = 8 + sum(((distance >= threshold).astype(jnp.int32) for threshold in bucket_limits))
    return (upper_half + jnp.where(distance < 8, distance, far_bucket)).astype(jnp.int32)

def self_attention(queries, all_keys, all_values, table, seq_ids):
    block_size = min(512, PACK)
    blocks = PACK // block_size
    places = jnp.arange(PACK, dtype=jnp.int32)
    key_heads = all_keys.reshape(PACK, HEADS, HEAD)
    value_heads = all_values.reshape(PACK, HEADS, HEAD)

    def one_block(query_block, query_places, query_ids):
        scores = jnp.einsum('qhd,khd->hqk', query_block.reshape(block_size, HEADS, HEAD), key_heads, precision=highest)
        bias_term = jnp.take(table, bucket_of(places[None, :] - query_places[:, None]), axis=0)
        scores = low_back(scores + jnp.transpose(bias_term, (2, 0, 1)))
        allowed = query_ids[:, None] == seq_ids[None, :]
        scores = jnp.where(allowed[None], scores, masked_score)
        attention_weights = jax.nn.softmax(scores, axis=-1)
        return jnp.einsum('hqk,khd->qhd', attention_weights, value_heads, precision=highest).reshape(block_size, D)
    saved_block = jax.checkpoint(one_block)

    def visit_block(pieces):
        return saved_block(pieces[0], pieces[1], pieces[2])
    outputs = lax.map(visit_block, (queries.reshape(blocks, block_size, D), places.reshape(blocks, block_size), seq_ids.reshape(blocks, block_size)))
    return outputs.reshape(PACK, D)

def embed_group(inputs, lengths_row, params):
    attention_gain, query_weight, key_weight, value_weight, attention_out, position_bias, feed_gain, feed_inner, feed_outer, encoder_gain, start_token, self_gain, self_value, self_out, cross_gain, cross_query, cross_key, cross_value, cross_out, second_gain, second_inner, second_outer, final_gain, pooler_weight = params
    places = jnp.arange(PACK, dtype=jnp.int32)
    seq_ends = jnp.cumsum(lengths_row).astype(jnp.int32)
    seq_ids = lax.optimization_barrier(jnp.sum((places[:, None] >= seq_ends[None, :]).astype(jnp.int32), axis=1)).astype(jnp.int32)
    normed = low(rms_norm(inputs, attention_gain))
    queries = low_both(matmul(normed, query_weight))
    all_keys = low_both(matmul(normed, key_weight))
    all_values = low_both(matmul(normed, value_weight))
    attended = low_both(self_attention(queries, all_keys, all_values, position_bias, seq_ids))
    hidden = inputs + low_back(matmul(attended, attention_out))
    inner_pre = low_back(matmul(low(rms_norm(hidden, feed_gain)), feed_inner))
    encoded = hidden + low_back(matmul(low(jax.nn.gelu(inner_pre)), feed_outer))
    context = low(rms_norm(encoded, encoder_gain))
    cross_keys = low_both(matmul(context, cross_key))
    cross_values = low_both(matmul(context, cross_value))
    start_rows = jnp.broadcast_to(start_token[None, :], (SEQS, D))
    self_vals = low_both(matmul(low(rms_norm(start_rows, self_gain)), self_value))
    after_self = start_rows + low_back(matmul(self_vals, self_out))
    cross_queries = low_both(matmul(low(rms_norm(after_self, cross_gain)), cross_query))
    cross_scores = jnp.einsum('shd,thd->sht', cross_queries.reshape(SEQS, HEADS, HEAD), cross_keys.reshape(PACK, HEADS, HEAD), precision=highest)
    member = seq_ids[None, :] == jnp.arange(SEQS, dtype=jnp.int32)[:, None]
    cross_scores = jnp.where(member[:, None, :], cross_scores, masked_score)
    cross_probs = jax.nn.softmax(cross_scores, axis=-1)
    cross_attended = jnp.einsum('sht,thd->shd', cross_probs, cross_values.reshape(PACK, HEADS, HEAD), precision=highest).reshape(SEQS, D)
    after_cross = after_self + low_back(matmul(low_both(cross_attended), cross_out))
    second_pre = low_back(matmul(low(rms_norm(after_cross, second_gain)), second_inner))
    decoded = after_cross + low_back(matmul(low(jax.nn.gelu(second_pre)), second_outer))
    pooled = low_back(matmul(low(rms_norm(decoded, final_gain)), pooler_weight))
    return unit_length(pooled)

def forward(inputs, params, lengths, labels):
    groups = inputs.reshape(GROUPS, PACK, D)

    def one_group(group_rows, group_lengths):
        return embed_group(group_rows, group_lengths, params)
    saved_group = jax.checkpoint(one_group)

    def visit_group(running, pieces):
        return (running, saved_group(pieces[0], pieces[1]))
    _, embedded = lax.scan(visit_group, jnp.zeros((), jnp.float32), (groups, lengths))
    embedded = embedded.reshape(ALL_SEQS, D)
    similar = logit_scale * jnp.dot(embedded, embedded.T, precision=highest)
    diagonal = jnp.arange(ALL_SEQS, dtype=jnp.int32)[:, None] == jnp.arange(ALL_SEQS, dtype=jnp.int32)[None, :]
    similar = jnp.where(diagonal, masked_score, similar)
    log_norm = jax.nn.logsumexp(similar, axis=1)
    picked = jnp.take_along_axis(similar, labels[:, None].astype(jnp.int32), axis=1)[:, 0]
    return (jnp.mean(log_norm - picked), embedded)

def reference(tokens, lengths, labels, attention_gain, query_weight, key_weight, value_weight, attention_out, position_bias, feed_gain, feed_inner, feed_outer, encoder_gain, start_token, self_gain, self_value, self_out, cross_gain, cross_query, cross_key, cross_value, cross_out, second_gain, second_inner, second_outer, final_gain, pooler_weight):
    floats = (tokens, attention_gain, query_weight, key_weight, value_weight, attention_out, position_bias, feed_gain, feed_inner, feed_outer, encoder_gain, start_token, self_gain, self_value, self_out, cross_gain, cross_query, cross_key, cross_value, cross_out, second_gain, second_inner, second_outer, final_gain, pooler_weight)
    floats = tuple((item_value.astype(jnp.float32) for item_value in floats))

    def objective(*arrays):
        return forward(arrays[0], arrays[1:], lengths, labels)
    loss_value, pullback, embedded = jax.vjp(objective, *floats, has_aux=True)
    grads = pullback(jnp.ones((), jnp.float32))
    return (loss_value.reshape(1), embedded, grads[0], grads[1], grads[2], grads[3], grads[4], grads[5], grads[6], grads[7], grads[8], grads[9], grads[10], grads[11], grads[12], grads[13], grads[14], grads[15], grads[16], grads[17], grads[18], grads[19], grads[20], grads[21], grads[22], grads[23], grads[24])
```

```python
import functools
import math

import jax
import jax.numpy as jnp
from jax import lax
from jax.experimental import pallas as pl
from jax.experimental.pallas import tpu as pltpu
from jax.sharding import PartitionSpec as P

HEADS = 12
HEAD = 64
BUCKETS = 32
LANES = 128
far_apart = float(2**30)

eps_norm = 1e-06
masked_score = -1000000000.0
logit_scale = 20.0
bucket_limits = (12, 16, 23, 32, 46, 64, 91)
highest = lax.Precision.HIGHEST
low = jnp.bfloat16
wide = jnp.float32


def rms_norm(values, gain_vector):
    return (
        values
        * lax.rsqrt(jnp.mean(values * values, axis=-1, keepdims=True) + eps_norm)
        * gain_vector
    )


def unit_length(values):
    return values * lax.rsqrt(jnp.sum(values * values, axis=-1, keepdims=True) + eps_norm)


def bucket_of(offsets):
    upper_half = jnp.where(offsets > 0, 16, 0).astype(jnp.int32)
    distance = jnp.abs(offsets)
    far_bucket = 8 + sum(((distance >= threshold).astype(jnp.int32) for threshold in bucket_limits))
    return upper_half + jnp.where(distance < 8, distance, far_bucket)


def product(left_side, right_side):
    return jnp.dot(left_side, right_side, preferred_element_type=wide)


def back_product(left_side, right_side):
    return lax.dot_general(
        left_side, right_side, (((1,), (1,)), ((), ())), preferred_element_type=wide
    )


def weight_grad(left_side, right_side):
    return lax.dot_general(
        left_side, right_side, (((0,), (0,)), ((), ())), preferred_element_type=wide
    )


def norm_back(values, gain_vector, grad_rows):
    _, pullback = jax.vjp(rms_norm, values, gain_vector)
    return pullback(grad_rows)


def gelu_back(values, grad_rows):
    _, pullback = jax.vjp(jax.nn.gelu, values)
    return pullback(grad_rows)[0]


def segment_of(places, ends):
    return (places >= ends[0]).astype(jnp.int32) + (places >= ends[1]).astype(jnp.int32)


def block_rows(rows):
    return 256 if rows % 256 == 0 else rows


def table_sizes(size, pack):
    slack = LANES if size % LANES else 0
    reach = -(-(size + slack + 91) // LANES) * LANES
    lead = -(-(size + slack) // LANES) * LANES
    middle = -(-(pack - size) // LANES) * LANES
    return middle, reach, lead, middle + max(pack, reach)


def offset_biases(table, size, pack, shift):
    _, reach, lead, _ = table_sizes(size, pack)
    offsets = jnp.arange(lead + reach + LANES, dtype=jnp.int32) - (lead + LANES) - shift
    onehot = (
        bucket_of(offsets)[None, :] == jnp.arange(BUCKETS, dtype=jnp.int32)[:, None]
    ).astype(low)
    return weight_grad(table, onehot)[:, None, :]


def turned_biases(row, size, lead):
    spread = jnp.broadcast_to(row, (size, row.shape[1]))
    return pltpu.roll(spread, 0, 1, stride=1, stride_axis=0)[:, lead:]


def attend_kernel(
    place, q_ref, k_ref, v_ref, near_ref, attended_ref, total_ref, bias, key_side, value_side
):
    pair = pl.program_id(0)
    block = pl.program_id(1)
    pack = k_ref.shape[0]
    size = q_ref.shape[0]
    middle, reach, lead, width = table_sizes(size, pack)
    ends = (place[0], place[1])
    first = place[2] + block * size
    shift = place[3]

    @pl.when(block == 0)
    def _():
        places = lax.broadcasted_iota(jnp.int32, (pack, LANES), 0)
        lane = lax.broadcasted_iota(jnp.int32, (pack, LANES), 1)
        key_side[:, :LANES] = k_ref[...]
        key_side[:, LANES:] = (segment_of(places, ends) == lane).astype(wide).astype(low)
        value_side[:, :LANES] = v_ref[...]
        value_side[:, LANES:] = jnp.ones((pack, LANES), low)
        for half in range(2):
            row = near_ref[half]
            before = middle - LANES
            after = middle + reach
            bias[half, :, before:after] = turned_biases(row, size, lead)
            if before > 0:
                bias[half, :, :before] = jnp.broadcast_to(row[:, :1], (size, before))
            if after < width:
                bias[half, :, after:] = jnp.broadcast_to(row[:, -1:], (size, width - after))

    lane = lax.broadcasted_iota(jnp.int32, (size, LANES), 1)
    rows = first + lax.broadcasted_iota(jnp.int32, (size, LANES), 0)
    apart = jnp.where((segment_of(rows, ends) != lane) & (lane < 3), -far_apart, 0.0).astype(low)
    own = pl.ds(pl.multiple_of(block * size, 64), size)
    start = pl.multiple_of(middle - (first - shift), LANES)
    queries = q_ref[...]
    outputs = []
    totals = total_ref[own, :]
    for half in range(2):
        mine = (lane >= HEAD) if half else (lane < HEAD)
        query_side = jnp.concatenate(
            [jnp.where(mine, queries, jnp.zeros_like(queries)), apart], axis=1
        )
        scores = back_product(query_side, key_side[...]) + bias[half, :, pl.ds(start, pack)]
        top = jnp.max(scores, axis=1, keepdims=True)
        weights = jnp.exp(scores - top).astype(low)
        output = product(weights, value_side[...])
        total = output[:, LANES:]
        outputs.append(output[:, :LANES] / total)
        totals = jnp.where(lane == 2 * pair + half, top + jnp.log(total), totals)
    attended_ref[...] = jnp.where(lane < HEAD, outputs[0], outputs[1])
    total_ref[own, :] = totals


def attend(queries, all_keys, all_values, near, place):
    rows, width = queries.shape
    pack = all_keys.shape[0]
    size = block_rows(rows)
    _, _, _, columns = table_sizes(size, pack)
    pairs = width // LANES
    return pl.pallas_call(
        attend_kernel,
        name="attend",
        grid=(pairs, rows // size),
        in_specs=[
            pl.BlockSpec(memory_space=pltpu.SMEM),
            pl.BlockSpec((size, LANES), lambda p, i: (i, p)),
            pl.BlockSpec((pack, LANES), lambda p, i: (0, p)),
            pl.BlockSpec((pack, LANES), lambda p, i: (0, p)),
            pl.BlockSpec((2, 1, near.shape[2]), lambda p, i: (p, 0, 0)),
        ],
        out_specs=[
            pl.BlockSpec((size, LANES), lambda p, i: (i, p)),
            pl.BlockSpec((rows, LANES), lambda p, i: (0, 0)),
        ],
        out_shape=[
            jax.ShapeDtypeStruct((rows, width), wide),
            jax.ShapeDtypeStruct((rows, LANES), wide),
        ],
        scratch_shapes=[
            pltpu.VMEM((2, size, columns), wide),
            pltpu.VMEM((pack, 2 * LANES), low),
            pltpu.VMEM((pack, 2 * LANES), low),
        ],
        compiler_params=pltpu.CompilerParams(vmem_limit_bytes=48 * 2**20),
        cost_estimate=pl.CostEstimate(
            flops=8 * rows * pack * width * 2, bytes_accessed=16 * pack * width, transcendentals=0
        ),
    )(place, queries, all_keys, all_values, near)


def attend_back_kernel(
    place,
    q_ref,
    k_ref,
    v_ref,
    grad_ref,
    attended_ref,
    total_ref,
    near_ref,
    grad_q_ref,
    grad_k_ref,
    grad_v_ref,
    band_ref,
    far_ref,
    bias,
    key_side,
    value_side,
    keys_turned,
    grad_scores,
    grad_k_sum,
    grad_v_sum,
    band_sum,
):
    pair = pl.program_id(0)
    block = pl.program_id(1)
    blocks = pl.num_programs(1)
    pack = k_ref.shape[0]
    size = q_ref.shape[0]
    middle, reach, lead, width = table_sizes(size, pack)
    ends = (place[0], place[1])
    first = place[2] + block * size
    shift = place[3]

    @pl.when(block == 0)
    def _():
        places = lax.broadcasted_iota(jnp.int32, (pack, LANES), 0)
        lane = lax.broadcasted_iota(jnp.int32, (pack, LANES), 1)
        key_side[:, :LANES] = k_ref[...]
        ones = (segment_of(places, ends) == lane) | ((lane >= 3) & (lane < 9))
        key_side[:, LANES:] = ones.astype(wide).astype(low)
        value_side[:, :LANES] = v_ref[...]
        value_side[:, LANES:] = (lane < 6).astype(wide).astype(low)
        keys_turned[...] = k_ref[...].T
        for half in range(2):
            row = near_ref[half]
            before = middle - LANES
            after = middle + reach
            bias[half, before:after, :] = turned_biases(row, size, lead).T
            if before > 0:
                bias[half, :before, :] = jnp.broadcast_to(row[:, :1], (before, size))
            if after < width:
                bias[half, after:, :] = jnp.broadcast_to(row[:, -1:], (width - after, size))
        grad_scores[...] = jnp.zeros_like(grad_scores)
        grad_k_sum[...] = jnp.zeros_like(grad_k_sum)
        grad_v_sum[...] = jnp.zeros_like(grad_v_sum)
        band_sum[...] = jnp.zeros_like(band_sum)

    lane = lax.broadcasted_iota(jnp.int32, (size, LANES), 1)
    rows = first + lax.broadcasted_iota(jnp.int32, (size, LANES), 0)
    apart = jnp.where((segment_of(rows, ends) != lane) & (lane < 3), -far_apart, 0.0)
    start = pl.multiple_of(middle - (first - shift), LANES)
    near_rows = pl.ds(pl.multiple_of(first - shift, LANES), LANES + reach)
    queries = q_ref[...]
    grads = grad_ref[...]
    products = grads.astype(wide) * attended_ref[...]
    totals = total_ref[...]

    def in_parts(column, at):
        head = column.astype(low).astype(wide)
        body = (column - head).astype(low).astype(wide)
        tail = column - head - body
        return jnp.where(
            lane == at,
            head,
            jnp.where(lane == at + 1, body, jnp.where(lane == at + 2, tail, 0.0)),
        )

    query_grads = []
    for half in range(2):
        mine = (lane >= HEAD) if half else (lane < HEAD)
        row_term = jnp.sum(jnp.where(mine, products, 0.0), axis=1, keepdims=True)
        row_total = jnp.sum(
            jnp.where(lane == 2 * pair + half, totals, 0.0), axis=1, keepdims=True
        )
        query_part = jnp.where(mine, queries, jnp.zeros_like(queries))
        grad_part = jnp.where(mine, grads, jnp.zeros_like(grads))
        query_side = jnp.concatenate(
            [query_part, (apart - in_parts(row_total, 3 + 3 * half)).astype(low)], axis=1
        )
        grad_side = jnp.concatenate(
            [grad_part, (-in_parts(row_term, 3 * half)).astype(low)], axis=1
        )
        weights = jnp.exp(
            back_product(key_side[...], query_side) + bias[half, pl.ds(start, pack), :]
        )
        grad_block = (weights * back_product(value_side[...], grad_side)).astype(low)
        grad_scores[LANES : LANES + pack, :] = grad_block
        grad_v_sum[...] += product(weights.astype(low), grad_part)
        block_lane = jnp.where(lane == 8 * half + block, 1.0, 0.0).astype(low)
        grad_k_sum[...] += product(
            grad_block, jnp.concatenate([query_part, block_lane], axis=1)
        )
        query_grads.append(product(keys_turned[HEAD * half : HEAD * (half + 1), :], grad_block))
        band_sum[half] += grad_scores[near_rows, :].astype(wide)
    grad_q_ref[...] = jnp.concatenate(query_grads, axis=0).T.astype(grad_q_ref.dtype)

    @pl.when(block == blocks - 1)
    def _():
        grad_k_ref[...] = grad_k_sum[:, :LANES].astype(grad_k_ref.dtype)
        grad_v_ref[...] = grad_v_sum[...].astype(grad_v_ref.dtype)
        key = lax.broadcasted_iota(jnp.int32, (pack, LANES), 0)
        which = lax.broadcasted_iota(jnp.int32, (pack, LANES), 1) % 8
        begin = place[2] - shift + size * which
        sums = grad_k_sum[:, LANES:]
        below = jnp.sum(jnp.where(key < begin - LANES, sums, 0.0), axis=0, keepdims=True)
        above = jnp.sum(jnp.where(key >= begin + reach, sums, 0.0), axis=0, keepdims=True)
        far_ref[0] = jnp.concatenate([below, above, jnp.zeros((6, LANES), wide)], axis=0)
        columns = band_ref.shape[2]
        mirror = (
            lax.broadcasted_iota(jnp.int32, (size, columns), 0)
            + lax.broadcasted_iota(jnp.int32, (size, columns), 1)
            == size - 1
        ).astype(wide)
        for half in range(2):
            flipped = jnp.dot(
                band_sum[half], mirror, precision=highest, preferred_element_type=wide
            )
            turned = pltpu.roll(flipped, 0, 1, stride=1, stride_axis=0)
            band_ref[0, half : half + 1, :] = jnp.sum(turned, axis=0, keepdims=True)
        band_ref[0, 2:, :] = jnp.zeros((6, columns), wide)


def attend_back(queries, all_keys, all_values, grads, attended, totals, near, place):
    rows, width = queries.shape
    pack = all_keys.shape[0]
    size = block_rows(rows)
    _, reach, _, columns = table_sizes(size, pack)
    band = -(-(size + LANES + reach) // LANES) * LANES
    pairs = width // LANES

    def own(p, i):
        return (i, p)

    def every(p, i):
        return (0, p)

    grad_q, grad_k, grad_v, band_sums, far_sums = pl.pallas_call(
        attend_back_kernel,
        name="attend_back",
        grid=(pairs, rows // size),
        in_specs=[
            pl.BlockSpec(memory_space=pltpu.SMEM),
            pl.BlockSpec((size, LANES), own),
            pl.BlockSpec((pack, LANES), every),
            pl.BlockSpec((pack, LANES), every),
            pl.BlockSpec((size, LANES), own),
            pl.BlockSpec((size, LANES), own),
            pl.BlockSpec((size, LANES), lambda p, i: (i, 0)),
            pl.BlockSpec((2, 1, near.shape[2]), lambda p, i: (p, 0, 0)),
        ],
        out_specs=[
            pl.BlockSpec((size, LANES), own),
            pl.BlockSpec((pack, LANES), every),
            pl.BlockSpec((pack, LANES), every),
            pl.BlockSpec((1, 8, band), lambda p, i: (p, 0, 0)),
            pl.BlockSpec((1, 8, LANES), lambda p, i: (p, 0, 0)),
        ],
        out_shape=[
            jax.ShapeDtypeStruct((rows, width), low),
            jax.ShapeDtypeStruct((pack, width), low),
            jax.ShapeDtypeStruct((pack, width), low),
            jax.ShapeDtypeStruct((pairs, 8, band), wide),
            jax.ShapeDtypeStruct((pairs, 8, LANES), wide),
        ],
        scratch_shapes=[
            pltpu.VMEM((2, columns, size), wide),
            pltpu.VMEM((pack, 2 * LANES), low),
            pltpu.VMEM((pack, 2 * LANES), low),
            pltpu.VMEM((LANES, pack), low),
            pltpu.VMEM((LANES + pack + reach, size), low),
            pltpu.VMEM((pack, 2 * LANES), wide),
            pltpu.VMEM((pack, LANES), wide),
            pltpu.VMEM((2, LANES + reach, size), wide),
        ],
        compiler_params=pltpu.CompilerParams(vmem_limit_bytes=56 * 2**20),
        cost_estimate=pl.CostEstimate(
            flops=20 * rows * pack * width * 2, bytes_accessed=16 * pack * width, transcendentals=0
        ),
    )(place, queries, all_keys, all_values, grads, attended, totals, near)
    offsets = jnp.arange(band, dtype=jnp.int32) - (size - 1) - LANES - place[3]
    buckets = jnp.arange(BUCKETS, dtype=jnp.int32)
    onehot = (bucket_of(offsets)[:, None] == buckets[None, :]).astype(wide)
    near_grad = jnp.dot(
        band_sums[:, :2].reshape(HEADS, band), onehot, precision=highest, preferred_element_type=wide
    )
    far_grad = jnp.sum(far_sums[:, :2, :16].reshape(pairs, 2, 2, 8), axis=3)
    far_grad = jnp.transpose(far_grad, (0, 2, 1)).reshape(HEADS, 2)
    grad_table = near_grad + far_grad[:, :1] * (buckets == 15) + far_grad[:, 1:] * (buckets == 31)
    return grad_q, grad_k, grad_v, grad_table.T


SEQ_ROWS = 8
HEAD_ROWS = 16
MESH = pl.DeviceIdType.MESH


def rms_factor(values):
    return lax.rsqrt(jnp.mean(values * values, axis=-1, keepdims=True) + eps_norm)


def rms_back(values, gain_row, grad_rows):
    factor = rms_factor(values)
    scaled = gain_row * grad_rows
    inner = jnp.mean(scaled * values, axis=-1, keepdims=True)
    return (
        factor * scaled - values * (factor * factor * factor) * inner,
        jnp.sum(grad_rows * values * factor, axis=0, keepdims=True),
    )


gelu_scale = 0.7978845608028654


def gelu_value(values):
    return 0.5 * values * (
        1.0 + jnp.tanh(gelu_scale * (values + 0.044715 * values * values * values))
    )


def gelu_slope(values):
    square = values * values
    bent = jnp.tanh(gelu_scale * (values + 0.044715 * square * values))
    return 0.5 * (1.0 + bent) + 0.5 * values * (1.0 - bent * bent) * gelu_scale * (
        1.0 + 0.134145 * square
    )


def decoder_kernel(
    groups,
    members,
    seqs,
    place,
    context_ref,
    third_ref,
    gains_ref,
    target_ref,
    embedded_ref,
    loss_ref,
    grad_context_ref,
    pieces_ref,
    mixed_ref,
    starts_ref,
    totals_ref,
    weights,
    everyone,
    shared,
    similar_ref,
    weight_sem,
    every_send,
    every_recv,
    share_send,
    share_recv,
):
    rows, width = context_ref.shape
    count, _, _ = third_ref.shape
    unit = width // count
    blocks = 4 * unit
    group = lax.axis_index("batch")
    member = lax.axis_index("seq")
    seq_total = groups * seqs

    barrier = pltpu.get_barrier_semaphore()
    for step in range(1, groups):
        pl.semaphore_signal(
            barrier,
            inc=1,
            device_id={"batch": lax.rem(group + step, groups)},
            device_id_type=MESH,
        )
    for step in range(1, members):
        pl.semaphore_signal(
            barrier,
            inc=1,
            device_id={"seq": lax.rem(member + step, members)},
            device_id_type=MESH,
        )

    sizes = [unit] * 7 + [unit] * 4 + [blocks]
    firsts = [sum(sizes[:i]) for i in range(len(sizes))]
    copies = [
        pltpu.make_async_copy(
            third_ref.at[:, first : first + size, :],
            weights.at[:, first : first + size, :],
            weight_sem.at[i],
        )
        for i, (first, size) in enumerate(zip(firsts, sizes))
    ]
    for copy in copies:
        copy.start()

    def weight(i):
        return weights[:, firsts[i] : firsts[i] + unit, :].reshape(width, width)

    def outer_weight(j):
        per = count // 4
        return weights[per * j : per * (j + 1), firsts[11] : firsts[11] + blocks, :].reshape(
            width, width
        )

    gain = {
        name: gains_ref[i : i + 1, :]
        for i, name in enumerate(
            ("attention", "feed", "encoder", "start", "own", "cross", "second", "final")
        )
    }
    context = context_ref[...]

    start = jnp.broadcast_to(gain["start"], (SEQ_ROWS, width))
    self_in = (start * rms_factor(start) * gain["own"]).astype(low)
    copies[0].wait()
    self_vals = product(self_in, weight(0)).astype(low)
    copies[1].wait()
    after_self = start + product(self_vals, weight(1))
    cross_in = (after_self * rms_factor(after_self) * gain["cross"]).astype(low)
    copies[2].wait()
    cross_query = product(cross_in, weight(2))
    head_row = lax.broadcasted_iota(jnp.int32, (HEAD_ROWS, width), 0)
    head_mask = head_row == lax.broadcasted_iota(jnp.int32, (HEAD_ROWS, width), 1) // HEAD
    query_heads = jnp.where(
        head_mask, jnp.broadcast_to(cross_query[:1], (HEAD_ROWS, width)), 0.0
    ).astype(low)
    copies[3].wait()
    key_rows = back_product(query_heads, weight(3)).astype(low)

    many = seqs * HEAD_ROWS
    scores = back_product(key_rows, context)
    scores = jnp.concatenate([scores] * seqs, axis=0)
    places = member * rows + lax.broadcasted_iota(jnp.int32, (many, rows), 1)
    row_seq = lax.broadcasted_iota(jnp.int32, (many, rows), 0) // HEAD_ROWS
    inside = segment_of(places, (place[0], place[1])) == row_seq
    scores = jnp.where(inside, scores, masked_score)
    part_top = jnp.max(scores, axis=1, keepdims=True)
    part_weights = jnp.where(inside, jnp.exp(scores - part_top), 0.0).astype(low)
    part_total = jnp.sum(part_weights.astype(wide), axis=1, keepdims=True)
    lane = lax.broadcasted_iota(jnp.int32, (many, LANES), 1)
    shared[0, :, :width] = product(part_weights, context)
    shared[0, :, width:] = jnp.where(lane == 0, part_top, part_total)

    pl.semaphore_wait(barrier, groups - 1 + members - 1)
    for step in range(1, members):
        pltpu.make_async_remote_copy(
            src_ref=shared.at[0],
            dst_ref=shared.at[step],
            send_sem=share_send.at[step - 1],
            recv_sem=share_recv.at[step - 1],
            device_id={"seq": lax.rem(member + step, members)},
            device_id_type=MESH,
        ).start()
    for step in range(1, members):
        pltpu.make_async_remote_copy(
            src_ref=shared.at[0],
            dst_ref=shared.at[step],
            send_sem=share_send.at[step - 1],
            recv_sem=share_recv.at[step - 1],
            device_id={"seq": lax.rem(member + step, members)},
            device_id_type=MESH,
        ).wait()
    top = shared[0, :, width : width + 1]
    for step in range(1, members):
        top = jnp.maximum(top, shared[step, :, width : width + 1])
    total = jnp.zeros((many, 1), wide)
    mixed = jnp.zeros((many, width), wide)
    for step in range(members):
        scale = jnp.exp(shared[step, :, width : width + 1] - top)
        total = total + shared[step, :, width + 1 : width + 2] * scale
        mixed = mixed + shared[step, :, :width] * scale
    mixed = (mixed / total).astype(low)
    mixed_ref[...] = mixed
    log_total = top + jnp.log(total)

    def by_seq(parts):
        row = lax.broadcasted_iota(jnp.int32, (SEQ_ROWS, width), 0)
        joined = jnp.zeros((SEQ_ROWS, width), wide)
        for i, part in enumerate(parts):
            joined = jnp.where(row == i, part, joined)
        return joined

    copies[4].wait()
    spread = product(mixed, weight(4))
    cross_attended = by_seq(
        [
            jnp.sum(
                jnp.where(head_mask, spread[HEAD_ROWS * i : HEAD_ROWS * (i + 1)], 0.0),
                axis=0,
                keepdims=True,
            )
            for i in range(seqs)
        ]
    )
    cross_low = cross_attended.astype(low)
    copies[5].wait()
    after_cross = after_self + product(cross_low, weight(5))
    second_in = (after_cross * rms_factor(after_cross) * gain["second"]).astype(low)
    for i in range(7, 12):
        copies[i].wait()
    second_pre = [product(second_in, weight(7 + j)) for j in range(4)]
    second_act = [gelu_value(second_pre[j]).astype(low) for j in range(4)]
    decoded = after_cross
    for j in range(4):
        decoded = decoded + product(second_act[j], outer_weight(j))
    pooled_in = (decoded * rms_factor(decoded) * gain["final"]).astype(low)
    copies[6].wait()
    pooled = product(pooled_in, weight(6))
    size = lax.rsqrt(jnp.sum(pooled * pooled, axis=-1, keepdims=True) + eps_norm)
    embedded = pooled * size
    embedded_ref[...] = embedded

    everyone[0] = embedded
    sends = []
    for step in range(1, groups):
        sends.append(
            pltpu.make_async_remote_copy(
                src_ref=everyone.at[0],
                dst_ref=everyone.at[step],
                send_sem=every_send,
                recv_sem=every_recv,
                device_id={"batch": lax.rem(group + step, groups)},
                device_id_type=MESH,
            )
        )
        sends[-1].start()
    arrival = pltpu.make_async_remote_copy(
        src_ref=everyone.at[pl.ds(1, groups - 1)],
        dst_ref=everyone.at[pl.ds(1, groups - 1)],
        send_sem=every_send,
        recv_sem=every_recv,
        device_id={"batch": lax.rem(group + 1, groups)},
        device_id_type=MESH,
    )
    arrival.wait_recv()
    arrival.wait_send()
    all_rows = everyone[...].reshape(groups * SEQ_ROWS, width)
    number = groups * SEQ_ROWS
    row = lax.broadcasted_iota(jnp.int32, (number, number), 0)
    column = lax.broadcasted_iota(jnp.int32, (number, number), 1)
    row_valid = row % SEQ_ROWS < seqs
    valid = row_valid & (column % SEQ_ROWS < seqs)
    similar = logit_scale * lax.dot_general(
        all_rows,
        all_rows,
        (((1,), (1,)), ((), ())),
        precision=highest,
        preferred_element_type=wide,
    )
    similar = jnp.where(valid & (row != column), similar, masked_score)
    best = jnp.max(similar, axis=1, keepdims=True)
    log_norm = best + jnp.log(jnp.sum(jnp.exp(similar - best), axis=1, keepdims=True))
    row_group = lax.rem(group - row // SEQ_ROWS + groups, groups)
    column_group = lax.rem(group - column // SEQ_ROWS + groups, groups)
    row_number = row_group * seqs + row % SEQ_ROWS
    column_number = column_group * seqs + column % SEQ_ROWS
    label = jnp.max(
        jnp.where(
            lax.broadcasted_iota(jnp.int32, (number, target_ref.shape[1]), 1)
            == row_number[:, : target_ref.shape[1]],
            target_ref[:1, :],
            -1.0,
        ),
        axis=1,
        keepdims=True,
    )
    target = (column_number.astype(wide) == label) & valid
    picked = jnp.sum(jnp.where(target, similar, 0.0), axis=1, keepdims=True)
    losses = jnp.where(row_valid[:, :1], log_norm - picked, 0.0)
    loss_ref[...] = jnp.broadcast_to(
        jnp.sum(losses, axis=0, keepdims=True) / seq_total, loss_ref.shape
    )
    grad_similar = jnp.where(
        valid, (jnp.exp(similar - log_norm) - target.astype(wide)) / seq_total, 0.0
    )
    similar_ref[...] = grad_similar + grad_similar.T
    grad_embedded = logit_scale * jnp.dot(
        similar_ref[:SEQ_ROWS, :], all_rows, precision=highest, preferred_element_type=wide
    )

    grad_pooled = (
        size
        * (grad_embedded - embedded * jnp.sum(embedded * grad_embedded, axis=-1, keepdims=True))
    ).astype(low)
    grad_decoded, grad_final_gain = rms_back(
        decoded, gain["final"], back_product(grad_pooled, weight(6))
    )
    grad_second_out = grad_decoded.astype(low)
    grad_second_pre = [
        (gelu_slope(second_pre[j]) * back_product(grad_second_out, outer_weight(j))).astype(low)
        for j in range(4)
    ]
    grad_second_in = back_product(grad_second_pre[0], weight(7))
    for j in range(1, 4):
        grad_second_in = grad_second_in + back_product(grad_second_pre[j], weight(7 + j))
    grad_after_cross, grad_second_gain = rms_back(after_cross, gain["second"], grad_second_in)
    grad_after_cross = grad_after_cross + grad_decoded
    grad_cross_branch = grad_after_cross.astype(low)
    grad_cross_att = back_product(grad_cross_branch, weight(5)).astype(low)
    grad_cross_wide = grad_cross_att.astype(wide)
    grad_heads = jnp.concatenate(
        [
            jnp.where(
                head_mask,
                jnp.broadcast_to(grad_cross_wide[i : i + 1], (HEAD_ROWS, width)),
                0.0,
            )
            for i in range(seqs)
        ],
        axis=0,
    )
    attended_heads = jnp.concatenate(
        [
            jnp.broadcast_to(cross_attended[i : i + 1], (HEAD_ROWS, width))
            for i in range(seqs)
        ],
        axis=0,
    )
    row_terms = jnp.sum(grad_heads * attended_heads, axis=1, keepdims=True)
    value_rows = back_product(grad_heads.astype(low), weight(4)).astype(low)
    probs = jnp.where(inside, jnp.exp(scores - log_total), 0.0)
    grad_scores = (probs * (back_product(value_rows, context) - row_terms)).astype(low)
    grad_context_ref[...] = weight_grad(
        jnp.concatenate([grad_scores, probs.astype(low)], axis=0),
        jnp.concatenate([key_rows] * seqs + [value_rows], axis=0),
    )
    key_sums = product(grad_scores, context)
    sums = key_sums[:HEAD_ROWS]
    for i in range(1, seqs):
        sums = sums + key_sums[HEAD_ROWS * i : HEAD_ROWS * (i + 1)]
    first_member = jnp.where(member == 0, 1.0, 0.0)
    totals_ref[:HEAD_ROWS, :] = sums
    totals_ref[HEAD_ROWS:, :] = first_member * by_seq(
        [jnp.sum(grad_after_cross, axis=0, keepdims=True), grad_final_gain, grad_second_gain]
    )
    for i, piece in enumerate(
        [cross_low, second_in]
        + second_act
        + [pooled_in, grad_cross_branch]
        + grad_second_pre
        + [grad_second_out, grad_pooled, grad_cross_att]
    ):
        pieces_ref[i] = piece.astype(wide)
    for i, piece in enumerate([start, self_in, self_vals, after_self, cross_in, cross_query]):
        starts_ref[i : i + 1, :] = piece[:1].astype(wide)
    starts_ref[6:, :] = jnp.zeros((2, width), wide)


def decoder_step(context, third, gains, labels, place, groups, members, seqs):
    rows, width = context.shape
    everything = pl.BlockSpec(memory_space=pltpu.VMEM)
    labels = jnp.pad(labels.astype(wide)[None], ((0, 7), (0, LANES - labels.shape[0])))
    number = groups * SEQ_ROWS
    return pl.pallas_call(
        functools.partial(decoder_kernel, groups, members, seqs),
        name="decoder",
        in_specs=[
            pl.BlockSpec(memory_space=pltpu.SMEM),
            everything,
            pl.BlockSpec(memory_space=pl.ANY),
            everything,
            everything,
        ],
        out_specs=[everything] * 7,
        out_shape=[
            jax.ShapeDtypeStruct((SEQ_ROWS, width), wide),
            jax.ShapeDtypeStruct((8, LANES), wide),
            jax.ShapeDtypeStruct((rows, width), wide),
            jax.ShapeDtypeStruct((15, SEQ_ROWS, width), wide),
            jax.ShapeDtypeStruct((seqs * HEAD_ROWS, width), low),
            jax.ShapeDtypeStruct((8, width), wide),
            jax.ShapeDtypeStruct((HEAD_ROWS + SEQ_ROWS, width), wide),
        ],
        scratch_shapes=[
            pltpu.VMEM(third.shape, low),
            pltpu.VMEM((groups, SEQ_ROWS, width), wide),
            pltpu.VMEM((members, seqs * HEAD_ROWS, width + LANES), wide),
            pltpu.VMEM((number, number), wide),
            pltpu.SemaphoreType.DMA((12,)),
            pltpu.SemaphoreType.DMA,
            pltpu.SemaphoreType.DMA,
            pltpu.SemaphoreType.DMA((max(members - 1, 1),)),
            pltpu.SemaphoreType.DMA((max(members - 1, 1),)),
        ],
        compiler_params=pltpu.CompilerParams(
            collective_id=0, has_side_effects=True, vmem_limit_bytes=56 * 2**20
        ),
        cost_estimate=pl.CostEstimate(
            flops=2 * rows * width * 300, bytes_accessed=2 * third.size, transcendentals=0
        ),
    )(place, context, third, gains, labels)


def seq_exchange(value):
    count = lax.axis_size("seq")
    return [value] + [
        lax.ppermute(value, "seq", [(i, (i - step) % count) for i in range(count)])
        for step in range(1, count)
    ]


def in_place_order(pieces):
    count = len(pieces)
    me = lax.axis_index("seq")
    ordered = []
    for place in range(count):
        chosen = pieces[0]
        for step in range(1, count):
            chosen = jnp.where((place - me) % count == step, pieces[step], chosen)
        ordered.append(chosen)
    return jnp.concatenate(ordered, axis=0)


def seq_sum(value):
    count = lax.axis_size("seq")
    total = value.astype(wide)
    for step in range(1, count):
        total = total + lax.ppermute(
            value, "seq", [(i, (i - step) % count) for i in range(count)]
        ).astype(wide)
    return total


def seq_scatter(value, rows):
    count = lax.axis_size("seq")
    me = lax.axis_index("seq")
    total = lax.dynamic_slice_in_dim(value, me * rows, rows)
    for step in range(1, count):
        other = lax.dynamic_slice_in_dim(value, (me + step) % count * rows, rows)
        total = total + lax.ppermute(
            other.astype(low), "seq", [(i, (i + step) % count) for i in range(count)]
        ).astype(wide)
    return total


def in_blocks(gathered, sizes):
    count, _, width = gathered.shape
    join = 16 // math.gcd(16, sizes[0])
    if join == 1:
        return gathered
    pieces, at = [], 0
    for size in sizes:
        piece = gathered[:, at : at + size].reshape(count // join, join * size, width)
        pieces.append(piece)
        at += size
    return jnp.concatenate(pieces, axis=1)


def column_blocks(weight, model_width):
    rows, columns = weight.shape
    blocks = columns // model_width
    return jnp.transpose(weight.reshape(rows, blocks, model_width), (1, 0, 2)).reshape(
        blocks * rows, model_width
    )


def shards(
    tokens,
    lengths,
    labels,
    attention_gain,
    query_weight,
    key_weight,
    value_weight,
    attention_out,
    position_bias,
    feed_gain,
    feed_inner,
    feed_outer,
    encoder_gain,
    start_token,
    self_gain,
    self_value,
    self_out,
    cross_gain,
    cross_query,
    cross_key,
    cross_value,
    cross_out,
    second_gain,
    second_inner,
    second_outer,
    final_gain,
    pooler_weight,
):
    rows, width = tokens.shape
    part = query_weight.shape[0]
    share = feed_outer.shape[0]
    groups = lax.axis_size("batch")
    members = lax.axis_size("seq")
    blocks = feed_inner.shape[1] // width
    pack = rows * members
    seqs = lengths.shape[1]
    group = lax.axis_index("batch")
    member = lax.axis_index("seq")
    own_first = member * rows
    ends = jnp.cumsum(lengths[0])
    place = jnp.stack(
        [ends[0], ends[1], own_first, own_first % LANES]
    ).astype(jnp.int32)

    vectors = jnp.stack(
        [
            attention_gain,
            feed_gain,
            encoder_gain,
            start_token,
            self_gain,
            cross_gain,
            second_gain,
            final_gain,
        ],
        axis=1,
    )
    bias_row = jnp.pad(position_bias.reshape(1, -1), ((0, part - 1), (0, 0)))
    extra = jnp.concatenate([vectors, bias_row], axis=1)
    extra = jnp.pad(extra, ((0, 0), (0, LANES - extra.shape[1])))
    first_part = jnp.concatenate([query_weight, key_weight, value_weight, extra], axis=1)
    first = lax.all_gather(first_part, "batch", axis=0, tiled=True)
    second_part = jnp.concatenate(
        [attention_out, column_blocks(feed_inner, width), feed_outer], axis=0
    )
    second = lax.all_gather(second_part, "batch", axis=0, tiled=False)
    third_part = jnp.concatenate(
        [
            self_value,
            self_out,
            cross_query,
            cross_key,
            cross_value,
            cross_out,
            pooler_weight,
            column_blocks(second_inner, width),
            second_outer,
        ],
        axis=0,
    )
    third = lax.all_gather(third_part, "batch", axis=0, tiled=False)

    def square(gathered, at):
        return gathered[:, at : at + part].reshape(groups * part, width)

    def tall(gathered, at):
        return gathered[:, at : at + share].reshape(groups * share, width)

    gains = first[:, 3 * width : 3 * width + 8].astype(wide).T
    (
        attention_gain_full,
        feed_gain_full,
        encoder_gain_full,
        start_full,
        self_gain_full,
        cross_gain_full,
        second_gain_full,
        final_gain_full,
    ) = [gains[i] for i in range(8)]
    table = first.reshape(groups, part, -1)[
        :, 0, 3 * width + 8 : 3 * width + 8 + position_bias.size
    ].reshape(BUCKETS, HEADS)
    query_full = first[:, :width]
    key_value_full = first[:, width : 3 * width]

    all_tokens = in_place_order(seq_exchange(tokens))
    inputs = tokens.astype(wide)
    normed_all = rms_norm(all_tokens.astype(wide), attention_gain_full).astype(low)
    normed = rms_norm(inputs, attention_gain_full).astype(low)
    queries = product(normed, query_full).astype(low)
    keys_values = product(normed_all, key_value_full).astype(low)
    all_keys = keys_values[:, :width]
    all_values = keys_values[:, width:]
    near = offset_biases(table, block_rows(rows), pack, place[3])
    attended, totals = attend(queries, all_keys, all_values, near, place)
    attended_low = attended.astype(low)
    out_full = square(second, 0)
    hidden = inputs + product(attended_low, out_full)

    inner_in = rms_norm(hidden, feed_gain_full).astype(low)
    inner_full = [square(second, part * (1 + j)) for j in range(blocks)]
    outer_full = tall(second, part * (1 + blocks)).reshape(blocks, -1, width)
    inner_pre = [product(inner_in, inner_full[j]) for j in range(blocks)]
    inner_act = [jax.nn.gelu(inner_pre[j]).astype(low) for j in range(blocks)]
    encoded = hidden
    for j in range(blocks):
        encoded = encoded + product(inner_act[j], outer_full[j])
    context = rms_norm(encoded, encoder_gain_full).astype(low)

    third_sizes = [part] * (7 + blocks) + [share]
    (
        embedded,
        loss,
        grad_context,
        pieces,
        mixed,
        starts,
        decoder_totals,
    ) = decoder_step(
        context, in_blocks(third, third_sizes), gains, labels, place, groups, members, seqs
    )
    contrastive_loss = loss[0, :1]
    embedded = embedded[:seqs]
    decoder_rows = jnp.concatenate(
        [
            pieces[:, :seqs].astype(low).reshape(-1, width),
            mixed.reshape(seqs, HEAD_ROWS, width)[:, :HEADS].reshape(-1, width),
        ],
        axis=0,
    )
    start_row, self_in, self_vals, after_self, cross_in, cross_query_row = [
        starts[i : i + 1] for i in range(6)
    ]
    head_of = jnp.arange(width, dtype=jnp.int32) // HEAD
    head_mask = head_of[None, :] == jnp.arange(HEADS, dtype=jnp.int32)[:, None]

    count = decoder_rows.shape[0]
    decoder_rows = jnp.pad(decoder_rows, ((0, -count % 16), (0, 0)))

    grad_encoded, grad_encoder_gain = norm_back(encoded, encoder_gain_full, grad_context)
    grad_feed_branch = grad_encoded.astype(low)
    grad_inner_pre = [
        gelu_back(inner_pre[j], back_product(grad_feed_branch, outer_full[j])).astype(low)
        for j in range(blocks)
    ]
    grad_inner_in = sum(back_product(grad_inner_pre[j], inner_full[j]) for j in range(blocks))
    grad_hidden, grad_feed_gain = norm_back(hidden, feed_gain_full, grad_inner_in)
    grad_hidden = grad_hidden + grad_encoded
    grad_attn_branch = grad_hidden.astype(low)
    second_grads = jnp.concatenate(
        [weight_grad(attended_low, grad_attn_branch).astype(low).reshape(groups, part, width)]
        + [
            weight_grad(inner_in, grad_inner_pre[j]).astype(low).reshape(groups, part, width)
            for j in range(blocks)
        ]
        + [
            jnp.concatenate(
                [weight_grad(inner_act[j], grad_feed_branch).astype(low) for j in range(blocks)],
                axis=0,
            ).reshape(groups, share, width)
        ],
        axis=1,
    )

    sums = lax.psum(
        jnp.concatenate(
            [decoder_totals[:HEADS], decoder_totals[HEAD_ROWS : HEAD_ROWS + 3], grad_encoder_gain[None]],
            axis=0,
        ),
        ("batch", "seq"),
    )

    grad_attended = back_product(grad_attn_branch, out_full).astype(low)
    grad_attended, second_grads = lax.optimization_barrier((grad_attended, second_grads))
    second_sums = lax.psum_scatter(second_grads, "batch", scatter_dimension=0, tiled=False)
    grad_query_low, grad_key_low, grad_value_low, grad_table = attend_back(
        queries, all_keys, all_values, grad_attended, attended, totals, near, place
    )
    first_grads = jnp.concatenate(
        [
            weight_grad(normed, grad_query_low).astype(low).reshape(groups, part, width),
            weight_grad(normed_all, grad_key_low).astype(low).reshape(groups, part, width),
            weight_grad(normed_all, grad_value_low).astype(low).reshape(groups, part, width),
        ],
        axis=1,
    )
    decoder_rows, grad_query_low = lax.optimization_barrier((decoder_rows, grad_query_low))
    decoder_rows = lax.all_gather(decoder_rows, "batch", axis=0, tiled=False)
    first_sums = lax.psum_scatter(first_grads, "batch", scatter_dimension=0, tiled=False)
    grad_normed_all = back_product(grad_key_low, key_value_full[:, :width]) + back_product(
        grad_value_low, key_value_full[:, width:]
    )
    grad_normed = seq_scatter(grad_normed_all, rows) + back_product(grad_query_low, query_full)
    grad_inputs, grad_attention_gain = norm_back(inputs, attention_gain_full, grad_normed)
    grad_inputs = grad_inputs + grad_hidden
    table_row = jnp.pad(grad_table.reshape(1, -1), ((0, 0), (0, width - grad_table.size)))
    last_sums = lax.psum(
        jnp.concatenate([grad_attention_gain[None], grad_feed_gain[None], table_row], axis=0),
        ("batch", "seq"),
    )

    self_value_full = square(third, 0)
    self_out_full = square(third, part)
    cross_query_full = square(third, 2 * part)
    cross_key_full = square(third, 3 * part)
    grad_cross_query_row = jnp.sum(
        jnp.where(head_mask, product(sums[:HEADS].astype(low), cross_key_full), 0.0),
        axis=0,
        keepdims=True,
    ).astype(low)
    grad_after_self, grad_cross_gain = norm_back(
        after_self, cross_gain_full, back_product(grad_cross_query_row, cross_query_full)
    )
    grad_after_self = grad_after_self + sums[HEADS : HEADS + 1]
    grad_self_branch = grad_after_self.astype(low)
    grad_self_vals = back_product(grad_self_branch, self_out_full).astype(low)
    grad_start, grad_self_gain = norm_back(
        start_row, self_gain_full, back_product(grad_self_vals, self_value_full)
    )
    grad_start = (grad_start + grad_after_self)[0]

    def mine(values, size=part):
        return lax.dynamic_slice_in_dim(values, group * size, size, values.ndim - 1)

    def outer(left_side, right_side):
        return mine(left_side).astype(wide).T * right_side.astype(wide)

    def every_row(at, size=seqs):
        return decoder_rows[:, at : at + size].reshape(groups * size, width)

    at = 0
    cross_rows = every_row(0)
    second_in_rows = every_row(seqs)
    act_rows = decoder_rows[:, 2 * seqs : (2 + blocks) * seqs].reshape(
        groups, blocks, seqs, width
    )
    act_rows = jnp.transpose(act_rows, (0, 2, 1, 3)).reshape(groups * seqs, blocks * width)
    at = (2 + blocks) * seqs
    pooled_rows = every_row(at)
    branch_rows = every_row(at + seqs)
    pre_rows = decoder_rows[:, at + 2 * seqs : at + (2 + blocks) * seqs].reshape(
        groups, blocks, seqs, width
    )
    pre_rows = jnp.transpose(pre_rows, (0, 2, 1, 3)).reshape(groups * seqs, blocks * width)
    at = at + (2 + blocks) * seqs
    out_rows = every_row(at)
    grad_pooled_rows = every_row(at + seqs)
    att_rows = every_row(at + 2 * seqs)
    context_rows = every_row(at + 3 * seqs, seqs * HEADS)
    att_heads = jnp.where(
        head_mask[None], att_rows[:, None, :], jnp.zeros((), low)
    ).reshape(-1, width)

    second_sums = seq_sum(second_sums)
    first_sums = seq_sum(first_sums)
    inner_sums = jnp.transpose(
        second_sums[part : part * (1 + blocks)].reshape(blocks, part, width), (1, 0, 2)
    ).reshape(part, blocks * width)
    key_totals = mine(sums[:HEADS])
    return (
        contrastive_loss,
        embedded,
        grad_inputs,
        mine(last_sums[0]),
        first_sums[:part],
        first_sums[part : 2 * part],
        first_sums[2 * part :],
        second_sums[:part],
        mine(last_sums[2, : BUCKETS * HEADS], BUCKETS * HEADS // groups).reshape(-1, HEADS),
        mine(last_sums[1]),
        inner_sums,
        second_sums[part * (1 + blocks) :],
        mine(sums[HEADS + 3]),
        mine(grad_start),
        mine(grad_self_gain),
        outer(self_in, grad_self_vals),
        outer(self_vals, grad_self_branch),
        mine(grad_cross_gain),
        outer(cross_in, grad_cross_query_row),
        jnp.repeat(key_totals.T, HEAD, axis=1) * cross_query_row.astype(wide),
        weight_grad(mine(context_rows), att_heads),
        weight_grad(mine(cross_rows), branch_rows),
        mine(sums[HEADS + 2]),
        weight_grad(mine(second_in_rows), pre_rows),
        weight_grad(mine(act_rows, share), out_rows),
        mine(sums[HEADS + 1]),
        weight_grad(mine(pooled_rows), grad_pooled_rows),
    )


def solution(mesh):
    placed = (
        P(("batch", "seq"), None),
        P("batch", None),
        P(),
        P("batch"),
        P("batch", None),
        P("batch", None),
        P("batch", None),
        P("batch", None),
        P("batch", None),
        P("batch"),
        P("batch", None),
        P("batch", None),
        P("batch"),
        P("batch"),
        P("batch"),
        P("batch", None),
        P("batch", None),
        P("batch"),
        P("batch", None),
        P("batch", None),
        P("batch", None),
        P("batch", None),
        P("batch"),
        P("batch", None),
        P("batch", None),
        P("batch"),
        P("batch", None),
    )
    return jax.shard_map(
        shards,
        mesh=mesh,
        in_specs=placed,
        out_specs=(
            P(),
            P("batch", None),
            P(("batch", "seq"), None),
            P("batch"),
            P("batch", None),
            P("batch", None),
            P("batch", None),
            P("batch", None),
            P("batch", None),
            P("batch"),
            P("batch", None),
            P("batch", None),
            P("batch"),
            P("batch"),
            P("batch"),
            P("batch", None),
            P("batch", None),
            P("batch"),
            P("batch", None),
            P("batch", None),
            P("batch", None),
            P("batch", None),
            P("batch"),
            P("batch", None),
            P("batch", None),
            P("batch"),
            P("batch", None),
        ),
        check_vma=False,
    )
```

```python
import functools
import math

import jax
import jax.numpy as jnp
from jax import lax
from jax.experimental import pallas as pl
from jax.experimental.pallas import tpu as pltpu
from jax.sharding import PartitionSpec as P

HEADS = 12
HEAD = 64
BUCKETS = 32
LANES = 128
far_apart = float(2**30)

eps_norm = 1e-06
masked_score = -1000000000.0
logit_scale = 20.0
bucket_limits = (12, 16, 23, 32, 46, 64, 91)
highest = lax.Precision.HIGHEST
low = jnp.bfloat16
wide = jnp.float32


def rms_norm(values, gain_vector):
    return (
        values
        * lax.rsqrt(jnp.mean(values * values, axis=-1, keepdims=True) + eps_norm)
        * gain_vector
    )


def unit_length(values):
    return values * lax.rsqrt(jnp.sum(values * values, axis=-1, keepdims=True) + eps_norm)


def bucket_of(offsets):
    upper_half = jnp.where(offsets > 0, 16, 0).astype(jnp.int32)
    distance = jnp.abs(offsets)
    far_bucket = 8 + sum(((distance >= threshold).astype(jnp.int32) for threshold in bucket_limits))
    return upper_half + jnp.where(distance < 8, distance, far_bucket)


def product(left_side, right_side):
    return jnp.dot(left_side, right_side, preferred_element_type=wide)


def back_product(left_side, right_side):
    return lax.dot_general(
        left_side, right_side, (((1,), (1,)), ((), ())), preferred_element_type=wide
    )


def weight_grad(left_side, right_side):
    return lax.dot_general(
        left_side, right_side, (((0,), (0,)), ((), ())), preferred_element_type=wide
    )


def norm_back(values, gain_vector, grad_rows):
    _, pullback = jax.vjp(rms_norm, values, gain_vector)
    return pullback(grad_rows)


def gelu_back(values, grad_rows):
    _, pullback = jax.vjp(jax.nn.gelu, values)
    return pullback(grad_rows)[0]


def segment_of(places, ends):
    return (places >= ends[0]).astype(jnp.int32) + (places >= ends[1]).astype(jnp.int32)


def block_rows(rows):
    return 256 if rows % 256 == 0 else rows


def table_sizes(size, pack):
    slack = LANES if size % LANES else 0
    reach = -(-(size + slack + 91) // LANES) * LANES
    lead = -(-(size + slack) // LANES) * LANES
    middle = -(-(pack - size) // LANES) * LANES
    return middle, reach, lead, middle + max(pack, reach)


def offset_biases(table, size, pack, shift):
    _, reach, lead, _ = table_sizes(size, pack)
    offsets = jnp.arange(lead + reach + LANES, dtype=jnp.int32) - (lead + LANES) - shift
    onehot = (
        bucket_of(offsets)[None, :] == jnp.arange(BUCKETS, dtype=jnp.int32)[:, None]
    ).astype(low)
    return weight_grad(table, onehot)[:, None, :]


def turned_biases(row, size, lead):
    spread = jnp.broadcast_to(row, (size, row.shape[1]))
    return pltpu.roll(spread, 0, 1, stride=1, stride_axis=0)[:, lead:]


def attend_kernel(
    place, q_ref, k_ref, v_ref, near_ref, attended_ref, total_ref, bias, key_side, value_side
):
    pair = pl.program_id(0)
    block = pl.program_id(1)
    pack = k_ref.shape[0]
    size = q_ref.shape[0]
    middle, reach, lead, width = table_sizes(size, pack)
    ends = (place[0], place[1])
    first = place[2] + block * size
    shift = place[3]

    @pl.when(block == 0)
    def _():
        places = lax.broadcasted_iota(jnp.int32, (pack, LANES), 0)
        lane = lax.broadcasted_iota(jnp.int32, (pack, LANES), 1)
        key_side[:, :LANES] = k_ref[...]
        key_side[:, LANES:] = (segment_of(places, ends) == lane).astype(wide).astype(low)
        value_side[:, :LANES] = v_ref[...]
        value_side[:, LANES:] = jnp.ones((pack, LANES), low)
        for half in range(2):
            row = near_ref[half]
            before = middle - LANES
            after = middle + reach
            bias[half, :, before:after] = turned_biases(row, size, lead)
            if before > 0:
                bias[half, :, :before] = jnp.broadcast_to(row[:, :1], (size, before))
            if after < width:
                bias[half, :, after:] = jnp.broadcast_to(row[:, -1:], (size, width - after))

    lane = lax.broadcasted_iota(jnp.int32, (size, LANES), 1)
    rows = first + lax.broadcasted_iota(jnp.int32, (size, LANES), 0)
    apart = jnp.where((segment_of(rows, ends) != lane) & (lane < 3), -far_apart, 0.0).astype(low)
    own = pl.ds(pl.multiple_of(block * size, 64), size)
    start = pl.multiple_of(middle - (first - shift), LANES)
    queries = q_ref[...]
    outputs = []
    totals = total_ref[own, :]
    for half in range(2):
        mine = (lane >= HEAD) if half else (lane < HEAD)
        query_side = jnp.concatenate(
            [jnp.where(mine, queries, jnp.zeros_like(queries)), apart], axis=1
        )
        scores = back_product(query_side, key_side[...]) + bias[half, :, pl.ds(start, pack)]
        top = jnp.max(scores, axis=1, keepdims=True)
        weights = jnp.exp(scores - top).astype(low)
        output = product(weights, value_side[...])
        total = output[:, LANES:]
        outputs.append(output[:, :LANES] / total)
        totals = jnp.where(lane == 2 * pair + half, top + jnp.log(total), totals)
    attended_ref[...] = jnp.where(lane < HEAD, outputs[0], outputs[1])
    total_ref[own, :] = totals


def attend(queries, all_keys, all_values, near, place):
    rows, width = queries.shape
    pack = all_keys.shape[0]
    size = block_rows(rows)
    _, _, _, columns = table_sizes(size, pack)
    pairs = width // LANES
    return pl.pallas_call(
        attend_kernel,
        name="attend",
        grid=(pairs, rows // size),
        in_specs=[
            pl.BlockSpec(memory_space=pltpu.SMEM),
            pl.BlockSpec((size, LANES), lambda p, i: (i, p)),
            pl.BlockSpec((pack, LANES), lambda p, i: (0, p)),
            pl.BlockSpec((pack, LANES), lambda p, i: (0, p)),
            pl.BlockSpec((2, 1, near.shape[2]), lambda p, i: (p, 0, 0)),
        ],
        out_specs=[
            pl.BlockSpec((size, LANES), lambda p, i: (i, p)),
            pl.BlockSpec((rows, LANES), lambda p, i: (0, 0)),
        ],
        out_shape=[
            jax.ShapeDtypeStruct((rows, width), wide),
            jax.ShapeDtypeStruct((rows, LANES), wide),
        ],
        scratch_shapes=[
            pltpu.VMEM((2, size, columns), wide),
            pltpu.VMEM((pack, 2 * LANES), low),
            pltpu.VMEM((pack, 2 * LANES), low),
        ],
        compiler_params=pltpu.CompilerParams(vmem_limit_bytes=48 * 2**20),
        cost_estimate=pl.CostEstimate(
            flops=8 * rows * pack * width * 2, bytes_accessed=16 * pack * width, transcendentals=0
        ),
    )(place, queries, all_keys, all_values, near)


SEQ_ROWS = 8
HEAD_ROWS = 16
MESH = pl.DeviceIdType.MESH


def rms_factor(values):
    return lax.rsqrt(jnp.mean(values * values, axis=-1, keepdims=True) + eps_norm)


def rms_back(values, gain_row, grad_rows):
    factor = rms_factor(values)
    scaled = gain_row * grad_rows
    inner = jnp.mean(scaled * values, axis=-1, keepdims=True)
    return (
        factor * scaled - values * (factor * factor * factor) * inner,
        jnp.sum(grad_rows * values * factor, axis=0, keepdims=True),
    )


gelu_scale = 0.7978845608028654


def gelu_value(values):
    return 0.5 * values * (
        1.0 + jnp.tanh(gelu_scale * (values + 0.044715 * values * values * values))
    )


def gelu_slope(values):
    square = values * values
    bent = jnp.tanh(gelu_scale * (values + 0.044715 * square * values))
    return 0.5 * (1.0 + bent) + 0.5 * values * (1.0 - bent * bent) * gelu_scale * (
        1.0 + 0.134145 * square
    )


def decoder_kernel(
    groups,
    members,
    seqs,
    place,
    context_ref,
    third_ref,
    gains_ref,
    target_ref,
    embedded_ref,
    loss_ref,
    grad_context_ref,
    pieces_ref,
    mixed_ref,
    starts_ref,
    totals_ref,
    weights,
    everyone,
    shared,
    similar_ref,
    weight_sem,
    every_send,
    every_recv,
    share_send,
    share_recv,
):
    rows, width = context_ref.shape
    count, _, _ = third_ref.shape
    unit = width // count
    blocks = 4 * unit
    group = lax.axis_index("batch")
    member = lax.axis_index("seq")
    seq_total = groups * seqs

    barrier = pltpu.get_barrier_semaphore()
    for step in range(1, groups):
        pl.semaphore_signal(
            barrier,
            inc=1,
            device_id={"batch": lax.rem(group + step, groups)},
            device_id_type=MESH,
        )
    for step in range(1, members):
        pl.semaphore_signal(
            barrier,
            inc=1,
            device_id={"seq": lax.rem(member + step, members)},
            device_id_type=MESH,
        )

    sizes = [unit] * 7 + [unit] * 4 + [blocks]
    firsts = [sum(sizes[:i]) for i in range(len(sizes))]
    copies = [
        pltpu.make_async_copy(
            third_ref.at[:, first : first + size, :],
            weights.at[:, first : first + size, :],
            weight_sem.at[i],
        )
        for i, (first, size) in enumerate(zip(firsts, sizes))
    ]
    for copy in copies:
        copy.start()

    def weight(i):
        return weights[:, firsts[i] : firsts[i] + unit, :].reshape(width, width)

    def outer_weight(j):
        per = count // 4
        return weights[per * j : per * (j + 1), firsts[11] : firsts[11] + blocks, :].reshape(
            width, width
        )

    gain = {
        name: gains_ref[i : i + 1, :]
        for i, name in enumerate(
            ("attention", "feed", "encoder", "start", "own", "cross", "second", "final")
        )
    }
    context = context_ref[...]

    start = jnp.broadcast_to(gain["start"], (SEQ_ROWS, width))
    self_in = (start * rms_factor(start) * gain["own"]).astype(low)
    copies[0].wait()
    self_vals = product(self_in, weight(0)).astype(low)
    copies[1].wait()
    after_self = start + product(self_vals, weight(1))
    cross_in = (after_self * rms_factor(after_self) * gain["cross"]).astype(low)
    copies[2].wait()
    cross_query = product(cross_in, weight(2))
    head_row = lax.broadcasted_iota(jnp.int32, (HEAD_ROWS, width), 0)
    head_mask = head_row == lax.broadcasted_iota(jnp.int32, (HEAD_ROWS, width), 1) // HEAD
    query_heads = jnp.where(
        head_mask, jnp.broadcast_to(cross_query[:1], (HEAD_ROWS, width)), 0.0
    ).astype(low)
    copies[3].wait()
    key_rows = back_product(query_heads, weight(3)).astype(low)

    many = seqs * HEAD_ROWS
    scores = back_product(key_rows, context)
    scores = jnp.concatenate([scores] * seqs, axis=0)
    places = member * rows + lax.broadcasted_iota(jnp.int32, (many, rows), 1)
    row_seq = lax.broadcasted_iota(jnp.int32, (many, rows), 0) // HEAD_ROWS
    inside = segment_of(places, (place[0], place[1])) == row_seq
    scores = jnp.where(inside, scores, masked_score)
    part_top = jnp.max(scores, axis=1, keepdims=True)
    part_weights = jnp.where(inside, jnp.exp(scores - part_top), 0.0).astype(low)
    part_total = jnp.sum(part_weights.astype(wide), axis=1, keepdims=True)
    lane = lax.broadcasted_iota(jnp.int32, (many, LANES), 1)
    shared[0, :, :width] = product(part_weights, context)
    shared[0, :, width:] = jnp.where(lane == 0, part_top, part_total)

    pl.semaphore_wait(barrier, groups - 1 + members - 1)
    for step in range(1, members):
        pltpu.make_async_remote_copy(
            src_ref=shared.at[0],
            dst_ref=shared.at[step],
            send_sem=share_send.at[step - 1],
            recv_sem=share_recv.at[step - 1],
            device_id={"seq": lax.rem(member + step, members)},
            device_id_type=MESH,
        ).start()
    for step in range(1, members):
        pltpu.make_async_remote_copy(
            src_ref=shared.at[0],
            dst_ref=shared.at[step],
            send_sem=share_send.at[step - 1],
            recv_sem=share_recv.at[step - 1],
            device_id={"seq": lax.rem(member + step, members)},
            device_id_type=MESH,
        ).wait()
    top = shared[0, :, width : width + 1]
    for step in range(1, members):
        top = jnp.maximum(top, shared[step, :, width : width + 1])
    total = jnp.zeros((many, 1), wide)
    mixed = jnp.zeros((many, width), wide)
    for step in range(members):
        scale = jnp.exp(shared[step, :, width : width + 1] - top)
        total = total + shared[step, :, width + 1 : width + 2] * scale
        mixed = mixed + shared[step, :, :width] * scale
    mixed = (mixed / total).astype(low)
    mixed_ref[...] = mixed
    log_total = top + jnp.log(total)

    def by_seq(parts):
        row = lax.broadcasted_iota(jnp.int32, (SEQ_ROWS, width), 0)
        joined = jnp.zeros((SEQ_ROWS, width), wide)
        for i, part in enumerate(parts):
            joined = jnp.where(row == i, part, joined)
        return joined

    copies[4].wait()
    spread = product(mixed, weight(4))
    cross_attended = by_seq(
        [
            jnp.sum(
                jnp.where(head_mask, spread[HEAD_ROWS * i : HEAD_ROWS * (i + 1)], 0.0),
                axis=0,
                keepdims=True,
            )
            for i in range(seqs)
        ]
    )
    cross_low = cross_attended.astype(low)
    copies[5].wait()
    after_cross = after_self + product(cross_low, weight(5))
    second_in = (after_cross * rms_factor(after_cross) * gain["second"]).astype(low)
    for i in range(7, 12):
        copies[i].wait()
    second_pre = [product(second_in, weight(7 + j)) for j in range(4)]
    second_act = [gelu_value(second_pre[j]).astype(low) for j in range(4)]
    decoded = after_cross
    for j in range(4):
        decoded = decoded + product(second_act[j], outer_weight(j))
    pooled_in = (decoded * rms_factor(decoded) * gain["final"]).astype(low)
    copies[6].wait()
    pooled = product(pooled_in, weight(6))
    size = lax.rsqrt(jnp.sum(pooled * pooled, axis=-1, keepdims=True) + eps_norm)
    embedded = pooled * size
    embedded_ref[...] = embedded

    everyone[0] = embedded
    sends = []
    for step in range(1, groups):
        sends.append(
            pltpu.make_async_remote_copy(
                src_ref=everyone.at[0],
                dst_ref=everyone.at[step],
                send_sem=every_send,
                recv_sem=every_recv,
                device_id={"batch": lax.rem(group + step, groups)},
                device_id_type=MESH,
            )
        )
        sends[-1].start()
    arrival = pltpu.make_async_remote_copy(
        src_ref=everyone.at[pl.ds(1, groups - 1)],
        dst_ref=everyone.at[pl.ds(1, groups - 1)],
        send_sem=every_send,
        recv_sem=every_recv,
        device_id={"batch": lax.rem(group + 1, groups)},
        device_id_type=MESH,
    )
    arrival.wait_recv()
    arrival.wait_send()
    all_rows = everyone[...].reshape(groups * SEQ_ROWS, width)
    number = groups * SEQ_ROWS
    row = lax.broadcasted_iota(jnp.int32, (number, number), 0)
    column = lax.broadcasted_iota(jnp.int32, (number, number), 1)
    row_valid = row % SEQ_ROWS < seqs
    valid = row_valid & (column % SEQ_ROWS < seqs)
    similar = logit_scale * lax.dot_general(
        all_rows,
        all_rows,
        (((1,), (1,)), ((), ())),
        precision=highest,
        preferred_element_type=wide,
    )
    similar = jnp.where(valid & (row != column), similar, masked_score)
    best = jnp.max(similar, axis=1, keepdims=True)
    log_norm = best + jnp.log(jnp.sum(jnp.exp(similar - best), axis=1, keepdims=True))
    row_group = lax.rem(group - row // SEQ_ROWS + groups, groups)
    column_group = lax.rem(group - column // SEQ_ROWS + groups, groups)
    row_number = row_group * seqs + row % SEQ_ROWS
    column_number = column_group * seqs + column % SEQ_ROWS
    label = jnp.max(
        jnp.where(
            lax.broadcasted_iota(jnp.int32, (number, target_ref.shape[1]), 1)
            == row_number[:, : target_ref.shape[1]],
            target_ref[:1, :],
            -1.0,
        ),
        axis=1,
        keepdims=True,
    )
    target = (column_number.astype(wide) == label) & valid
    picked = jnp.sum(jnp.where(target, similar, 0.0), axis=1, keepdims=True)
    losses = jnp.where(row_valid[:, :1], log_norm - picked, 0.0)
    loss_ref[...] = jnp.broadcast_to(
        jnp.sum(losses, axis=0, keepdims=True) / seq_total, loss_ref.shape
    )
    grad_similar = jnp.where(
        valid, (jnp.exp(similar - log_norm) - target.astype(wide)) / seq_total, 0.0
    )
    similar_ref[...] = grad_similar + grad_similar.T
    grad_embedded = logit_scale * jnp.dot(
        similar_ref[:SEQ_ROWS, :], all_rows, precision=highest, preferred_element_type=wide
    )

    grad_pooled = (
        size
        * (grad_embedded - embedded * jnp.sum(embedded * grad_embedded, axis=-1, keepdims=True))
    ).astype(low)
    grad_decoded, grad_final_gain = rms_back(
        decoded, gain["final"], back_product(grad_pooled, weight(6))
    )
    grad_second_out = grad_decoded.astype(low)
    grad_second_pre = [
        (gelu_slope(second_pre[j]) * back_product(grad_second_out, outer_weight(j))).astype(low)
        for j in range(4)
    ]
    grad_second_in = back_product(grad_second_pre[0], weight(7))
    for j in range(1, 4):
        grad_second_in = grad_second_in + back_product(grad_second_pre[j], weight(7 + j))
    grad_after_cross, grad_second_gain = rms_back(after_cross, gain["second"], grad_second_in)
    grad_after_cross = grad_after_cross + grad_decoded
    grad_cross_branch = grad_after_cross.astype(low)
    grad_cross_att = back_product(grad_cross_branch, weight(5)).astype(low)
    grad_cross_wide = grad_cross_att.astype(wide)
    grad_heads = jnp.concatenate(
        [
            jnp.where(
                head_mask,
                jnp.broadcast_to(grad_cross_wide[i : i + 1], (HEAD_ROWS, width)),
                0.0,
            )
            for i in range(seqs)
        ],
        axis=0,
    )
    attended_heads = jnp.concatenate(
        [
            jnp.broadcast_to(cross_attended[i : i + 1], (HEAD_ROWS, width))
            for i in range(seqs)
        ],
        axis=0,
    )
    row_terms = jnp.sum(grad_heads * attended_heads, axis=1, keepdims=True)
    value_rows = back_product(grad_heads.astype(low), weight(4)).astype(low)
    probs = jnp.where(inside, jnp.exp(scores - log_total), 0.0)
    grad_scores = (probs * (back_product(value_rows, context) - row_terms)).astype(low)
    grad_context_ref[...] = weight_grad(
        jnp.concatenate([grad_scores, probs.astype(low)], axis=0),
        jnp.concatenate([key_rows] * seqs + [value_rows], axis=0),
    )
    key_sums = product(grad_scores, context)
    sums = key_sums[:HEAD_ROWS]
    for i in range(1, seqs):
        sums = sums + key_sums[HEAD_ROWS * i : HEAD_ROWS * (i + 1)]
    first_member = jnp.where(member == 0, 1.0, 0.0)
    totals_ref[:HEAD_ROWS, :] = sums
    totals_ref[HEAD_ROWS:, :] = first_member * by_seq(
        [jnp.sum(grad_after_cross, axis=0, keepdims=True), grad_final_gain, grad_second_gain]
    )
    for i, piece in enumerate(
        [cross_low, second_in]
        + second_act
        + [pooled_in, grad_cross_branch]
        + grad_second_pre
        + [grad_second_out, grad_pooled, grad_cross_att]
    ):
        pieces_ref[i] = piece.astype(wide)
    for i, piece in enumerate([start, self_in, self_vals, after_self, cross_in, cross_query]):
        starts_ref[i : i + 1, :] = piece[:1].astype(wide)
    starts_ref[6:, :] = jnp.zeros((2, width), wide)


def decoder_step(context, third, gains, labels, place, groups, members, seqs):
    rows, width = context.shape
    everything = pl.BlockSpec(memory_space=pltpu.VMEM)
    labels = jnp.pad(labels.astype(wide)[None], ((0, 7), (0, LANES - labels.shape[0])))
    number = groups * SEQ_ROWS
    return pl.pallas_call(
        functools.partial(decoder_kernel, groups, members, seqs),
        name="decoder",
        in_specs=[
            pl.BlockSpec(memory_space=pltpu.SMEM),
            everything,
            pl.BlockSpec(memory_space=pl.ANY),
            everything,
            everything,
        ],
        out_specs=[everything] * 7,
        out_shape=[
            jax.ShapeDtypeStruct((SEQ_ROWS, width), wide),
            jax.ShapeDtypeStruct((8, LANES), wide),
            jax.ShapeDtypeStruct((rows, width), wide),
            jax.ShapeDtypeStruct((15, SEQ_ROWS, width), wide),
            jax.ShapeDtypeStruct((seqs * HEAD_ROWS, width), low),
            jax.ShapeDtypeStruct((8, width), wide),
            jax.ShapeDtypeStruct((HEAD_ROWS + SEQ_ROWS, width), wide),
        ],
        scratch_shapes=[
            pltpu.VMEM(third.shape, low),
            pltpu.VMEM((groups, SEQ_ROWS, width), wide),
            pltpu.VMEM((members, seqs * HEAD_ROWS, width + LANES), wide),
            pltpu.VMEM((number, number), wide),
            pltpu.SemaphoreType.DMA((12,)),
            pltpu.SemaphoreType.DMA,
            pltpu.SemaphoreType.DMA,
            pltpu.SemaphoreType.DMA((max(members - 1, 1),)),
            pltpu.SemaphoreType.DMA((max(members - 1, 1),)),
        ],
        compiler_params=pltpu.CompilerParams(
            collective_id=0, has_side_effects=True, vmem_limit_bytes=56 * 2**20
        ),
        cost_estimate=pl.CostEstimate(
            flops=2 * rows * width * 300, bytes_accessed=2 * third.size, transcendentals=0
        ),
    )(place, context, third, gains, labels)


class Summing:
    def __init__(self, groups, members, buffers):
        self.groups = groups
        self.members = members
        self.lines = groups // 4
        self.group = lax.axis_index("batch")
        self.member = lax.axis_index("seq")
        self.z = self.group // 4
        self.y = lax.rem(self.group // 2, 2)
        self.core = lax.rem(self.group, 2)
        (
            self.chip,
            self.pairs,
            self.line,
            self.shares,
            self.chip_send,
            self.chip_recv,
            self.pair_send,
            self.pair_recv,
            self.line_send,
            self.line_recv,
            self.share_send,
            self.share_recv,
        ) = buffers
        self.stages = 3 + self.lines

    def batch_id(self, offset):
        return {"batch": self.group + offset}

    def neighbours(self):
        found = [
            (None, self.batch_id(1 - 2 * self.core)),
            (None, self.batch_id(2 - 4 * self.y)),
            (self.z > 0, self.batch_id(-4)),
            (self.z < self.lines - 1, self.batch_id(4)),
        ]
        for step in range(1, self.members):
            found.append((None, {"seq": lax.rem(self.member + step, self.members)}))
        return found

    def greet(self, barrier):
        for condition, device in self.neighbours():
            if condition is None:
                pl.semaphore_signal(barrier, inc=1, device_id=device, device_id_type=MESH)
            else:

                @pl.when(condition)
                def _():
                    pl.semaphore_signal(barrier, inc=1, device_id=device, device_id_type=MESH)

    def greeted(self, barrier):
        ends = (self.z > 0).astype(jnp.int32) + (self.z < self.lines - 1).astype(jnp.int32)
        pl.semaphore_wait(barrier, 2 + self.members - 1 + ends)

    def copy(self, source, target, send, recv, device):
        return pltpu.make_async_remote_copy(
            src_ref=source,
            dst_ref=target,
            send_sem=send,
            recv_sem=recv,
            device_id=device,
            device_id_type=MESH,
        )

    def chip_copy(self, chunk, source):
        return self.copy(
            source,
            self.chip.at[chunk],
            self.chip_send.at[chunk],
            self.chip_recv.at[chunk],
            self.batch_id(1 - 2 * self.core),
        )

    def pair_copy(self, chunk):
        return self.copy(
            self.chip.at[chunk, :, 1 - self.y],
            self.pairs.at[chunk],
            self.pair_send.at[chunk],
            self.pair_recv.at[chunk],
            self.batch_id(2 - 4 * self.y),
        )

    def line_copy(self, chunk, way, first, last, source):
        return self.copy(
            source.at[chunk, pl.ds(first, last - first)]
            if source is self.pairs
            else source.at[chunk, way, pl.ds(first, last - first)],
            self.line.at[chunk, way, pl.ds(first, last - first)],
            self.line_send.at[chunk, way],
            self.line_recv.at[chunk, way],
            self.batch_id(-4 if way else 4),
        )

    def share_copy(self, chunk, step):
        return self.copy(
            self.shares.at[chunk, self.member],
            self.shares.at[chunk, self.member],
            self.share_send.at[chunk, step - 1],
            self.share_recv.at[chunk, step - 1],
            {"seq": lax.rem(self.member + step, self.members)},
        )

    def start(self, chunk, source):
        self.chip_copy(chunk, source).start()

    def to_pair(self, chunk, source, own):
        self.chip_copy(chunk, source).wait()
        self.chip[chunk] = (self.chip[chunk].astype(wide) + own.astype(wide)).astype(low)
        self.pair_copy(chunk).start()

    def to_line(self, chunk, step):
        lines = self.lines
        if step == 0:
            self.pair_copy(chunk).wait()
            self.pairs[chunk] = (
                self.pairs[chunk].astype(wide) + self.chip[chunk, :, self.y].astype(wide)
            ).astype(low)
        for way in range(2):
            at = lines - 1 - step if way else step
            first, last = (0, at) if way else (at + 1, lines)

            @pl.when(self.z == at)
            def _():
                if step > 0:
                    kept = (0, at + 1) if way else (at, lines)
                    self.line_copy(chunk, way, kept[0], kept[1], self.line).wait_recv()
                    span = pl.ds(first, last - first)
                    self.line[chunk, way, span] = (
                        self.line[chunk, way, span].astype(wide)
                        + self.pairs[chunk, span].astype(wide)
                    ).astype(low)
                self.line_copy(
                    chunk, way, first, last, self.line if step > 0 else self.pairs
                ).start()

    def to_members(self, chunk, held):
        lines = self.lines
        for way in range(2):
            end = 0 if way else lines - 1

            @pl.when(self.z == end)
            def _():
                kept = (0, 1) if way else (lines - 1, lines)
                self.line_copy(chunk, way, kept[0], kept[1], self.line).wait_recv()

            for step in range(lines - 1):
                at = lines - 1 - step if way else step
                first, last = (0, at) if way else (at + 1, lines)

                @pl.when(self.z == at)
                def _():
                    self.line_copy(chunk, way, first, last, self.line).wait_send()

        held[...] = self.pairs[chunk, self.z].astype(wide)

        @pl.when(self.z > 0)
        def _():
            held[...] += self.line[chunk, 0, self.z].astype(wide)

        @pl.when(self.z < lines - 1)
        def _():
            held[...] += self.line[chunk, 1, self.z].astype(wide)

        self.shares[chunk, self.member] = held[...].astype(low)
        for step in range(1, self.members):
            self.share_copy(chunk, step).start()

    def result(self, chunk):
        for step in range(1, self.members):
            self.share_copy(chunk, step).wait()
        total = self.shares[chunk, 0].astype(wide)
        for member in range(1, self.members):
            total = total + self.shares[chunk, member].astype(wide)
        return total


def summing_scratch(groups, members, chunks, rows, columns):
    lines = groups // 4
    return [
        pltpu.VMEM((chunks, lines, 2, rows, columns), low),
        pltpu.VMEM((chunks, lines, rows, columns), low),
        pltpu.VMEM((chunks, 2, lines, rows, columns), low),
        pltpu.VMEM((chunks, members, rows, columns), low),
        pltpu.SemaphoreType.DMA((chunks,)),
        pltpu.SemaphoreType.DMA((chunks,)),
        pltpu.SemaphoreType.DMA((chunks,)),
        pltpu.SemaphoreType.DMA((chunks,)),
        pltpu.SemaphoreType.DMA((chunks, 2)),
        pltpu.SemaphoreType.DMA((chunks, 2)),
        pltpu.SemaphoreType.DMA((chunks, max(members - 1, 1))),
        pltpu.SemaphoreType.DMA((chunks, max(members - 1, 1))),
    ]


def stage_delays(lines):
    return [1, 3] + [4 + step for step in range(lines - 2)] + [lines + 2, lines + 3]


def attend_back_kernel(
    groups,
    members,
    place,
    q_ref,
    k_ref,
    v_ref,
    grad_ref,
    attended_ref,
    total_ref,
    near_ref,
    own_turned_ref,
    all_turned_ref,
    parts_ref,
    grad_q_ref,
    grad_k_ref,
    grad_v_ref,
    band_ref,
    far_ref,
    feed_sums_ref,
    pair_sums_ref,
    bias,
    key_side,
    value_side,
    keys_turned,
    grad_scores,
    grad_k_sum,
    grad_v_sum,
    band_sum,
    grad_q_sum,
    pair_grads,
    fetched,
    held,
    fetch_sem,
    *buffers,
):
    pair = pl.program_id(0)
    block = pl.program_id(1)
    blocks = pl.num_programs(1)
    pairs = pl.num_programs(0)
    now = pair * blocks + block
    pack = k_ref.shape[0]
    size = q_ref.shape[0]
    middle, reach, lead, width = table_sizes(size, pack)
    ends = (place[0], place[1])
    rows_here = size * blocks
    summing = Summing(groups, members, buffers)
    first = summing.member * rows_here + block * size
    shift = lax.rem(summing.member * rows_here, LANES) if size % LANES else 0
    barrier = pltpu.get_barrier_semaphore()
    feed_chunks = 2 * parts_ref.shape[3]
    half_width = fetched.shape[-1]
    part = fetched.shape[-2]
    lines = groups // 4
    delays = stage_delays(lines)

    @pl.when(now == 0)
    def _():
        summing.greet(barrier)
        summing.greeted(barrier)

    def feed_part(chunk, core):
        return parts_ref.at[
            :, :, core, chunk // 2, :, pl.ds(pl.multiple_of(lax.rem(chunk, 2) * half_width, LANES), half_width)
        ]

    def fetch(chunk):
        slot = lax.rem(chunk, 4)
        return pltpu.make_async_copy(
            feed_part(chunk, summing.core), fetched.at[slot], fetch_sem.at[slot]
        )

    def feed_stage(stage, chunk):
        if stage == 0:
            summing.start(chunk, feed_part(chunk, 1 - summing.core))
            fetch(chunk).start()
        elif stage == 1:
            fetch(chunk).wait()
            summing.to_pair(
                chunk, feed_part(chunk, 1 - summing.core), fetched[lax.rem(chunk, 4)]
            )
        elif stage <= lines:
            summing.to_line(chunk, stage - 2)
        elif stage == lines + 1:
            summing.to_members(chunk, held)
        else:
            total = summing.result(chunk)
            column = pl.multiple_of(lax.rem(chunk, 2) * half_width, LANES)
            feed_sums_ref[chunk // 2, :, pl.ds(column, half_width)] = total

    def pair_stage(stage, which):
        chunk = feed_chunks + which
        if stage == 0:
            summing.start(chunk, pair_grads.at[which, :, :, 1 - summing.core])
        elif stage == 1:
            summing.to_pair(
                chunk,
                pair_grads.at[which, :, :, 1 - summing.core],
                pair_grads[which, :, :, summing.core],
            )
        elif stage <= lines:
            summing.to_line(chunk, stage - 2)
        elif stage == lines + 1:
            summing.to_members(chunk, held)
        else:
            pair_sums_ref[which] = summing.result(chunk)

    stages = 3 + lines
    starts = [0] + delays
    total_steps = pairs * blocks

    def run_stages(step):
        for stage in reversed(range(stages)):
            chunk = step - starts[stage]

            @pl.when((chunk >= 0) & (chunk < feed_chunks))
            def _():
                feed_stage(stage, chunk)

            late = step - (blocks - 1) - starts[stage]

            @pl.when((late >= 0) & (lax.rem(late + 64 * blocks, blocks) == 0) & (late < total_steps))
            def _():
                pair_stage(stage, late // blocks)

    @pl.when(block == 0)
    def _():
        places = lax.broadcasted_iota(jnp.int32, (pack, LANES), 0)
        lane = lax.broadcasted_iota(jnp.int32, (pack, LANES), 1)
        key_side[:, :LANES] = k_ref[...]
        ones = (segment_of(places, ends) == lane) | ((lane >= 3) & (lane < 9))
        key_side[:, LANES:] = ones.astype(wide).astype(low)
        value_side[:, :LANES] = v_ref[...]
        value_side[:, LANES:] = (lane < 6).astype(wide).astype(low)
        keys_turned[...] = k_ref[...].T
        for half in range(2):
            row = near_ref[half]
            before = middle - LANES
            after = middle + reach
            bias[half, before:after, :] = turned_biases(row, size, lead).T
            if before > 0:
                bias[half, :before, :] = jnp.broadcast_to(row[:, :1], (before, size))
            if after < width:
                bias[half, after:, :] = jnp.broadcast_to(row[:, -1:], (width - after, size))
        grad_scores[...] = jnp.zeros_like(grad_scores)
        grad_k_sum[...] = jnp.zeros_like(grad_k_sum)
        grad_v_sum[...] = jnp.zeros_like(grad_v_sum)
        band_sum[...] = jnp.zeros_like(band_sum)

    lane = lax.broadcasted_iota(jnp.int32, (size, LANES), 1)
    rows = first + lax.broadcasted_iota(jnp.int32, (size, LANES), 0)
    apart = jnp.where((segment_of(rows, ends) != lane) & (lane < 3), -far_apart, 0.0)
    start = pl.multiple_of(middle - (first - shift), LANES)
    near_rows = pl.ds(pl.multiple_of(first - shift, LANES), LANES + reach)
    queries = q_ref[...]
    grads = grad_ref[...]
    products = grads.astype(wide) * attended_ref[...]
    totals = total_ref[...]

    def in_parts(column, at):
        head = column.astype(low).astype(wide)
        body = (column - head).astype(low).astype(wide)
        tail = column - head - body
        return jnp.where(
            lane == at,
            head,
            jnp.where(lane == at + 1, body, jnp.where(lane == at + 2, tail, 0.0)),
        )

    query_grads = []
    for half in range(2):
        mine = (lane >= HEAD) if half else (lane < HEAD)
        row_term = jnp.sum(jnp.where(mine, products, 0.0), axis=1, keepdims=True)
        row_total = jnp.sum(
            jnp.where(lane == 2 * pair + half, totals, 0.0), axis=1, keepdims=True
        )
        query_part = jnp.where(mine, queries, jnp.zeros_like(queries))
        grad_part = jnp.where(mine, grads, jnp.zeros_like(grads))
        query_side = jnp.concatenate(
            [query_part, (apart - in_parts(row_total, 3 + 3 * half)).astype(low)], axis=1
        )
        grad_side = jnp.concatenate(
            [grad_part, (-in_parts(row_term, 3 * half)).astype(low)], axis=1
        )
        weights = jnp.exp(
            back_product(key_side[...], query_side) + bias[half, pl.ds(start, pack), :]
        )
        grad_block = (weights * back_product(value_side[...], grad_side)).astype(low)
        grad_scores[LANES : LANES + pack, :] = grad_block
        grad_v_sum[...] += product(weights.astype(low), grad_part)
        block_lane = jnp.where(lane == 8 * half + block, 1.0, 0.0).astype(low)
        grad_k_sum[...] += product(
            grad_block, jnp.concatenate([query_part, block_lane], axis=1)
        )
        query_grads.append(product(keys_turned[HEAD * half : HEAD * (half + 1), :], grad_block))
        band_sum[half] += grad_scores[near_rows, :].astype(wide)
    grad_query = jnp.concatenate(query_grads, axis=0).T.astype(low)
    grad_q_ref[...] = grad_query
    grad_q_sum[pl.ds(pl.multiple_of(block * size, 64), size), :] = grad_query

    @pl.when(block == blocks - 1)
    def _():
        grad_key = grad_k_sum[:, :LANES].astype(low)
        grad_value = grad_v_sum[...].astype(low)
        grad_k_ref[...] = grad_key
        grad_v_ref[...] = grad_value
        for i, gradient in enumerate(
            (
                product(own_turned_ref[...], grad_q_sum[...]),
                product(all_turned_ref[...], grad_key),
                product(all_turned_ref[...], grad_value),
            )
        ):
            pair_grads[pair, :, :, :, :, LANES * i : LANES * (i + 1)] = gradient.reshape(
                lines, 2, 2, part, LANES
            ).astype(low)
        key = lax.broadcasted_iota(jnp.int32, (pack, LANES), 0)
        which = lax.broadcasted_iota(jnp.int32, (pack, LANES), 1) % 8
        begin = summing.member * rows_here - shift + size * which
        sums = grad_k_sum[:, LANES:]
        below = jnp.sum(jnp.where(key < begin - LANES, sums, 0.0), axis=0, keepdims=True)
        above = jnp.sum(jnp.where(key >= begin + reach, sums, 0.0), axis=0, keepdims=True)
        far_ref[0] = jnp.concatenate([below, above, jnp.zeros((6, LANES), wide)], axis=0)
        columns = band_ref.shape[2]
        mirror = (
            lax.broadcasted_iota(jnp.int32, (size, columns), 0)
            + lax.broadcasted_iota(jnp.int32, (size, columns), 1)
            == size - 1
        ).astype(wide)
        for half in range(2):
            flipped = jnp.dot(
                band_sum[half], mirror, precision=highest, preferred_element_type=wide
            )
            turned = pltpu.roll(flipped, 0, 1, stride=1, stride_axis=0)
            band_ref[0, half : half + 1, :] = jnp.sum(turned, axis=0, keepdims=True)
        band_ref[0, 2:, :] = jnp.zeros((6, columns), wide)

    run_stages(now)

    @pl.when(now == total_steps - 1)
    def _():
        def drain(step, carry):
            run_stages(step)
            return carry

        lax.fori_loop(total_steps, total_steps + starts[-1] + 1, drain, 0)


def attend_back(
    queries, all_keys, all_values, grads, attended, totals, near, place, own_turned, all_turned, parts
):
    rows, width = queries.shape
    pack = all_keys.shape[0]
    size = block_rows(rows)
    _, reach, _, columns = table_sizes(size, pack)
    band = -(-(size + LANES + reach) // LANES) * LANES
    pairs = width // LANES
    members = pack // rows
    pieces = parts.shape[3]
    part = parts.shape[4]
    groups = 4 * parts.shape[0]
    half_width = width // 2
    chunks = 2 * pieces + pairs

    def own(p, i):
        return (i, p)

    def every(p, i):
        return (0, p)

    whole = pl.BlockSpec(memory_space=pltpu.VMEM)
    grad_q, grad_k, grad_v, band_sums, far_sums, feed_sums, pair_sums = pl.pallas_call(
        functools.partial(attend_back_kernel, groups, members),
        name="attend_back",
        grid=(pairs, rows // size),
        in_specs=[
            pl.BlockSpec(memory_space=pltpu.SMEM),
            pl.BlockSpec((size, LANES), own),
            pl.BlockSpec((pack, LANES), every),
            pl.BlockSpec((pack, LANES), every),
            pl.BlockSpec((size, LANES), own),
            pl.BlockSpec((size, LANES), own),
            pl.BlockSpec((size, LANES), lambda p, i: (i, 0)),
            pl.BlockSpec((2, 1, near.shape[2]), lambda p, i: (p, 0, 0)),
            whole,
            whole,
            pl.BlockSpec(memory_space=pl.ANY),
        ],
        out_specs=[
            pl.BlockSpec((size, LANES), own),
            pl.BlockSpec((pack, LANES), every),
            pl.BlockSpec((pack, LANES), every),
            pl.BlockSpec((1, 8, band), lambda p, i: (p, 0, 0)),
            pl.BlockSpec((1, 8, LANES), lambda p, i: (p, 0, 0)),
            whole,
            whole,
        ],
        out_shape=[
            jax.ShapeDtypeStruct((rows, width), low),
            jax.ShapeDtypeStruct((pack, width), low),
            jax.ShapeDtypeStruct((pack, width), low),
            jax.ShapeDtypeStruct((pairs, 8, band), wide),
            jax.ShapeDtypeStruct((pairs, 8, LANES), wide),
            jax.ShapeDtypeStruct((pieces, part, width), wide),
            jax.ShapeDtypeStruct((pairs, part, half_width), wide),
        ],
        scratch_shapes=[
            pltpu.VMEM((2, columns, size), wide),
            pltpu.VMEM((pack, 2 * LANES), low),
            pltpu.VMEM((pack, 2 * LANES), low),
            pltpu.VMEM((LANES, pack), low),
            pltpu.VMEM((LANES + pack + reach, size), low),
            pltpu.VMEM((pack, 2 * LANES), wide),
            pltpu.VMEM((pack, LANES), wide),
            pltpu.VMEM((2, LANES + reach, size), wide),
            pltpu.VMEM((rows, LANES), low),
            pltpu.VMEM((pairs, groups // 4, 2, 2, part, half_width), low),
            pltpu.VMEM((4, groups // 4, 2, part, half_width), low),
            pltpu.VMEM((part, half_width), wide),
            pltpu.SemaphoreType.DMA((4,)),
        ]
        + summing_scratch(groups, members, chunks, part, half_width),
        compiler_params=pltpu.CompilerParams(
            collective_id=1, has_side_effects=True, vmem_limit_bytes=62 * 2**20
        ),
        cost_estimate=pl.CostEstimate(
            flops=20 * rows * pack * width * 2, bytes_accessed=16 * pack * width, transcendentals=0
        ),
    )(
        place,
        queries,
        all_keys,
        all_values,
        grads,
        attended,
        totals,
        near,
        own_turned,
        all_turned,
        parts,
    )
    offsets = jnp.arange(band, dtype=jnp.int32) - (size - 1) - LANES - place[3]
    buckets = jnp.arange(BUCKETS, dtype=jnp.int32)
    onehot = (bucket_of(offsets)[:, None] == buckets[None, :]).astype(wide)
    near_grad = jnp.dot(
        band_sums[:, :2].reshape(HEADS, band), onehot, precision=highest, preferred_element_type=wide
    )
    far_grad = jnp.sum(far_sums[:, :2, :16].reshape(pairs, 2, 2, 8), axis=3)
    far_grad = jnp.transpose(far_grad, (0, 2, 1)).reshape(HEADS, 2)
    grad_table = near_grad + far_grad[:, :1] * (buckets == 15) + far_grad[:, 1:] * (buckets == 31)
    return grad_q, grad_k, grad_v, grad_table.T, feed_sums, pair_sums


def finish_kernel(
    groups,
    members,
    rows_ref,
    third_ref,
    starts_ref,
    gains_ref,
    sums_ref,
    backs_ref,
    weights,
    parts,
    weight_sem,
    send_sem,
    recv_sem,
):
    count, _, width = third_ref.shape
    unit = width // count
    group = lax.axis_index("batch")
    member = lax.axis_index("seq")
    partners = []
    for axis, place, number in (("batch", group, groups), ("seq", member, members)):
        span = 1
        while span < number:
            bit = lax.rem(place // span, 2)
            partners.append({axis: place + span * (1 - 2 * bit)})
            span *= 2
    barrier = pltpu.get_barrier_semaphore()
    for partner in partners:
        pl.semaphore_signal(barrier, inc=1, device_id=partner, device_id_type=MESH)
    copies = [
        pltpu.make_async_copy(
            third_ref.at[:, unit * i : unit * (i + 1), :], weights.at[i], weight_sem.at[i]
        )
        for i in range(4)
    ]
    for copy in copies:
        copy.start()
    parts[0] = rows_ref[...]
    pl.semaphore_wait(barrier, len(partners))
    for i, partner in enumerate(partners):
        copy = pltpu.make_async_remote_copy(
            src_ref=parts.at[2 * i],
            dst_ref=parts.at[2 * i + 1],
            send_sem=send_sem.at[i],
            recv_sem=recv_sem.at[i],
            device_id=partner,
            device_id_type=MESH,
        )
        copy.start()
        copy.wait()
        parts[2 * i + 2] = parts[2 * i] + parts[2 * i + 1]
    sums = parts[2 * len(partners)]
    sums_ref[...] = sums
    for copy in copies:
        copy.wait()

    def weight(i):
        return weights[i].reshape(width, width)

    head_row = lax.broadcasted_iota(jnp.int32, (HEAD_ROWS, width), 0)
    head_mask = head_row == lax.broadcasted_iota(jnp.int32, (HEAD_ROWS, width), 1) // HEAD
    spread = product(sums[:HEAD_ROWS].astype(low), weight(3))
    grad_cross_query = jnp.sum(jnp.where(head_mask, spread, 0.0), axis=0, keepdims=True)
    grad_cross_query = grad_cross_query.astype(low)

    def widened(row):
        return jnp.broadcast_to(row.astype(wide), (SEQ_ROWS, width))

    start = widened(starts_ref[0:1, :])
    after_self = widened(starts_ref[3:4, :])
    grad_rows = back_product(widened(grad_cross_query).astype(low), weight(2))
    grad_after_self, _ = rms_back(after_self, gains_ref[5:6, :], grad_rows)
    cross_gain = grad_rows * after_self * rms_factor(after_self)
    grad_after_self = grad_after_self + widened(sums[HEAD_ROWS : HEAD_ROWS + 1])
    grad_branch = grad_after_self.astype(low)
    grad_self_vals = back_product(grad_branch, weight(1)).astype(low)
    grad_rows = back_product(grad_self_vals, weight(0))
    grad_start, _ = rms_back(start, gains_ref[4:5, :], grad_rows)
    self_gain = grad_rows * start * rms_factor(start)
    for i, row in enumerate(
        (
            grad_start + grad_after_self,
            self_gain,
            cross_gain,
            grad_cross_query,
            grad_branch,
            grad_self_vals,
        )
    ):
        backs_ref[i : i + 1, :] = row[:1].astype(wide)
    backs_ref[6:, :] = jnp.zeros((2, width), wide)


def finish(rows, third, starts, gains, groups, members):
    many, width = rows.shape
    partners = (groups.bit_length() - 1) + (members.bit_length() - 1)
    count = third.shape[0]
    whole = pl.BlockSpec(memory_space=pltpu.VMEM)
    return pl.pallas_call(
        functools.partial(finish_kernel, groups, members),
        name="finish",
        in_specs=[whole, pl.BlockSpec(memory_space=pl.ANY), whole, whole],
        out_specs=[whole, whole],
        out_shape=[
            jax.ShapeDtypeStruct((many, width), wide),
            jax.ShapeDtypeStruct((8, width), wide),
        ],
        scratch_shapes=[
            pltpu.VMEM((4, count, width // count, width), low),
            pltpu.VMEM((2 * partners + 1, many, width), wide),
            pltpu.SemaphoreType.DMA((4,)),
            pltpu.SemaphoreType.DMA((partners,)),
            pltpu.SemaphoreType.DMA((partners,)),
        ],
        compiler_params=pltpu.CompilerParams(
            collective_id=2, has_side_effects=True, vmem_limit_bytes=32 * 2**20
        ),
        cost_estimate=pl.CostEstimate(
            flops=2**30, bytes_accessed=8 * width * width, transcendentals=0
        ),
    )(rows, third, starts, gains)


def seq_exchange(value):
    count = lax.axis_size("seq")
    return [value] + [
        lax.ppermute(value, "seq", [(i, (i - step) % count) for i in range(count)])
        for step in range(1, count)
    ]


def in_place_order(pieces):
    count = len(pieces)
    me = lax.axis_index("seq")
    ordered = []
    for place in range(count):
        chosen = pieces[0]
        for step in range(1, count):
            chosen = jnp.where((place - me) % count == step, pieces[step], chosen)
        ordered.append(chosen)
    return jnp.concatenate(ordered, axis=0)


def seq_scatter(value, rows):
    count = lax.axis_size("seq")
    me = lax.axis_index("seq")
    total = lax.dynamic_slice_in_dim(value, me * rows, rows)
    for step in range(1, count):
        other = lax.dynamic_slice_in_dim(value, (me + step) % count * rows, rows)
        total = total + lax.ppermute(
            other.astype(low), "seq", [(i, (i + step) % count) for i in range(count)]
        ).astype(wide)
    return total


def in_blocks(gathered, sizes):
    count, _, width = gathered.shape
    join = 16 // math.gcd(16, sizes[0])
    if join == 1:
        return gathered
    pieces, at = [], 0
    for size in sizes:
        piece = gathered[:, at : at + size].reshape(count // join, join * size, width)
        pieces.append(piece)
        at += size
    return jnp.concatenate(pieces, axis=1)


def column_blocks(weight, model_width):
    rows, columns = weight.shape
    blocks = columns // model_width
    return jnp.transpose(weight.reshape(rows, blocks, model_width), (1, 0, 2)).reshape(
        blocks * rows, model_width
    )


def shards(
    tokens,
    lengths,
    labels,
    attention_gain,
    query_weight,
    key_weight,
    value_weight,
    attention_out,
    position_bias,
    feed_gain,
    feed_inner,
    feed_outer,
    encoder_gain,
    start_token,
    self_gain,
    self_value,
    self_out,
    cross_gain,
    cross_query,
    cross_key,
    cross_value,
    cross_out,
    second_gain,
    second_inner,
    second_outer,
    final_gain,
    pooler_weight,
):
    rows, width = tokens.shape
    part = query_weight.shape[0]
    share = feed_outer.shape[0]
    groups = lax.axis_size("batch")
    members = lax.axis_size("seq")
    blocks = feed_inner.shape[1] // width
    pack = rows * members
    seqs = lengths.shape[1]
    group = lax.axis_index("batch")
    member = lax.axis_index("seq")
    own_first = member * rows
    ends = jnp.cumsum(lengths[0])
    place = jnp.stack(
        [ends[0], ends[1], own_first, own_first % LANES]
    ).astype(jnp.int32)

    vectors = jnp.stack(
        [
            attention_gain,
            feed_gain,
            encoder_gain,
            start_token,
            self_gain,
            cross_gain,
            second_gain,
            final_gain,
        ],
        axis=1,
    )
    bias_row = jnp.pad(position_bias.reshape(1, -1), ((0, part - 1), (0, 0)))
    extra = jnp.concatenate([vectors, bias_row], axis=1)
    extra = jnp.pad(extra, ((0, 0), (0, LANES - extra.shape[1])))
    first_part = jnp.concatenate([query_weight, key_weight, value_weight, extra], axis=1)
    first = lax.all_gather(first_part, "batch", axis=0, tiled=True)
    second_part = jnp.concatenate(
        [attention_out, column_blocks(feed_inner, width), feed_outer], axis=0
    )
    second = lax.all_gather(second_part, "batch", axis=0, tiled=False)
    third_part = jnp.concatenate(
        [
            self_value,
            self_out,
            cross_query,
            cross_key,
            cross_value,
            cross_out,
            pooler_weight,
            column_blocks(second_inner, width),
            second_outer,
        ],
        axis=0,
    )
    third = lax.all_gather(third_part, "batch", axis=0, tiled=False)

    def square(gathered, at):
        return gathered[:, at : at + part].reshape(groups * part, width)

    def tall(gathered, at):
        return gathered[:, at : at + share].reshape(groups * share, width)

    gains = first[:, 3 * width : 3 * width + 8].astype(wide).T
    (
        attention_gain_full,
        feed_gain_full,
        encoder_gain_full,
        start_full,
        self_gain_full,
        cross_gain_full,
        second_gain_full,
        final_gain_full,
    ) = [gains[i] for i in range(8)]
    table = first.reshape(groups, part, -1)[
        :, 0, 3 * width + 8 : 3 * width + 8 + position_bias.size
    ].reshape(BUCKETS, HEADS)
    query_full = first[:, :width]
    key_value_full = first[:, width : 3 * width]

    all_tokens = in_place_order(seq_exchange(tokens))
    inputs = tokens.astype(wide)
    normed_all = rms_norm(all_tokens.astype(wide), attention_gain_full).astype(low)
    normed = rms_norm(inputs, attention_gain_full).astype(low)
    queries = product(normed, query_full).astype(low)
    keys_values = product(normed_all, key_value_full).astype(low)
    all_keys = keys_values[:, :width]
    all_values = keys_values[:, width:]
    near = offset_biases(table, block_rows(rows), pack, place[3])
    attended, totals = attend(queries, all_keys, all_values, near, place)
    attended_low = attended.astype(low)
    out_full = square(second, 0)
    hidden = inputs + product(attended_low, out_full)

    inner_in = rms_norm(hidden, feed_gain_full).astype(low)
    inner_full = [square(second, part * (1 + j)) for j in range(blocks)]
    outer_full = tall(second, part * (1 + blocks)).reshape(blocks, -1, width)
    inner_pre = [product(inner_in, inner_full[j]) for j in range(blocks)]
    inner_act = [jax.nn.gelu(inner_pre[j]).astype(low) for j in range(blocks)]
    encoded = hidden
    for j in range(blocks):
        encoded = encoded + product(inner_act[j], outer_full[j])
    context = rms_norm(encoded, encoder_gain_full).astype(low)

    third_blocks = in_blocks(third, [part] * (7 + blocks) + [share])
    (
        embedded,
        loss,
        grad_context,
        pieces,
        mixed,
        starts,
        decoder_totals,
    ) = decoder_step(
        context, third_blocks, gains, labels, place, groups, members, seqs
    )
    contrastive_loss = loss[0, :1]
    embedded = embedded[:seqs]
    decoder_rows = jnp.concatenate(
        [
            pieces[:, :seqs].astype(low).reshape(-1, width),
            mixed.reshape(seqs, HEAD_ROWS, width)[:, :HEADS].reshape(-1, width),
        ],
        axis=0,
    )
    start_row, self_in, self_vals, after_self, cross_in, cross_query_row = [
        starts[i : i + 1] for i in range(6)
    ]
    head_of = jnp.arange(width, dtype=jnp.int32) // HEAD
    head_mask = head_of[None, :] == jnp.arange(HEADS, dtype=jnp.int32)[:, None]

    count = decoder_rows.shape[0]
    decoder_rows = jnp.pad(decoder_rows, ((0, -count % 16), (0, 0)))
    decoder_rows = lax.all_gather(decoder_rows, "batch", axis=0, tiled=False)

    grad_encoded, grad_encoder_gain = norm_back(encoded, encoder_gain_full, grad_context)
    grad_feed_branch = grad_encoded.astype(low)
    grad_inner_pre = [
        gelu_back(inner_pre[j], back_product(grad_feed_branch, outer_full[j])).astype(low)
        for j in range(blocks)
    ]
    grad_inner_in = sum(back_product(grad_inner_pre[j], inner_full[j]) for j in range(blocks))
    grad_hidden, grad_feed_gain = norm_back(hidden, feed_gain_full, grad_inner_in)
    grad_hidden = grad_hidden + grad_encoded
    grad_attn_branch = grad_hidden.astype(low)
    second_grads = jnp.concatenate(
        [weight_grad(attended_low, grad_attn_branch).astype(low).reshape(groups, 1, part, width)]
        + [
            weight_grad(inner_in, grad_inner_pre[j]).astype(low).reshape(groups, 1, part, width)
            for j in range(blocks)
        ]
        + [
            jnp.concatenate(
                [weight_grad(inner_act[j], grad_feed_branch).astype(low) for j in range(blocks)],
                axis=0,
            ).reshape(groups, blocks, part, width)
        ],
        axis=1,
    ).reshape(groups // 4, 2, 2, 1 + 2 * blocks, part, width)

    grad_attended = back_product(grad_attn_branch, out_full).astype(low)
    grad_query_low, grad_key_low, grad_value_low, grad_table, second_sums, first_sums = attend_back(
        queries,
        all_keys,
        all_values,
        grad_attended,
        attended,
        totals,
        near,
        place,
        normed.T,
        normed_all.T,
        second_grads,
    )
    grad_normed_all = back_product(grad_key_low, key_value_full[:, :width]) + back_product(
        grad_value_low, key_value_full[:, width:]
    )
    grad_normed_own = back_product(grad_query_low, query_full)
    all_inputs = all_tokens.astype(wide)
    grad_attention_gain = jnp.sum(
        grad_normed_all * (all_inputs * rms_factor(all_inputs)), axis=0
    ) + jnp.sum(grad_normed_own * (inputs * rms_factor(inputs)), axis=0)
    grad_normed = seq_scatter(grad_normed_all, rows) + grad_normed_own
    grad_inputs, _ = norm_back(inputs, attention_gain_full, grad_normed)
    grad_inputs = grad_inputs + grad_hidden

    table_row = jnp.pad(grad_table.reshape(1, -1), ((0, 0), (0, width - grad_table.size)))
    last_rows = jnp.concatenate(
        [
            decoder_totals[: HEAD_ROWS + 3],
            grad_encoder_gain[None],
            grad_feed_gain[None],
            grad_attention_gain[None],
            table_row,
        ],
        axis=0,
    )
    last_rows = jnp.pad(last_rows, ((0, -last_rows.shape[0] % 8), (0, 0)))
    sums, backs = finish(last_rows, third_blocks, starts, gains, groups, members)
    (
        grad_start,
        grad_self_gain,
        grad_cross_gain,
        grad_cross_query_row,
        grad_self_branch,
        grad_self_vals,
    ) = [backs[i] for i in range(6)]

    def mine(values, size=part):
        return lax.dynamic_slice_in_dim(values, group * size, size, values.ndim - 1)

    def outer(left_side, right_side):
        return mine(left_side).astype(wide).T * right_side.astype(wide)

    def every_row(at, size=seqs):
        return decoder_rows[:, at : at + size].reshape(groups * size, width)

    at = 0
    cross_rows = every_row(0)
    second_in_rows = every_row(seqs)
    act_rows = decoder_rows[:, 2 * seqs : (2 + blocks) * seqs].reshape(
        groups, blocks, seqs, width
    )
    act_rows = jnp.transpose(act_rows, (0, 2, 1, 3)).reshape(groups * seqs, blocks * width)
    at = (2 + blocks) * seqs
    pooled_rows = every_row(at)
    branch_rows = every_row(at + seqs)
    pre_rows = decoder_rows[:, at + 2 * seqs : at + (2 + blocks) * seqs].reshape(
        groups, blocks, seqs, width
    )
    pre_rows = jnp.transpose(pre_rows, (0, 2, 1, 3)).reshape(groups * seqs, blocks * width)
    at = at + (2 + blocks) * seqs
    out_rows = every_row(at)
    grad_pooled_rows = every_row(at + seqs)
    att_rows = every_row(at + 2 * seqs)
    context_rows = every_row(at + 3 * seqs, seqs * HEADS)
    att_heads = jnp.where(
        head_mask[None], att_rows[:, None, :], jnp.zeros((), low)
    ).reshape(-1, width)

    inner_sums = jnp.transpose(second_sums[1 : 1 + blocks], (1, 0, 2)).reshape(
        part, blocks * width
    )
    query_sums, key_sums, value_sums = [
        jnp.transpose(first_sums[:, :, LANES * i : LANES * (i + 1)], (1, 0, 2)).reshape(part, width)
        for i in range(3)
    ]
    key_totals = mine(sums[:HEADS])
    other_sums = sums[HEAD_ROWS:]
    return (
        contrastive_loss,
        embedded,
        grad_inputs,
        mine(other_sums[5]),
        query_sums,
        key_sums,
        value_sums,
        second_sums[0],
        mine(other_sums[6, : BUCKETS * HEADS], BUCKETS * HEADS // groups).reshape(-1, HEADS),
        mine(other_sums[4]),
        inner_sums,
        second_sums[1 + blocks :].reshape(share, width),
        mine(other_sums[3]),
        mine(grad_start),
        mine(grad_self_gain),
        outer(self_in, grad_self_vals[None]),
        outer(self_vals, grad_self_branch[None]),
        mine(grad_cross_gain),
        outer(cross_in, grad_cross_query_row[None]),
        jnp.repeat(key_totals.T, HEAD, axis=1) * cross_query_row.astype(low).astype(wide),
        weight_grad(mine(context_rows), att_heads),
        weight_grad(mine(cross_rows), branch_rows),
        mine(other_sums[2]),
        weight_grad(mine(second_in_rows), pre_rows),
        weight_grad(mine(act_rows, share), out_rows),
        mine(other_sums[1]),
        weight_grad(mine(pooled_rows), grad_pooled_rows),
    )


def solution(mesh):
    placed = (
        P(("batch", "seq"), None),
        P("batch", None),
        P(),
        P("batch"),
        P("batch", None),
        P("batch", None),
        P("batch", None),
        P("batch", None),
        P("batch", None),
        P("batch"),
        P("batch", None),
        P("batch", None),
        P("batch"),
        P("batch"),
        P("batch"),
        P("batch", None),
        P("batch", None),
        P("batch"),
        P("batch", None),
        P("batch", None),
        P("batch", None),
        P("batch", None),
        P("batch"),
        P("batch", None),
        P("batch", None),
        P("batch"),
        P("batch", None),
    )
    return jax.shard_map(
        shards,
        mesh=mesh,
        in_specs=placed,
        out_specs=(
            P(),
            P("batch", None),
            P(("batch", "seq"), None),
            P("batch"),
            P("batch", None),
            P("batch", None),
            P("batch", None),
            P("batch", None),
            P("batch", None),
            P("batch"),
            P("batch", None),
            P("batch", None),
            P("batch"),
            P("batch"),
            P("batch"),
            P("batch", None),
            P("batch", None),
            P("batch"),
            P("batch", None),
            P("batch", None),
            P("batch", None),
            P("batch", None),
            P("batch"),
            P("batch", None),
            P("batch", None),
            P("batch"),
            P("batch", None),
        ),
        check_vma=False,
    )
```

```python
import functools
import math

import jax
import jax.numpy as jnp
from jax import lax
from jax.experimental import pallas as pl
from jax.experimental.pallas import tpu as pltpu
from jax.sharding import PartitionSpec as P

HEADS = 12
HEAD = 64
BUCKETS = 32
LANES = 128
far_apart = float(2**30)

eps_norm = 1e-06
masked_score = -1000000000.0
logit_scale = 20.0
bucket_limits = (12, 16, 23, 32, 46, 64, 91)
highest = lax.Precision.HIGHEST
low = jnp.bfloat16
wide = jnp.float32
MESH = pl.DeviceIdType.MESH


def rms_factor(values):
    return lax.rsqrt(jnp.mean(values * values, axis=-1, keepdims=True) + eps_norm)


def rms_norm(values, gain_vector):
    return (
        values
        * lax.rsqrt(jnp.mean(values * values, axis=-1, keepdims=True) + eps_norm)
        * gain_vector
    )


def unit_length(values):
    return values * lax.rsqrt(jnp.sum(values * values, axis=-1, keepdims=True) + eps_norm)


def bucket_of(offsets):
    upper_half = jnp.where(offsets > 0, 16, 0).astype(jnp.int32)
    distance = jnp.abs(offsets)
    far_bucket = 8 + sum(((distance >= threshold).astype(jnp.int32) for threshold in bucket_limits))
    return upper_half + jnp.where(distance < 8, distance, far_bucket)


def product(left_side, right_side):
    return jnp.dot(left_side, right_side, preferred_element_type=wide)


def back_product(left_side, right_side):
    return lax.dot_general(
        left_side, right_side, (((1,), (1,)), ((), ())), preferred_element_type=wide
    )


def weight_grad(left_side, right_side):
    return lax.dot_general(
        left_side, right_side, (((0,), (0,)), ((), ())), preferred_element_type=wide
    )


def norm_back(values, gain_vector, grad_rows):
    _, pullback = jax.vjp(rms_norm, values, gain_vector)
    return pullback(grad_rows)


def gelu_back(values, grad_rows):
    _, pullback = jax.vjp(jax.nn.gelu, values)
    return pullback(grad_rows)[0]


def segment_of(places, ends):
    return (places >= ends[0]).astype(jnp.int32) + (places >= ends[1]).astype(jnp.int32)


def block_rows(rows):
    return 256 if rows % 256 == 0 else rows


def table_sizes(size, pack):
    slack = LANES if size % LANES else 0
    reach = -(-(size + slack + 91) // LANES) * LANES
    lead = -(-(size + slack) // LANES) * LANES
    middle = -(-(pack - size) // LANES) * LANES
    return middle, reach, lead, middle + max(pack, reach)


def offset_biases(table, size, pack, shift):
    _, reach, lead, _ = table_sizes(size, pack)
    offsets = jnp.arange(lead + reach + LANES, dtype=jnp.int32) - (lead + LANES) - shift
    onehot = (
        bucket_of(offsets)[None, :] == jnp.arange(BUCKETS, dtype=jnp.int32)[:, None]
    ).astype(low)
    return weight_grad(table, onehot)[:, None, :]


def turned_biases(row, size, lead):
    spread = jnp.broadcast_to(row, (size, row.shape[1]))
    return pltpu.roll(spread, 0, 1, stride=1, stride_axis=0)[:, lead:]


class Gathering:
    def __init__(self, groups, members, sems):
        self.groups = groups
        self.members = members
        self.lines = groups // 4
        self.group = lax.axis_index("batch")
        self.member = lax.axis_index("seq")
        self.z = self.group // 4
        self.y = lax.rem(self.group // 2, 2)
        self.core = lax.rem(self.group, 2)
        self.line_send, self.line_recv, self.pair_sems, self.chip_sems, self.share_sems = sems

    def batch_id(self, offset):
        return {"batch": self.group + offset}

    def neighbours(self):
        found = [
            (None, self.batch_id(1 - 2 * self.core)),
            (None, self.batch_id(2 - 4 * self.y)),
            (self.z > 0, self.batch_id(-4)),
            (self.z < self.lines - 1, self.batch_id(4)),
        ]
        for step in range(1, self.members):
            found.append((None, {"seq": lax.rem(self.member + step, self.members)}))
        return found

    def greet(self, barrier):
        for condition, device in self.neighbours():
            if condition is None:
                pl.semaphore_signal(barrier, inc=1, device_id=device, device_id_type=MESH)
            else:

                @pl.when(condition)
                def _():
                    pl.semaphore_signal(barrier, inc=1, device_id=device, device_id_type=MESH)

    def greeted(self, barrier):
        ends = (self.z > 0).astype(jnp.int32) + (self.z < self.lines - 1).astype(jnp.int32)
        pl.semaphore_wait(barrier, 2 + self.members - 1 + ends)

    def copy(self, source, target, send, recv, device):
        return pltpu.make_async_remote_copy(
            src_ref=source,
            dst_ref=target,
            send_sem=send,
            recv_sem=recv,
            device_id=device,
            device_id_type=MESH,
        )

    def line_copy(self, item, source, full, way, step):
        place = self.z + step if way else self.z - step
        block = full.at[place, self.y, self.core]
        return self.copy(
            source if step == 0 else block,
            block,
            self.line_send.at[item, way, step],
            self.line_recv.at[item, way, step],
            self.batch_id(-4 if way else 4),
        )

    def line_sends(self, way, step):
        if way:
            return (self.z > 0) & (self.z + step < self.lines)
        return (self.z < self.lines - 1) & (self.z - step >= 0)

    def line_arrives(self, way, step):
        return self.z + step < self.lines if way else self.z - step >= 0

    def send_line(self, item, source, full, step):
        for way in range(2):

            @pl.when(self.line_sends(way, step))
            def _():
                self.line_copy(item, source, full, way, step).start()

    def pair_copy(self, item, full):
        span = full.at[:, self.y, self.core]
        return self.copy(
            span,
            span,
            self.pair_sems.at[item, 0],
            self.pair_sems.at[item, 1],
            self.batch_id(2 - 4 * self.y),
        )

    def share_copy(self, item, full):
        span = full.at[:, :, self.core]
        return self.copy(
            span,
            span,
            self.share_sems.at[item, 0],
            self.share_sems.at[item, 1],
            {"seq": 1 - self.member},
        )

    def chip_copy(self, item, which, full):
        span = full.at[:, :, self.core]
        return self.copy(
            span,
            span,
            self.chip_sems.at[item, which, 0],
            self.chip_sems.at[item, which, 1],
            self.batch_id(1 - 2 * self.core),
        )

    def stages(self, split):
        return self.lines + (3 if split else 2)

    def stage(self, number, item, source, full, other=None):
        lines = self.lines
        if number == 0:
            own = pltpu.make_async_copy(
                source, full.at[self.z, self.y, self.core], self.chip_sems.at[item, 0, 0]
            )
            own.start()
            self.send_line(item, source, full, 0)
            own.wait()
        elif number < lines:
            for way in range(2):

                @pl.when(self.line_arrives(way, number))
                def _():
                    self.line_copy(item, source, full, way, number - 1).wait_recv()

            if number < lines - 1:
                self.send_line(item, source, full, number)
            else:
                self.pair_copy(item, full).start()
        elif number == lines:
            self.pair_copy(item, full).wait()
            if other is not None:
                self.share_copy(item, full).start()
            self.chip_copy(item, 0, full).start()
        elif number == lines + 1 and other is not None:
            self.share_copy(item, full).wait()
            self.chip_copy(item, 1, other).start()
        else:
            self.chip_copy(item, 0, full).wait()
            if other is not None:
                self.chip_copy(item, 1, other).wait()
            for way in range(2):
                for step in range(lines - 1):

                    @pl.when(self.line_sends(way, step))
                    def _():
                        self.line_copy(item, source, full, way, step).wait_send()


def gathering_sems(groups, items):
    lines = groups // 4
    return [
        pltpu.SemaphoreType.DMA((items, 2, lines)),
        pltpu.SemaphoreType.DMA((items, 2, lines)),
        pltpu.SemaphoreType.DMA((items, 2)),
        pltpu.SemaphoreType.DMA((items, 2, 2)),
        pltpu.SemaphoreType.DMA((items, 2)),
    ]


def joined_rows(blocks):
    size, width = blocks.shape[-2:]
    rows = size * math.prod(blocks.shape[:-2])
    if size % 16:
        return blocks.astype(wide).reshape(rows, width).astype(low)
    return blocks.reshape(rows, width)


def first_kernel(
    groups,
    members,
    tokens_ref,
    extra_ref,
    query_ref,
    key_ref,
    value_ref,
    queries_ref,
    keys_ref,
    values_ref,
    normed_ref,
    gains_ref,
    weights_ref,
    all_tokens,
    all_extra,
    all_query,
    all_key,
    all_value,
    token_send,
    token_recv,
    *sems,
):
    parts = (extra_ref, query_ref, key_ref, value_ref)
    fulls = (all_extra, all_query, all_key, all_value)
    gathering = Gathering(groups, members, sems)
    member = gathering.member
    rows, width = tokens_ref.shape
    barrier = pltpu.get_barrier_semaphore()
    gathering.greet(barrier)
    gathering.greeted(barrier)
    copies = []
    for step in range(1, members):
        copies.append(
            pltpu.make_async_remote_copy(
                src_ref=tokens_ref,
                dst_ref=all_tokens.at[member],
                send_sem=token_send.at[step - 1],
                recv_sem=token_recv.at[step - 1],
                device_id={"seq": lax.rem(member + step, members)},
                device_id_type=MESH,
            )
        )
        copies[-1].start()
    all_tokens[member] = tokens_ref[...]

    def normed(values):
        values = values.astype(wide)
        return (values * rms_factor(values) * gains_ref[:1, :]).astype(low)

    def finished(item):
        if item == 0:
            total = jnp.zeros((16, width), wide)
            for z in range(groups // 4):
                for y in range(2):
                    for core in range(2):
                        total = total + all_extra[z, y, core].astype(wide)
            gains_ref[...] = total
        elif item == 1:
            weights_ref[0] = joined_rows(all_query[...])
            queries_ref[...] = product(normed(tokens_ref[...]), weights_ref[0]).astype(low)
        elif item == 2:
            for copy in copies:
                copy.wait()
            weights_ref[1] = joined_rows(all_key[...])
            for part in range(members):
                span = slice(rows * part, rows * (part + 1))
                normed_ref[span, :] = normed(all_tokens[part])
                keys_ref[span, :] = product(normed_ref[span, :], weights_ref[1]).astype(low)
        else:
            weights_ref[2] = joined_rows(all_value[...])
            for part in range(members):
                span = slice(rows * part, rows * (part + 1))
                values_ref[span, :] = product(normed_ref[span, :], weights_ref[2]).astype(low)

    stages = gathering.stages(False)
    for step in range(len(parts) + stages - 1):
        for stage in reversed(range(stages)):
            if 0 <= step - stage < len(parts):
                item = step - stage
                gathering.stage(stage, item, parts[item], fulls[item])
        if step - (stages - 1) >= 0:
            finished(step - (stages - 1))


def project(tokens, extra, parts, groups, members):
    rows, width = tokens.shape
    whole = pl.BlockSpec(memory_space=pltpu.VMEM)
    lines = groups // 4
    items = [extra] + list(parts)
    pack = members * rows
    return pl.pallas_call(
        functools.partial(first_kernel, groups, members),
        name="project",
        in_specs=[whole] * 5,
        out_specs=[whole] * 6,
        out_shape=[
            jax.ShapeDtypeStruct((rows, width), low),
            jax.ShapeDtypeStruct((pack, width), low),
            jax.ShapeDtypeStruct((pack, width), low),
            jax.ShapeDtypeStruct((pack, width), low),
            jax.ShapeDtypeStruct((16, width), wide),
            jax.ShapeDtypeStruct((3, width, width), low),
        ],
        scratch_shapes=[pltpu.VMEM((members,) + tokens.shape, low)]
        + [pltpu.VMEM((lines, 2, 2) + item.shape, low) for item in items]
        + [
            pltpu.SemaphoreType.DMA((max(members - 1, 1),)),
            pltpu.SemaphoreType.DMA((max(members - 1, 1),)),
        ]
        + gathering_sems(groups, len(items)),
        compiler_params=pltpu.CompilerParams(
            collective_id=3, has_side_effects=True, vmem_limit_bytes=48 * 2**20
        ),
        cost_estimate=pl.CostEstimate(
            flops=2**31, bytes_accessed=32 * pack * width, transcendentals=0
        ),
    )(tokens, extra, *parts)


def attend_kernel(
    place, q_ref, k_ref, v_ref, near_ref, attended_ref, total_ref, bias, key_side, value_side
):
    pair = pl.program_id(0)
    block = pl.program_id(1)
    pack = k_ref.shape[0]
    size = q_ref.shape[0]
    middle, reach, lead, width = table_sizes(size, pack)
    ends = (place[0], place[1])
    first = place[2] + block * size
    shift = place[3]

    @pl.when(block == 0)
    def _():
        places = lax.broadcasted_iota(jnp.int32, (pack, LANES), 0)
        lane = lax.broadcasted_iota(jnp.int32, (pack, LANES), 1)
        key_side[:, :LANES] = k_ref[...]
        key_side[:, LANES:] = (segment_of(places, ends) == lane).astype(wide).astype(low)
        value_side[:, :LANES] = v_ref[...]
        value_side[:, LANES:] = jnp.ones((pack, LANES), low)
        for half in range(2):
            row = near_ref[half]
            before = middle - LANES
            after = middle + reach
            bias[half, :, before:after] = turned_biases(row, size, lead)
            if before > 0:
                bias[half, :, :before] = jnp.broadcast_to(row[:, :1], (size, before))
            if after < width:
                bias[half, :, after:] = jnp.broadcast_to(row[:, -1:], (size, width - after))

    lane = lax.broadcasted_iota(jnp.int32, (size, LANES), 1)
    rows = first + lax.broadcasted_iota(jnp.int32, (size, LANES), 0)
    apart = jnp.where((segment_of(rows, ends) != lane) & (lane < 3), -far_apart, 0.0).astype(low)
    own = pl.ds(pl.multiple_of(block * size, 64), size)
    start = pl.multiple_of(middle - (first - shift), LANES)
    queries = q_ref[...]
    outputs = []
    totals = total_ref[own, :]
    for half in range(2):
        mine = (lane >= HEAD) if half else (lane < HEAD)
        query_side = jnp.concatenate(
            [jnp.where(mine, queries, jnp.zeros_like(queries)), apart], axis=1
        )
        scores = back_product(query_side, key_side[...]) + bias[half, :, pl.ds(start, pack)]
        top = jnp.max(scores, axis=1, keepdims=True)
        weights = jnp.exp(scores - top).astype(low)
        output = product(weights, value_side[...])
        total = output[:, LANES:]
        outputs.append(output[:, :LANES] / total)
        totals = jnp.where(lane == 2 * pair + half, top + jnp.log(total), totals)
    attended_ref[...] = jnp.where(lane < HEAD, outputs[0], outputs[1])
    total_ref[own, :] = totals


def attend(queries, all_keys, all_values, near, place):
    rows, width = queries.shape
    pack = all_keys.shape[0]
    size = block_rows(rows)
    _, _, _, columns = table_sizes(size, pack)
    pairs = width // LANES
    return pl.pallas_call(
        attend_kernel,
        name="attend",
        grid=(pairs, rows // size),
        in_specs=[
            pl.BlockSpec(memory_space=pltpu.SMEM),
            pl.BlockSpec((size, LANES), lambda p, i: (i, p)),
            pl.BlockSpec((pack, LANES), lambda p, i: (0, p)),
            pl.BlockSpec((pack, LANES), lambda p, i: (0, p)),
            pl.BlockSpec((2, 1, near.shape[2]), lambda p, i: (p, 0, 0)),
        ],
        out_specs=[
            pl.BlockSpec((size, LANES), lambda p, i: (i, p)),
            pl.BlockSpec((rows, LANES), lambda p, i: (0, 0)),
        ],
        out_shape=[
            jax.ShapeDtypeStruct((rows, width), wide),
            jax.ShapeDtypeStruct((rows, LANES), wide),
        ],
        scratch_shapes=[
            pltpu.VMEM((2, size, columns), wide),
            pltpu.VMEM((pack, 2 * LANES), low),
            pltpu.VMEM((pack, 2 * LANES), low),
        ],
        compiler_params=pltpu.CompilerParams(vmem_limit_bytes=48 * 2**20),
        cost_estimate=pl.CostEstimate(
            flops=8 * rows * pack * width * 2, bytes_accessed=16 * pack * width, transcendentals=0
        ),
    )(place, queries, all_keys, all_values, near)


SEQ_ROWS = 8
HEAD_ROWS = 16


def rms_back(values, gain_row, grad_rows):
    factor = rms_factor(values)
    scaled = gain_row * grad_rows
    inner = jnp.mean(scaled * values, axis=-1, keepdims=True)
    return (
        factor * scaled - values * (factor * factor * factor) * inner,
        jnp.sum(grad_rows * values * factor, axis=0, keepdims=True),
    )


gelu_scale = 0.7978845608028654


def gelu_value(values):
    return 0.5 * values * (
        1.0 + jnp.tanh(gelu_scale * (values + 0.044715 * values * values * values))
    )


def gelu_slope(values):
    square = values * values
    bent = jnp.tanh(gelu_scale * (values + 0.044715 * square * values))
    return 0.5 * (1.0 + bent) + 0.5 * values * (1.0 - bent * bent) * gelu_scale * (
        1.0 + 0.134145 * square
    )


def decoder_kernel(
    base,
    groups,
    members,
    seqs,
    place,
    context_ref,
    third_ref,
    gains_ref,
    target_ref,
    embedded_ref,
    loss_ref,
    grad_context_ref,
    pieces_ref,
    mixed_ref,
    starts_ref,
    totals_ref,
    weights,
    everyone,
    shared,
    similar_ref,
    halves_sent,
    halves_got,
    weight_sem,
    every_send,
    every_recv,
    share_send,
    share_recv,
    half_send,
    half_recv,
):
    rows, width = context_ref.shape
    count, _, _ = third_ref.shape
    unit = width // count
    halves = 2 if members == 2 else 1
    feeds = 4 // halves
    blocks = feeds * unit
    group = lax.axis_index("batch")
    member = lax.axis_index("seq")
    seq_total = groups * seqs

    barrier = pltpu.get_barrier_semaphore()
    for step in range(1, groups):
        pl.semaphore_signal(
            barrier,
            inc=1,
            device_id={"batch": lax.rem(group + step, groups)},
            device_id_type=MESH,
        )
    for step in range(1, members):
        pl.semaphore_signal(
            barrier,
            inc=1,
            device_id={"seq": lax.rem(member + step, members)},
            device_id_type=MESH,
        )

    sizes = [unit] * 7 + [unit] * feeds + [blocks]
    firsts = [sum(sizes[:i]) for i in range(len(sizes))]
    copies = [
        pltpu.make_async_copy(
            third_ref.at[:, base + first : base + first + size, :],
            weights.at[:, first : first + size, :],
            weight_sem.at[i],
        )
        for i, (first, size) in enumerate(zip(firsts, sizes))
    ]
    for copy in copies:
        copy.start()

    def weight(i):
        return weights[:, firsts[i] : firsts[i] + unit, :].reshape(width, width)

    def outer_weight(j):
        per = count // feeds
        return weights[per * j : per * (j + 1), firsts[-1] : firsts[-1] + blocks, :].reshape(
            width, width
        )

    def half_copy(which, first, number):
        span = pl.ds(first, number)
        return pltpu.make_async_remote_copy(
            src_ref=halves_sent.at[span],
            dst_ref=halves_got.at[span],
            send_sem=half_send.at[which],
            recv_sem=half_recv.at[which],
            device_id={"seq": 1 - member},
            device_id_type=MESH,
        )

    def joined(which, part):
        if halves == 1:
            return part
        halves_sent[which] = part
        copy = half_copy(which, which, 1)
        copy.start()
        copy.wait()
        return part + halves_got[which]

    gain = {
        name: gains_ref[i : i + 1, :]
        for i, name in enumerate(
            ("attention", "feed", "encoder", "start", "own", "cross", "second", "final")
        )
    }
    context = context_ref[...]

    start = jnp.broadcast_to(gain["start"], (SEQ_ROWS, width))
    self_in = (start * rms_factor(start) * gain["own"]).astype(low)
    copies[0].wait()
    self_vals = product(self_in, weight(0)).astype(low)
    copies[1].wait()
    after_self = start + product(self_vals, weight(1))
    cross_in = (after_self * rms_factor(after_self) * gain["cross"]).astype(low)
    copies[2].wait()
    cross_query = product(cross_in, weight(2))
    head_row = lax.broadcasted_iota(jnp.int32, (HEAD_ROWS, width), 0)
    head_mask = head_row == lax.broadcasted_iota(jnp.int32, (HEAD_ROWS, width), 1) // HEAD
    query_heads = jnp.where(
        head_mask, jnp.broadcast_to(cross_query[:1], (HEAD_ROWS, width)), 0.0
    ).astype(low)
    copies[3].wait()
    key_rows = back_product(query_heads, weight(3)).astype(low)

    many = seqs * HEAD_ROWS
    scores = back_product(key_rows, context)
    scores = jnp.concatenate([scores] * seqs, axis=0)
    places = member * rows + lax.broadcasted_iota(jnp.int32, (many, rows), 1)
    row_seq = lax.broadcasted_iota(jnp.int32, (many, rows), 0) // HEAD_ROWS
    inside = segment_of(places, (place[0], place[1])) == row_seq
    scores = jnp.where(inside, scores, masked_score)
    part_top = jnp.max(scores, axis=1, keepdims=True)
    part_weights = jnp.where(inside, jnp.exp(scores - part_top), 0.0).astype(low)
    part_total = jnp.sum(part_weights.astype(wide), axis=1, keepdims=True)
    lane = lax.broadcasted_iota(jnp.int32, (many, LANES), 1)
    shared[0, :, :width] = product(part_weights, context)
    shared[0, :, width:] = jnp.where(lane == 0, part_top, part_total)

    pl.semaphore_wait(barrier, groups - 1 + members - 1)
    for step in range(1, members):
        pltpu.make_async_remote_copy(
            src_ref=shared.at[0],
            dst_ref=shared.at[step],
            send_sem=share_send.at[step - 1],
            recv_sem=share_recv.at[step - 1],
            device_id={"seq": lax.rem(member + step, members)},
            device_id_type=MESH,
        ).start()
    for step in range(1, members):
        pltpu.make_async_remote_copy(
            src_ref=shared.at[0],
            dst_ref=shared.at[step],
            send_sem=share_send.at[step - 1],
            recv_sem=share_recv.at[step - 1],
            device_id={"seq": lax.rem(member + step, members)},
            device_id_type=MESH,
        ).wait()
    top = shared[0, :, width : width + 1]
    for step in range(1, members):
        top = jnp.maximum(top, shared[step, :, width : width + 1])
    total = jnp.zeros((many, 1), wide)
    mixed = jnp.zeros((many, width), wide)
    for step in range(members):
        scale = jnp.exp(shared[step, :, width : width + 1] - top)
        total = total + shared[step, :, width + 1 : width + 2] * scale
        mixed = mixed + shared[step, :, :width] * scale
    mixed = (mixed / total).astype(low)
    mixed_ref[...] = mixed
    log_total = top + jnp.log(total)

    def by_seq(parts):
        row = lax.broadcasted_iota(jnp.int32, (SEQ_ROWS, width), 0)
        joined = jnp.zeros((SEQ_ROWS, width), wide)
        for i, part in enumerate(parts):
            joined = jnp.where(row == i, part, joined)
        return joined

    copies[4].wait()
    spread = product(mixed, weight(4))
    cross_attended = by_seq(
        [
            jnp.sum(
                jnp.where(head_mask, spread[HEAD_ROWS * i : HEAD_ROWS * (i + 1)], 0.0),
                axis=0,
                keepdims=True,
            )
            for i in range(seqs)
        ]
    )
    cross_low = cross_attended.astype(low)
    copies[5].wait()
    after_cross = after_self + product(cross_low, weight(5))
    second_in = (after_cross * rms_factor(after_cross) * gain["second"]).astype(low)
    for copy in copies[7:]:
        copy.wait()
    second_pre = [product(second_in, weight(7 + j)) for j in range(feeds)]
    second_act = [gelu_value(second_pre[j]).astype(low) for j in range(feeds)]
    second_out = product(second_act[0], outer_weight(0))
    for j in range(1, feeds):
        second_out = second_out + product(second_act[j], outer_weight(j))
    decoded = after_cross + joined(0, second_out)
    pooled_in = (decoded * rms_factor(decoded) * gain["final"]).astype(low)
    copies[6].wait()
    pooled = product(pooled_in, weight(6))
    size = lax.rsqrt(jnp.sum(pooled * pooled, axis=-1, keepdims=True) + eps_norm)
    embedded = pooled * size
    embedded_ref[...] = embedded

    everyone[0] = embedded
    sends = []
    for step in range(1, groups):
        sends.append(
            pltpu.make_async_remote_copy(
                src_ref=everyone.at[0],
                dst_ref=everyone.at[step],
                send_sem=every_send,
                recv_sem=every_recv,
                device_id={"batch": lax.rem(group + step, groups)},
                device_id_type=MESH,
            )
        )
        sends[-1].start()
    arrival = pltpu.make_async_remote_copy(
        src_ref=everyone.at[pl.ds(1, groups - 1)],
        dst_ref=everyone.at[pl.ds(1, groups - 1)],
        send_sem=every_send,
        recv_sem=every_recv,
        device_id={"batch": lax.rem(group + 1, groups)},
        device_id_type=MESH,
    )
    arrival.wait_recv()
    arrival.wait_send()
    all_rows = everyone[...].reshape(groups * SEQ_ROWS, width)
    number = groups * SEQ_ROWS
    row = lax.broadcasted_iota(jnp.int32, (number, number), 0)
    column = lax.broadcasted_iota(jnp.int32, (number, number), 1)
    row_valid = row % SEQ_ROWS < seqs
    valid = row_valid & (column % SEQ_ROWS < seqs)
    similar = logit_scale * lax.dot_general(
        all_rows,
        all_rows,
        (((1,), (1,)), ((), ())),
        precision=highest,
        preferred_element_type=wide,
    )
    similar = jnp.where(valid & (row != column), similar, masked_score)
    best = jnp.max(similar, axis=1, keepdims=True)
    log_norm = best + jnp.log(jnp.sum(jnp.exp(similar - best), axis=1, keepdims=True))
    row_group = lax.rem(group - row // SEQ_ROWS + groups, groups)
    column_group = lax.rem(group - column // SEQ_ROWS + groups, groups)
    row_number = row_group * seqs + row % SEQ_ROWS
    column_number = column_group * seqs + column % SEQ_ROWS
    label = jnp.max(
        jnp.where(
            lax.broadcasted_iota(jnp.int32, (number, target_ref.shape[1]), 1)
            == row_number[:, : target_ref.shape[1]],
            target_ref[:1, :],
            -1.0,
        ),
        axis=1,
        keepdims=True,
    )
    target = (column_number.astype(wide) == label) & valid
    picked = jnp.sum(jnp.where(target, similar, 0.0), axis=1, keepdims=True)
    losses = jnp.where(row_valid[:, :1], log_norm - picked, 0.0)
    loss_ref[...] = jnp.broadcast_to(
        jnp.sum(losses, axis=0, keepdims=True) / seq_total, loss_ref.shape
    )
    grad_similar = jnp.where(
        valid, (jnp.exp(similar - log_norm) - target.astype(wide)) / seq_total, 0.0
    )
    similar_ref[...] = grad_similar + grad_similar.T
    grad_embedded = logit_scale * jnp.dot(
        similar_ref[:SEQ_ROWS, :], all_rows, precision=highest, preferred_element_type=wide
    )

    grad_pooled = (
        size
        * (grad_embedded - embedded * jnp.sum(embedded * grad_embedded, axis=-1, keepdims=True))
    ).astype(low)
    grad_decoded, grad_final_gain = rms_back(
        decoded, gain["final"], back_product(grad_pooled, weight(6))
    )
    grad_second_out = grad_decoded.astype(low)
    grad_second_pre = [
        (gelu_slope(second_pre[j]) * back_product(grad_second_out, outer_weight(j))).astype(low)
        for j in range(feeds)
    ]
    if halves == 2:
        for j in range(feeds):
            halves_sent[2 + j] = second_act[j].astype(wide)
            halves_sent[2 + feeds + j] = grad_second_pre[j].astype(wide)
        half_copy(2, 2, 2 * feeds).start()
    grad_second_in = back_product(grad_second_pre[0], weight(7))
    for j in range(1, feeds):
        grad_second_in = grad_second_in + back_product(grad_second_pre[j], weight(7 + j))
    grad_second_in = joined(1, grad_second_in)
    grad_after_cross, grad_second_gain = rms_back(after_cross, gain["second"], grad_second_in)
    grad_after_cross = grad_after_cross + grad_decoded
    grad_cross_branch = grad_after_cross.astype(low)
    grad_cross_att = back_product(grad_cross_branch, weight(5)).astype(low)
    grad_cross_wide = grad_cross_att.astype(wide)
    grad_heads = jnp.concatenate(
        [
            jnp.where(
                head_mask,
                jnp.broadcast_to(grad_cross_wide[i : i + 1], (HEAD_ROWS, width)),
                0.0,
            )
            for i in range(seqs)
        ],
        axis=0,
    )
    attended_heads = jnp.concatenate(
        [
            jnp.broadcast_to(cross_attended[i : i + 1], (HEAD_ROWS, width))
            for i in range(seqs)
        ],
        axis=0,
    )
    row_terms = jnp.sum(grad_heads * attended_heads, axis=1, keepdims=True)
    value_rows = back_product(grad_heads.astype(low), weight(4)).astype(low)
    probs = jnp.where(inside, jnp.exp(scores - log_total), 0.0)
    grad_scores = (probs * (back_product(value_rows, context) - row_terms)).astype(low)
    grad_context_ref[...] = weight_grad(
        jnp.concatenate([grad_scores, probs.astype(low)], axis=0),
        jnp.concatenate([key_rows] * seqs + [value_rows], axis=0),
    )
    key_sums = product(grad_scores, context)
    sums = key_sums[:HEAD_ROWS]
    for i in range(1, seqs):
        sums = sums + key_sums[HEAD_ROWS * i : HEAD_ROWS * (i + 1)]
    first_member = jnp.where(member == 0, 1.0, 0.0)
    totals_ref[:HEAD_ROWS, :] = sums
    totals_ref[HEAD_ROWS:, :] = first_member * by_seq(
        [jnp.sum(grad_after_cross, axis=0, keepdims=True), grad_final_gain, grad_second_gain]
    )
    for i, piece in zip(
        (0, 1, 6, 7, 12, 13, 14),
        (
            cross_low,
            second_in,
            pooled_in,
            grad_cross_branch,
            grad_second_out,
            grad_pooled,
            grad_cross_att,
        ),
    ):
        pieces_ref[i] = piece.astype(wide)
    if halves == 2:
        half_copy(2, 2, 2 * feeds).wait()
    for first, values, got in ((2, second_act, 2), (8, grad_second_pre, 2 + feeds)):
        for j in range(feeds):
            if halves == 1:
                pieces_ref[first + j] = values[j].astype(wide)
            else:
                pieces_ref[first + feeds * member + j] = values[j].astype(wide)
                pieces_ref[first + feeds * (1 - member) + j] = halves_got[got + j]
    for i, piece in enumerate([start, self_in, self_vals, after_self, cross_in, cross_query]):
        starts_ref[i : i + 1, :] = piece[:1].astype(wide)
    starts_ref[6:, :] = jnp.zeros((2, width), wide)


def decoder_step(context, third, base, gains, labels, place, groups, members, seqs):
    rows, width = context.shape
    everything = pl.BlockSpec(memory_space=pltpu.VMEM)
    labels = jnp.pad(labels.astype(wide)[None], ((0, 7), (0, LANES - labels.shape[0])))
    number = groups * SEQ_ROWS
    return pl.pallas_call(
        functools.partial(decoder_kernel, base, groups, members, seqs),
        name="decoder",
        in_specs=[
            pl.BlockSpec(memory_space=pltpu.SMEM),
            everything,
            pl.BlockSpec(memory_space=pl.ANY),
            everything,
            everything,
        ],
        out_specs=[everything] * 7,
        out_shape=[
            jax.ShapeDtypeStruct((SEQ_ROWS, width), wide),
            jax.ShapeDtypeStruct((8, LANES), wide),
            jax.ShapeDtypeStruct((rows, width), wide),
            jax.ShapeDtypeStruct((15, SEQ_ROWS, width), wide),
            jax.ShapeDtypeStruct((seqs * HEAD_ROWS, width), low),
            jax.ShapeDtypeStruct((8, width), wide),
            jax.ShapeDtypeStruct((HEAD_ROWS + SEQ_ROWS, width), wide),
        ],
        scratch_shapes=[
            pltpu.VMEM((third.shape[0], third.shape[1] - base, width), low),
            pltpu.VMEM((groups, SEQ_ROWS, width), wide),
            pltpu.VMEM((members, seqs * HEAD_ROWS, width + LANES), wide),
            pltpu.VMEM((number, number), wide),
            pltpu.VMEM((10, SEQ_ROWS, width), wide),
            pltpu.VMEM((10, SEQ_ROWS, width), wide),
            pltpu.SemaphoreType.DMA((12,)),
            pltpu.SemaphoreType.DMA,
            pltpu.SemaphoreType.DMA,
            pltpu.SemaphoreType.DMA((max(members - 1, 1),)),
            pltpu.SemaphoreType.DMA((max(members - 1, 1),)),
            pltpu.SemaphoreType.DMA((3,)),
            pltpu.SemaphoreType.DMA((3,)),
        ],
        compiler_params=pltpu.CompilerParams(
            collective_id=0, has_side_effects=True, vmem_limit_bytes=56 * 2**20
        ),
        cost_estimate=pl.CostEstimate(
            flops=2 * rows * width * 300, bytes_accessed=2 * third.size, transcendentals=0
        ),
    )(place, context, third, gains, labels)


class Summing:
    def __init__(self, groups, members, buffers):
        self.groups = groups
        self.members = members
        self.lines = groups // 4
        self.group = lax.axis_index("batch")
        self.member = lax.axis_index("seq")
        self.z = self.group // 4
        self.y = lax.rem(self.group // 2, 2)
        self.core = lax.rem(self.group, 2)
        (
            self.chip,
            self.pairs,
            self.line,
            self.shares,
            self.chip_send,
            self.chip_recv,
            self.pair_send,
            self.pair_recv,
            self.line_send,
            self.line_recv,
            self.share_send,
            self.share_recv,
        ) = buffers
        self.stages = 3 + self.lines

    def batch_id(self, offset):
        return {"batch": self.group + offset}

    def neighbours(self):
        found = [
            (None, self.batch_id(1 - 2 * self.core)),
            (None, self.batch_id(2 - 4 * self.y)),
            (self.z > 0, self.batch_id(-4)),
            (self.z < self.lines - 1, self.batch_id(4)),
        ]
        for step in range(1, self.members):
            found.append((None, {"seq": lax.rem(self.member + step, self.members)}))
        return found

    def greet(self, barrier):
        for condition, device in self.neighbours():
            if condition is None:
                pl.semaphore_signal(barrier, inc=1, device_id=device, device_id_type=MESH)
            else:

                @pl.when(condition)
                def _():
                    pl.semaphore_signal(barrier, inc=1, device_id=device, device_id_type=MESH)

    def greeted(self, barrier):
        ends = (self.z > 0).astype(jnp.int32) + (self.z < self.lines - 1).astype(jnp.int32)
        pl.semaphore_wait(barrier, 2 + self.members - 1 + ends)

    def copy(self, source, target, send, recv, device):
        return pltpu.make_async_remote_copy(
            src_ref=source,
            dst_ref=target,
            send_sem=send,
            recv_sem=recv,
            device_id=device,
            device_id_type=MESH,
        )

    def chip_copy(self, chunk, source):
        return self.copy(
            source,
            self.chip.at[chunk],
            self.chip_send.at[chunk],
            self.chip_recv.at[chunk],
            self.batch_id(1 - 2 * self.core),
        )

    def pair_copy(self, chunk):
        return self.copy(
            self.chip.at[chunk, :, 1 - self.y],
            self.pairs.at[chunk],
            self.pair_send.at[chunk],
            self.pair_recv.at[chunk],
            self.batch_id(2 - 4 * self.y),
        )

    def line_copy(self, chunk, way, first, last, source):
        return self.copy(
            source.at[chunk, pl.ds(first, last - first)]
            if source is self.pairs
            else source.at[chunk, way, pl.ds(first, last - first)],
            self.line.at[chunk, way, pl.ds(first, last - first)],
            self.line_send.at[chunk, way],
            self.line_recv.at[chunk, way],
            self.batch_id(-4 if way else 4),
        )

    def share_copy(self, chunk, step):
        return self.copy(
            self.shares.at[chunk, self.member],
            self.shares.at[chunk, self.member],
            self.share_send.at[chunk, step - 1],
            self.share_recv.at[chunk, step - 1],
            {"seq": lax.rem(self.member + step, self.members)},
        )

    def start(self, chunk, source):
        self.chip_copy(chunk, source).start()

    def to_pair(self, chunk, source, own):
        self.chip_copy(chunk, source).wait()
        self.chip[chunk] = (self.chip[chunk].astype(wide) + own.astype(wide)).astype(low)
        self.pair_copy(chunk).start()

    def to_line(self, chunk, step):
        lines = self.lines
        if step == 0:
            self.pair_copy(chunk).wait()
            self.pairs[chunk] = (
                self.pairs[chunk].astype(wide) + self.chip[chunk, :, self.y].astype(wide)
            ).astype(low)
        for way in range(2):
            at = lines - 1 - step if way else step
            first, last = (0, at) if way else (at + 1, lines)

            @pl.when(self.z == at)
            def _():
                if step > 0:
                    kept = (0, at + 1) if way else (at, lines)
                    self.line_copy(chunk, way, kept[0], kept[1], self.line).wait_recv()
                    span = pl.ds(first, last - first)
                    self.line[chunk, way, span] = (
                        self.line[chunk, way, span].astype(wide)
                        + self.pairs[chunk, span].astype(wide)
                    ).astype(low)
                self.line_copy(
                    chunk, way, first, last, self.line if step > 0 else self.pairs
                ).start()

    def to_members(self, chunk, held):
        lines = self.lines
        for way in range(2):
            end = 0 if way else lines - 1

            @pl.when(self.z == end)
            def _():
                kept = (0, 1) if way else (lines - 1, lines)
                self.line_copy(chunk, way, kept[0], kept[1], self.line).wait_recv()

            for step in range(lines - 1):
                at = lines - 1 - step if way else step
                first, last = (0, at) if way else (at + 1, lines)

                @pl.when(self.z == at)
                def _():
                    self.line_copy(chunk, way, first, last, self.line).wait_send()

        held[...] = self.pairs[chunk, self.z].astype(wide)

        @pl.when(self.z > 0)
        def _():
            held[...] += self.line[chunk, 0, self.z].astype(wide)

        @pl.when(self.z < lines - 1)
        def _():
            held[...] += self.line[chunk, 1, self.z].astype(wide)

        self.shares[chunk, self.member] = held[...].astype(low)
        for step in range(1, self.members):
            self.share_copy(chunk, step).start()

    def result(self, chunk):
        for step in range(1, self.members):
            self.share_copy(chunk, step).wait()
        total = self.shares[chunk, 0].astype(wide)
        for member in range(1, self.members):
            total = total + self.shares[chunk, member].astype(wide)
        return total


def summing_scratch(groups, members, chunks, rows, columns):
    lines = groups // 4
    return [
        pltpu.VMEM((chunks, lines, 2, rows, columns), low),
        pltpu.VMEM((chunks, lines, rows, columns), low),
        pltpu.VMEM((chunks, 2, lines, rows, columns), low),
        pltpu.VMEM((chunks, members, rows, columns), low),
        pltpu.SemaphoreType.DMA((chunks,)),
        pltpu.SemaphoreType.DMA((chunks,)),
        pltpu.SemaphoreType.DMA((chunks,)),
        pltpu.SemaphoreType.DMA((chunks,)),
        pltpu.SemaphoreType.DMA((chunks, 2)),
        pltpu.SemaphoreType.DMA((chunks, 2)),
        pltpu.SemaphoreType.DMA((chunks, max(members - 1, 1))),
        pltpu.SemaphoreType.DMA((chunks, max(members - 1, 1))),
    ]


def stage_delays(lines):
    return [1, 3] + [4 + step for step in range(lines - 2)] + [lines + 2, lines + 3]


def attend_back_kernel(
    groups,
    members,
    place,
    q_ref,
    k_ref,
    v_ref,
    grad_ref,
    attended_ref,
    total_ref,
    near_ref,
    own_turned_ref,
    all_turned_ref,
    parts_ref,
    grad_q_ref,
    grad_k_ref,
    grad_v_ref,
    band_ref,
    far_ref,
    feed_sums_ref,
    pair_sums_ref,
    bias,
    key_side,
    value_side,
    keys_turned,
    grad_scores,
    grad_k_sum,
    grad_v_sum,
    band_sum,
    grad_q_sum,
    pair_grads,
    fetched,
    held,
    fetch_sem,
    *buffers,
):
    pair = pl.program_id(0)
    block = pl.program_id(1)
    blocks = pl.num_programs(1)
    pairs = pl.num_programs(0)
    now = pair * blocks + block
    pack = k_ref.shape[0]
    size = q_ref.shape[0]
    middle, reach, lead, width = table_sizes(size, pack)
    ends = (place[0], place[1])
    rows_here = size * blocks
    summing = Summing(groups, members, buffers)
    first = summing.member * rows_here + block * size
    shift = lax.rem(summing.member * rows_here, LANES) if size % LANES else 0
    barrier = pltpu.get_barrier_semaphore()
    feed_chunks = 2 * parts_ref.shape[3]
    half_width = fetched.shape[-1]
    part = fetched.shape[-2]
    lines = groups // 4
    delays = stage_delays(lines)

    @pl.when(now == 0)
    def _():
        summing.greet(barrier)
        summing.greeted(barrier)

    def feed_part(chunk, core):
        return parts_ref.at[
            :, :, core, chunk // 2, :, pl.ds(pl.multiple_of(lax.rem(chunk, 2) * half_width, LANES), half_width)
        ]

    def fetch(chunk):
        slot = lax.rem(chunk, 4)
        return pltpu.make_async_copy(
            feed_part(chunk, summing.core), fetched.at[slot], fetch_sem.at[slot]
        )

    def feed_stage(stage, chunk):
        if stage == 0:
            summing.start(chunk, feed_part(chunk, 1 - summing.core))
            fetch(chunk).start()
        elif stage == 1:
            fetch(chunk).wait()
            summing.to_pair(
                chunk, feed_part(chunk, 1 - summing.core), fetched[lax.rem(chunk, 4)]
            )
        elif stage <= lines:
            summing.to_line(chunk, stage - 2)
        elif stage == lines + 1:
            summing.to_members(chunk, held)
        else:
            total = summing.result(chunk)
            column = pl.multiple_of(lax.rem(chunk, 2) * half_width, LANES)
            feed_sums_ref[chunk // 2, :, pl.ds(column, half_width)] = total

    def pair_stage(stage, which):
        chunk = feed_chunks + which
        if stage == 0:
            summing.start(chunk, pair_grads.at[which, :, :, 1 - summing.core])
        elif stage == 1:
            summing.to_pair(
                chunk,
                pair_grads.at[which, :, :, 1 - summing.core],
                pair_grads[which, :, :, summing.core],
            )
        elif stage <= lines:
            summing.to_line(chunk, stage - 2)
        elif stage == lines + 1:
            summing.to_members(chunk, held)
        else:
            pair_sums_ref[which] = summing.result(chunk)

    stages = 3 + lines
    starts = [0] + delays
    total_steps = pairs * blocks

    def run_stages(step):
        for stage in reversed(range(stages)):
            chunk = step - starts[stage]

            @pl.when((chunk >= 0) & (chunk < feed_chunks))
            def _():
                feed_stage(stage, chunk)

            late = step - (blocks - 1) - starts[stage]

            @pl.when((late >= 0) & (lax.rem(late + 64 * blocks, blocks) == 0) & (late < total_steps))
            def _():
                pair_stage(stage, late // blocks)

    @pl.when(block == 0)
    def _():
        places = lax.broadcasted_iota(jnp.int32, (pack, LANES), 0)
        lane = lax.broadcasted_iota(jnp.int32, (pack, LANES), 1)
        key_side[:, :LANES] = k_ref[...]
        ones = (segment_of(places, ends) == lane) | ((lane >= 3) & (lane < 9))
        key_side[:, LANES:] = ones.astype(wide).astype(low)
        value_side[:, :LANES] = v_ref[...]
        value_side[:, LANES:] = (lane < 6).astype(wide).astype(low)
        keys_turned[...] = k_ref[...].T
        for half in range(2):
            row = near_ref[half]
            before = middle - LANES
            after = middle + reach
            bias[half, before:after, :] = turned_biases(row, size, lead).T
            if before > 0:
                bias[half, :before, :] = jnp.broadcast_to(row[:, :1], (before, size))
            if after < width:
                bias[half, after:, :] = jnp.broadcast_to(row[:, -1:], (width - after, size))
        grad_scores[...] = jnp.zeros_like(grad_scores)
        grad_k_sum[...] = jnp.zeros_like(grad_k_sum)
        grad_v_sum[...] = jnp.zeros_like(grad_v_sum)
        band_sum[...] = jnp.zeros_like(band_sum)

    lane = lax.broadcasted_iota(jnp.int32, (size, LANES), 1)
    rows = first + lax.broadcasted_iota(jnp.int32, (size, LANES), 0)
    apart = jnp.where((segment_of(rows, ends) != lane) & (lane < 3), -far_apart, 0.0)
    start = pl.multiple_of(middle - (first - shift), LANES)
    near_rows = pl.ds(pl.multiple_of(first - shift, LANES), LANES + reach)
    queries = q_ref[...]
    grads = grad_ref[...]
    products = grads.astype(wide) * attended_ref[...]
    totals = total_ref[...]

    def in_parts(column, at):
        head = column.astype(low).astype(wide)
        body = (column - head).astype(low).astype(wide)
        tail = column - head - body
        return jnp.where(
            lane == at,
            head,
            jnp.where(lane == at + 1, body, jnp.where(lane == at + 2, tail, 0.0)),
        )

    query_grads = []
    for half in range(2):
        mine = (lane >= HEAD) if half else (lane < HEAD)
        row_term = jnp.sum(jnp.where(mine, products, 0.0), axis=1, keepdims=True)
        row_total = jnp.sum(
            jnp.where(lane == 2 * pair + half, totals, 0.0), axis=1, keepdims=True
        )
        query_part = jnp.where(mine, queries, jnp.zeros_like(queries))
        grad_part = jnp.where(mine, grads, jnp.zeros_like(grads))
        query_side = jnp.concatenate(
            [query_part, (apart - in_parts(row_total, 3 + 3 * half)).astype(low)], axis=1
        )
        grad_side = jnp.concatenate(
            [grad_part, (-in_parts(row_term, 3 * half)).astype(low)], axis=1
        )
        weights = jnp.exp(
            back_product(key_side[...], query_side) + bias[half, pl.ds(start, pack), :]
        )
        grad_block = (weights * back_product(value_side[...], grad_side)).astype(low)
        grad_scores[LANES : LANES + pack, :] = grad_block
        grad_v_sum[...] += product(weights.astype(low), grad_part)
        block_lane = jnp.where(lane == 8 * half + block, 1.0, 0.0).astype(low)
        grad_k_sum[...] += product(
            grad_block, jnp.concatenate([query_part, block_lane], axis=1)
        )
        query_grads.append(product(keys_turned[HEAD * half : HEAD * (half + 1), :], grad_block))
        band_sum[half] += grad_scores[near_rows, :].astype(wide)
    grad_query = jnp.concatenate(query_grads, axis=0).T.astype(low)
    grad_q_ref[...] = grad_query
    grad_q_sum[pl.ds(pl.multiple_of(block * size, 64), size), :] = grad_query

    @pl.when(block == blocks - 1)
    def _():
        grad_key = grad_k_sum[:, :LANES].astype(low)
        grad_value = grad_v_sum[...].astype(low)
        grad_k_ref[...] = grad_key
        grad_v_ref[...] = grad_value
        for i, gradient in enumerate(
            (
                product(own_turned_ref[...], grad_q_sum[...]),
                product(all_turned_ref[...], grad_key),
                product(all_turned_ref[...], grad_value),
            )
        ):
            pair_grads[pair, :, :, :, :, LANES * i : LANES * (i + 1)] = gradient.reshape(
                lines, 2, 2, part, LANES
            ).astype(low)
        key = lax.broadcasted_iota(jnp.int32, (pack, LANES), 0)
        which = lax.broadcasted_iota(jnp.int32, (pack, LANES), 1) % 8
        begin = summing.member * rows_here - shift + size * which
        sums = grad_k_sum[:, LANES:]
        below = jnp.sum(jnp.where(key < begin - LANES, sums, 0.0), axis=0, keepdims=True)
        above = jnp.sum(jnp.where(key >= begin + reach, sums, 0.0), axis=0, keepdims=True)
        far_ref[0] = jnp.concatenate([below, above, jnp.zeros((6, LANES), wide)], axis=0)
        columns = band_ref.shape[2]
        mirror = (
            lax.broadcasted_iota(jnp.int32, (size, columns), 0)
            + lax.broadcasted_iota(jnp.int32, (size, columns), 1)
            == size - 1
        ).astype(wide)
        for half in range(2):
            flipped = jnp.dot(
                band_sum[half], mirror, precision=highest, preferred_element_type=wide
            )
            turned = pltpu.roll(flipped, 0, 1, stride=1, stride_axis=0)
            band_ref[0, half : half + 1, :] = jnp.sum(turned, axis=0, keepdims=True)
        band_ref[0, 2:, :] = jnp.zeros((6, columns), wide)

    run_stages(now)

    @pl.when(now == total_steps - 1)
    def _():
        def drain(step, carry):
            run_stages(step)
            return carry

        lax.fori_loop(total_steps, total_steps + starts[-1] + 1, drain, 0)


def attend_back(
    queries, all_keys, all_values, grads, attended, totals, near, place, own_turned, all_turned, parts
):
    rows, width = queries.shape
    pack = all_keys.shape[0]
    size = block_rows(rows)
    _, reach, _, columns = table_sizes(size, pack)
    band = -(-(size + LANES + reach) // LANES) * LANES
    pairs = width // LANES
    members = pack // rows
    pieces = parts.shape[3]
    part = parts.shape[4]
    groups = 4 * parts.shape[0]
    half_width = width // 2
    chunks = 2 * pieces + pairs

    def own(p, i):
        return (i, p)

    def every(p, i):
        return (0, p)

    whole = pl.BlockSpec(memory_space=pltpu.VMEM)
    grad_q, grad_k, grad_v, band_sums, far_sums, feed_sums, pair_sums = pl.pallas_call(
        functools.partial(attend_back_kernel, groups, members),
        name="attend_back",
        grid=(pairs, rows // size),
        in_specs=[
            pl.BlockSpec(memory_space=pltpu.SMEM),
            pl.BlockSpec((size, LANES), own),
            pl.BlockSpec((pack, LANES), every),
            pl.BlockSpec((pack, LANES), every),
            pl.BlockSpec((size, LANES), own),
            pl.BlockSpec((size, LANES), own),
            pl.BlockSpec((size, LANES), lambda p, i: (i, 0)),
            pl.BlockSpec((2, 1, near.shape[2]), lambda p, i: (p, 0, 0)),
            whole,
            whole,
            pl.BlockSpec(memory_space=pl.ANY),
        ],
        out_specs=[
            pl.BlockSpec((size, LANES), own),
            pl.BlockSpec((pack, LANES), every),
            pl.BlockSpec((pack, LANES), every),
            pl.BlockSpec((1, 8, band), lambda p, i: (p, 0, 0)),
            pl.BlockSpec((1, 8, LANES), lambda p, i: (p, 0, 0)),
            whole,
            whole,
        ],
        out_shape=[
            jax.ShapeDtypeStruct((rows, width), low),
            jax.ShapeDtypeStruct((pack, width), low),
            jax.ShapeDtypeStruct((pack, width), low),
            jax.ShapeDtypeStruct((pairs, 8, band), wide),
            jax.ShapeDtypeStruct((pairs, 8, LANES), wide),
            jax.ShapeDtypeStruct((pieces, part, width), wide),
            jax.ShapeDtypeStruct((pairs, part, half_width), wide),
        ],
        scratch_shapes=[
            pltpu.VMEM((2, columns, size), wide),
            pltpu.VMEM((pack, 2 * LANES), low),
            pltpu.VMEM((pack, 2 * LANES), low),
            pltpu.VMEM((LANES, pack), low),
            pltpu.VMEM((LANES + pack + reach, size), low),
            pltpu.VMEM((pack, 2 * LANES), wide),
            pltpu.VMEM((pack, LANES), wide),
            pltpu.VMEM((2, LANES + reach, size), wide),
            pltpu.VMEM((rows, LANES), low),
            pltpu.VMEM((pairs, groups // 4, 2, 2, part, half_width), low),
            pltpu.VMEM((4, groups // 4, 2, part, half_width), low),
            pltpu.VMEM((part, half_width), wide),
            pltpu.SemaphoreType.DMA((4,)),
        ]
        + summing_scratch(groups, members, chunks, part, half_width),
        compiler_params=pltpu.CompilerParams(
            collective_id=1, has_side_effects=True, vmem_limit_bytes=62 * 2**20
        ),
        cost_estimate=pl.CostEstimate(
            flops=20 * rows * pack * width * 2, bytes_accessed=16 * pack * width, transcendentals=0
        ),
    )(
        place,
        queries,
        all_keys,
        all_values,
        grads,
        attended,
        totals,
        near,
        own_turned,
        all_turned,
        parts,
    )
    offsets = jnp.arange(band, dtype=jnp.int32) - (size - 1) - LANES - place[3]
    buckets = jnp.arange(BUCKETS, dtype=jnp.int32)
    onehot = (bucket_of(offsets)[:, None] == buckets[None, :]).astype(wide)
    near_grad = jnp.dot(
        band_sums[:, :2].reshape(HEADS, band), onehot, precision=highest, preferred_element_type=wide
    )
    far_grad = jnp.sum(far_sums[:, :2, :16].reshape(pairs, 2, 2, 8), axis=3)
    far_grad = jnp.transpose(far_grad, (0, 2, 1)).reshape(HEADS, 2)
    grad_table = near_grad + far_grad[:, :1] * (buckets == 15) + far_grad[:, 1:] * (buckets == 31)
    return grad_q, grad_k, grad_v, grad_table.T, feed_sums, pair_sums


def finish_kernel(
    base,
    groups,
    members,
    rows_ref,
    third_ref,
    starts_ref,
    gains_ref,
    sums_ref,
    backs_ref,
    weights,
    parts,
    weight_sem,
    send_sem,
    recv_sem,
):
    count, _, width = third_ref.shape
    unit = width // count
    group = lax.axis_index("batch")
    member = lax.axis_index("seq")
    partners = []
    for axis, place, number in (("batch", group, groups), ("seq", member, members)):
        span = 1
        while span < number:
            bit = lax.rem(place // span, 2)
            partners.append({axis: place + span * (1 - 2 * bit)})
            span *= 2
    barrier = pltpu.get_barrier_semaphore()
    for partner in partners:
        pl.semaphore_signal(barrier, inc=1, device_id=partner, device_id_type=MESH)
    copies = [
        pltpu.make_async_copy(
            third_ref.at[:, base + unit * i : base + unit * (i + 1), :], weights.at[i], weight_sem.at[i]
        )
        for i in range(4)
    ]
    for copy in copies:
        copy.start()
    parts[0] = rows_ref[...]
    pl.semaphore_wait(barrier, len(partners))
    for i, partner in enumerate(partners):
        copy = pltpu.make_async_remote_copy(
            src_ref=parts.at[2 * i],
            dst_ref=parts.at[2 * i + 1],
            send_sem=send_sem.at[i],
            recv_sem=recv_sem.at[i],
            device_id=partner,
            device_id_type=MESH,
        )
        copy.start()
        copy.wait()
        parts[2 * i + 2] = parts[2 * i] + parts[2 * i + 1]
    sums = parts[2 * len(partners)]
    sums_ref[...] = sums
    for copy in copies:
        copy.wait()

    def weight(i):
        return weights[i].reshape(width, width)

    head_row = lax.broadcasted_iota(jnp.int32, (HEAD_ROWS, width), 0)
    head_mask = head_row == lax.broadcasted_iota(jnp.int32, (HEAD_ROWS, width), 1) // HEAD
    spread = product(sums[:HEAD_ROWS].astype(low), weight(3))
    grad_cross_query = jnp.sum(jnp.where(head_mask, spread, 0.0), axis=0, keepdims=True)
    grad_cross_query = grad_cross_query.astype(low)

    def widened(row):
        return jnp.broadcast_to(row.astype(wide), (SEQ_ROWS, width))

    start = widened(starts_ref[0:1, :])
    after_self = widened(starts_ref[3:4, :])
    grad_rows = back_product(widened(grad_cross_query).astype(low), weight(2))
    grad_after_self, _ = rms_back(after_self, gains_ref[5:6, :], grad_rows)
    cross_gain = grad_rows * after_self * rms_factor(after_self)
    grad_after_self = grad_after_self + widened(sums[HEAD_ROWS : HEAD_ROWS + 1])
    grad_branch = grad_after_self.astype(low)
    grad_self_vals = back_product(grad_branch, weight(1)).astype(low)
    grad_rows = back_product(grad_self_vals, weight(0))
    grad_start, _ = rms_back(start, gains_ref[4:5, :], grad_rows)
    self_gain = grad_rows * start * rms_factor(start)
    for i, row in enumerate(
        (
            grad_start + grad_after_self,
            self_gain,
            cross_gain,
            grad_cross_query,
            grad_branch,
            grad_self_vals,
        )
    ):
        backs_ref[i : i + 1, :] = row[:1].astype(wide)
    backs_ref[6:, :] = jnp.zeros((2, width), wide)


def finish(rows, third, base, starts, gains, groups, members):
    many, width = rows.shape
    partners = (groups.bit_length() - 1) + (members.bit_length() - 1)
    count = third.shape[0]
    whole = pl.BlockSpec(memory_space=pltpu.VMEM)
    return pl.pallas_call(
        functools.partial(finish_kernel, base, groups, members),
        name="finish",
        in_specs=[whole, pl.BlockSpec(memory_space=pl.ANY), whole, whole],
        out_specs=[whole, whole],
        out_shape=[
            jax.ShapeDtypeStruct((many, width), wide),
            jax.ShapeDtypeStruct((8, width), wide),
        ],
        scratch_shapes=[
            pltpu.VMEM((4, count, width // count, width), low),
            pltpu.VMEM((2 * partners + 1, many, width), wide),
            pltpu.SemaphoreType.DMA((4,)),
            pltpu.SemaphoreType.DMA((partners,)),
            pltpu.SemaphoreType.DMA((partners,)),
        ],
        compiler_params=pltpu.CompilerParams(
            collective_id=2, has_side_effects=True, vmem_limit_bytes=32 * 2**20
        ),
        cost_estimate=pl.CostEstimate(
            flops=2**30, bytes_accessed=8 * width * width, transcendentals=0
        ),
    )(rows, third, starts, gains)


def seq_scatter(value, rows):
    count = lax.axis_size("seq")
    me = lax.axis_index("seq")
    total = lax.dynamic_slice_in_dim(value, me * rows, rows)
    for step in range(1, count):
        other = lax.dynamic_slice_in_dim(value, (me + step) % count * rows, rows)
        total = total + lax.ppermute(
            other.astype(low), "seq", [(i, (i + step) % count) for i in range(count)]
        ).astype(wide)
    return total


def in_blocks(gathered, sizes):
    count, _, width = gathered.shape
    join = 16 // math.gcd(16, sizes[0])
    if join == 1:
        return gathered
    pieces, at = [], 0
    for size in sizes:
        piece = gathered[:, at : at + size].reshape(count // join, join * size, width)
        pieces.append(piece)
        at += size
    return jnp.concatenate(pieces, axis=1)


def column_blocks(weight, model_width):
    rows, columns = weight.shape
    blocks = columns // model_width
    return jnp.transpose(weight.reshape(rows, blocks, model_width), (1, 0, 2)).reshape(
        blocks * rows, model_width
    )


def shards(
    tokens,
    lengths,
    labels,
    attention_gain,
    query_weight,
    key_weight,
    value_weight,
    attention_out,
    position_bias,
    feed_gain,
    feed_inner,
    feed_outer,
    encoder_gain,
    start_token,
    self_gain,
    self_value,
    self_out,
    cross_gain,
    cross_query,
    cross_key,
    cross_value,
    cross_out,
    second_gain,
    second_inner,
    second_outer,
    final_gain,
    pooler_weight,
):
    rows, width = tokens.shape
    part = query_weight.shape[0]
    share = feed_outer.shape[0]
    groups = lax.axis_size("batch")
    members = lax.axis_size("seq")
    blocks = feed_inner.shape[1] // width
    pack = rows * members
    seqs = lengths.shape[1]
    group = lax.axis_index("batch")
    member = lax.axis_index("seq")
    own_first = member * rows
    ends = jnp.cumsum(lengths[0])
    place = jnp.stack(
        [ends[0], ends[1], own_first, own_first % LANES]
    ).astype(jnp.int32)

    vectors = jnp.stack(
        [
            attention_gain,
            feed_gain,
            encoder_gain,
            start_token,
            self_gain,
            cross_gain,
            second_gain,
            final_gain,
        ],
        axis=0,
    )
    bias_part = position_bias.reshape(1, -1)
    bias_size = bias_part.shape[1]
    extra = jnp.zeros((16, width), low)
    extra = lax.dynamic_update_slice(extra, vectors, (0, group * part))
    extra = lax.dynamic_update_slice(extra, bias_part, (8, group * bias_size))
    queries, all_keys, all_values, normed_all, gains, first_full = project(
        tokens, extra, [query_weight, key_weight, value_weight], groups, members
    )
    normed = lax.dynamic_slice_in_dim(normed_all, own_first, rows)
    table = gains[8, : BUCKETS * HEADS].reshape(BUCKETS, HEADS).astype(low)
    second_part = jnp.concatenate(
        [
            attention_out[None],
            column_blocks(feed_inner, width).reshape(blocks, part, width),
            feed_outer.reshape(blocks, part, width),
        ],
        axis=0,
    )
    halves = 2 if members == 2 else 1
    half_share = share // halves
    half_inner = lax.dynamic_slice_in_dim(
        second_inner.reshape(part, groups, share), member % halves * half_share, half_share, 2
    ).reshape(part, groups * half_share)
    half_outer = lax.dynamic_slice_in_dim(second_outer, member % halves * half_share, half_share)
    rest_part = jnp.concatenate(
        [
            second_part.reshape(-1, width),
            self_value,
            self_out,
            cross_query,
            cross_key,
            cross_value,
            cross_out,
            pooler_weight,
            column_blocks(half_inner, width),
            half_outer,
        ],
        axis=0,
    )
    rest = lax.all_gather(rest_part, "batch", axis=0, tiled=False)
    second = rest

    def square(gathered, at):
        return gathered[:, at : at + part].reshape(groups * part, width)

    def tall(gathered, at):
        return gathered[:, at : at + share].reshape(groups * share, width)

    (
        attention_gain_full,
        feed_gain_full,
        encoder_gain_full,
        start_full,
        self_gain_full,
        cross_gain_full,
        second_gain_full,
        final_gain_full,
    ) = [gains[i] for i in range(8)]
    inputs = tokens.astype(wide)
    near = offset_biases(table, block_rows(rows), pack, place[3])
    attended, totals = attend(queries, all_keys, all_values, near, place)
    attended_low = attended.astype(low)
    out_full = square(second, 0)
    hidden = inputs + product(attended_low, out_full)

    inner_in = rms_norm(hidden, feed_gain_full).astype(low)
    inner_full = [square(second, part * (1 + j)) for j in range(blocks)]
    outer_full = tall(second, part * (1 + blocks)).reshape(blocks, -1, width)
    inner_pre = [product(inner_in, inner_full[j]) for j in range(blocks)]
    inner_act = [jax.nn.gelu(inner_pre[j]).astype(low) for j in range(blocks)]
    encoded = hidden
    for j in range(blocks):
        encoded = encoded + product(inner_act[j], outer_full[j])
    context = rms_norm(encoded, encoder_gain_full).astype(low)

    third_blocks = in_blocks(
        rest,
        [part] * (1 + blocks) + [share] + [part] * (7 + blocks // halves) + [half_share],
    )
    base = (1 + 2 * blocks) * (width // third_blocks.shape[0])
    (
        embedded,
        loss,
        grad_context,
        pieces,
        mixed,
        starts,
        decoder_totals,
    ) = decoder_step(
        context, third_blocks, base, gains, labels, place, groups, members, seqs
    )
    contrastive_loss = loss[0, :1]
    embedded = embedded[:seqs]
    decoder_rows = jnp.concatenate(
        [
            pieces[:, :seqs].astype(low).reshape(-1, width),
            mixed.reshape(seqs, HEAD_ROWS, width)[:, :HEADS].reshape(-1, width),
        ],
        axis=0,
    )
    start_row, self_in, self_vals, after_self, cross_in, cross_query_row = [
        starts[i : i + 1] for i in range(6)
    ]
    head_of = jnp.arange(width, dtype=jnp.int32) // HEAD
    head_mask = head_of[None, :] == jnp.arange(HEADS, dtype=jnp.int32)[:, None]

    count = decoder_rows.shape[0]
    decoder_rows = jnp.pad(decoder_rows, ((0, -count % 16), (0, 0)))
    decoder_rows = lax.all_gather(decoder_rows, "batch", axis=0, tiled=False)

    grad_encoded, _ = norm_back(encoded, encoder_gain_full, grad_context)
    grad_feed_branch = grad_encoded.astype(low)
    grad_inner_pre = [
        gelu_back(inner_pre[j], back_product(grad_feed_branch, outer_full[j])).astype(low)
        for j in range(blocks)
    ]
    grad_inner_in = sum(back_product(grad_inner_pre[j], inner_full[j]) for j in range(blocks))
    grad_hidden, _ = norm_back(hidden, feed_gain_full, grad_inner_in)
    grad_hidden = grad_hidden + grad_encoded
    grad_attn_branch = grad_hidden.astype(low)
    second_grads = jnp.concatenate(
        [weight_grad(attended_low, grad_attn_branch).astype(low).reshape(groups, 1, part, width)]
        + [
            weight_grad(inner_in, grad_inner_pre[j]).astype(low).reshape(groups, 1, part, width)
            for j in range(blocks)
        ]
        + [
            jnp.concatenate(
                [weight_grad(inner_act[j], grad_feed_branch).astype(low) for j in range(blocks)],
                axis=0,
            ).reshape(groups, blocks, part, width)
        ],
        axis=1,
    ).reshape(groups // 4, 2, 2, 1 + 2 * blocks, part, width)

    grad_attended = back_product(grad_attn_branch, out_full).astype(low)
    grad_query_low, grad_key_low, grad_value_low, grad_table, second_sums, first_sums = attend_back(
        queries,
        all_keys,
        all_values,
        grad_attended,
        attended,
        totals,
        near,
        place,
        normed.T,
        normed_all.T,
        second_grads,
    )
    grad_normed_all = back_product(grad_key_low, first_full[1]) + back_product(
        grad_value_low, first_full[2]
    )
    grad_normed_own = back_product(grad_query_low, first_full[0])
    grad_normed = seq_scatter(grad_normed_all, rows) + grad_normed_own
    grad_inputs, _ = norm_back(inputs, attention_gain_full, grad_normed)
    grad_inputs = grad_inputs + grad_hidden

    table_row = jnp.pad(grad_table.reshape(1, -1), ((0, 0), (0, width - grad_table.size)))
    last_rows = jnp.concatenate(
        [
            decoder_totals[: HEAD_ROWS + 3],
            table_row,
        ],
        axis=0,
    )
    last_rows = jnp.pad(last_rows, ((0, -last_rows.shape[0] % 8), (0, 0)))
    sums, backs = finish(last_rows, third_blocks, base, starts, gains, groups, members)
    (
        grad_start,
        grad_self_gain,
        grad_cross_gain,
        grad_cross_query_row,
        grad_self_branch,
        grad_self_vals,
    ) = [backs[i] for i in range(6)]

    def mine(values, size=part):
        return lax.dynamic_slice_in_dim(values, group * size, size, values.ndim - 1)

    def outer(left_side, right_side):
        return mine(left_side).astype(wide).T * right_side.astype(wide)

    def every_row(at, size=seqs):
        return decoder_rows[:, at : at + size].reshape(groups * size, width)

    at = 0
    cross_rows = every_row(0)
    second_in_rows = every_row(seqs)
    act_rows = decoder_rows[:, 2 * seqs : (2 + blocks) * seqs].reshape(
        groups, blocks, seqs, width
    )
    act_rows = jnp.transpose(act_rows, (0, 2, 1, 3)).reshape(
        groups * seqs, halves, groups, half_share
    )
    act_rows = lax.dynamic_slice_in_dim(act_rows, group, 1, 2).reshape(groups * seqs, share)
    at = (2 + blocks) * seqs
    pooled_rows = every_row(at)
    branch_rows = every_row(at + seqs)
    pre_rows = decoder_rows[:, at + 2 * seqs : at + (2 + blocks) * seqs].reshape(
        groups, blocks, seqs, width
    )
    pre_rows = jnp.transpose(pre_rows, (0, 2, 1, 3)).reshape(
        groups * seqs, halves, groups, half_share
    )
    pre_rows = jnp.transpose(pre_rows, (0, 2, 1, 3)).reshape(groups * seqs, blocks * width)
    at = at + (2 + blocks) * seqs
    out_rows = every_row(at)
    grad_pooled_rows = every_row(at + seqs)
    att_rows = every_row(at + 2 * seqs)
    context_rows = every_row(at + 3 * seqs, seqs * HEADS)
    att_heads = jnp.where(
        head_mask[None], att_rows[:, None, :], jnp.zeros((), low)
    ).reshape(-1, width)

    inner_sums = jnp.transpose(second_sums[1 : 1 + blocks], (1, 0, 2)).reshape(
        part, blocks * width
    )
    query_sums, key_sums, value_sums = [
        jnp.transpose(first_sums[:, :, LANES * i : LANES * (i + 1)], (1, 0, 2)).reshape(part, width)
        for i in range(3)
    ]
    key_totals = mine(sums[:HEADS])
    other_sums = sums[HEAD_ROWS:]
    def gain_grad(gain, *pairs):
        total = sum(jnp.sum(weight.astype(wide) * grads, axis=1) for weight, grads in pairs)
        return total / gain.astype(wide)

    cross_key_sums = jnp.repeat(key_totals.T, HEAD, axis=1) * cross_query_row.astype(low).astype(
        wide
    )
    cross_value_sums = weight_grad(mine(context_rows), att_heads)
    return (
        contrastive_loss,
        embedded,
        grad_inputs,
        gain_grad(
            attention_gain,
            (query_weight, query_sums),
            (key_weight, key_sums),
            (value_weight, value_sums),
        ),
        query_sums,
        key_sums,
        value_sums,
        second_sums[0],
        mine(other_sums[3, : BUCKETS * HEADS], BUCKETS * HEADS // groups).reshape(-1, HEADS),
        gain_grad(feed_gain, (feed_inner, inner_sums)),
        inner_sums,
        second_sums[1 + blocks :].reshape(share, width),
        gain_grad(encoder_gain, (cross_key, cross_key_sums), (cross_value, cross_value_sums)),
        mine(grad_start),
        mine(grad_self_gain),
        outer(self_in, grad_self_vals[None]),
        outer(self_vals, grad_self_branch[None]),
        mine(grad_cross_gain),
        outer(cross_in, grad_cross_query_row[None]),
        cross_key_sums,
        cross_value_sums,
        weight_grad(mine(cross_rows), branch_rows),
        mine(other_sums[2]),
        weight_grad(mine(second_in_rows), pre_rows),
        weight_grad(act_rows, out_rows),
        mine(other_sums[1]),
        weight_grad(mine(pooled_rows), grad_pooled_rows),
    )


def solution(mesh):
    placed = (
        P(("batch", "seq"), None),
        P("batch", None),
        P(),
        P("batch"),
        P("batch", None),
        P("batch", None),
        P("batch", None),
        P("batch", None),
        P("batch", None),
        P("batch"),
        P("batch", None),
        P("batch", None),
        P("batch"),
        P("batch"),
        P("batch"),
        P("batch", None),
        P("batch", None),
        P("batch"),
        P("batch", None),
        P("batch", None),
        P("batch", None),
        P("batch", None),
        P("batch"),
        P("batch", None),
        P("batch", None),
        P("batch"),
        P("batch", None),
    )
    return jax.shard_map(
        shards,
        mesh=mesh,
        in_specs=placed,
        out_specs=(
            P(),
            P("batch", None),
            P(("batch", "seq"), None),
            P("batch"),
            P("batch", None),
            P("batch", None),
            P("batch", None),
            P("batch", None),
            P("batch", None),
            P("batch"),
            P("batch", None),
            P("batch", None),
            P("batch"),
            P("batch"),
            P("batch"),
            P("batch", None),
            P("batch", None),
            P("batch"),
            P("batch", None),
            P("batch", None),
            P("batch", None),
            P("batch", None),
            P("batch"),
            P("batch", None),
            P("batch", None),
            P("batch"),
            P("batch", None),
        ),
        check_vma=False,
    )
```

```python
import functools
import math

import jax
import jax.numpy as jnp
from jax import lax
from jax.experimental import pallas as pl
from jax.experimental.pallas import tpu as pltpu
from jax.sharding import PartitionSpec as P

HEADS = 12
HEAD = 64
BUCKETS = 32
LANES = 128
far_apart = float(2**30)

eps_norm = 1e-06
masked_score = -1000000000.0
logit_scale = 20.0
bucket_limits = (12, 16, 23, 32, 46, 64, 91)
highest = lax.Precision.HIGHEST
low = jnp.bfloat16
wide = jnp.float32
MESH = pl.DeviceIdType.MESH


def rms_factor(values):
    return lax.rsqrt(jnp.mean(values * values, axis=-1, keepdims=True) + eps_norm)


def rms_norm(values, gain_vector):
    return (
        values
        * lax.rsqrt(jnp.mean(values * values, axis=-1, keepdims=True) + eps_norm)
        * gain_vector
    )


def unit_length(values):
    return values * lax.rsqrt(jnp.sum(values * values, axis=-1, keepdims=True) + eps_norm)


def bucket_of(offsets):
    upper_half = jnp.where(offsets > 0, 16, 0).astype(jnp.int32)
    distance = jnp.abs(offsets)
    far_bucket = 8 + sum(((distance >= threshold).astype(jnp.int32) for threshold in bucket_limits))
    return upper_half + jnp.where(distance < 8, distance, far_bucket)


def product(left_side, right_side):
    return jnp.dot(left_side, right_side, preferred_element_type=wide)


def back_product(left_side, right_side):
    return lax.dot_general(
        left_side, right_side, (((1,), (1,)), ((), ())), preferred_element_type=wide
    )


def weight_grad(left_side, right_side):
    return lax.dot_general(
        left_side, right_side, (((0,), (0,)), ((), ())), preferred_element_type=wide
    )


def norm_back(values, gain_vector, grad_rows):
    _, pullback = jax.vjp(rms_norm, values, gain_vector)
    return pullback(grad_rows)


def gelu_back(values, grad_rows):
    _, pullback = jax.vjp(jax.nn.gelu, values)
    return pullback(grad_rows)[0]


def segment_of(places, ends):
    return (places >= ends[0]).astype(jnp.int32) + (places >= ends[1]).astype(jnp.int32)


def block_rows(rows):
    return 256 if rows % 256 == 0 else rows


def table_sizes(size, pack):
    slack = LANES if size % LANES else 0
    reach = -(-(size + slack + 91) // LANES) * LANES
    lead = -(-(size + slack) // LANES) * LANES
    middle = -(-(pack - size) // LANES) * LANES
    return middle, reach, lead, middle + max(pack, reach)


def offset_biases(table, size, pack, shift):
    _, reach, lead, _ = table_sizes(size, pack)
    offsets = jnp.arange(lead + reach + LANES, dtype=jnp.int32) - (lead + LANES) - shift
    onehot = (
        bucket_of(offsets)[None, :] == jnp.arange(BUCKETS, dtype=jnp.int32)[:, None]
    ).astype(low)
    return weight_grad(table, onehot)[:, None, :]


def turned_biases(row, size, lead):
    spread = jnp.broadcast_to(row, (size, row.shape[1]))
    return pltpu.roll(spread, 0, 1, stride=1, stride_axis=0)[:, lead:]


class Gathering:
    def __init__(self, groups, members, sems):
        self.groups = groups
        self.members = members
        self.lines = groups // 4
        self.group = lax.axis_index("batch")
        self.member = lax.axis_index("seq")
        self.z = self.group // 4
        self.y = lax.rem(self.group // 2, 2)
        self.core = lax.rem(self.group, 2)
        self.line_send, self.line_recv, self.pair_sems, self.chip_sems, self.share_sems = sems

    def batch_id(self, offset):
        return {"batch": self.group + offset}

    def neighbours(self):
        found = [
            (None, self.batch_id(1 - 2 * self.core)),
            (None, self.batch_id(2 - 4 * self.y)),
            (self.z > 0, self.batch_id(-4)),
            (self.z < self.lines - 1, self.batch_id(4)),
        ]
        for step in range(1, self.members):
            found.append((None, {"seq": lax.rem(self.member + step, self.members)}))
        return found

    def greet(self, barrier):
        for condition, device in self.neighbours():
            if condition is None:
                pl.semaphore_signal(barrier, inc=1, device_id=device, device_id_type=MESH)
            else:

                @pl.when(condition)
                def _():
                    pl.semaphore_signal(barrier, inc=1, device_id=device, device_id_type=MESH)

    def greeted(self, barrier):
        ends = (self.z > 0).astype(jnp.int32) + (self.z < self.lines - 1).astype(jnp.int32)
        pl.semaphore_wait(barrier, 2 + self.members - 1 + ends)

    def copy(self, source, target, send, recv, device):
        return pltpu.make_async_remote_copy(
            src_ref=source,
            dst_ref=target,
            send_sem=send,
            recv_sem=recv,
            device_id=device,
            device_id_type=MESH,
        )

    def line_copy(self, item, source, full, way, step):
        place = self.z + step if way else self.z - step
        block = full.at[place, self.y, self.core]
        return self.copy(
            source if step == 0 else block,
            block,
            self.line_send.at[item, way, step],
            self.line_recv.at[item, way, step],
            self.batch_id(-4 if way else 4),
        )

    def line_sends(self, way, step):
        if way:
            return (self.z > 0) & (self.z + step < self.lines)
        return (self.z < self.lines - 1) & (self.z - step >= 0)

    def line_arrives(self, way, step):
        return self.z + step < self.lines if way else self.z - step >= 0

    def send_line(self, item, source, full, step):
        for way in range(2):

            @pl.when(self.line_sends(way, step))
            def _():
                self.line_copy(item, source, full, way, step).start()

    def pair_copy(self, item, full):
        span = full.at[:, self.y, self.core]
        return self.copy(
            span,
            span,
            self.pair_sems.at[item, 0],
            self.pair_sems.at[item, 1],
            self.batch_id(2 - 4 * self.y),
        )

    def share_copy(self, item, full):
        span = full.at[:, :, self.core]
        return self.copy(
            span,
            span,
            self.share_sems.at[item, 0],
            self.share_sems.at[item, 1],
            {"seq": 1 - self.member},
        )

    def chip_copy(self, item, which, full):
        span = full.at[:, :, self.core]
        return self.copy(
            span,
            span,
            self.chip_sems.at[item, which, 0],
            self.chip_sems.at[item, which, 1],
            self.batch_id(1 - 2 * self.core),
        )

    def stages(self, split):
        return self.lines + (3 if split else 2)

    def stage(self, number, item, source, full, other=None):
        lines = self.lines
        if number == 0:
            own = pltpu.make_async_copy(
                source, full.at[self.z, self.y, self.core], self.chip_sems.at[item, 0, 0]
            )
            own.start()
            self.send_line(item, source, full, 0)
            own.wait()
        elif number < lines:
            for way in range(2):

                @pl.when(self.line_arrives(way, number))
                def _():
                    self.line_copy(item, source, full, way, number - 1).wait_recv()

            if number < lines - 1:
                self.send_line(item, source, full, number)
            else:
                self.pair_copy(item, full).start()
        elif number == lines:
            self.pair_copy(item, full).wait()
            if other is not None:
                self.share_copy(item, full).start()
            self.chip_copy(item, 0, full).start()
        elif number == lines + 1 and other is not None:
            self.share_copy(item, full).wait()
            self.chip_copy(item, 1, other).start()
        else:
            self.chip_copy(item, 0, full).wait()
            if other is not None:
                self.chip_copy(item, 1, other).wait()
            for way in range(2):
                for step in range(lines - 1):

                    @pl.when(self.line_sends(way, step))
                    def _():
                        self.line_copy(item, source, full, way, step).wait_send()


def gathering_sems(groups, items):
    lines = groups // 4
    return [
        pltpu.SemaphoreType.DMA((items, 2, lines)),
        pltpu.SemaphoreType.DMA((items, 2, lines)),
        pltpu.SemaphoreType.DMA((items, 2)),
        pltpu.SemaphoreType.DMA((items, 2, 2)),
        pltpu.SemaphoreType.DMA((items, 2)),
    ]


def joined_rows(blocks):
    size, width = blocks.shape[-2:]
    rows = size * math.prod(blocks.shape[:-2])
    if size % 16:
        return blocks.astype(wide).reshape(rows, width).astype(low)
    return blocks.reshape(rows, width)


def first_kernel(
    groups,
    members,
    tokens_ref,
    extra_ref,
    query_ref,
    key_ref,
    value_ref,
    queries_ref,
    keys_ref,
    values_ref,
    normed_ref,
    gains_ref,
    weights_ref,
    all_tokens,
    all_extra,
    all_query,
    all_key,
    all_value,
    token_send,
    token_recv,
    *sems,
):
    parts = (extra_ref, query_ref, key_ref, value_ref)
    fulls = (all_extra, all_query, all_key, all_value)
    gathering = Gathering(groups, members, sems)
    member = gathering.member
    rows, width = tokens_ref.shape
    barrier = pltpu.get_barrier_semaphore()
    gathering.greet(barrier)
    gathering.greeted(barrier)
    copies = []
    for step in range(1, members):
        copies.append(
            pltpu.make_async_remote_copy(
                src_ref=tokens_ref,
                dst_ref=all_tokens.at[member],
                send_sem=token_send.at[step - 1],
                recv_sem=token_recv.at[step - 1],
                device_id={"seq": lax.rem(member + step, members)},
                device_id_type=MESH,
            )
        )
        copies[-1].start()
    all_tokens[member] = tokens_ref[...]

    def normed(values):
        values = values.astype(wide)
        return (values * rms_factor(values) * gains_ref[:1, :]).astype(low)

    def finished(item):
        if item == 0:
            total = jnp.zeros((16, width), wide)
            for z in range(groups // 4):
                for y in range(2):
                    for core in range(2):
                        total = total + all_extra[z, y, core].astype(wide)
            gains_ref[...] = total
        elif item == 1:
            weights_ref[0] = joined_rows(all_query[...])
            queries_ref[...] = product(normed(tokens_ref[...]), weights_ref[0]).astype(low)
        elif item == 2:
            for copy in copies:
                copy.wait()
            weights_ref[1] = joined_rows(all_key[...])
            for part in range(members):
                span = slice(rows * part, rows * (part + 1))
                normed_ref[span, :] = normed(all_tokens[part])
                keys_ref[span, :] = product(normed_ref[span, :], weights_ref[1]).astype(low)
        else:
            weights_ref[2] = joined_rows(all_value[...])
            for part in range(members):
                span = slice(rows * part, rows * (part + 1))
                values_ref[span, :] = product(normed_ref[span, :], weights_ref[2]).astype(low)

    stages = gathering.stages(False)
    for step in range(len(parts) + stages - 1):
        for stage in reversed(range(stages)):
            if 0 <= step - stage < len(parts):
                item = step - stage
                gathering.stage(stage, item, parts[item], fulls[item])
        if step - (stages - 1) >= 0:
            finished(step - (stages - 1))


def project(tokens, extra, parts, groups, members):
    rows, width = tokens.shape
    whole = pl.BlockSpec(memory_space=pltpu.VMEM)
    lines = groups // 4
    items = [extra] + list(parts)
    pack = members * rows
    return pl.pallas_call(
        functools.partial(first_kernel, groups, members),
        name="project",
        in_specs=[whole] * 5,
        out_specs=[whole] * 6,
        out_shape=[
            jax.ShapeDtypeStruct((rows, width), low),
            jax.ShapeDtypeStruct((pack, width), low),
            jax.ShapeDtypeStruct((pack, width), low),
            jax.ShapeDtypeStruct((pack, width), low),
            jax.ShapeDtypeStruct((16, width), wide),
            jax.ShapeDtypeStruct((3, width, width), low),
        ],
        scratch_shapes=[pltpu.VMEM((members,) + tokens.shape, low)]
        + [pltpu.VMEM((lines, 2, 2) + item.shape, low) for item in items]
        + [
            pltpu.SemaphoreType.DMA((max(members - 1, 1),)),
            pltpu.SemaphoreType.DMA((max(members - 1, 1),)),
        ]
        + gathering_sems(groups, len(items)),
        compiler_params=pltpu.CompilerParams(
            collective_id=3, has_side_effects=True, vmem_limit_bytes=48 * 2**20
        ),
        cost_estimate=pl.CostEstimate(
            flops=2**31, bytes_accessed=32 * pack * width, transcendentals=0
        ),
    )(tokens, extra, *parts)


def attend_kernel(
    place, q_ref, k_ref, v_ref, near_ref, attended_ref, total_ref, bias, key_side, value_side
):
    pair = pl.program_id(0)
    block = pl.program_id(1)
    pack = k_ref.shape[0]
    size = q_ref.shape[0]
    middle, reach, lead, width = table_sizes(size, pack)
    ends = (place[0], place[1])
    first = place[2] + block * size
    shift = place[3]

    @pl.when(block == 0)
    def _():
        places = lax.broadcasted_iota(jnp.int32, (pack, LANES), 0)
        lane = lax.broadcasted_iota(jnp.int32, (pack, LANES), 1)
        key_side[:, :LANES] = k_ref[...]
        key_side[:, LANES:] = (segment_of(places, ends) == lane).astype(wide).astype(low)
        value_side[:, :LANES] = v_ref[...]
        value_side[:, LANES:] = jnp.ones((pack, LANES), low)
        for half in range(2):
            row = near_ref[half]
            before = middle - LANES
            after = middle + reach
            bias[half, :, before:after] = turned_biases(row, size, lead)
            if before > 0:
                bias[half, :, :before] = jnp.broadcast_to(row[:, :1], (size, before))
            if after < width:
                bias[half, :, after:] = jnp.broadcast_to(row[:, -1:], (size, width - after))

    lane = lax.broadcasted_iota(jnp.int32, (size, LANES), 1)
    rows = first + lax.broadcasted_iota(jnp.int32, (size, LANES), 0)
    apart = jnp.where((segment_of(rows, ends) != lane) & (lane < 3), -far_apart, 0.0).astype(low)
    own = pl.ds(pl.multiple_of(block * size, 64), size)
    start = pl.multiple_of(middle - (first - shift), LANES)
    queries = q_ref[...]
    outputs = []
    totals = total_ref[own, :]
    for half in range(2):
        mine = (lane >= HEAD) if half else (lane < HEAD)
        query_side = jnp.concatenate(
            [jnp.where(mine, queries, jnp.zeros_like(queries)), apart], axis=1
        )
        scores = back_product(query_side, key_side[...]) + bias[half, :, pl.ds(start, pack)]
        top = jnp.max(scores, axis=1, keepdims=True)
        weights = jnp.exp(scores - top).astype(low)
        output = product(weights, value_side[...])
        total = output[:, LANES:]
        outputs.append(output[:, :LANES] / total)
        totals = jnp.where(lane == 2 * pair + half, top + jnp.log(total), totals)
    attended_ref[...] = jnp.where(lane < HEAD, outputs[0], outputs[1])
    total_ref[own, :] = totals


def attend(queries, all_keys, all_values, near, place):
    rows, width = queries.shape
    pack = all_keys.shape[0]
    size = block_rows(rows)
    _, _, _, columns = table_sizes(size, pack)
    pairs = width // LANES
    return pl.pallas_call(
        attend_kernel,
        name="attend",
        grid=(pairs, rows // size),
        in_specs=[
            pl.BlockSpec(memory_space=pltpu.SMEM),
            pl.BlockSpec((size, LANES), lambda p, i: (i, p)),
            pl.BlockSpec((pack, LANES), lambda p, i: (0, p)),
            pl.BlockSpec((pack, LANES), lambda p, i: (0, p)),
            pl.BlockSpec((2, 1, near.shape[2]), lambda p, i: (p, 0, 0)),
        ],
        out_specs=[
            pl.BlockSpec((size, LANES), lambda p, i: (i, p)),
            pl.BlockSpec((rows, LANES), lambda p, i: (0, 0)),
        ],
        out_shape=[
            jax.ShapeDtypeStruct((rows, width), wide),
            jax.ShapeDtypeStruct((rows, LANES), wide),
        ],
        scratch_shapes=[
            pltpu.VMEM((2, size, columns), wide),
            pltpu.VMEM((pack, 2 * LANES), low),
            pltpu.VMEM((pack, 2 * LANES), low),
        ],
        compiler_params=pltpu.CompilerParams(vmem_limit_bytes=48 * 2**20),
        cost_estimate=pl.CostEstimate(
            flops=8 * rows * pack * width * 2, bytes_accessed=16 * pack * width, transcendentals=0
        ),
    )(place, queries, all_keys, all_values, near)


SEQ_ROWS = 8
HEAD_ROWS = 16


def rms_back(values, gain_row, grad_rows):
    factor = rms_factor(values)
    scaled = gain_row * grad_rows
    inner = jnp.mean(scaled * values, axis=-1, keepdims=True)
    return (
        factor * scaled - values * (factor * factor * factor) * inner,
        jnp.sum(grad_rows * values * factor, axis=0, keepdims=True),
    )


gelu_scale = 0.7978845608028654


def gelu_value(values):
    return 0.5 * values * (
        1.0 + jnp.tanh(gelu_scale * (values + 0.044715 * values * values * values))
    )


def gelu_slope(values):
    square = values * values
    bent = jnp.tanh(gelu_scale * (values + 0.044715 * square * values))
    return 0.5 * (1.0 + bent) + 0.5 * values * (1.0 - bent * bent) * gelu_scale * (
        1.0 + 0.134145 * square
    )


def decoder_kernel(
    base,
    groups,
    members,
    seqs,
    place,
    context_ref,
    third_ref,
    gains_ref,
    target_ref,
    embedded_ref,
    loss_ref,
    grad_context_ref,
    pieces_ref,
    starts_ref,
    totals_ref,
    weights,
    everyone,
    shared,
    similar_ref,
    halves_sent,
    halves_got,
    piece_rows,
    weight_sem,
    every_send,
    every_recv,
    share_send,
    share_recv,
    half_send,
    half_recv,
):
    rows, width = context_ref.shape
    count, _, _ = third_ref.shape
    unit = width // count
    halves = 2 if members == 2 else 1
    feeds = 4 // halves
    blocks = feeds * unit
    group = lax.axis_index("batch")
    member = lax.axis_index("seq")
    seq_total = groups * seqs

    barrier = pltpu.get_barrier_semaphore()
    for step in range(1, groups):
        pl.semaphore_signal(
            barrier,
            inc=1,
            device_id={"batch": lax.rem(group + step, groups)},
            device_id_type=MESH,
        )
    for step in range(1, members):
        pl.semaphore_signal(
            barrier,
            inc=1,
            device_id={"seq": lax.rem(member + step, members)},
            device_id_type=MESH,
        )

    sizes = [unit] * 7 + [unit] * feeds + [blocks]
    firsts = [sum(sizes[:i]) for i in range(len(sizes))]
    copies = [
        pltpu.make_async_copy(
            third_ref.at[:, base + first : base + first + size, :],
            weights.at[:, first : first + size, :],
            weight_sem.at[i],
        )
        for i, (first, size) in enumerate(zip(firsts, sizes))
    ]
    for copy in copies:
        copy.start()

    def weight(i):
        return weights[:, firsts[i] : firsts[i] + unit, :].reshape(width, width)

    def outer_weight(j):
        per = count // feeds
        return weights[per * j : per * (j + 1), firsts[-1] : firsts[-1] + blocks, :].reshape(
            width, width
        )

    def half_copy(which, first, number):
        span = pl.ds(first, number)
        return pltpu.make_async_remote_copy(
            src_ref=halves_sent.at[span],
            dst_ref=halves_got.at[span],
            send_sem=half_send.at[which],
            recv_sem=half_recv.at[which],
            device_id={"seq": 1 - member},
            device_id_type=MESH,
        )

    def joined(which, part):
        if halves == 1:
            return part
        halves_sent[which] = part
        copy = half_copy(which, which, 1)
        copy.start()
        copy.wait()
        return part + halves_got[which]

    gain = {
        name: gains_ref[i : i + 1, :]
        for i, name in enumerate(
            ("attention", "feed", "encoder", "start", "own", "cross", "second", "final")
        )
    }
    context = context_ref[...]

    start = jnp.broadcast_to(gain["start"], (SEQ_ROWS, width))
    self_in = (start * rms_factor(start) * gain["own"]).astype(low)
    copies[0].wait()
    self_vals = product(self_in, weight(0)).astype(low)
    copies[1].wait()
    after_self = start + product(self_vals, weight(1))
    cross_in = (after_self * rms_factor(after_self) * gain["cross"]).astype(low)
    copies[2].wait()
    cross_query = product(cross_in, weight(2))
    head_row = lax.broadcasted_iota(jnp.int32, (HEAD_ROWS, width), 0)
    head_mask = head_row == lax.broadcasted_iota(jnp.int32, (HEAD_ROWS, width), 1) // HEAD
    query_heads = jnp.where(
        head_mask, jnp.broadcast_to(cross_query[:1], (HEAD_ROWS, width)), 0.0
    ).astype(low)
    copies[3].wait()
    key_rows = back_product(query_heads, weight(3)).astype(low)

    many = seqs * HEAD_ROWS
    scores = back_product(key_rows, context)
    scores = jnp.concatenate([scores] * seqs, axis=0)
    places = member * rows + lax.broadcasted_iota(jnp.int32, (many, rows), 1)
    row_seq = lax.broadcasted_iota(jnp.int32, (many, rows), 0) // HEAD_ROWS
    inside = segment_of(places, (place[0], place[1])) == row_seq
    scores = jnp.where(inside, scores, masked_score)
    part_top = jnp.max(scores, axis=1, keepdims=True)
    part_weights = jnp.where(inside, jnp.exp(scores - part_top), 0.0).astype(low)
    part_total = jnp.sum(part_weights.astype(wide), axis=1, keepdims=True)
    lane = lax.broadcasted_iota(jnp.int32, (many, LANES), 1)
    shared[0, :, :width] = product(part_weights, context)
    shared[0, :, width:] = jnp.where(lane == 0, part_top, part_total)

    pl.semaphore_wait(barrier, groups - 1 + members - 1)
    for step in range(1, members):
        pltpu.make_async_remote_copy(
            src_ref=shared.at[0],
            dst_ref=shared.at[step],
            send_sem=share_send.at[step - 1],
            recv_sem=share_recv.at[step - 1],
            device_id={"seq": lax.rem(member + step, members)},
            device_id_type=MESH,
        ).start()
    for step in range(1, members):
        pltpu.make_async_remote_copy(
            src_ref=shared.at[0],
            dst_ref=shared.at[step],
            send_sem=share_send.at[step - 1],
            recv_sem=share_recv.at[step - 1],
            device_id={"seq": lax.rem(member + step, members)},
            device_id_type=MESH,
        ).wait()
    top = shared[0, :, width : width + 1]
    for step in range(1, members):
        top = jnp.maximum(top, shared[step, :, width : width + 1])
    total = jnp.zeros((many, 1), wide)
    mixed = jnp.zeros((many, width), wide)
    for step in range(members):
        scale = jnp.exp(shared[step, :, width : width + 1] - top)
        total = total + shared[step, :, width + 1 : width + 2] * scale
        mixed = mixed + shared[step, :, :width] * scale
    mixed = (mixed / total).astype(low)
    log_total = top + jnp.log(total)

    def by_seq(parts):
        row = lax.broadcasted_iota(jnp.int32, (SEQ_ROWS, width), 0)
        joined = jnp.zeros((SEQ_ROWS, width), wide)
        for i, part in enumerate(parts):
            joined = jnp.where(row == i, part, joined)
        return joined

    copies[4].wait()
    spread = product(mixed, weight(4))
    cross_attended = by_seq(
        [
            jnp.sum(
                jnp.where(head_mask, spread[HEAD_ROWS * i : HEAD_ROWS * (i + 1)], 0.0),
                axis=0,
                keepdims=True,
            )
            for i in range(seqs)
        ]
    )
    cross_low = cross_attended.astype(low)
    copies[5].wait()
    after_cross = after_self + product(cross_low, weight(5))
    second_in = (after_cross * rms_factor(after_cross) * gain["second"]).astype(low)
    for copy in copies[7:]:
        copy.wait()
    second_pre = [product(second_in, weight(7 + j)) for j in range(feeds)]
    second_act = [gelu_value(second_pre[j]).astype(low) for j in range(feeds)]
    second_out = product(second_act[0], outer_weight(0))
    for j in range(1, feeds):
        second_out = second_out + product(second_act[j], outer_weight(j))
    decoded = after_cross + joined(0, second_out)
    pooled_in = (decoded * rms_factor(decoded) * gain["final"]).astype(low)
    copies[6].wait()
    pooled = product(pooled_in, weight(6))
    size = lax.rsqrt(jnp.sum(pooled * pooled, axis=-1, keepdims=True) + eps_norm)
    embedded = pooled * size
    embedded_ref[...] = embedded

    everyone[0] = embedded
    sends = []
    for step in range(1, groups):
        sends.append(
            pltpu.make_async_remote_copy(
                src_ref=everyone.at[0],
                dst_ref=everyone.at[step],
                send_sem=every_send,
                recv_sem=every_recv,
                device_id={"batch": lax.rem(group + step, groups)},
                device_id_type=MESH,
            )
        )
        sends[-1].start()
    arrival = pltpu.make_async_remote_copy(
        src_ref=everyone.at[pl.ds(1, groups - 1)],
        dst_ref=everyone.at[pl.ds(1, groups - 1)],
        send_sem=every_send,
        recv_sem=every_recv,
        device_id={"batch": lax.rem(group + 1, groups)},
        device_id_type=MESH,
    )
    arrival.wait_recv()
    arrival.wait_send()
    all_rows = everyone[...].reshape(groups * SEQ_ROWS, width)
    number = groups * SEQ_ROWS
    row = lax.broadcasted_iota(jnp.int32, (number, number), 0)
    column = lax.broadcasted_iota(jnp.int32, (number, number), 1)
    row_valid = row % SEQ_ROWS < seqs
    valid = row_valid & (column % SEQ_ROWS < seqs)
    similar = logit_scale * lax.dot_general(
        all_rows,
        all_rows,
        (((1,), (1,)), ((), ())),
        precision=highest,
        preferred_element_type=wide,
    )
    similar = jnp.where(valid & (row != column), similar, masked_score)
    best = jnp.max(similar, axis=1, keepdims=True)
    log_norm = best + jnp.log(jnp.sum(jnp.exp(similar - best), axis=1, keepdims=True))
    row_group = lax.rem(group - row // SEQ_ROWS + groups, groups)
    column_group = lax.rem(group - column // SEQ_ROWS + groups, groups)
    row_number = row_group * seqs + row % SEQ_ROWS
    column_number = column_group * seqs + column % SEQ_ROWS
    label = jnp.max(
        jnp.where(
            lax.broadcasted_iota(jnp.int32, (number, target_ref.shape[1]), 1)
            == row_number[:, : target_ref.shape[1]],
            target_ref[:1, :],
            -1.0,
        ),
        axis=1,
        keepdims=True,
    )
    target = (column_number.astype(wide) == label) & valid
    picked = jnp.sum(jnp.where(target, similar, 0.0), axis=1, keepdims=True)
    losses = jnp.where(row_valid[:, :1], log_norm - picked, 0.0)
    loss_ref[...] = jnp.broadcast_to(
        jnp.sum(losses, axis=0, keepdims=True) / seq_total, loss_ref.shape
    )
    grad_similar = jnp.where(
        valid, (jnp.exp(similar - log_norm) - target.astype(wide)) / seq_total, 0.0
    )
    similar_ref[...] = grad_similar + grad_similar.T
    grad_embedded = logit_scale * jnp.dot(
        similar_ref[:SEQ_ROWS, :], all_rows, precision=highest, preferred_element_type=wide
    )

    grad_pooled = (
        size
        * (grad_embedded - embedded * jnp.sum(embedded * grad_embedded, axis=-1, keepdims=True))
    ).astype(low)
    grad_decoded, grad_final_gain = rms_back(
        decoded, gain["final"], back_product(grad_pooled, weight(6))
    )
    grad_second_out = grad_decoded.astype(low)
    grad_second_pre = [
        (gelu_slope(second_pre[j]) * back_product(grad_second_out, outer_weight(j))).astype(low)
        for j in range(feeds)
    ]
    if halves == 2:
        for j in range(feeds):
            halves_sent[2 + j] = second_act[j].astype(wide)
            halves_sent[2 + feeds + j] = grad_second_pre[j].astype(wide)
        half_copy(2, 2, 2 * feeds).start()
    grad_second_in = back_product(grad_second_pre[0], weight(7))
    for j in range(1, feeds):
        grad_second_in = grad_second_in + back_product(grad_second_pre[j], weight(7 + j))
    grad_second_in = joined(1, grad_second_in)
    grad_after_cross, grad_second_gain = rms_back(after_cross, gain["second"], grad_second_in)
    grad_after_cross = grad_after_cross + grad_decoded
    grad_cross_branch = grad_after_cross.astype(low)
    grad_cross_att = back_product(grad_cross_branch, weight(5)).astype(low)
    grad_cross_wide = grad_cross_att.astype(wide)
    grad_heads = jnp.concatenate(
        [
            jnp.where(
                head_mask,
                jnp.broadcast_to(grad_cross_wide[i : i + 1], (HEAD_ROWS, width)),
                0.0,
            )
            for i in range(seqs)
        ],
        axis=0,
    )
    attended_heads = jnp.concatenate(
        [
            jnp.broadcast_to(cross_attended[i : i + 1], (HEAD_ROWS, width))
            for i in range(seqs)
        ],
        axis=0,
    )
    row_terms = jnp.sum(grad_heads * attended_heads, axis=1, keepdims=True)
    value_rows = back_product(grad_heads.astype(low), weight(4)).astype(low)
    probs = jnp.where(inside, jnp.exp(scores - log_total), 0.0)
    grad_scores = (probs * (back_product(value_rows, context) - row_terms)).astype(low)
    grad_context_ref[...] = weight_grad(
        jnp.concatenate([grad_scores, probs.astype(low)], axis=0),
        jnp.concatenate([key_rows] * seqs + [value_rows], axis=0),
    )
    key_sums = product(grad_scores, context)
    sums = key_sums[:HEAD_ROWS]
    for i in range(1, seqs):
        sums = sums + key_sums[HEAD_ROWS * i : HEAD_ROWS * (i + 1)]
    first_member = jnp.where(member == 0, 1.0, 0.0)
    totals_ref[:HEAD_ROWS, :] = sums
    totals_ref[HEAD_ROWS:, :] = first_member * by_seq(
        [jnp.sum(grad_after_cross, axis=0, keepdims=True), grad_final_gain, grad_second_gain]
    )
    def put(at, values):
        for i in range(seqs):
            piece_rows[i, pl.ds(at, 1), :] = values[i : i + 1].astype(wide)

    piece_rows[...] = jnp.zeros_like(piece_rows)
    for i, piece in zip(
        (0, 1, 6, 7, 12, 13, 14),
        (
            cross_low,
            second_in,
            pooled_in,
            grad_cross_branch,
            grad_second_out,
            grad_pooled,
            grad_cross_att,
        ),
    ):
        put(i, piece)
    if halves == 2:
        half_copy(2, 2, 2 * feeds).wait()
    for first, values, got in ((2, second_act, 2), (8, grad_second_pre, 2 + feeds)):
        for j in range(feeds):
            if halves == 1:
                put(first + j, values[j])
            else:
                put(first + feeds * member + j, values[j])
                put(first + feeds * (1 - member) + j, halves_got[got + j])
    for i in range(seqs):
        piece_rows[i, HEAD_ROWS:, :] = mixed[HEAD_ROWS * i : HEAD_ROWS * (i + 1)].astype(wide)
    pieces_ref[...] = piece_rows[...].astype(low)
    for i, piece in enumerate([start, self_in, self_vals, after_self, cross_in, cross_query]):
        starts_ref[i : i + 1, :] = piece[:1].astype(wide)
    starts_ref[6:, :] = jnp.zeros((2, width), wide)


def decoder_step(context, third, base, gains, labels, place, groups, members, seqs):
    rows, width = context.shape
    everything = pl.BlockSpec(memory_space=pltpu.VMEM)
    labels = jnp.pad(labels.astype(wide)[None], ((0, 7), (0, LANES - labels.shape[0])))
    number = groups * SEQ_ROWS
    return pl.pallas_call(
        functools.partial(decoder_kernel, base, groups, members, seqs),
        name="decoder",
        in_specs=[
            pl.BlockSpec(memory_space=pltpu.SMEM),
            everything,
            pl.BlockSpec(memory_space=pl.ANY),
            everything,
            everything,
        ],
        out_specs=[everything] * 6,
        out_shape=[
            jax.ShapeDtypeStruct((SEQ_ROWS, width), wide),
            jax.ShapeDtypeStruct((8, LANES), wide),
            jax.ShapeDtypeStruct((rows, width), wide),
            jax.ShapeDtypeStruct((seqs, 2 * HEAD_ROWS, width), low),
            jax.ShapeDtypeStruct((8, width), wide),
            jax.ShapeDtypeStruct((HEAD_ROWS + SEQ_ROWS, width), wide),
        ],
        scratch_shapes=[
            pltpu.VMEM((third.shape[0], third.shape[1] - base, width), low),
            pltpu.VMEM((groups, SEQ_ROWS, width), wide),
            pltpu.VMEM((members, seqs * HEAD_ROWS, width + LANES), wide),
            pltpu.VMEM((number, number), wide),
            pltpu.VMEM((10, SEQ_ROWS, width), wide),
            pltpu.VMEM((10, SEQ_ROWS, width), wide),
            pltpu.VMEM((seqs, 2 * HEAD_ROWS, width), wide),
            pltpu.SemaphoreType.DMA((12,)),
            pltpu.SemaphoreType.DMA,
            pltpu.SemaphoreType.DMA,
            pltpu.SemaphoreType.DMA((max(members - 1, 1),)),
            pltpu.SemaphoreType.DMA((max(members - 1, 1),)),
            pltpu.SemaphoreType.DMA((3,)),
            pltpu.SemaphoreType.DMA((3,)),
        ],
        compiler_params=pltpu.CompilerParams(
            collective_id=0, has_side_effects=True, vmem_limit_bytes=56 * 2**20
        ),
        cost_estimate=pl.CostEstimate(
            flops=2 * rows * width * 300, bytes_accessed=2 * third.size, transcendentals=0
        ),
    )(place, context, third, gains, labels)


def feed_weights(rest_ref, out, inner, outer, sem):
    count, _, width = rest_ref.shape
    unit = width // count
    feeds = inner.shape[0]
    per = count // feeds
    copies = [pltpu.make_async_copy(rest_ref.at[:, :unit, :], out, sem.at[0])]
    for j in range(feeds):
        first = unit * (1 + j)
        copies.append(
            pltpu.make_async_copy(
                rest_ref.at[:, first : first + unit, :], inner.at[j], sem.at[1 + j]
            )
        )
    first = unit * (1 + feeds)
    for j in range(feeds):
        copies.append(
            pltpu.make_async_copy(
                rest_ref.at[per * j : per * (j + 1), first : first + feeds * unit, :],
                outer.at[j],
                sem.at[1 + feeds + j],
            )
        )
    return copies


def feed_buffers(rest, feeds):
    count, _, width = rest.shape
    unit = width // count
    return [
        pltpu.VMEM((count, unit, width), low),
        pltpu.VMEM((feeds, count, unit, width), low),
        pltpu.VMEM((feeds, count // feeds, feeds * unit, width), low),
        pltpu.SemaphoreType.DMA((1 + 2 * feeds,)),
    ]


def feed_kernel(
    attended_ref,
    tokens_ref,
    rest_ref,
    gains_ref,
    hidden_ref,
    pre_ref,
    encoded_ref,
    context_ref,
    out,
    inner,
    outer,
    sem,
    inner_in,
):
    width = tokens_ref.shape[1]
    feeds = pre_ref.shape[0]
    copies = feed_weights(rest_ref, out, inner, outer, sem)
    for copy in copies:
        copy.start()
    copies[0].wait()
    hidden = tokens_ref[...].astype(wide) + product(
        attended_ref[...].astype(low), out[...].reshape(width, width)
    )
    hidden_ref[...] = hidden
    inner_in[...] = (hidden * rms_factor(hidden) * gains_ref[1:2, :]).astype(low)
    encoded_ref[...] = hidden
    for copy in copies[1:]:
        copy.wait()

    def step(j, carry):
        pre = product(inner_in[...], inner[j].reshape(width, width))
        pre_ref[j] = pre.astype(low)
        encoded_ref[...] += product(
            gelu_value(pre).astype(low), outer[j].reshape(width, width)
        )
        return carry

    lax.fori_loop(0, feeds, step, 0)
    encoded = encoded_ref[...]
    context_ref[...] = (encoded * rms_factor(encoded) * gains_ref[2:3, :]).astype(low)


def feed_forward(attended, tokens, rest, gains, feeds):
    rows, width = tokens.shape
    whole = pl.BlockSpec(memory_space=pltpu.VMEM)
    return pl.pallas_call(
        feed_kernel,
        name="feed_forward",
        in_specs=[whole, whole, pl.BlockSpec(memory_space=pl.ANY), whole],
        out_specs=[whole] * 4,
        out_shape=[
            jax.ShapeDtypeStruct((rows, width), wide),
            jax.ShapeDtypeStruct((feeds, rows, width), low),
            jax.ShapeDtypeStruct((rows, width), wide),
            jax.ShapeDtypeStruct((rows, width), low),
        ],
        scratch_shapes=feed_buffers(rest, feeds) + [pltpu.VMEM((rows, width), low)],
        compiler_params=pltpu.CompilerParams(vmem_limit_bytes=50 * 2**20),
        cost_estimate=pl.CostEstimate(
            flops=18 * rows * width * width, bytes_accessed=40 * width * width, transcendentals=0
        ),
    )(attended, tokens, rest, gains)


def feed_back_kernel(
    base,
    groups,
    members,
    grad_context_ref,
    encoded_ref,
    hidden_ref,
    pre_ref,
    attended_ref,
    rest_ref,
    gains_ref,
    rows_ref,
    starts_ref,
    parts_ref,
    grad_hidden_ref,
    grad_attended_ref,
    sums_ref,
    backs_ref,
    out,
    inner,
    outer,
    sem,
    inner_in,
    grad_branch,
    grad_inner_in,
    outer_grad,
    inner_grad,
    grad_sem,
    weights,
    sides,
    weight_sem,
    send_sem,
    recv_sem,
):
    rows, width = encoded_ref.shape
    feeds = pre_ref.shape[0]
    count = rest_ref.shape[0]
    unit = width // count
    lines = groups // 4
    group = lax.axis_index("batch")
    member = lax.axis_index("seq")

    partners = []
    for axis, place, number in (("batch", group, groups), ("seq", member, members)):
        span = 1
        while span < number:
            bit = lax.rem(place // span, 2)
            partners.append({axis: place + span * (1 - 2 * bit)})
            span *= 2
    barrier = pltpu.get_barrier_semaphore()
    for partner in partners:
        pl.semaphore_signal(barrier, inc=1, device_id=partner, device_id_type=MESH)

    def swap(i):
        return pltpu.make_async_remote_copy(
            src_ref=sides.at[2 * i],
            dst_ref=sides.at[2 * i + 1],
            send_sem=send_sem.at[i],
            recv_sem=recv_sem.at[i],
            device_id=partners[i],
            device_id_type=MESH,
        )

    def swapped(i):
        swap(i).wait()
        sides[2 * i + 2] = sides[2 * i] + sides[2 * i + 1]
        if i + 1 < len(partners):
            swap(i + 1).start()

    copies = feed_weights(rest_ref, out, inner, outer, sem)
    for copy in copies[1 + feeds :] + copies[1 : 1 + feeds] + copies[:1]:
        copy.start()
    start_copies = [
        pltpu.make_async_copy(
            rest_ref.at[:, base + unit * i : base + unit * (i + 1), :],
            weights.at[i],
            weight_sem.at[i],
        )
        for i in range(4)
    ]
    for copy in start_copies:
        copy.start()
    sides[0] = rows_ref[...]
    hidden = hidden_ref[...]
    inner_in[...] = (hidden * rms_factor(hidden) * gains_ref[1:2, :]).astype(low)
    grad_encoded, _ = rms_back(encoded_ref[...], gains_ref[2:3, :], grad_context_ref[...])
    grad_hidden_ref[...] = grad_encoded
    grad_branch[...] = grad_encoded.astype(low)
    grad_inner_in[...] = jnp.zeros_like(grad_inner_in)
    pl.semaphore_wait(barrier, len(partners))
    swap(0).start()
    for copy in copies[1:]:
        copy.wait()

    def outer_put(j, slot):
        per = lines // feeds
        return pltpu.make_async_copy(
            outer_grad.at[slot],
            parts_ref.at[pl.ds(j * per, per), :, :, 1 + feeds :],
            grad_sem.at[0, slot],
        )

    def inner_put(j, slot):
        return pltpu.make_async_copy(
            inner_grad.at[slot], parts_ref.at[:, :, :, 1 + j], grad_sem.at[1, slot]
        )

    def step(j, carry):
        slot = lax.rem(j, 2)
        pre = pre_ref[j].astype(wide)
        grad_act = back_product(grad_branch[...], outer[j].reshape(width, width))
        grad_pre = (gelu_slope(pre) * grad_act).astype(low)
        grad_inner_in[...] += back_product(grad_pre, inner[j].reshape(width, width))
        act = gelu_value(pre).astype(low)

        @pl.when(j >= 2)
        def _():
            outer_put(j - 2, slot).wait()
            inner_put(j - 2, slot).wait()

        outer_grad[slot] = (
            weight_grad(act, grad_branch[...]).reshape(outer_grad.shape[1:]).astype(low)
        )
        outer_put(j, slot).start()
        inner_grad[slot] = (
            weight_grad(inner_in[...], grad_pre).reshape(inner_grad.shape[1:]).astype(low)
        )
        inner_put(j, slot).start()
        for i in range(min(feeds, len(partners))):

            @pl.when(j == i)
            def _():
                swapped(i)

        return carry

    lax.fori_loop(0, feeds, step, 0)
    grad_hidden, _ = rms_back(hidden_ref[...], gains_ref[1:2, :], grad_inner_in[...])
    grad_hidden = grad_hidden + grad_hidden_ref[...]
    grad_hidden_ref[...] = grad_hidden
    grad_branch[...] = grad_hidden.astype(low)
    copies[0].wait()
    grad_attended_ref[...] = back_product(
        grad_branch[...], out[...].reshape(width, width)
    ).astype(low)
    for j in range(feeds - 2, feeds):
        outer_put(j, j % 2).wait()
        inner_put(j, j % 2).wait()
    inner_grad[0] = (
        weight_grad(attended_ref[...].astype(low), grad_branch[...])
        .reshape(inner_grad.shape[1:])
        .astype(low)
    )
    out_put = pltpu.make_async_copy(
        inner_grad.at[0], parts_ref.at[:, :, :, 0], grad_sem.at[1, 0]
    )
    out_put.start()

    for i in range(feeds, len(partners)):
        swapped(i)
    sums = sides[2 * len(partners)]
    sums_ref[...] = sums
    for copy in start_copies:
        copy.wait()

    def weight(i):
        return weights[i].reshape(width, width)

    head_row = lax.broadcasted_iota(jnp.int32, (HEAD_ROWS, width), 0)
    head_mask = head_row == lax.broadcasted_iota(jnp.int32, (HEAD_ROWS, width), 1) // HEAD
    spread = product(sums[:HEAD_ROWS].astype(low), weight(3))
    grad_cross_query = jnp.sum(jnp.where(head_mask, spread, 0.0), axis=0, keepdims=True)
    grad_cross_query = grad_cross_query.astype(low)

    def widened(row):
        return jnp.broadcast_to(row.astype(wide), (SEQ_ROWS, width))

    start = widened(starts_ref[0:1, :])
    after_self = widened(starts_ref[3:4, :])
    grad_rows = back_product(widened(grad_cross_query).astype(low), weight(2))
    grad_after_self, _ = rms_back(after_self, gains_ref[5:6, :], grad_rows)
    cross_gain = grad_rows * after_self * rms_factor(after_self)
    grad_after_self = grad_after_self + widened(sums[HEAD_ROWS : HEAD_ROWS + 1])
    grad_self_branch = grad_after_self.astype(low)
    grad_self_vals = back_product(grad_self_branch, weight(1)).astype(low)
    grad_rows = back_product(grad_self_vals, weight(0))
    grad_start, _ = rms_back(start, gains_ref[4:5, :], grad_rows)
    self_gain = grad_rows * start * rms_factor(start)
    for i, row in enumerate(
        (
            grad_start + grad_after_self,
            self_gain,
            cross_gain,
            grad_cross_query,
            grad_self_branch,
            grad_self_vals,
        )
    ):
        backs_ref[i : i + 1, :] = row[:1].astype(wide)
    backs_ref[6:, :] = jnp.zeros((2, width), wide)
    out_put.wait()


def feed_back(
    grad_context, encoded, hidden, pre, attended, rest, base, gains, sum_rows, starts, groups, members, part
):
    rows, width = encoded.shape
    feeds = pre.shape[0]
    lines = groups // 4
    count = rest.shape[0]
    many = sum_rows.shape[0]
    partners = (groups.bit_length() - 1) + (members.bit_length() - 1)
    whole = pl.BlockSpec(memory_space=pltpu.VMEM)
    anywhere = pl.BlockSpec(memory_space=pl.ANY)
    return pl.pallas_call(
        functools.partial(feed_back_kernel, base, groups, members),
        name="feed_back",
        in_specs=[whole] * 5 + [anywhere] + [whole] * 3,
        out_specs=[anywhere] + [whole] * 4,
        out_shape=[
            jax.ShapeDtypeStruct((lines, 2, 2, 1 + 2 * feeds, part, width), low),
            jax.ShapeDtypeStruct((rows, width), wide),
            jax.ShapeDtypeStruct((rows, width), low),
            jax.ShapeDtypeStruct((many, width), wide),
            jax.ShapeDtypeStruct((8, width), wide),
        ],
        scratch_shapes=feed_buffers(rest, feeds)
        + [
            pltpu.VMEM((rows, width), low),
            pltpu.VMEM((rows, width), low),
            pltpu.VMEM((rows, width), wide),
            pltpu.VMEM((2, lines // feeds, 2, 2, feeds, part, width), low),
            pltpu.VMEM((2, lines, 2, 2, part, width), low),
            pltpu.SemaphoreType.DMA((2, 2)),
            pltpu.VMEM((4, count, width // count, width), low),
            pltpu.VMEM((2 * partners + 1, many, width), wide),
            pltpu.SemaphoreType.DMA((4,)),
            pltpu.SemaphoreType.DMA((partners,)),
            pltpu.SemaphoreType.DMA((partners,)),
        ],
        compiler_params=pltpu.CompilerParams(
            collective_id=2, has_side_effects=True, vmem_limit_bytes=60 * 2**20
        ),
        cost_estimate=pl.CostEstimate(
            flops=36 * rows * width * width, bytes_accessed=80 * width * width, transcendentals=0
        ),
    )(
        grad_context, encoded, hidden, pre, attended, rest, gains, sum_rows, starts
    )


class Summing:
    def __init__(self, groups, members, buffers):
        self.groups = groups
        self.members = members
        self.lines = groups // 4
        self.group = lax.axis_index("batch")
        self.member = lax.axis_index("seq")
        self.z = self.group // 4
        self.y = lax.rem(self.group // 2, 2)
        self.core = lax.rem(self.group, 2)
        (
            self.chip,
            self.pairs,
            self.line,
            self.shares,
            self.chip_send,
            self.chip_recv,
            self.pair_send,
            self.pair_recv,
            self.line_send,
            self.line_recv,
            self.share_send,
            self.share_recv,
        ) = buffers
        self.stages = 3 + self.lines

    def batch_id(self, offset):
        return {"batch": self.group + offset}

    def neighbours(self):
        found = [
            (None, self.batch_id(1 - 2 * self.core)),
            (None, self.batch_id(2 - 4 * self.y)),
            (self.z > 0, self.batch_id(-4)),
            (self.z < self.lines - 1, self.batch_id(4)),
        ]
        for step in range(1, self.members):
            found.append((None, {"seq": lax.rem(self.member + step, self.members)}))
        return found

    def greet(self, barrier):
        for condition, device in self.neighbours():
            if condition is None:
                pl.semaphore_signal(barrier, inc=1, device_id=device, device_id_type=MESH)
            else:

                @pl.when(condition)
                def _():
                    pl.semaphore_signal(barrier, inc=1, device_id=device, device_id_type=MESH)

    def greeted(self, barrier):
        ends = (self.z > 0).astype(jnp.int32) + (self.z < self.lines - 1).astype(jnp.int32)
        pl.semaphore_wait(barrier, 2 + self.members - 1 + ends)

    def copy(self, source, target, send, recv, device):
        return pltpu.make_async_remote_copy(
            src_ref=source,
            dst_ref=target,
            send_sem=send,
            recv_sem=recv,
            device_id=device,
            device_id_type=MESH,
        )

    def chip_copy(self, chunk, source):
        return self.copy(
            source,
            self.chip.at[chunk],
            self.chip_send.at[chunk],
            self.chip_recv.at[chunk],
            self.batch_id(1 - 2 * self.core),
        )

    def pair_copy(self, chunk):
        return self.copy(
            self.chip.at[chunk, :, 1 - self.y],
            self.pairs.at[chunk],
            self.pair_send.at[chunk],
            self.pair_recv.at[chunk],
            self.batch_id(2 - 4 * self.y),
        )

    def line_copy(self, chunk, way, first, last, source):
        return self.copy(
            source.at[chunk, pl.ds(first, last - first)]
            if source is self.pairs
            else source.at[chunk, way, pl.ds(first, last - first)],
            self.line.at[chunk, way, pl.ds(first, last - first)],
            self.line_send.at[chunk, way],
            self.line_recv.at[chunk, way],
            self.batch_id(-4 if way else 4),
        )

    def share_copy(self, chunk, step):
        return self.copy(
            self.shares.at[chunk, self.member],
            self.shares.at[chunk, self.member],
            self.share_send.at[chunk, step - 1],
            self.share_recv.at[chunk, step - 1],
            {"seq": lax.rem(self.member + step, self.members)},
        )

    def start(self, chunk, source):
        self.chip_copy(chunk, source).start()

    def to_pair(self, chunk, source, own):
        self.chip_copy(chunk, source).wait()
        self.chip[chunk] = (self.chip[chunk].astype(wide) + own.astype(wide)).astype(low)
        self.pair_copy(chunk).start()

    def to_line(self, chunk, step):
        lines = self.lines
        if step == 0:
            self.pair_copy(chunk).wait()
            self.pairs[chunk] = (
                self.pairs[chunk].astype(wide) + self.chip[chunk, :, self.y].astype(wide)
            ).astype(low)
        for way in range(2):
            at = lines - 1 - step if way else step
            first, last = (0, at) if way else (at + 1, lines)

            @pl.when(self.z == at)
            def _():
                if step > 0:
                    kept = (0, at + 1) if way else (at, lines)
                    self.line_copy(chunk, way, kept[0], kept[1], self.line).wait_recv()
                    span = pl.ds(first, last - first)
                    self.line[chunk, way, span] = (
                        self.line[chunk, way, span].astype(wide)
                        + self.pairs[chunk, span].astype(wide)
                    ).astype(low)
                self.line_copy(
                    chunk, way, first, last, self.line if step > 0 else self.pairs
                ).start()

    def to_members(self, chunk, held):
        lines = self.lines
        for way in range(2):
            end = 0 if way else lines - 1

            @pl.when(self.z == end)
            def _():
                kept = (0, 1) if way else (lines - 1, lines)
                self.line_copy(chunk, way, kept[0], kept[1], self.line).wait_recv()

            for step in range(lines - 1):
                at = lines - 1 - step if way else step
                first, last = (0, at) if way else (at + 1, lines)

                @pl.when(self.z == at)
                def _():
                    self.line_copy(chunk, way, first, last, self.line).wait_send()

        held[...] = self.pairs[chunk, self.z].astype(wide)

        @pl.when(self.z > 0)
        def _():
            held[...] += self.line[chunk, 0, self.z].astype(wide)

        @pl.when(self.z < lines - 1)
        def _():
            held[...] += self.line[chunk, 1, self.z].astype(wide)

        self.shares[chunk, self.member] = held[...].astype(low)
        for step in range(1, self.members):
            self.share_copy(chunk, step).start()

    def result(self, chunk):
        for step in range(1, self.members):
            self.share_copy(chunk, step).wait()
        total = self.shares[chunk, 0].astype(wide)
        for member in range(1, self.members):
            total = total + self.shares[chunk, member].astype(wide)
        return total


def summing_scratch(groups, members, chunks, rows, columns):
    lines = groups // 4
    return [
        pltpu.VMEM((chunks, lines, 2, rows, columns), low),
        pltpu.VMEM((chunks, lines, rows, columns), low),
        pltpu.VMEM((chunks, 2, lines, rows, columns), low),
        pltpu.VMEM((chunks, members, rows, columns), low),
        pltpu.SemaphoreType.DMA((chunks,)),
        pltpu.SemaphoreType.DMA((chunks,)),
        pltpu.SemaphoreType.DMA((chunks,)),
        pltpu.SemaphoreType.DMA((chunks,)),
        pltpu.SemaphoreType.DMA((chunks, 2)),
        pltpu.SemaphoreType.DMA((chunks, 2)),
        pltpu.SemaphoreType.DMA((chunks, max(members - 1, 1))),
        pltpu.SemaphoreType.DMA((chunks, max(members - 1, 1))),
    ]


def stage_delays(lines):
    return [1, 3] + [4 + step for step in range(lines - 2)] + [lines + 2, lines + 3]


def attend_back_kernel(
    groups,
    members,
    place,
    q_ref,
    k_ref,
    v_ref,
    grad_ref,
    attended_ref,
    total_ref,
    near_ref,
    own_turned_ref,
    all_turned_ref,
    parts_ref,
    grad_q_ref,
    grad_k_ref,
    grad_v_ref,
    table_ref,
    out_sums_ref,
    inner_sums_ref,
    outer_sums_ref,
    query_sums_ref,
    key_sums_ref,
    value_sums_ref,
    bias,
    key_side,
    value_side,
    keys_turned,
    grad_scores,
    grad_k_sum,
    grad_v_sum,
    band_sum,
    grad_q_sum,
    pair_grads,
    fetched,
    held,
    fetch_sem,
    bands,
    kept,
    sent,
    got,
    keep_send,
    keep_recv,
    tables,
    table_send,
    table_recv,
    *buffers,
):
    pair = pl.program_id(0)
    block = pl.program_id(1)
    blocks = pl.num_programs(1)
    pairs = pl.num_programs(0)
    now = pair * blocks + block
    pack = k_ref.shape[0]
    size = q_ref.shape[0]
    middle, reach, lead, width = table_sizes(size, pack)
    ends = (place[0], place[1])
    rows_here = size * blocks
    summing = Summing(groups, members, buffers)
    first = summing.member * rows_here + block * size
    shift = lax.rem(summing.member * rows_here, LANES) if size % LANES else 0
    barrier = pltpu.get_barrier_semaphore()
    feed_chunks = 2 * parts_ref.shape[3]
    feeds = (parts_ref.shape[3] - 1) // 2
    half_width = fetched.shape[-1]
    part = fetched.shape[-2]
    lines = groups // 4
    delays = stage_delays(lines)

    def feed_part(chunk, core):
        return parts_ref.at[
            :, :, core, chunk // 2, :, pl.ds(pl.multiple_of(lax.rem(chunk, 2) * half_width, LANES), half_width)
        ]

    def fetch(chunk):
        slot = lax.rem(chunk, 4)
        return pltpu.make_async_copy(
            feed_part(chunk, summing.core), fetched.at[slot], fetch_sem.at[slot]
        )

    def feed_stage(stage, chunk):
        if stage == 0:
            summing.start(chunk, feed_part(chunk, 1 - summing.core))
            fetch(chunk).start()
        elif stage == 1:
            fetch(chunk).wait()
            summing.to_pair(
                chunk, feed_part(chunk, 1 - summing.core), fetched[lax.rem(chunk, 4)]
            )
        elif stage <= lines:
            summing.to_line(chunk, stage - 2)
        elif stage == lines + 1:
            summing.to_members(chunk, held)
        else:
            total = summing.result(chunk)
            piece = chunk // 2
            column = pl.multiple_of(lax.rem(chunk, 2) * half_width, LANES)

            @pl.when(piece == 0)
            def _():
                out_sums_ref[:, pl.ds(column, half_width)] = total

            @pl.when((piece > 0) & (piece <= feeds))
            def _():
                at = pl.multiple_of((piece - 1) * 2 * half_width + column, LANES)
                inner_sums_ref[:, pl.ds(at, half_width)] = total

            @pl.when(piece > feeds)
            def _():
                at = pl.multiple_of((piece - 1 - feeds) * part, 8)
                outer_sums_ref[pl.ds(at, part), pl.ds(column, half_width)] = total

    def pair_stage(stage, which):
        chunk = feed_chunks + which
        if stage == 0:
            summing.start(chunk, pair_grads.at[which, :, :, 1 - summing.core])
        elif stage == 1:
            summing.to_pair(
                chunk,
                pair_grads.at[which, :, :, 1 - summing.core],
                pair_grads[which, :, :, summing.core],
            )
        elif stage <= lines:
            summing.to_line(chunk, stage - 2)
        elif stage == lines + 1:
            summing.to_members(chunk, held)
        else:
            total = summing.result(chunk)
            span = pl.ds(pl.multiple_of(which * LANES, LANES), LANES)
            for i, sums_ref in enumerate((query_sums_ref, key_sums_ref, value_sums_ref)):
                sums_ref[:, span] = total[:, LANES * i : LANES * (i + 1)]

    def keep_copy(which, step):
        return summing.copy(
            sent.at[which, step - 1],
            got.at[which, step - 1],
            keep_send.at[which, step - 1],
            keep_recv.at[which, step - 1],
            {"seq": lax.rem(summing.member + step, members)},
        )

    def keep_result(which):
        total = [kept[lax.rem(which, 2), i] for i in range(2)]
        for step in range(1, members):
            keep_copy(which, step).wait()
            total = [total[i] + got[which, step - 1, i].astype(wide) for i in range(2)]
        span = pl.ds(pl.multiple_of(which * LANES, LANES), LANES)
        grad_k_ref[:, span] = total[0].astype(low)
        grad_v_ref[:, span] = total[1].astype(low)

    partners = []
    for axis, spot, number in (
        ("batch", summing.group, groups),
        ("seq", summing.member, members),
    ):
        reach_out = 1
        while reach_out < number:
            bit = lax.rem(spot // reach_out, 2)
            partners.append({axis: spot + reach_out * (1 - 2 * bit)})
            reach_out *= 2

    def swap(i):
        return summing.copy(
            tables.at[2 * i],
            tables.at[2 * i + 1],
            table_send.at[i],
            table_recv.at[i],
            partners[i],
        )

    def swapped(i):
        swap(i).wait()
        tables[2 * i + 2] = tables[2 * i] + tables[2 * i + 1]
        if i + 1 < len(partners):
            swap(i + 1).start()

    @pl.when(now == 0)
    def _():
        peers = summing.neighbours()
        for i in range(len(partners)):
            peers.append((None, partners[i]))
        for condition, device in peers:
            if condition is None:
                pl.semaphore_signal(barrier, inc=1, device_id=device, device_id_type=MESH)
            else:

                @pl.when(condition)
                def _():
                    pl.semaphore_signal(barrier, inc=1, device_id=device, device_id_type=MESH)

        edges = (summing.z > 0).astype(jnp.int32) + (summing.z < lines - 1).astype(jnp.int32)
        pl.semaphore_wait(barrier, 2 + members - 1 + edges + len(partners))

    stages = 3 + lines
    starts = [0] + delays
    total_steps = pairs * blocks

    def run_stages(step):
        for stage in reversed(range(stages)):
            chunk = step - starts[stage]

            @pl.when((chunk >= 0) & (chunk < feed_chunks))
            def _():
                feed_stage(stage, chunk)

            late = step - (blocks - 1) - starts[stage]

            @pl.when((late >= 0) & (lax.rem(late + 64 * blocks, blocks) == 0) & (late < total_steps))
            def _():
                pair_stage(stage, late // blocks)

    @pl.when(now == 0)
    def _():
        tables[0] = jnp.zeros_like(tables[0])
        bands[...] = jnp.zeros_like(bands)

    @pl.when(block == 0)
    def _():
        places = lax.broadcasted_iota(jnp.int32, (pack, LANES), 0)
        lane = lax.broadcasted_iota(jnp.int32, (pack, LANES), 1)
        key_side[:, :LANES] = k_ref[...]
        ones = (segment_of(places, ends) == lane) | ((lane >= 3) & (lane < 9))
        key_side[:, LANES:] = ones.astype(wide).astype(low)
        value_side[:, :LANES] = v_ref[...]
        value_side[:, LANES:] = (lane < 6).astype(wide).astype(low)
        keys_turned[...] = k_ref[...].T
        for half in range(2):
            row = near_ref[half]
            before = middle - LANES
            after = middle + reach
            bias[half, before:after, :] = turned_biases(row, size, lead).T
            if before > 0:
                bias[half, :before, :] = jnp.broadcast_to(row[:, :1], (before, size))
            if after < width:
                bias[half, after:, :] = jnp.broadcast_to(row[:, -1:], (width - after, size))
        grad_scores[...] = jnp.zeros_like(grad_scores)
        grad_k_sum[...] = jnp.zeros_like(grad_k_sum)
        grad_v_sum[...] = jnp.zeros_like(grad_v_sum)
        band_sum[...] = jnp.zeros_like(band_sum)

    lane = lax.broadcasted_iota(jnp.int32, (size, LANES), 1)
    rows = first + lax.broadcasted_iota(jnp.int32, (size, LANES), 0)
    apart = jnp.where((segment_of(rows, ends) != lane) & (lane < 3), -far_apart, 0.0)
    start = pl.multiple_of(middle - (first - shift), LANES)
    near_rows = pl.ds(pl.multiple_of(first - shift, LANES), LANES + reach)
    queries = q_ref[...]
    grads = grad_ref[...]
    products = grads.astype(wide) * attended_ref[...]
    totals = total_ref[...]

    def in_parts(column, at):
        head = column.astype(low).astype(wide)
        body = (column - head).astype(low).astype(wide)
        tail = column - head - body
        return jnp.where(
            lane == at,
            head,
            jnp.where(lane == at + 1, body, jnp.where(lane == at + 2, tail, 0.0)),
        )

    query_grads = []
    for half in range(2):
        mine = (lane >= HEAD) if half else (lane < HEAD)
        row_term = jnp.sum(jnp.where(mine, products, 0.0), axis=1, keepdims=True)
        row_total = jnp.sum(
            jnp.where(lane == 2 * pair + half, totals, 0.0), axis=1, keepdims=True
        )
        query_part = jnp.where(mine, queries, jnp.zeros_like(queries))
        grad_part = jnp.where(mine, grads, jnp.zeros_like(grads))
        query_side = jnp.concatenate(
            [query_part, (apart - in_parts(row_total, 3 + 3 * half)).astype(low)], axis=1
        )
        grad_side = jnp.concatenate(
            [grad_part, (-in_parts(row_term, 3 * half)).astype(low)], axis=1
        )
        weights = jnp.exp(
            back_product(key_side[...], query_side) + bias[half, pl.ds(start, pack), :]
        )
        grad_block = (weights * back_product(value_side[...], grad_side)).astype(low)
        grad_scores[LANES : LANES + pack, :] = grad_block
        grad_v_sum[...] += product(weights.astype(low), grad_part)
        block_lane = jnp.where(lane == 8 * half + block, 1.0, 0.0).astype(low)
        grad_k_sum[...] += product(
            grad_block, jnp.concatenate([query_part, block_lane], axis=1)
        )
        query_grads.append(product(keys_turned[HEAD * half : HEAD * (half + 1), :], grad_block))
        band_sum[half] += grad_scores[near_rows, :].astype(wide)
    grad_query = jnp.concatenate(query_grads, axis=0).T.astype(low)
    grad_q_ref[...] = grad_query
    grad_q_sum[pl.ds(pl.multiple_of(block * size, 64), size), :] = grad_query

    @pl.when(block == blocks - 1)
    def _():
        grad_key = grad_k_sum[:, :LANES].astype(low)
        grad_value = grad_v_sum[...].astype(low)

        @pl.when(pair > 0)
        def _():
            keep_result(pair - 1)

        for step in range(1, members):
            other = pl.multiple_of(lax.rem(summing.member + step, members) * rows_here, 64)
            sent[pair, step - 1, 0] = grad_k_sum[pl.ds(other, rows_here), :LANES].astype(low)
            sent[pair, step - 1, 1] = grad_v_sum[pl.ds(other, rows_here), :].astype(low)
            keep_copy(pair, step).start()
        mine_rows = pl.ds(pl.multiple_of(summing.member * rows_here, 64), rows_here)
        kept[lax.rem(pair, 2), 0] = grad_k_sum[mine_rows, :LANES]
        kept[lax.rem(pair, 2), 1] = grad_v_sum[mine_rows, :]
        for i, gradient in enumerate(
            (
                product(own_turned_ref[...], grad_q_sum[...]),
                product(all_turned_ref[...], grad_key),
                product(all_turned_ref[...], grad_value),
            )
        ):
            pair_grads[pair, :, :, :, :, LANES * i : LANES * (i + 1)] = gradient.reshape(
                lines, 2, 2, part, LANES
            ).astype(low)
        key = lax.broadcasted_iota(jnp.int32, (pack, LANES), 0)
        which = lax.broadcasted_iota(jnp.int32, (pack, LANES), 1) % 8
        begin = summing.member * rows_here - shift + size * which
        sums = grad_k_sum[:, LANES:]
        below = jnp.sum(jnp.where(key < begin - LANES, sums, 0.0), axis=0, keepdims=True)
        above = jnp.sum(jnp.where(key >= begin + reach, sums, 0.0), axis=0, keepdims=True)
        columns = bands.shape[1]
        mirror = (
            lax.broadcasted_iota(jnp.int32, (size, columns), 0)
            + lax.broadcasted_iota(jnp.int32, (size, columns), 1)
            == size - 1
        ).astype(wide)
        row_lane = lax.broadcasted_iota(jnp.int32, (1, LANES), 1)
        for half in range(2):
            flipped = jnp.dot(
                band_sum[half], mirror, precision=highest, preferred_element_type=wide
            )
            turned = pltpu.roll(flipped, 0, 1, stride=1, stride_axis=0)
            head = pl.ds(2 * pair + half, 1)
            bands[head, :] = jnp.sum(turned, axis=0, keepdims=True)
            own_lanes = row_lane // 8 == half
            low_sum = jnp.sum(jnp.where(own_lanes, below, 0.0), axis=1, keepdims=True)
            high_sum = jnp.sum(jnp.where(own_lanes, above, 0.0), axis=1, keepdims=True)
            tables[0, head, :] = jnp.where(row_lane == 15, low_sum, 0.0) + jnp.where(
                row_lane == 31, high_sum, 0.0
            )

    run_stages(now)

    @pl.when(now == total_steps - 1)
    def _():
        columns = bands.shape[1]
        offset = (
            lax.broadcasted_iota(jnp.int32, (columns, LANES), 0) - (size - 1) - LANES - shift
        )
        onehot = (
            bucket_of(offset) == lax.broadcasted_iota(jnp.int32, (columns, LANES), 1)
        ).astype(wide)
        tables[0] += jnp.dot(
            bands[...], onehot, precision=highest, preferred_element_type=wide
        )
        swap(0).start()

        def drain(step, carry):
            run_stages(step)
            for i in range(len(partners)):

                @pl.when(step == total_steps + i)
                def _():
                    swapped(i)

            return carry

        final = max(starts[-1] + 1, len(partners))
        lax.fori_loop(total_steps, total_steps + final, drain, 0)
        keep_result(pairs - 1)
        table_ref[...] = tables[2 * len(partners)]


def attend_back(
    queries, all_keys, all_values, grads, attended, totals, near, place, own_turned, all_turned, parts
):
    rows, width = queries.shape
    pack = all_keys.shape[0]
    size = block_rows(rows)
    _, reach, _, columns = table_sizes(size, pack)
    band = -(-(size + LANES + reach) // LANES) * LANES
    pairs = width // LANES
    members = pack // rows
    pieces = parts.shape[3]
    part = parts.shape[4]
    groups = 4 * parts.shape[0]
    half_width = width // 2
    chunks = 2 * pieces + pairs

    def own(p, i):
        return (i, p)

    def every(p, i):
        return (0, p)

    whole = pl.BlockSpec(memory_space=pltpu.VMEM)
    partners = (groups.bit_length() - 1) + (members.bit_length() - 1)
    feeds = (pieces - 1) // 2
    return pl.pallas_call(
        functools.partial(attend_back_kernel, groups, members),
        name="attend_back",
        grid=(pairs, rows // size),
        in_specs=[
            pl.BlockSpec(memory_space=pltpu.SMEM),
            pl.BlockSpec((size, LANES), own),
            pl.BlockSpec((pack, LANES), every),
            pl.BlockSpec((pack, LANES), every),
            pl.BlockSpec((size, LANES), own),
            pl.BlockSpec((size, LANES), own),
            pl.BlockSpec((size, LANES), lambda p, i: (i, 0)),
            pl.BlockSpec((2, 1, near.shape[2]), lambda p, i: (p, 0, 0)),
            whole,
            whole,
            pl.BlockSpec(memory_space=pl.ANY),
        ],
        out_specs=[
            pl.BlockSpec((size, LANES), own),
        ]
        + [whole] * 9,
        out_shape=[
            jax.ShapeDtypeStruct((rows, width), low),
            jax.ShapeDtypeStruct((rows, width), low),
            jax.ShapeDtypeStruct((rows, width), low),
            jax.ShapeDtypeStruct((16, LANES), wide),
            jax.ShapeDtypeStruct((part, width), wide),
            jax.ShapeDtypeStruct((part, feeds * width), wide),
            jax.ShapeDtypeStruct((feeds * part, width), wide),
            jax.ShapeDtypeStruct((part, width), wide),
            jax.ShapeDtypeStruct((part, width), wide),
            jax.ShapeDtypeStruct((part, width), wide),
        ],
        scratch_shapes=[
            pltpu.VMEM((2, columns, size), wide),
            pltpu.VMEM((pack, 2 * LANES), low),
            pltpu.VMEM((pack, 2 * LANES), low),
            pltpu.VMEM((LANES, pack), low),
            pltpu.VMEM((LANES + pack + reach, size), low),
            pltpu.VMEM((pack, 2 * LANES), wide),
            pltpu.VMEM((pack, LANES), wide),
            pltpu.VMEM((2, LANES + reach, size), wide),
            pltpu.VMEM((rows, LANES), low),
            pltpu.VMEM((pairs, groups // 4, 2, 2, part, half_width), low),
            pltpu.VMEM((4, groups // 4, 2, part, half_width), low),
            pltpu.VMEM((part, half_width), wide),
            pltpu.SemaphoreType.DMA((4,)),
            pltpu.VMEM((16, band), wide),
            pltpu.VMEM((2, 2, rows, LANES), wide),
            pltpu.VMEM((pairs, max(members - 1, 1), 2, rows, LANES), low),
            pltpu.VMEM((pairs, max(members - 1, 1), 2, rows, LANES), low),
            pltpu.SemaphoreType.DMA((pairs, max(members - 1, 1))),
            pltpu.SemaphoreType.DMA((pairs, max(members - 1, 1))),
            pltpu.VMEM((2 * partners + 1, 16, LANES), wide),
            pltpu.SemaphoreType.DMA((partners,)),
            pltpu.SemaphoreType.DMA((partners,)),
        ]
        + summing_scratch(groups, members, chunks, part, half_width),
        compiler_params=pltpu.CompilerParams(
            collective_id=1, has_side_effects=True, vmem_limit_bytes=62 * 2**20
        ),
        cost_estimate=pl.CostEstimate(
            flops=20 * rows * pack * width * 2, bytes_accessed=16 * pack * width, transcendentals=0
        ),
    )(
        place,
        queries,
        all_keys,
        all_values,
        grads,
        attended,
        totals,
        near,
        own_turned,
        all_turned,
        parts,
    )


def last_kernel(
    groups,
    seqs,
    halves,
    grad_q_ref,
    grad_k_ref,
    grad_v_ref,
    first_ref,
    tokens_ref,
    grad_hidden_ref,
    gains_ref,
    rows_ref,
    sums_ref,
    starts_ref,
    backs_ref,
    query_ref,
    key_ref,
    value_ref,
    inner_ref,
    cross_key_ref,
    cross_value_ref,
    query_sums_ref,
    key_sums_ref,
    value_sums_ref,
    inner_sums_ref,
    grad_tokens_ref,
    vectors_ref,
    grad_self_value_ref,
    grad_self_out_ref,
    grad_cross_query_ref,
    grad_cross_key_ref,
    grad_cross_value_ref,
    grad_cross_out_ref,
    grad_second_inner_ref,
    grad_second_outer_ref,
    grad_pooler_ref,
    pieces,
):
    rows, width = tokens_ref.shape
    part = query_ref.shape[0]
    feeds = inner_ref.shape[1] // width
    number = groups * seqs
    every = 2 * HEAD_ROWS
    group = lax.axis_index("batch")
    grad_normed = (
        back_product(grad_q_ref[...], first_ref[0])
        + back_product(grad_k_ref[...], first_ref[1])
        + back_product(grad_v_ref[...], first_ref[2])
    )
    grad_tokens, _ = rms_back(tokens_ref[...].astype(wide), gains_ref[:1, :], grad_normed)
    grad_tokens_ref[...] = grad_tokens + grad_hidden_ref[...]

    def chooser(count, first):
        row = lax.broadcasted_iota(jnp.int32, (count, width), 0)
        column = lax.broadcasted_iota(jnp.int32, (count, width), 1)
        return column == first + row

    chosen = chooser(part, group * part)
    choose = chosen.astype(wide).astype(low)
    tiles = width // LANES
    for i in range(tiles):
        pieces[i] = (
            rows_ref[:, :, LANES * i : LANES * (i + 1)].reshape(number * every, LANES).astype(wide)
        )

    def piece(at):
        return jnp.concatenate(
            [pieces[i, pl.ds(at, number, stride=every), :] for i in range(tiles)], axis=1
        ).astype(low)

    def own(values, which=None):
        which = choose if which is None else which
        return lax.dot_general(
            which, values, (((1,), (1,)), ((), ())), preferred_element_type=wide
        ).astype(low)

    def pair(left, right):
        return product(left, right)

    grad_cross_out_ref[...] = pair(own(piece(0)), piece(7))
    second_in = own(piece(1))
    grad_second_inner = [pair(second_in, piece(8 + j)) for j in range(feeds)]
    share = grad_second_outer_ref.shape[0]
    half = share // halves
    per = width // half
    grad_out = piece(12)
    for i in range(halves):
        chunk = group // per
        at = lax.rem(group, per) * half
        which = chooser(half, at).astype(wide).astype(low)
        found = jnp.zeros((half, number), wide)
        for j in range(feeds // halves):
            here = own(piece(2 + feeds // halves * i + j), which).astype(wide)
            found = jnp.where(chunk == j, here, found)
        grad_second_outer_ref[half * i : half * (i + 1), :] = pair(found.astype(low), grad_out)
    for j in range(feeds):
        grad_second_inner_ref[:, width * j : width * (j + 1)] = grad_second_inner[j]
    grad_pooler_ref[...] = pair(own(piece(6)), piece(13))

    mixed = rows_ref[:, HEAD_ROWS:, :].reshape(number * HEAD_ROWS, width)
    repeat = (
        lax.broadcasted_iota(jnp.int32, (number * HEAD_ROWS, number), 0) // HEAD_ROWS
        == lax.broadcasted_iota(jnp.int32, (number * HEAD_ROWS, number), 1)
    )
    heads = product(repeat.astype(wide).astype(low), piece(14))
    head = lax.broadcasted_iota(jnp.int32, heads.shape, 0) % HEAD_ROWS
    head_column = lax.broadcasted_iota(jnp.int32, heads.shape, 1) // HEAD
    heads = jnp.where(head == head_column, heads, 0.0).astype(low)
    grad_cross_value = pair(own(mixed), heads)
    grad_cross_value_ref[...] = grad_cross_value

    def exact(left, right):
        return lax.dot_general(
            left,
            right,
            (((1,), (1,)), ((), ())),
            precision=highest,
            preferred_element_type=wide,
        )

    chosen = chosen.astype(wide)
    key_rows = exact(chosen, sums_ref[:HEAD_ROWS, :])
    head_row = lax.broadcasted_iota(jnp.int32, (HEAD_ROWS, width), 0)
    head_mask = head_row == lax.broadcasted_iota(jnp.int32, (HEAD_ROWS, width), 1) // HEAD
    query_row = starts_ref[5:6, :].astype(low).astype(wide)
    query_heads = jnp.where(head_mask, jnp.broadcast_to(query_row, (HEAD_ROWS, width)), 0.0)
    grad_cross_key = jnp.dot(
        key_rows, query_heads, precision=highest, preferred_element_type=wide
    )
    grad_cross_key_ref[...] = grad_cross_key
    starts = exact(chosen, starts_ref[...])
    grad_self_value_ref[...] = starts[:, 1:2] * backs_ref[5:6, :]
    grad_self_out_ref[...] = starts[:, 2:3] * backs_ref[4:5, :]
    grad_cross_query_ref[...] = starts[:, 4:5] * backs_ref[3:4, :]

    def gain_sum(weight, grads):
        ones = jnp.ones((8, grads.shape[1]), wide)
        return exact(ones, weight.astype(wide) * grads)[:1]

    attention = (
        gain_sum(query_ref[...], query_sums_ref[...])
        + gain_sum(key_ref[...], key_sums_ref[...])
        + gain_sum(value_ref[...], value_sums_ref[...])
    )
    feed = gain_sum(inner_ref[...], inner_sums_ref[...])
    encoder = gain_sum(cross_key_ref[...], grad_cross_key) + gain_sum(
        cross_value_ref[...], grad_cross_value
    )
    gains = exact(gains_ref[:8, :], chosen)
    backs = exact(backs_ref[...], chosen)
    others = exact(sums_ref[HEAD_ROWS:, :], chosen)
    for i, row in enumerate(
        (
            attention / gains[0:1],
            feed / gains[1:2],
            encoder / gains[2:3],
            backs[0:1],
            backs[1:2],
            backs[2:3],
            others[2:3],
            others[1:2],
        )
    ):
        vectors_ref[i] = row


def last_step(groups, seqs, halves, tokens, part, share, feeds, *arrays):
    rows, width = tokens.shape
    whole = pl.BlockSpec(memory_space=pltpu.VMEM)
    square = jax.ShapeDtypeStruct((part, width), wide)
    return pl.pallas_call(
        functools.partial(last_kernel, groups, seqs, halves),
        name="last",
        in_specs=[whole] * len(arrays),
        out_specs=[whole] * 11,
        out_shape=[
            jax.ShapeDtypeStruct((rows, width), wide),
            jax.ShapeDtypeStruct((8, 1, part), wide),
            square,
            square,
            square,
            square,
            square,
            square,
            jax.ShapeDtypeStruct((part, feeds * width), wide),
            jax.ShapeDtypeStruct((share, width), wide),
            square,
        ],
        scratch_shapes=[
            pltpu.VMEM((width // LANES, groups * seqs * 2 * HEAD_ROWS, LANES), wide)
        ],
        compiler_params=pltpu.CompilerParams(vmem_limit_bytes=50 * 2**20),
    )(*arrays)


def in_blocks(gathered, sizes):
    count, _, width = gathered.shape
    join = 16 // math.gcd(16, sizes[0])
    if join == 1:
        return gathered
    pieces, at = [], 0
    for size in sizes:
        piece = gathered[:, at : at + size].reshape(count // join, join * size, width)
        pieces.append(piece)
        at += size
    return jnp.concatenate(pieces, axis=1)


def column_blocks(weight, model_width):
    rows, columns = weight.shape
    blocks = columns // model_width
    return jnp.transpose(weight.reshape(rows, blocks, model_width), (1, 0, 2)).reshape(
        blocks * rows, model_width
    )


def shards(
    tokens,
    lengths,
    labels,
    attention_gain,
    query_weight,
    key_weight,
    value_weight,
    attention_out,
    position_bias,
    feed_gain,
    feed_inner,
    feed_outer,
    encoder_gain,
    start_token,
    self_gain,
    self_value,
    self_out,
    cross_gain,
    cross_query,
    cross_key,
    cross_value,
    cross_out,
    second_gain,
    second_inner,
    second_outer,
    final_gain,
    pooler_weight,
):
    rows, width = tokens.shape
    part = query_weight.shape[0]
    share = feed_outer.shape[0]
    groups = lax.axis_size("batch")
    members = lax.axis_size("seq")
    blocks = feed_inner.shape[1] // width
    pack = rows * members
    seqs = lengths.shape[1]
    group = lax.axis_index("batch")
    member = lax.axis_index("seq")
    own_first = member * rows
    ends = jnp.cumsum(lengths[0])
    place = jnp.stack(
        [ends[0], ends[1], own_first, own_first % LANES]
    ).astype(jnp.int32)

    vectors = jnp.stack(
        [
            attention_gain,
            feed_gain,
            encoder_gain,
            start_token,
            self_gain,
            cross_gain,
            second_gain,
            final_gain,
        ],
        axis=0,
    )
    bias_part = position_bias.reshape(1, -1)
    bias_size = bias_part.shape[1]
    extra = jnp.zeros((16, width), low)
    extra = lax.dynamic_update_slice(extra, vectors, (0, group * part))
    extra = lax.dynamic_update_slice(extra, bias_part, (8, group * bias_size))
    queries, all_keys, all_values, normed_all, gains, first_full = project(
        tokens, extra, [query_weight, key_weight, value_weight], groups, members
    )
    table = gains[8, : BUCKETS * HEADS].reshape(BUCKETS, HEADS).astype(low)
    second_part = jnp.concatenate(
        [
            attention_out[None],
            column_blocks(feed_inner, width).reshape(blocks, part, width),
            feed_outer.reshape(blocks, part, width),
        ],
        axis=0,
    )
    halves = 2 if members == 2 else 1
    half_share = share // halves
    half_inner = lax.dynamic_slice_in_dim(
        second_inner.reshape(part, groups, share), member % halves * half_share, half_share, 2
    ).reshape(part, groups * half_share)
    half_outer = lax.dynamic_slice_in_dim(second_outer, member % halves * half_share, half_share)
    rest_part = jnp.concatenate(
        [
            second_part.reshape(-1, width),
            self_value,
            self_out,
            cross_query,
            cross_key,
            cross_value,
            cross_out,
            pooler_weight,
            column_blocks(half_inner, width),
            half_outer,
        ],
        axis=0,
    )
    rest = lax.all_gather(rest_part, "batch", axis=0, tiled=False)

    near = offset_biases(table, block_rows(rows), pack, place[3])
    attended, totals = attend(queries, all_keys, all_values, near, place)
    rest_blocks = in_blocks(
        rest,
        [part] * (1 + blocks) + [share] + [part] * (7 + blocks // halves) + [half_share],
    )
    base = (1 + 2 * blocks) * (width // rest_blocks.shape[0])
    hidden, inner_pre, encoded, context = feed_forward(
        attended, tokens, rest_blocks, gains, blocks
    )

    embedded, loss, grad_context, decoder_rows, starts, decoder_totals = decoder_step(
        context, rest_blocks, base, gains, labels, place, groups, members, seqs
    )
    contrastive_loss = loss[0, :1]
    embedded = embedded[:seqs]
    decoder_rows = lax.all_gather(
        decoder_rows.reshape(seqs * 2 * HEAD_ROWS, width), "batch", axis=0, tiled=False
    )

    second_grads, grad_hidden, grad_attended, sums, backs = feed_back(
        grad_context,
        encoded,
        hidden,
        inner_pre,
        attended,
        rest_blocks,
        base,
        gains,
        decoder_totals,
        starts,
        groups,
        members,
        part,
    )
    normed = lax.dynamic_slice_in_dim(normed_all, own_first, rows)
    (
        grad_query_rows,
        grad_key_rows,
        grad_value_rows,
        table_sums,
        out_sums,
        inner_sums,
        outer_sums,
        query_sums,
        key_sums,
        value_sums,
    ) = attend_back(
        queries,
        all_keys,
        all_values,
        grad_attended,
        attended,
        totals,
        near,
        place,
        normed.T,
        normed_all.T,
        second_grads,
    )
    (
        grad_tokens,
        vectors,
        grad_self_value,
        grad_self_out,
        grad_cross_query,
        grad_cross_key,
        grad_cross_value,
        grad_cross_out,
        grad_second_inner,
        grad_second_outer,
        grad_pooler,
    ) = last_step(
        groups,
        seqs,
        halves,
        tokens,
        part,
        share,
        blocks,
        grad_query_rows,
        grad_key_rows,
        grad_value_rows,
        first_full,
        tokens,
        grad_hidden,
        gains,
        decoder_rows.reshape(groups * seqs, 2 * HEAD_ROWS, width),
        sums,
        starts,
        backs,
        query_weight,
        key_weight,
        value_weight,
        feed_inner,
        cross_key,
        cross_value,
        query_sums,
        key_sums,
        value_sums,
        inner_sums,
    )
    half_share = share // halves
    grad_second_inner = jnp.transpose(
        grad_second_inner.reshape(part, halves, groups, half_share), (0, 2, 1, 3)
    ).reshape(part, blocks * width)
    vectors = vectors.reshape(8, part)
    own_buckets = BUCKETS // groups
    grad_table = lax.dynamic_slice_in_dim(table_sums, group * own_buckets, own_buckets, 1)[:HEADS].T
    return (
        contrastive_loss,
        embedded,
        grad_tokens,
        vectors[0],
        query_sums,
        key_sums,
        value_sums,
        out_sums,
        grad_table,
        vectors[1],
        inner_sums,
        outer_sums,
        vectors[2],
        vectors[3],
        vectors[4],
        grad_self_value,
        grad_self_out,
        vectors[5],
        grad_cross_query,
        grad_cross_key,
        grad_cross_value,
        grad_cross_out,
        vectors[6],
        grad_second_inner,
        grad_second_outer,
        vectors[7],
        grad_pooler,
    )


def solution(mesh):
    placed = (
        P(("batch", "seq"), None),
        P("batch", None),
        P(),
        P("batch"),
        P("batch", None),
        P("batch", None),
        P("batch", None),
        P("batch", None),
        P("batch", None),
        P("batch"),
        P("batch", None),
        P("batch", None),
        P("batch"),
        P("batch"),
        P("batch"),
        P("batch", None),
        P("batch", None),
        P("batch"),
        P("batch", None),
        P("batch", None),
        P("batch", None),
        P("batch", None),
        P("batch"),
        P("batch", None),
        P("batch", None),
        P("batch"),
        P("batch", None),
    )
    return jax.shard_map(
        shards,
        mesh=mesh,
        in_specs=placed,
        out_specs=(
            P(),
            P("batch", None),
            P(("batch", "seq"), None),
            P("batch"),
            P("batch", None),
            P("batch", None),
            P("batch", None),
            P("batch", None),
            P("batch", None),
            P("batch"),
            P("batch", None),
            P("batch", None),
            P("batch"),
            P("batch"),
            P("batch"),
            P("batch", None),
            P("batch", None),
            P("batch"),
            P("batch", None),
            P("batch", None),
            P("batch", None),
            P("batch", None),
            P("batch"),
            P("batch", None),
            P("batch", None),
            P("batch"),
            P("batch", None),
        ),
        check_vma=False,
    )
```

```python
import functools
import math

import jax
import jax.numpy as jnp
from jax import lax
from jax.experimental import pallas as pl
from jax.experimental.pallas import tpu as pltpu
from jax.sharding import PartitionSpec as P

HEADS = 12
HEAD = 64
BUCKETS = 32
LANES = 128
far_apart = float(2**30)

eps_norm = 1e-06
masked_score = -1000000000.0
logit_scale = 20.0
bucket_limits = (12, 16, 23, 32, 46, 64, 91)
highest = lax.Precision.HIGHEST
low = jnp.bfloat16
wide = jnp.float32
MESH = pl.DeviceIdType.MESH


def rms_factor(values):
    return lax.rsqrt(jnp.mean(values * values, axis=-1, keepdims=True) + eps_norm)


def rms_norm(values, gain_vector):
    return (
        values
        * lax.rsqrt(jnp.mean(values * values, axis=-1, keepdims=True) + eps_norm)
        * gain_vector
    )


def unit_length(values):
    return values * lax.rsqrt(jnp.sum(values * values, axis=-1, keepdims=True) + eps_norm)


def bucket_of(offsets):
    upper_half = jnp.where(offsets > 0, 16, 0).astype(jnp.int32)
    distance = jnp.abs(offsets)
    far_bucket = 8 + sum(((distance >= threshold).astype(jnp.int32) for threshold in bucket_limits))
    return upper_half + jnp.where(distance < 8, distance, far_bucket)


def product(left_side, right_side):
    return jnp.dot(left_side, right_side, preferred_element_type=wide)


def back_product(left_side, right_side):
    return lax.dot_general(
        left_side, right_side, (((1,), (1,)), ((), ())), preferred_element_type=wide
    )


def weight_grad(left_side, right_side):
    return lax.dot_general(
        left_side, right_side, (((0,), (0,)), ((), ())), preferred_element_type=wide
    )


def norm_back(values, gain_vector, grad_rows):
    _, pullback = jax.vjp(rms_norm, values, gain_vector)
    return pullback(grad_rows)


def gelu_back(values, grad_rows):
    _, pullback = jax.vjp(jax.nn.gelu, values)
    return pullback(grad_rows)[0]


def segment_of(places, ends):
    return (places >= ends[0]).astype(jnp.int32) + (places >= ends[1]).astype(jnp.int32)


def block_rows(rows):
    return 256 if rows % 256 == 0 else rows


def table_sizes(size, pack):
    slack = LANES if size % LANES else 0
    reach = -(-(size + slack + 91) // LANES) * LANES
    lead = -(-(size + slack) // LANES) * LANES
    middle = -(-(pack - size) // LANES) * LANES
    return middle, reach, lead, middle + max(pack, reach)


def offset_biases(table, size, pack, shift):
    _, reach, lead, _ = table_sizes(size, pack)
    offsets = jnp.arange(lead + reach + LANES, dtype=jnp.int32) - (lead + LANES) - shift
    onehot = (
        bucket_of(offsets)[None, :] == jnp.arange(BUCKETS, dtype=jnp.int32)[:, None]
    ).astype(low)
    return weight_grad(table, onehot)[:, None, :]


def turned_biases(row, size, lead):
    spread = jnp.broadcast_to(row, (size, row.shape[1]))
    return pltpu.roll(spread, 0, 1, stride=1, stride_axis=0)[:, lead:]


class Gathering:
    def __init__(self, groups, members, sems):
        self.groups = groups
        self.members = members
        self.lines = groups // 4
        self.group = lax.axis_index("batch")
        self.member = lax.axis_index("seq")
        self.z = self.group // 4
        self.y = lax.rem(self.group // 2, 2)
        self.core = lax.rem(self.group, 2)
        self.line_send, self.line_recv, self.pair_sems, self.chip_sems, self.share_sems = sems

    def batch_id(self, offset):
        return {"batch": self.group + offset}

    def neighbours(self):
        found = [
            (None, self.batch_id(1 - 2 * self.core)),
            (None, self.batch_id(2 - 4 * self.y)),
            (self.z > 0, self.batch_id(-4)),
            (self.z < self.lines - 1, self.batch_id(4)),
        ]
        for step in range(1, self.members):
            found.append((None, {"seq": lax.rem(self.member + step, self.members)}))
        return found

    def greet(self, barrier):
        for condition, device in self.neighbours():
            if condition is None:
                pl.semaphore_signal(barrier, inc=1, device_id=device, device_id_type=MESH)
            else:

                @pl.when(condition)
                def _():
                    pl.semaphore_signal(barrier, inc=1, device_id=device, device_id_type=MESH)

    def greeted(self, barrier):
        ends = (self.z > 0).astype(jnp.int32) + (self.z < self.lines - 1).astype(jnp.int32)
        pl.semaphore_wait(barrier, 2 + self.members - 1 + ends)

    def copy(self, source, target, send, recv, device):
        return pltpu.make_async_remote_copy(
            src_ref=source,
            dst_ref=target,
            send_sem=send,
            recv_sem=recv,
            device_id=device,
            device_id_type=MESH,
        )

    def line_copy(self, item, source, full, way, step):
        place = self.z + step if way else self.z - step
        block = full.at[place, self.y, self.core]
        return self.copy(
            source if step == 0 else block,
            block,
            self.line_send.at[item, way, step],
            self.line_recv.at[item, way, step],
            self.batch_id(-4 if way else 4),
        )

    def line_sends(self, way, step):
        if way:
            return (self.z > 0) & (self.z + step < self.lines)
        return (self.z < self.lines - 1) & (self.z - step >= 0)

    def line_arrives(self, way, step):
        return self.z + step < self.lines if way else self.z - step >= 0

    def send_line(self, item, source, full, step):
        for way in range(2):

            @pl.when(self.line_sends(way, step))
            def _():
                self.line_copy(item, source, full, way, step).start()

    def pair_copy(self, item, full):
        span = full.at[:, self.y, self.core]
        return self.copy(
            span,
            span,
            self.pair_sems.at[item, 0],
            self.pair_sems.at[item, 1],
            self.batch_id(2 - 4 * self.y),
        )

    def share_copy(self, item, full):
        span = full.at[:, :, self.core]
        return self.copy(
            span,
            span,
            self.share_sems.at[item, 0],
            self.share_sems.at[item, 1],
            {"seq": 1 - self.member},
        )

    def chip_copy(self, item, which, full):
        span = full.at[:, :, self.core]
        return self.copy(
            span,
            span,
            self.chip_sems.at[item, which, 0],
            self.chip_sems.at[item, which, 1],
            self.batch_id(1 - 2 * self.core),
        )

    def stages(self, split):
        return self.lines + (3 if split else 2)

    def stage(self, number, item, source, full, other=None):
        lines = self.lines
        if number == 0:
            own = pltpu.make_async_copy(
                source, full.at[self.z, self.y, self.core], self.chip_sems.at[item, 0, 0]
            )
            own.start()
            self.send_line(item, source, full, 0)
            own.wait()
        elif number < lines:
            for way in range(2):

                @pl.when(self.line_arrives(way, number))
                def _():
                    self.line_copy(item, source, full, way, number - 1).wait_recv()

            if number < lines - 1:
                self.send_line(item, source, full, number)
            else:
                self.pair_copy(item, full).start()
        elif number == lines:
            self.pair_copy(item, full).wait()
            if other is not None:
                self.share_copy(item, full).start()
            self.chip_copy(item, 0, full).start()
        elif number == lines + 1 and other is not None:
            self.share_copy(item, full).wait()
            self.chip_copy(item, 1, other).start()
        else:
            self.chip_copy(item, 0, full).wait()
            if other is not None:
                self.chip_copy(item, 1, other).wait()
            for way in range(2):
                for step in range(lines - 1):

                    @pl.when(self.line_sends(way, step))
                    def _():
                        self.line_copy(item, source, full, way, step).wait_send()


def gathering_sems(groups, items):
    lines = groups // 4
    return [
        pltpu.SemaphoreType.DMA((items, 2, lines)),
        pltpu.SemaphoreType.DMA((items, 2, lines)),
        pltpu.SemaphoreType.DMA((items, 2)),
        pltpu.SemaphoreType.DMA((items, 2, 2)),
        pltpu.SemaphoreType.DMA((items, 2)),
    ]


def joined_rows(blocks):
    size, width = blocks.shape[-2:]
    rows = size * math.prod(blocks.shape[:-2])
    if size % 16:
        return blocks.astype(wide).reshape(rows, width).astype(low)
    return blocks.reshape(rows, width)


def first_kernel(
    groups,
    members,
    tokens_ref,
    extra_ref,
    query_ref,
    key_ref,
    value_ref,
    queries_ref,
    keys_ref,
    values_ref,
    normed_ref,
    gains_ref,
    weights_ref,
    all_tokens,
    all_extra,
    all_query,
    all_key,
    all_value,
    token_send,
    token_recv,
    *sems,
):
    parts = (extra_ref, query_ref, key_ref, value_ref)
    fulls = (all_extra, all_query, all_key, all_value)
    gathering = Gathering(groups, members, sems)
    member = gathering.member
    rows, width = tokens_ref.shape
    barrier = pltpu.get_barrier_semaphore()
    gathering.greet(barrier)
    gathering.greeted(barrier)
    copies = []
    for step in range(1, members):
        copies.append(
            pltpu.make_async_remote_copy(
                src_ref=tokens_ref,
                dst_ref=all_tokens.at[member],
                send_sem=token_send.at[step - 1],
                recv_sem=token_recv.at[step - 1],
                device_id={"seq": lax.rem(member + step, members)},
                device_id_type=MESH,
            )
        )
        copies[-1].start()
    all_tokens[member] = tokens_ref[...]

    def normed(values):
        values = values.astype(wide)
        return (values * rms_factor(values) * gains_ref[:1, :]).astype(low)

    def finished(item):
        if item == 0:
            total = jnp.zeros((16, width), wide)
            for z in range(groups // 4):
                for y in range(2):
                    for core in range(2):
                        total = total + all_extra[z, y, core].astype(wide)
            gains_ref[...] = total
        elif item == 1:
            weights_ref[0] = joined_rows(all_query[...])
            queries_ref[...] = product(normed(tokens_ref[...]), weights_ref[0]).astype(low)
        elif item == 2:
            for copy in copies:
                copy.wait()
            weights_ref[1] = joined_rows(all_key[...])
            for part in range(members):
                span = slice(rows * part, rows * (part + 1))
                normed_ref[span, :] = normed(all_tokens[part])
                keys_ref[span, :] = product(normed_ref[span, :], weights_ref[1]).astype(low)
        else:
            weights_ref[2] = joined_rows(all_value[...])
            for part in range(members):
                span = slice(rows * part, rows * (part + 1))
                values_ref[span, :] = product(normed_ref[span, :], weights_ref[2]).astype(low)

    stages = gathering.stages(False)
    for step in range(len(parts) + stages - 1):
        for stage in reversed(range(stages)):
            if 0 <= step - stage < len(parts):
                item = step - stage
                gathering.stage(stage, item, parts[item], fulls[item])
        if step - (stages - 1) >= 0:
            finished(step - (stages - 1))


def project(tokens, extra, parts, groups, members):
    rows, width = tokens.shape
    whole = pl.BlockSpec(memory_space=pltpu.VMEM)
    lines = groups // 4
    items = [extra] + list(parts)
    pack = members * rows
    return pl.pallas_call(
        functools.partial(first_kernel, groups, members),
        name="project",
        in_specs=[whole] * 5,
        out_specs=[whole] * 6,
        out_shape=[
            jax.ShapeDtypeStruct((rows, width), low),
            jax.ShapeDtypeStruct((pack, width), low),
            jax.ShapeDtypeStruct((pack, width), low),
            jax.ShapeDtypeStruct((pack, width), low),
            jax.ShapeDtypeStruct((16, width), wide),
            jax.ShapeDtypeStruct((3, width, width), low),
        ],
        scratch_shapes=[pltpu.VMEM((members,) + tokens.shape, low)]
        + [pltpu.VMEM((lines, 2, 2) + item.shape, low) for item in items]
        + [
            pltpu.SemaphoreType.DMA((max(members - 1, 1),)),
            pltpu.SemaphoreType.DMA((max(members - 1, 1),)),
        ]
        + gathering_sems(groups, len(items)),
        compiler_params=pltpu.CompilerParams(
            collective_id=3, has_side_effects=True, vmem_limit_bytes=48 * 2**20
        ),
        cost_estimate=pl.CostEstimate(
            flops=2**31, bytes_accessed=32 * pack * width, transcendentals=0
        ),
    )(tokens, extra, *parts)


FAR_LANE = 3


def key_lanes(places, lane, ends, near, begins, reach):
    blocks = len(begins)
    values = jnp.where((segment_of(places, ends) == lane) & (lane < 3), 1.0, 0.0)
    for half in range(2):
        row = near[half]
        for i, begin in enumerate(begins):
            far = jnp.where(
                places < begin - LANES,
                row[:, :1],
                jnp.where(places >= begin + reach, row[:, -1:], 0.0),
            )
            values = jnp.where(lane == FAR_LANE + half * blocks + i, far, values)
    return values.astype(low)


def attend_kernel(
    place, q_ref, k_ref, v_ref, near_ref, attended_ref, total_ref, key_side, value_side, scores_ref
):
    pair = pl.program_id(0)
    pack = k_ref.shape[0]
    rows = q_ref.shape[0]
    size = block_rows(rows)
    blocks = rows // size
    _, reach, lead, _ = table_sizes(size, pack)
    ends = (place[0], place[1])
    shift = place[3]
    begins = [place[2] - shift + size * i for i in range(blocks)]
    near = [near_ref[half] for half in range(2)]
    places = lax.broadcasted_iota(jnp.int32, (pack, LANES), 0)
    lane = lax.broadcasted_iota(jnp.int32, (pack, LANES), 1)
    key_side[:, :LANES] = k_ref[...]
    key_side[:, LANES:] = key_lanes(places, lane, ends, near, begins, reach)
    value_side[:, :LANES] = v_ref[...]
    value_side[:, LANES:] = jnp.ones((pack, LANES), low)

    lane = lax.broadcasted_iota(jnp.int32, (rows, LANES), 1)
    row = lax.broadcasted_iota(jnp.int32, (rows, LANES), 0)
    apart = jnp.where(
        (segment_of(place[2] + row, ends) != lane) & (lane < 3), -far_apart, 0.0
    )
    queries = q_ref[...]
    outputs = []
    totals = total_ref[...]
    for half in range(2):
        mine = (lane >= HEAD) if half else (lane < HEAD)
        side = jnp.where(lane == FAR_LANE + half * blocks + row // size, 1.0, apart).astype(low)
        query_side = jnp.concatenate(
            [jnp.where(mine, queries, jnp.zeros_like(queries)), side], axis=1
        )
        scores_ref[half, :, LANES : LANES + pack] = back_product(query_side, key_side[...])
        band = turned_biases(near[half], size, lead)
        for i in range(blocks):
            span = slice(size * i, size * (i + 1))
            columns = pl.ds(pl.multiple_of(begins[i], LANES), LANES + reach)
            scores_ref[half, span, columns] += band
        scores = scores_ref[half, :, LANES : LANES + pack]
        top = jnp.max(scores, axis=1, keepdims=True)
        weights = jnp.exp(scores - top).astype(low)
        output = product(weights, value_side[...])
        total = output[:, LANES:]
        outputs.append(output[:, :LANES] / total)
        totals = jnp.where(lane == 2 * pair + half, top + jnp.log(total), totals)
    attended_ref[...] = jnp.where(lane < HEAD, outputs[0], outputs[1])
    total_ref[...] = totals


def attend(queries, all_keys, all_values, near, place):
    rows, width = queries.shape
    pack = all_keys.shape[0]
    size = block_rows(rows)
    _, reach, _, _ = table_sizes(size, pack)
    pairs = width // LANES
    return pl.pallas_call(
        attend_kernel,
        name="attend",
        grid=(pairs,),
        in_specs=[
            pl.BlockSpec(memory_space=pltpu.SMEM),
            pl.BlockSpec((rows, LANES), lambda p: (0, p)),
            pl.BlockSpec((pack, LANES), lambda p: (0, p)),
            pl.BlockSpec((pack, LANES), lambda p: (0, p)),
            pl.BlockSpec((2, 1, near.shape[2]), lambda p: (p, 0, 0)),
        ],
        out_specs=[
            pl.BlockSpec((rows, LANES), lambda p: (0, p)),
            pl.BlockSpec((rows, LANES), lambda p: (0, 0)),
        ],
        out_shape=[
            jax.ShapeDtypeStruct((rows, width), wide),
            jax.ShapeDtypeStruct((rows, LANES), wide),
        ],
        scratch_shapes=[
            pltpu.VMEM((pack, 2 * LANES), low),
            pltpu.VMEM((pack, 2 * LANES), low),
            pltpu.VMEM((2, rows, LANES + pack + reach), wide),
        ],
        compiler_params=pltpu.CompilerParams(vmem_limit_bytes=56 * 2**20),
        cost_estimate=pl.CostEstimate(
            flops=8 * rows * pack * width * 2, bytes_accessed=16 * pack * width, transcendentals=0
        ),
    )(place, queries, all_keys, all_values, near)


SEQ_ROWS = 8
HEAD_ROWS = 16


def rms_back(values, gain_row, grad_rows):
    factor = rms_factor(values)
    scaled = gain_row * grad_rows
    inner = jnp.mean(scaled * values, axis=-1, keepdims=True)
    return (
        factor * scaled - values * (factor * factor * factor) * inner,
        jnp.sum(grad_rows * values * factor, axis=0, keepdims=True),
    )


gelu_scale = 0.7978845608028654


def gelu_value(values):
    return 0.5 * values * (
        1.0 + jnp.tanh(gelu_scale * (values + 0.044715 * values * values * values))
    )


def gelu_slope(values):
    square = values * values
    bent = jnp.tanh(gelu_scale * (values + 0.044715 * square * values))
    return 0.5 * (1.0 + bent) + 0.5 * values * (1.0 - bent * bent) * gelu_scale * (
        1.0 + 0.134145 * square
    )


def decoder_kernel(
    base,
    groups,
    members,
    seqs,
    place,
    context_ref,
    third_ref,
    gains_ref,
    target_ref,
    embedded_ref,
    loss_ref,
    grad_context_ref,
    pieces_ref,
    starts_ref,
    totals_ref,
    weights,
    everyone,
    shared,
    similar_ref,
    halves_sent,
    halves_got,
    piece_rows,
    weight_sem,
    every_send,
    every_recv,
    share_send,
    share_recv,
    half_send,
    half_recv,
):
    rows, width = context_ref.shape
    count, _, _ = third_ref.shape
    unit = width // count
    halves = 2 if members == 2 else 1
    feeds = 4 // halves
    blocks = feeds * unit
    group = lax.axis_index("batch")
    member = lax.axis_index("seq")
    seq_total = groups * seqs

    barrier = pltpu.get_barrier_semaphore()
    for step in range(1, groups):
        pl.semaphore_signal(
            barrier,
            inc=1,
            device_id={"batch": lax.rem(group + step, groups)},
            device_id_type=MESH,
        )
    for step in range(1, members):
        pl.semaphore_signal(
            barrier,
            inc=1,
            device_id={"seq": lax.rem(member + step, members)},
            device_id_type=MESH,
        )

    sizes = [unit] * 7 + [unit] * feeds + [blocks]
    firsts = [sum(sizes[:i]) for i in range(len(sizes))]
    copies = [
        pltpu.make_async_copy(
            third_ref.at[:, base + first : base + first + size, :],
            weights.at[:, first : first + size, :],
            weight_sem.at[i],
        )
        for i, (first, size) in enumerate(zip(firsts, sizes))
    ]
    for copy in copies:
        copy.start()

    def weight(i):
        return weights[:, firsts[i] : firsts[i] + unit, :].reshape(width, width)

    def outer_weight(j):
        per = count // feeds
        return weights[per * j : per * (j + 1), firsts[-1] : firsts[-1] + blocks, :].reshape(
            width, width
        )

    def half_copy(which, first, number):
        span = pl.ds(first, number)
        return pltpu.make_async_remote_copy(
            src_ref=halves_sent.at[span],
            dst_ref=halves_got.at[span],
            send_sem=half_send.at[which],
            recv_sem=half_recv.at[which],
            device_id={"seq": 1 - member},
            device_id_type=MESH,
        )

    def joined(which, part):
        if halves == 1:
            return part
        halves_sent[which] = part
        copy = half_copy(which, which, 1)
        copy.start()
        copy.wait()
        return part + halves_got[which]

    gain = {
        name: gains_ref[i : i + 1, :]
        for i, name in enumerate(
            ("attention", "feed", "encoder", "start", "own", "cross", "second", "final")
        )
    }
    context = context_ref[...]

    start = jnp.broadcast_to(gain["start"], (SEQ_ROWS, width))
    self_in = (start * rms_factor(start) * gain["own"]).astype(low)
    copies[0].wait()
    self_vals = product(self_in, weight(0)).astype(low)
    copies[1].wait()
    after_self = start + product(self_vals, weight(1))
    cross_in = (after_self * rms_factor(after_self) * gain["cross"]).astype(low)
    copies[2].wait()
    cross_query = product(cross_in, weight(2))
    head_row = lax.broadcasted_iota(jnp.int32, (HEAD_ROWS, width), 0)
    head_mask = head_row == lax.broadcasted_iota(jnp.int32, (HEAD_ROWS, width), 1) // HEAD
    query_heads = jnp.where(
        head_mask, jnp.broadcast_to(cross_query[:1], (HEAD_ROWS, width)), 0.0
    ).astype(low)
    copies[3].wait()
    key_rows = back_product(query_heads, weight(3)).astype(low)

    many = seqs * HEAD_ROWS
    scores = back_product(key_rows, context)
    scores = jnp.concatenate([scores] * seqs, axis=0)
    places = member * rows + lax.broadcasted_iota(jnp.int32, (many, rows), 1)
    row_seq = lax.broadcasted_iota(jnp.int32, (many, rows), 0) // HEAD_ROWS
    inside = segment_of(places, (place[0], place[1])) == row_seq
    scores = jnp.where(inside, scores, masked_score)
    part_top = jnp.max(scores, axis=1, keepdims=True)
    part_weights = jnp.where(inside, jnp.exp(scores - part_top), 0.0).astype(low)
    part_total = jnp.sum(part_weights.astype(wide), axis=1, keepdims=True)
    lane = lax.broadcasted_iota(jnp.int32, (many, LANES), 1)
    shared[0, :, :width] = product(part_weights, context)
    shared[0, :, width:] = jnp.where(lane == 0, part_top, part_total)

    pl.semaphore_wait(barrier, groups - 1 + members - 1)
    for step in range(1, members):
        pltpu.make_async_remote_copy(
            src_ref=shared.at[0],
            dst_ref=shared.at[step],
            send_sem=share_send.at[step - 1],
            recv_sem=share_recv.at[step - 1],
            device_id={"seq": lax.rem(member + step, members)},
            device_id_type=MESH,
        ).start()
    for step in range(1, members):
        pltpu.make_async_remote_copy(
            src_ref=shared.at[0],
            dst_ref=shared.at[step],
            send_sem=share_send.at[step - 1],
            recv_sem=share_recv.at[step - 1],
            device_id={"seq": lax.rem(member + step, members)},
            device_id_type=MESH,
        ).wait()
    top = shared[0, :, width : width + 1]
    for step in range(1, members):
        top = jnp.maximum(top, shared[step, :, width : width + 1])
    total = jnp.zeros((many, 1), wide)
    mixed = jnp.zeros((many, width), wide)
    for step in range(members):
        scale = jnp.exp(shared[step, :, width : width + 1] - top)
        total = total + shared[step, :, width + 1 : width + 2] * scale
        mixed = mixed + shared[step, :, :width] * scale
    mixed = (mixed / total).astype(low)
    log_total = top + jnp.log(total)

    def by_seq(parts):
        row = lax.broadcasted_iota(jnp.int32, (SEQ_ROWS, width), 0)
        joined = jnp.zeros((SEQ_ROWS, width), wide)
        for i, part in enumerate(parts):
            joined = jnp.where(row == i, part, joined)
        return joined

    copies[4].wait()
    spread = product(mixed, weight(4))
    cross_attended = by_seq(
        [
            jnp.sum(
                jnp.where(head_mask, spread[HEAD_ROWS * i : HEAD_ROWS * (i + 1)], 0.0),
                axis=0,
                keepdims=True,
            )
            for i in range(seqs)
        ]
    )
    cross_low = cross_attended.astype(low)
    copies[5].wait()
    after_cross = after_self + product(cross_low, weight(5))
    second_in = (after_cross * rms_factor(after_cross) * gain["second"]).astype(low)
    for copy in copies[7:]:
        copy.wait()
    second_pre = [product(second_in, weight(7 + j)) for j in range(feeds)]
    second_act = [gelu_value(second_pre[j]).astype(low) for j in range(feeds)]
    second_out = product(second_act[0], outer_weight(0))
    for j in range(1, feeds):
        second_out = second_out + product(second_act[j], outer_weight(j))
    decoded = after_cross + joined(0, second_out)
    pooled_in = (decoded * rms_factor(decoded) * gain["final"]).astype(low)
    copies[6].wait()
    pooled = product(pooled_in, weight(6))
    size = lax.rsqrt(jnp.sum(pooled * pooled, axis=-1, keepdims=True) + eps_norm)
    embedded = pooled * size
    embedded_ref[...] = embedded

    everyone[0] = embedded
    sends = []
    for step in range(1, groups):
        sends.append(
            pltpu.make_async_remote_copy(
                src_ref=everyone.at[0],
                dst_ref=everyone.at[step],
                send_sem=every_send,
                recv_sem=every_recv,
                device_id={"batch": lax.rem(group + step, groups)},
                device_id_type=MESH,
            )
        )
        sends[-1].start()
    arrival = pltpu.make_async_remote_copy(
        src_ref=everyone.at[pl.ds(1, groups - 1)],
        dst_ref=everyone.at[pl.ds(1, groups - 1)],
        send_sem=every_send,
        recv_sem=every_recv,
        device_id={"batch": lax.rem(group + 1, groups)},
        device_id_type=MESH,
    )
    arrival.wait_recv()
    arrival.wait_send()
    all_rows = everyone[...].reshape(groups * SEQ_ROWS, width)
    number = groups * SEQ_ROWS
    row = lax.broadcasted_iota(jnp.int32, (number, number), 0)
    column = lax.broadcasted_iota(jnp.int32, (number, number), 1)
    row_valid = row % SEQ_ROWS < seqs
    valid = row_valid & (column % SEQ_ROWS < seqs)
    similar = logit_scale * lax.dot_general(
        all_rows,
        all_rows,
        (((1,), (1,)), ((), ())),
        precision=highest,
        preferred_element_type=wide,
    )
    similar = jnp.where(valid & (row != column), similar, masked_score)
    best = jnp.max(similar, axis=1, keepdims=True)
    log_norm = best + jnp.log(jnp.sum(jnp.exp(similar - best), axis=1, keepdims=True))
    row_group = lax.rem(group - row // SEQ_ROWS + groups, groups)
    column_group = lax.rem(group - column // SEQ_ROWS + groups, groups)
    row_number = row_group * seqs + row % SEQ_ROWS
    column_number = column_group * seqs + column % SEQ_ROWS
    label = jnp.max(
        jnp.where(
            lax.broadcasted_iota(jnp.int32, (number, target_ref.shape[1]), 1)
            == row_number[:, : target_ref.shape[1]],
            target_ref[:1, :],
            -1.0,
        ),
        axis=1,
        keepdims=True,
    )
    target = (column_number.astype(wide) == label) & valid
    picked = jnp.sum(jnp.where(target, similar, 0.0), axis=1, keepdims=True)
    losses = jnp.where(row_valid[:, :1], log_norm - picked, 0.0)
    loss_ref[...] = jnp.broadcast_to(
        jnp.sum(losses, axis=0, keepdims=True) / seq_total, loss_ref.shape
    )
    grad_similar = jnp.where(
        valid, (jnp.exp(similar - log_norm) - target.astype(wide)) / seq_total, 0.0
    )
    similar_ref[...] = grad_similar + grad_similar.T
    grad_embedded = logit_scale * jnp.dot(
        similar_ref[:SEQ_ROWS, :], all_rows, precision=highest, preferred_element_type=wide
    )

    grad_pooled = (
        size
        * (grad_embedded - embedded * jnp.sum(embedded * grad_embedded, axis=-1, keepdims=True))
    ).astype(low)
    grad_decoded, grad_final_gain = rms_back(
        decoded, gain["final"], back_product(grad_pooled, weight(6))
    )
    grad_second_out = grad_decoded.astype(low)
    grad_second_pre = [
        (gelu_slope(second_pre[j]) * back_product(grad_second_out, outer_weight(j))).astype(low)
        for j in range(feeds)
    ]
    if halves == 2:
        for j in range(feeds):
            halves_sent[2 + j] = second_act[j].astype(wide)
            halves_sent[2 + feeds + j] = grad_second_pre[j].astype(wide)
        half_copy(2, 2, 2 * feeds).start()
    grad_second_in = back_product(grad_second_pre[0], weight(7))
    for j in range(1, feeds):
        grad_second_in = grad_second_in + back_product(grad_second_pre[j], weight(7 + j))
    grad_second_in = joined(1, grad_second_in)
    grad_after_cross, grad_second_gain = rms_back(after_cross, gain["second"], grad_second_in)
    grad_after_cross = grad_after_cross + grad_decoded
    grad_cross_branch = grad_after_cross.astype(low)
    grad_cross_att = back_product(grad_cross_branch, weight(5)).astype(low)
    grad_cross_wide = grad_cross_att.astype(wide)
    grad_heads = jnp.concatenate(
        [
            jnp.where(
                head_mask,
                jnp.broadcast_to(grad_cross_wide[i : i + 1], (HEAD_ROWS, width)),
                0.0,
            )
            for i in range(seqs)
        ],
        axis=0,
    )
    attended_heads = jnp.concatenate(
        [
            jnp.broadcast_to(cross_attended[i : i + 1], (HEAD_ROWS, width))
            for i in range(seqs)
        ],
        axis=0,
    )
    row_terms = jnp.sum(grad_heads * attended_heads, axis=1, keepdims=True)
    value_rows = back_product(grad_heads.astype(low), weight(4)).astype(low)
    probs = jnp.where(inside, jnp.exp(scores - log_total), 0.0)
    grad_scores = (probs * (back_product(value_rows, context) - row_terms)).astype(low)
    grad_context_ref[...] = weight_grad(
        jnp.concatenate([grad_scores, probs.astype(low)], axis=0),
        jnp.concatenate([key_rows] * seqs + [value_rows], axis=0),
    )
    key_sums = product(grad_scores, context)
    sums = key_sums[:HEAD_ROWS]
    for i in range(1, seqs):
        sums = sums + key_sums[HEAD_ROWS * i : HEAD_ROWS * (i + 1)]
    first_member = jnp.where(member == 0, 1.0, 0.0)
    totals_ref[:HEAD_ROWS, :] = sums
    totals_ref[HEAD_ROWS:, :] = first_member * by_seq(
        [jnp.sum(grad_after_cross, axis=0, keepdims=True), grad_final_gain, grad_second_gain]
    )
    def put(at, values):
        for i in range(seqs):
            piece_rows[i, pl.ds(at, 1), :] = values[i : i + 1].astype(wide)

    piece_rows[...] = jnp.zeros_like(piece_rows)
    for i, piece in zip(
        (0, 1, 6, 7, 12, 13, 14),
        (
            cross_low,
            second_in,
            pooled_in,
            grad_cross_branch,
            grad_second_out,
            grad_pooled,
            grad_cross_att,
        ),
    ):
        put(i, piece)
    if halves == 2:
        half_copy(2, 2, 2 * feeds).wait()
    for first, values, got in ((2, second_act, 2), (8, grad_second_pre, 2 + feeds)):
        for j in range(feeds):
            if halves == 1:
                put(first + j, values[j])
            else:
                put(first + feeds * member + j, values[j])
                put(first + feeds * (1 - member) + j, halves_got[got + j])
    for i in range(seqs):
        piece_rows[i, HEAD_ROWS:, :] = mixed[HEAD_ROWS * i : HEAD_ROWS * (i + 1)].astype(wide)
    pieces_ref[...] = piece_rows[...].astype(low)
    for i, piece in enumerate([start, self_in, self_vals, after_self, cross_in, cross_query]):
        starts_ref[i : i + 1, :] = piece[:1].astype(wide)
    starts_ref[6:, :] = jnp.zeros((2, width), wide)


def decoder_step(context, third, base, gains, labels, place, groups, members, seqs):
    rows, width = context.shape
    everything = pl.BlockSpec(memory_space=pltpu.VMEM)
    labels = jnp.pad(labels.astype(wide)[None], ((0, 7), (0, LANES - labels.shape[0])))
    number = groups * SEQ_ROWS
    return pl.pallas_call(
        functools.partial(decoder_kernel, base, groups, members, seqs),
        name="decoder",
        in_specs=[
            pl.BlockSpec(memory_space=pltpu.SMEM),
            everything,
            pl.BlockSpec(memory_space=pl.ANY),
            everything,
            everything,
        ],
        out_specs=[everything] * 6,
        out_shape=[
            jax.ShapeDtypeStruct((SEQ_ROWS, width), wide),
            jax.ShapeDtypeStruct((8, LANES), wide),
            jax.ShapeDtypeStruct((rows, width), wide),
            jax.ShapeDtypeStruct((seqs, 2 * HEAD_ROWS, width), low),
            jax.ShapeDtypeStruct((8, width), wide),
            jax.ShapeDtypeStruct((HEAD_ROWS + SEQ_ROWS, width), wide),
        ],
        scratch_shapes=[
            pltpu.VMEM((third.shape[0], third.shape[1] - base, width), low),
            pltpu.VMEM((groups, SEQ_ROWS, width), wide),
            pltpu.VMEM((members, seqs * HEAD_ROWS, width + LANES), wide),
            pltpu.VMEM((number, number), wide),
            pltpu.VMEM((10, SEQ_ROWS, width), wide),
            pltpu.VMEM((10, SEQ_ROWS, width), wide),
            pltpu.VMEM((seqs, 2 * HEAD_ROWS, width), wide),
            pltpu.SemaphoreType.DMA((12,)),
            pltpu.SemaphoreType.DMA,
            pltpu.SemaphoreType.DMA,
            pltpu.SemaphoreType.DMA((max(members - 1, 1),)),
            pltpu.SemaphoreType.DMA((max(members - 1, 1),)),
            pltpu.SemaphoreType.DMA((3,)),
            pltpu.SemaphoreType.DMA((3,)),
        ],
        compiler_params=pltpu.CompilerParams(
            collective_id=0, has_side_effects=True, vmem_limit_bytes=56 * 2**20
        ),
        cost_estimate=pl.CostEstimate(
            flops=2 * rows * width * 300, bytes_accessed=2 * third.size, transcendentals=0
        ),
    )(place, context, third, gains, labels)


class Summing:
    def __init__(self, groups, members, buffers):
        self.groups = groups
        self.members = members
        self.lines = groups // 4
        self.group = lax.axis_index("batch")
        self.member = lax.axis_index("seq")
        self.z = self.group // 4
        self.y = lax.rem(self.group // 2, 2)
        self.core = lax.rem(self.group, 2)
        (
            self.chip,
            self.pairs,
            self.line,
            self.shares,
            self.chip_send,
            self.chip_recv,
            self.pair_send,
            self.pair_recv,
            self.line_send,
            self.line_recv,
            self.share_send,
            self.share_recv,
        ) = buffers
        self.stages = 3 + self.lines

    def batch_id(self, offset):
        return {"batch": self.group + offset}

    def neighbours(self):
        found = [
            (None, self.batch_id(1 - 2 * self.core)),
            (None, self.batch_id(2 - 4 * self.y)),
            (self.z > 0, self.batch_id(-4)),
            (self.z < self.lines - 1, self.batch_id(4)),
        ]
        for step in range(1, self.members):
            found.append((None, {"seq": lax.rem(self.member + step, self.members)}))
        return found

    def greet(self, barrier):
        for condition, device in self.neighbours():
            if condition is None:
                pl.semaphore_signal(barrier, inc=1, device_id=device, device_id_type=MESH)
            else:

                @pl.when(condition)
                def _():
                    pl.semaphore_signal(barrier, inc=1, device_id=device, device_id_type=MESH)

    def greeted(self, barrier):
        ends = (self.z > 0).astype(jnp.int32) + (self.z < self.lines - 1).astype(jnp.int32)
        pl.semaphore_wait(barrier, 2 + self.members - 1 + ends)

    def copy(self, source, target, send, recv, device):
        return pltpu.make_async_remote_copy(
            src_ref=source,
            dst_ref=target,
            send_sem=send,
            recv_sem=recv,
            device_id=device,
            device_id_type=MESH,
        )

    def chip_copy(self, chunk, source):
        return self.copy(
            source,
            self.chip.at[chunk],
            self.chip_send.at[chunk],
            self.chip_recv.at[chunk],
            self.batch_id(1 - 2 * self.core),
        )

    def pair_copy(self, chunk):
        return self.copy(
            self.chip.at[chunk, :, 1 - self.y],
            self.pairs.at[chunk],
            self.pair_send.at[chunk],
            self.pair_recv.at[chunk],
            self.batch_id(2 - 4 * self.y),
        )

    def line_copy(self, chunk, way, first, last, source):
        return self.copy(
            source.at[chunk, pl.ds(first, last - first)]
            if source is self.pairs
            else source.at[chunk, way, pl.ds(first, last - first)],
            self.line.at[chunk, way, pl.ds(first, last - first)],
            self.line_send.at[chunk, way],
            self.line_recv.at[chunk, way],
            self.batch_id(-4 if way else 4),
        )

    def share_copy(self, chunk, step):
        return self.copy(
            self.shares.at[chunk, self.member],
            self.shares.at[chunk, self.member],
            self.share_send.at[chunk, step - 1],
            self.share_recv.at[chunk, step - 1],
            {"seq": lax.rem(self.member + step, self.members)},
        )

    def start(self, chunk, source):
        self.chip_copy(chunk, source).start()

    def to_pair(self, chunk, source, own):
        self.chip_copy(chunk, source).wait()
        self.chip[chunk] = self.chip[chunk] + own
        self.pair_copy(chunk).start()

    def to_line(self, chunk, step):
        lines = self.lines
        if step == 0:
            self.pair_copy(chunk).wait()
            self.pairs[chunk] = self.pairs[chunk] + self.chip[chunk, :, self.y]
        for way in range(2):
            at = lines - 1 - step if way else step
            first, last = (0, at) if way else (at + 1, lines)

            @pl.when(self.z == at)
            def _():
                if step > 0:
                    kept = (0, at + 1) if way else (at, lines)
                    self.line_copy(chunk, way, kept[0], kept[1], self.line).wait_recv()
                    span = pl.ds(first, last - first)
                    self.line[chunk, way, span] = (
                        self.line[chunk, way, span] + self.pairs[chunk, span]
                    )
                self.line_copy(
                    chunk, way, first, last, self.line if step > 0 else self.pairs
                ).start()

    def to_members(self, chunk, held):
        lines = self.lines
        for way in range(2):
            end = 0 if way else lines - 1

            @pl.when(self.z == end)
            def _():
                kept = (0, 1) if way else (lines - 1, lines)
                self.line_copy(chunk, way, kept[0], kept[1], self.line).wait_recv()

            for step in range(lines - 1):
                at = lines - 1 - step if way else step
                first, last = (0, at) if way else (at + 1, lines)

                @pl.when(self.z == at)
                def _():
                    self.line_copy(chunk, way, first, last, self.line).wait_send()

        held[...] = self.pairs[chunk, self.z].astype(wide)

        @pl.when(self.z > 0)
        def _():
            held[...] += self.line[chunk, 0, self.z].astype(wide)

        @pl.when(self.z < lines - 1)
        def _():
            held[...] += self.line[chunk, 1, self.z].astype(wide)

        self.shares[chunk, self.member] = held[...].astype(low)
        for step in range(1, self.members):
            self.share_copy(chunk, step).start()

    def result(self, chunk):
        for step in range(1, self.members):
            self.share_copy(chunk, step).wait()
        total = self.shares[chunk, 0].astype(wide)
        for member in range(1, self.members):
            total = total + self.shares[chunk, member].astype(wide)
        return total


def summing_scratch(groups, members, chunks, rows, columns):
    lines = groups // 4
    return [
        pltpu.VMEM((chunks, lines, 2, rows, columns), low),
        pltpu.VMEM((chunks, lines, rows, columns), low),
        pltpu.VMEM((chunks, 2, lines, rows, columns), low),
        pltpu.VMEM((chunks, members, rows, columns), low),
        pltpu.SemaphoreType.DMA((chunks,)),
        pltpu.SemaphoreType.DMA((chunks,)),
        pltpu.SemaphoreType.DMA((chunks,)),
        pltpu.SemaphoreType.DMA((chunks,)),
        pltpu.SemaphoreType.DMA((chunks, 2)),
        pltpu.SemaphoreType.DMA((chunks, 2)),
        pltpu.SemaphoreType.DMA((chunks, max(members - 1, 1))),
        pltpu.SemaphoreType.DMA((chunks, max(members - 1, 1))),
    ]


def stage_delays(lines):
    return [1, 4] + [6 + 2 * step for step in range(lines - 2)] + [2 * lines + 2, 2 * lines + 6]


def feed_weights(rest_ref, out, inner, outer, sem):
    count, _, width = rest_ref.shape
    unit = width // count
    feeds = inner.shape[0]
    per = count // feeds
    copies = [pltpu.make_async_copy(rest_ref.at[:, :unit, :], out, sem.at[0])]
    for j in range(feeds):
        first = unit * (1 + j)
        copies.append(
            pltpu.make_async_copy(
                rest_ref.at[:, first : first + unit, :], inner.at[j], sem.at[1 + j]
            )
        )
    first = unit * (1 + feeds)
    for j in range(feeds):
        copies.append(
            pltpu.make_async_copy(
                rest_ref.at[per * j : per * (j + 1), first : first + feeds * unit, :],
                outer.at[j],
                sem.at[1 + feeds + j],
            )
        )
    return copies


def feed_arrival(rest_ref, inner, outer, sem, j):
    feeds = inner.shape[0]
    unit = inner.shape[2]
    pltpu.make_async_copy(rest_ref.at[:, :unit, :], inner.at[j], sem.at[1 + j]).wait()
    pltpu.make_async_copy(
        rest_ref.at[: outer.shape[1], : outer.shape[2], :], outer.at[j], sem.at[1 + feeds + j]
    ).wait()


def feed_buffers(rest, feeds):
    count, _, width = rest.shape
    unit = width // count
    return [
        pltpu.VMEM((count, unit, width), low),
        pltpu.VMEM((feeds, count, unit, width), low),
        pltpu.VMEM((feeds, count // feeds, feeds * unit, width), low),
        pltpu.SemaphoreType.DMA((1 + 2 * feeds,)),
    ]


def feed_kernel(
    attended_ref,
    tokens_ref,
    rest_ref,
    gains_ref,
    hidden_ref,
    pre_ref,
    encoded_ref,
    context_ref,
    out,
    inner,
    outer,
    sem,
    inner_in,
):
    width = tokens_ref.shape[1]
    feeds = pre_ref.shape[0]
    copies = feed_weights(rest_ref, out, inner, outer, sem)
    copies[0].start()
    for j in range(feeds):
        copies[1 + j].start()
        copies[1 + feeds + j].start()
    copies[0].wait()
    hidden = tokens_ref[...].astype(wide) + product(
        attended_ref[...].astype(low), out[...].reshape(width, width)
    )
    hidden_ref[...] = hidden
    inner_in[...] = (hidden * rms_factor(hidden) * gains_ref[1:2, :]).astype(low)
    encoded_ref[...] = hidden

    def step(j, carry):
        feed_arrival(rest_ref, inner, outer, sem, j)
        pre = product(inner_in[...], inner[j].reshape(width, width))
        pre_ref[j] = pre.astype(low)
        encoded_ref[...] += product(
            gelu_value(pre).astype(low), outer[j].reshape(width, width)
        )
        return carry

    lax.fori_loop(0, feeds, step, 0)
    encoded = encoded_ref[...]
    context_ref[...] = (encoded * rms_factor(encoded) * gains_ref[2:3, :]).astype(low)


def feed_forward(attended, tokens, rest, gains, feeds):
    rows, width = tokens.shape
    whole = pl.BlockSpec(memory_space=pltpu.VMEM)
    return pl.pallas_call(
        feed_kernel,
        name="feed_forward",
        in_specs=[whole, whole, pl.BlockSpec(memory_space=pl.ANY), whole],
        out_specs=[whole] * 4,
        out_shape=[
            jax.ShapeDtypeStruct((rows, width), wide),
            jax.ShapeDtypeStruct((feeds, rows, width), low),
            jax.ShapeDtypeStruct((rows, width), wide),
            jax.ShapeDtypeStruct((rows, width), low),
        ],
        scratch_shapes=feed_buffers(rest, feeds) + [pltpu.VMEM((rows, width), low)],
        compiler_params=pltpu.CompilerParams(vmem_limit_bytes=50 * 2**20),
        cost_estimate=pl.CostEstimate(
            flops=18 * rows * width * width, bytes_accessed=40 * width * width, transcendentals=0
        ),
    )(attended, tokens, rest, gains)


def feed_back_kernel(
    base,
    groups,
    members,
    grad_context_ref,
    encoded_ref,
    hidden_ref,
    pre_ref,
    attended_ref,
    rest_ref,
    gains_ref,
    rows_ref,
    starts_ref,
    parts_ref,
    grad_hidden_ref,
    grad_attended_ref,
    sums_ref,
    backs_ref,
    out,
    inner,
    outer,
    sem,
    inner_in,
    grad_branch,
    grad_inner_in,
    outer_grad,
    inner_grad,
    grad_sem,
    weights,
    sides,
    weight_sem,
    send_sem,
    recv_sem,
):
    rows, width = encoded_ref.shape
    feeds = pre_ref.shape[0]
    count = rest_ref.shape[0]
    unit = width // count
    lines = groups // 4
    group = lax.axis_index("batch")
    member = lax.axis_index("seq")

    partners = []
    for axis, place, number in (("batch", group, groups), ("seq", member, members)):
        span = 1
        while span < number:
            bit = lax.rem(place // span, 2)
            partners.append({axis: place + span * (1 - 2 * bit)})
            span *= 2
    barrier = pltpu.get_barrier_semaphore()
    for partner in partners:
        pl.semaphore_signal(barrier, inc=1, device_id=partner, device_id_type=MESH)

    def swap(i):
        return pltpu.make_async_remote_copy(
            src_ref=sides.at[2 * i],
            dst_ref=sides.at[2 * i + 1],
            send_sem=send_sem.at[i],
            recv_sem=recv_sem.at[i],
            device_id=partners[i],
            device_id_type=MESH,
        )

    def swapped(i):
        swap(i).wait()
        sides[2 * i + 2] = sides[2 * i] + sides[2 * i + 1]
        if i + 1 < len(partners):
            swap(i + 1).start()

    copies = feed_weights(rest_ref, out, inner, outer, sem)
    for j in range(feeds):
        copies[1 + feeds + j].start()
        copies[1 + j].start()
    copies[0].start()
    start_copies = [
        pltpu.make_async_copy(
            rest_ref.at[:, base + unit * i : base + unit * (i + 1), :],
            weights.at[i],
            weight_sem.at[i],
        )
        for i in range(4)
    ]
    for copy in start_copies:
        copy.start()
    sides[0] = rows_ref[...]
    hidden = hidden_ref[...]
    inner_in[...] = (hidden * rms_factor(hidden) * gains_ref[1:2, :]).astype(low)
    grad_encoded, _ = rms_back(encoded_ref[...], gains_ref[2:3, :], grad_context_ref[...])
    grad_hidden_ref[...] = grad_encoded
    grad_branch[...] = grad_encoded.astype(low)
    grad_inner_in[...] = jnp.zeros_like(grad_inner_in)
    pl.semaphore_wait(barrier, len(partners))
    swap(0).start()

    def outer_put(j, slot):
        per = lines // feeds
        return pltpu.make_async_copy(
            outer_grad.at[slot],
            parts_ref.at[pl.ds(j * per, per), :, :, 1 + feeds :],
            grad_sem.at[0, slot],
        )

    def inner_put(j, slot):
        return pltpu.make_async_copy(
            inner_grad.at[slot], parts_ref.at[:, :, :, 1 + j], grad_sem.at[1, slot]
        )

    def step(j, carry):
        slot = lax.rem(j, 2)
        feed_arrival(rest_ref, inner, outer, sem, j)
        pre = pre_ref[j].astype(wide)
        grad_act = back_product(grad_branch[...], outer[j].reshape(width, width))
        grad_pre = (gelu_slope(pre) * grad_act).astype(low)
        grad_inner_in[...] += back_product(grad_pre, inner[j].reshape(width, width))
        act = gelu_value(pre).astype(low)

        @pl.when(j >= 2)
        def _():
            outer_put(j - 2, slot).wait()
            inner_put(j - 2, slot).wait()

        outer_grad[slot] = (
            weight_grad(act, grad_branch[...]).reshape(outer_grad.shape[1:]).astype(low)
        )
        outer_put(j, slot).start()
        inner_grad[slot] = (
            weight_grad(inner_in[...], grad_pre).reshape(inner_grad.shape[1:]).astype(low)
        )
        inner_put(j, slot).start()
        for i in range(min(feeds, len(partners))):

            @pl.when(j == i)
            def _():
                swapped(i)

        return carry

    lax.fori_loop(0, feeds, step, 0)
    grad_hidden, _ = rms_back(hidden_ref[...], gains_ref[1:2, :], grad_inner_in[...])
    grad_hidden = grad_hidden + grad_hidden_ref[...]
    grad_hidden_ref[...] = grad_hidden
    grad_branch[...] = grad_hidden.astype(low)
    copies[0].wait()
    grad_attended_ref[...] = back_product(
        grad_branch[...], out[...].reshape(width, width)
    ).astype(low)
    for j in range(feeds - 2, feeds):
        outer_put(j, j % 2).wait()
        inner_put(j, j % 2).wait()
    inner_grad[0] = (
        weight_grad(attended_ref[...].astype(low), grad_branch[...])
        .reshape(inner_grad.shape[1:])
        .astype(low)
    )
    out_put = pltpu.make_async_copy(
        inner_grad.at[0], parts_ref.at[:, :, :, 0], grad_sem.at[1, 0]
    )
    out_put.start()

    for i in range(feeds, len(partners)):
        swapped(i)
    sums = sides[2 * len(partners)]
    sums_ref[...] = sums
    for copy in start_copies:
        copy.wait()

    def weight(i):
        return weights[i].reshape(width, width)

    head_row = lax.broadcasted_iota(jnp.int32, (HEAD_ROWS, width), 0)
    head_mask = head_row == lax.broadcasted_iota(jnp.int32, (HEAD_ROWS, width), 1) // HEAD
    spread = product(sums[:HEAD_ROWS].astype(low), weight(3))
    grad_cross_query = jnp.sum(jnp.where(head_mask, spread, 0.0), axis=0, keepdims=True)
    grad_cross_query = grad_cross_query.astype(low)

    def widened(row):
        return jnp.broadcast_to(row.astype(wide), (SEQ_ROWS, width))

    start = widened(starts_ref[0:1, :])
    after_self = widened(starts_ref[3:4, :])
    grad_rows = back_product(widened(grad_cross_query).astype(low), weight(2))
    grad_after_self, _ = rms_back(after_self, gains_ref[5:6, :], grad_rows)
    cross_gain = grad_rows * after_self * rms_factor(after_self)
    grad_after_self = grad_after_self + widened(sums[HEAD_ROWS : HEAD_ROWS + 1])
    grad_self_branch = grad_after_self.astype(low)
    grad_self_vals = back_product(grad_self_branch, weight(1)).astype(low)
    grad_rows = back_product(grad_self_vals, weight(0))
    grad_start, _ = rms_back(start, gains_ref[4:5, :], grad_rows)
    self_gain = grad_rows * start * rms_factor(start)
    for i, row in enumerate(
        (
            grad_start + grad_after_self,
            self_gain,
            cross_gain,
            grad_cross_query,
            grad_self_branch,
            grad_self_vals,
        )
    ):
        backs_ref[i : i + 1, :] = row[:1].astype(wide)
    backs_ref[6:, :] = jnp.zeros((2, width), wide)
    out_put.wait()


def feed_back(
    grad_context, encoded, hidden, pre, attended, rest, base, gains, sum_rows, starts, groups, members, part
):
    rows, width = encoded.shape
    feeds = pre.shape[0]
    lines = groups // 4
    count = rest.shape[0]
    many = sum_rows.shape[0]
    partners = (groups.bit_length() - 1) + (members.bit_length() - 1)
    whole = pl.BlockSpec(memory_space=pltpu.VMEM)
    anywhere = pl.BlockSpec(memory_space=pl.ANY)
    return pl.pallas_call(
        functools.partial(feed_back_kernel, base, groups, members),
        name="feed_back",
        in_specs=[whole] * 5 + [anywhere] + [whole] * 3,
        out_specs=[anywhere] + [whole] * 4,
        out_shape=[
            jax.ShapeDtypeStruct((lines, 2, 2, 1 + 2 * feeds, part, width), low),
            jax.ShapeDtypeStruct((rows, width), wide),
            jax.ShapeDtypeStruct((rows, width), low),
            jax.ShapeDtypeStruct((many, width), wide),
            jax.ShapeDtypeStruct((8, width), wide),
        ],
        scratch_shapes=feed_buffers(rest, feeds)
        + [
            pltpu.VMEM((rows, width), low),
            pltpu.VMEM((rows, width), low),
            pltpu.VMEM((rows, width), wide),
            pltpu.VMEM((2, lines // feeds, 2, 2, feeds, part, width), low),
            pltpu.VMEM((2, lines, 2, 2, part, width), low),
            pltpu.SemaphoreType.DMA((2, 2)),
            pltpu.VMEM((4, count, width // count, width), low),
            pltpu.VMEM((2 * partners + 1, many, width), wide),
            pltpu.SemaphoreType.DMA((4,)),
            pltpu.SemaphoreType.DMA((partners,)),
            pltpu.SemaphoreType.DMA((partners,)),
        ],
        compiler_params=pltpu.CompilerParams(
            collective_id=2, has_side_effects=True, vmem_limit_bytes=60 * 2**20
        ),
        cost_estimate=pl.CostEstimate(
            flops=36 * rows * width * width, bytes_accessed=80 * width * width, transcendentals=0
        ),
    )(
        grad_context, encoded, hidden, pre, attended, rest, gains, sum_rows, starts
    )


def attend_back_kernel(
    groups,
    members,
    place,
    q_ref,
    k_ref,
    v_ref,
    grad_ref,
    attended_ref,
    total_ref,
    near_ref,
    own_turned_ref,
    all_turned_ref,
    parts_ref,
    grad_q_ref,
    grad_k_ref,
    grad_v_ref,
    table_ref,
    out_sums_ref,
    inner_sums_ref,
    outer_sums_ref,
    query_sums_ref,
    key_sums_ref,
    value_sums_ref,
    bias,
    key_side,
    value_side,
    keys_turned,
    grad_scores,
    grad_k_sum,
    grad_v_sum,
    band_sum,
    grad_q_sum,
    pair_grads,
    fetched,
    held,
    fetch_sem,
    bands,
    kept,
    sent,
    got,
    keep_send,
    keep_recv,
    tables,
    table_send,
    table_recv,
    *buffers,
):
    pair = pl.program_id(0)
    block = pl.program_id(1)
    blocks = pl.num_programs(1)
    pairs = pl.num_programs(0)
    now = pair * blocks + block
    pack = k_ref.shape[0]
    size = q_ref.shape[0]
    middle, reach, lead, width = table_sizes(size, pack)
    ends = (place[0], place[1])
    rows_here = size * blocks
    summing = Summing(groups, members, buffers)
    first = summing.member * rows_here + block * size
    shift = lax.rem(summing.member * rows_here, LANES) if size % LANES else 0
    barrier = pltpu.get_barrier_semaphore()
    feed_chunks = 2 * parts_ref.shape[3]
    feeds = (parts_ref.shape[3] - 1) // 2
    half_width = fetched.shape[-1]
    part = fetched.shape[-2]
    lines = groups // 4
    delays = stage_delays(lines)

    def feed_part(chunk, core):
        return parts_ref.at[
            :, :, core, chunk // 2, :, pl.ds(pl.multiple_of(lax.rem(chunk, 2) * half_width, LANES), half_width)
        ]

    def fetch(chunk):
        slot = lax.rem(chunk, 4)
        return pltpu.make_async_copy(
            feed_part(chunk, summing.core), fetched.at[slot], fetch_sem.at[slot]
        )

    def feed_stage(stage, chunk):
        if stage == 0:
            summing.start(chunk, feed_part(chunk, 1 - summing.core))
            fetch(chunk).start()
        elif stage == 1:
            fetch(chunk).wait()
            summing.to_pair(
                chunk, feed_part(chunk, 1 - summing.core), fetched[lax.rem(chunk, 4)]
            )
        elif stage <= lines:
            summing.to_line(chunk, stage - 2)
        elif stage == lines + 1:
            summing.to_members(chunk, held)
        else:
            total = summing.result(chunk)
            piece = chunk // 2
            column = pl.multiple_of(lax.rem(chunk, 2) * half_width, LANES)

            @pl.when(piece == 0)
            def _():
                out_sums_ref[:, pl.ds(column, half_width)] = total

            @pl.when((piece > 0) & (piece <= feeds))
            def _():
                at = pl.multiple_of((piece - 1) * 2 * half_width + column, LANES)
                inner_sums_ref[:, pl.ds(at, half_width)] = total

            @pl.when(piece > feeds)
            def _():
                at = pl.multiple_of((piece - 1 - feeds) * part, 8)
                outer_sums_ref[pl.ds(at, part), pl.ds(column, half_width)] = total

    def pair_stage(stage, which):
        chunk = feed_chunks + which
        if stage == 0:
            summing.start(chunk, pair_grads.at[which, :, :, 1 - summing.core])
        elif stage == 1:
            summing.to_pair(
                chunk,
                pair_grads.at[which, :, :, 1 - summing.core],
                pair_grads[which, :, :, summing.core],
            )
        elif stage <= lines:
            summing.to_line(chunk, stage - 2)
        elif stage == lines + 1:
            summing.to_members(chunk, held)
        else:
            total = summing.result(chunk)
            span = pl.ds(pl.multiple_of(which * LANES, LANES), LANES)
            for i, sums_ref in enumerate((query_sums_ref, key_sums_ref, value_sums_ref)):
                sums_ref[:, span] = total[:, LANES * i : LANES * (i + 1)]

    def keep_copy(which, step):
        return summing.copy(
            sent.at[which, step - 1],
            got.at[which, step - 1],
            keep_send.at[which, step - 1],
            keep_recv.at[which, step - 1],
            {"seq": lax.rem(summing.member + step, members)},
        )

    def keep_result(which):
        total = [kept[lax.rem(which, 2), i] for i in range(2)]
        for step in range(1, members):
            keep_copy(which, step).wait()
            total = [total[i] + got[which, step - 1, i].astype(wide) for i in range(2)]
        span = pl.ds(pl.multiple_of(which * LANES, LANES), LANES)
        grad_k_ref[:, span] = total[0].astype(low)
        grad_v_ref[:, span] = total[1].astype(low)

    partners = []
    for axis, spot, number in (
        ("batch", summing.group, groups),
        ("seq", summing.member, members),
    ):
        reach_out = 1
        while reach_out < number:
            bit = lax.rem(spot // reach_out, 2)
            partners.append({axis: spot + reach_out * (1 - 2 * bit)})
            reach_out *= 2

    def swap(i):
        return summing.copy(
            tables.at[2 * i],
            tables.at[2 * i + 1],
            table_send.at[i],
            table_recv.at[i],
            partners[i],
        )

    def swapped(i):
        swap(i).wait()
        tables[2 * i + 2] = tables[2 * i] + tables[2 * i + 1]
        if i + 1 < len(partners):
            swap(i + 1).start()

    @pl.when(now == 0)
    def _():
        peers = summing.neighbours()
        for i in range(len(partners)):
            peers.append((None, partners[i]))
        for condition, device in peers:
            if condition is None:
                pl.semaphore_signal(barrier, inc=1, device_id=device, device_id_type=MESH)
            else:

                @pl.when(condition)
                def _():
                    pl.semaphore_signal(barrier, inc=1, device_id=device, device_id_type=MESH)

        edges = (summing.z > 0).astype(jnp.int32) + (summing.z < lines - 1).astype(jnp.int32)
        pl.semaphore_wait(barrier, 2 + members - 1 + edges + len(partners))

    stages = 3 + lines
    starts = [0] + delays
    total_steps = pairs * blocks

    def run_stages(step):
        for stage in reversed(range(stages)):
            chunk = step - starts[stage]

            @pl.when((chunk >= 0) & (chunk < feed_chunks))
            def _():
                feed_stage(stage, chunk)

            late = step - (blocks - 1) - starts[stage]

            @pl.when((late >= 0) & (lax.rem(late + 64 * blocks, blocks) == 0) & (late < total_steps))
            def _():
                pair_stage(stage, late // blocks)

    @pl.when(now == 0)
    def _():
        tables[0] = jnp.zeros_like(tables[0])
        bands[...] = jnp.zeros_like(bands)

    @pl.when(block == 0)
    def _():
        places = lax.broadcasted_iota(jnp.int32, (pack, LANES), 0)
        lane = lax.broadcasted_iota(jnp.int32, (pack, LANES), 1)
        key_side[:, :LANES] = k_ref[...]
        ones = (segment_of(places, ends) == lane) | ((lane >= 3) & (lane < 9))
        key_side[:, LANES:] = ones.astype(wide).astype(low)
        value_side[:, :LANES] = v_ref[...]
        value_side[:, LANES:] = (lane < 6).astype(wide).astype(low)
        keys_turned[...] = k_ref[...].T
        for half in range(2):
            row = near_ref[half]
            before = middle - LANES
            after = middle + reach
            bias[half, before:after, :] = turned_biases(row, size, lead).T.astype(low)
            if before > 0:
                bias[half, :before, :] = jnp.broadcast_to(row[:, :1], (before, size)).astype(low)
            if after < width:
                bias[half, after:, :] = jnp.broadcast_to(
                    row[:, -1:], (width - after, size)
                ).astype(low)
        grad_scores[...] = jnp.zeros_like(grad_scores)
        grad_k_sum[...] = jnp.zeros_like(grad_k_sum)
        grad_v_sum[...] = jnp.zeros_like(grad_v_sum)
        band_sum[...] = jnp.zeros_like(band_sum)

    lane = lax.broadcasted_iota(jnp.int32, (size, LANES), 1)
    rows = first + lax.broadcasted_iota(jnp.int32, (size, LANES), 0)
    apart = jnp.where((segment_of(rows, ends) != lane) & (lane < 3), -far_apart, 0.0)
    start = pl.multiple_of(middle - (first - shift), LANES)
    near_rows = pl.ds(pl.multiple_of(first - shift, LANES), LANES + reach)
    queries = q_ref[...]
    grads = grad_ref[...]
    products = grads.astype(wide) * attended_ref[...]
    totals = total_ref[...]

    def in_parts(column, at):
        head = column.astype(low).astype(wide)
        body = (column - head).astype(low).astype(wide)
        tail = column - head - body
        return jnp.where(
            lane == at,
            head,
            jnp.where(lane == at + 1, body, jnp.where(lane == at + 2, tail, 0.0)),
        )

    query_grads = []
    for half in range(2):
        mine = (lane >= HEAD) if half else (lane < HEAD)
        row_term = jnp.sum(jnp.where(mine, products, 0.0), axis=1, keepdims=True)
        row_total = jnp.sum(
            jnp.where(lane == 2 * pair + half, totals, 0.0), axis=1, keepdims=True
        )
        query_part = jnp.where(mine, queries, jnp.zeros_like(queries))
        grad_part = jnp.where(mine, grads, jnp.zeros_like(grads))
        query_side = jnp.concatenate(
            [query_part, (apart - in_parts(row_total, 3 + 3 * half)).astype(low)], axis=1
        )
        grad_side = jnp.concatenate(
            [grad_part, (-in_parts(row_term, 3 * half)).astype(low)], axis=1
        )
        weights = jnp.exp(
            back_product(key_side[...], query_side)
            + bias[half, pl.ds(start, pack), :].astype(wide)
        )
        grad_block = (weights * back_product(value_side[...], grad_side)).astype(low)
        grad_scores[LANES : LANES + pack, :] = grad_block
        grad_v_sum[...] += product(weights.astype(low), grad_part)
        block_lane = jnp.where(lane == 8 * half + block, 1.0, 0.0).astype(low)
        grad_k_sum[...] += product(
            grad_block, jnp.concatenate([query_part, block_lane], axis=1)
        )
        query_grads.append(product(keys_turned[HEAD * half : HEAD * (half + 1), :], grad_block))
        band_sum[half] += grad_scores[near_rows, :].astype(wide)
    grad_query = jnp.concatenate(query_grads, axis=0).T.astype(low)
    grad_q_ref[...] = grad_query
    grad_q_sum[pl.ds(pl.multiple_of(block * size, 64), size), :] = grad_query

    @pl.when(block == blocks - 1)
    def _():
        grad_key = grad_k_sum[:, :LANES].astype(low)
        grad_value = grad_v_sum[...].astype(low)

        @pl.when(pair > 0)
        def _():
            keep_result(pair - 1)

        for step in range(1, members):
            other = pl.multiple_of(lax.rem(summing.member + step, members) * rows_here, 64)
            sent[pair, step - 1, 0] = grad_k_sum[pl.ds(other, rows_here), :LANES].astype(low)
            sent[pair, step - 1, 1] = grad_v_sum[pl.ds(other, rows_here), :].astype(low)
            keep_copy(pair, step).start()
        mine_rows = pl.ds(pl.multiple_of(summing.member * rows_here, 64), rows_here)
        kept[lax.rem(pair, 2), 0] = grad_k_sum[mine_rows, :LANES]
        kept[lax.rem(pair, 2), 1] = grad_v_sum[mine_rows, :]
        for i, gradient in enumerate(
            (
                product(own_turned_ref[...], grad_q_sum[...]),
                product(all_turned_ref[...], grad_key),
                product(all_turned_ref[...], grad_value),
            )
        ):
            pair_grads[pair, :, :, :, :, LANES * i : LANES * (i + 1)] = gradient.reshape(
                lines, 2, 2, part, LANES
            ).astype(low)
        key = lax.broadcasted_iota(jnp.int32, (pack, LANES), 0)
        which = lax.broadcasted_iota(jnp.int32, (pack, LANES), 1) % 8
        begin = summing.member * rows_here - shift + size * which
        sums = grad_k_sum[:, LANES:]
        below = jnp.sum(jnp.where(key < begin - LANES, sums, 0.0), axis=0, keepdims=True)
        above = jnp.sum(jnp.where(key >= begin + reach, sums, 0.0), axis=0, keepdims=True)
        columns = bands.shape[1]
        mirror = (
            lax.broadcasted_iota(jnp.int32, (size, size), 0)
            + lax.broadcasted_iota(jnp.int32, (size, size), 1)
            == size - 1
        ).astype(wide).astype(low)
        row_lane = lax.broadcasted_iota(jnp.int32, (1, LANES), 1)
        for half in range(2):
            rest = band_sum[half]
            flipped = jnp.zeros_like(rest)
            for _ in range(3):
                head_part = rest.astype(low)
                flipped = flipped + product(head_part, mirror)
                rest = rest - head_part.astype(wide)
            padded = jnp.concatenate(
                [flipped, jnp.zeros((rest.shape[0], columns - size), wide)], axis=1
            )
            turned = pltpu.roll(padded, 0, 1, stride=1, stride_axis=0)
            head = pl.ds(2 * pair + half, 1)
            bands[head, :] = jnp.sum(turned, axis=0, keepdims=True)
            own_lanes = row_lane // 8 == half
            low_sum = jnp.sum(jnp.where(own_lanes, below, 0.0), axis=1, keepdims=True)
            high_sum = jnp.sum(jnp.where(own_lanes, above, 0.0), axis=1, keepdims=True)
            tables[0, head, :] = jnp.where(row_lane == 15, low_sum, 0.0) + jnp.where(
                row_lane == 31, high_sum, 0.0
            )

    run_stages(now)

    @pl.when(now == total_steps - 1)
    def _():
        columns = bands.shape[1]
        offset = (
            lax.broadcasted_iota(jnp.int32, (columns, LANES), 0) - (size - 1) - LANES - shift
        )
        onehot = (
            bucket_of(offset) == lax.broadcasted_iota(jnp.int32, (columns, LANES), 1)
        ).astype(wide)
        tables[0] += jnp.dot(
            bands[...], onehot, precision=highest, preferred_element_type=wide
        )
        swap(0).start()

        def drain(step, carry):
            run_stages(step)
            for i in range(len(partners)):

                @pl.when(step == total_steps + i)
                def _():
                    swapped(i)

            return carry

        final = max(starts[-1] + 1, len(partners))
        lax.fori_loop(total_steps, total_steps + final, drain, 0)
        keep_result(pairs - 1)
        table_ref[...] = tables[2 * len(partners)]


def attend_back(
    queries, all_keys, all_values, grads, attended, totals, near, place, own_turned, all_turned, parts
):
    rows, width = queries.shape
    pack = all_keys.shape[0]
    size = block_rows(rows)
    _, reach, _, columns = table_sizes(size, pack)
    band = -(-(size + LANES + reach) // LANES) * LANES
    pairs = width // LANES
    members = pack // rows
    pieces = parts.shape[3]
    part = parts.shape[4]
    groups = 4 * parts.shape[0]
    half_width = width // 2
    chunks = 2 * pieces + pairs

    def own(p, i):
        return (i, p)

    def every(p, i):
        return (0, p)

    whole = pl.BlockSpec(memory_space=pltpu.VMEM)
    partners = (groups.bit_length() - 1) + (members.bit_length() - 1)
    feeds = (pieces - 1) // 2
    return pl.pallas_call(
        functools.partial(attend_back_kernel, groups, members),
        name="attend_back",
        grid=(pairs, rows // size),
        in_specs=[
            pl.BlockSpec(memory_space=pltpu.SMEM),
            pl.BlockSpec((size, LANES), own),
            pl.BlockSpec((pack, LANES), every),
            pl.BlockSpec((pack, LANES), every),
            pl.BlockSpec((size, LANES), own),
            pl.BlockSpec((size, LANES), own),
            pl.BlockSpec((size, LANES), lambda p, i: (i, 0)),
            pl.BlockSpec((2, 1, near.shape[2]), lambda p, i: (p, 0, 0)),
            whole,
            whole,
            pl.BlockSpec(memory_space=pl.ANY),
        ],
        out_specs=[
            pl.BlockSpec((size, LANES), own),
        ]
        + [whole] * 9,
        out_shape=[
            jax.ShapeDtypeStruct((rows, width), low),
            jax.ShapeDtypeStruct((rows, width), low),
            jax.ShapeDtypeStruct((rows, width), low),
            jax.ShapeDtypeStruct((16, LANES), wide),
            jax.ShapeDtypeStruct((part, width), wide),
            jax.ShapeDtypeStruct((part, feeds * width), wide),
            jax.ShapeDtypeStruct((feeds * part, width), wide),
            jax.ShapeDtypeStruct((part, width), wide),
            jax.ShapeDtypeStruct((part, width), wide),
            jax.ShapeDtypeStruct((part, width), wide),
        ],
        scratch_shapes=[
            pltpu.VMEM((2, columns, size), low),
            pltpu.VMEM((pack, 2 * LANES), low),
            pltpu.VMEM((pack, 2 * LANES), low),
            pltpu.VMEM((LANES, pack), low),
            pltpu.VMEM((LANES + pack + reach, size), low),
            pltpu.VMEM((pack, 2 * LANES), wide),
            pltpu.VMEM((pack, LANES), wide),
            pltpu.VMEM((2, LANES + reach, size), wide),
            pltpu.VMEM((rows, LANES), low),
            pltpu.VMEM((pairs, groups // 4, 2, 2, part, half_width), low),
            pltpu.VMEM((4, groups // 4, 2, part, half_width), low),
            pltpu.VMEM((part, half_width), wide),
            pltpu.SemaphoreType.DMA((4,)),
            pltpu.VMEM((16, band), wide),
            pltpu.VMEM((2, 2, rows, LANES), wide),
            pltpu.VMEM((pairs, max(members - 1, 1), 2, rows, LANES), low),
            pltpu.VMEM((pairs, max(members - 1, 1), 2, rows, LANES), low),
            pltpu.SemaphoreType.DMA((pairs, max(members - 1, 1))),
            pltpu.SemaphoreType.DMA((pairs, max(members - 1, 1))),
            pltpu.VMEM((2 * partners + 1, 16, LANES), wide),
            pltpu.SemaphoreType.DMA((partners,)),
            pltpu.SemaphoreType.DMA((partners,)),
        ]
        + summing_scratch(groups, members, chunks, part, half_width),
        compiler_params=pltpu.CompilerParams(
            collective_id=1, has_side_effects=True, vmem_limit_bytes=62 * 2**20
        ),
        cost_estimate=pl.CostEstimate(
            flops=20 * rows * pack * width * 2, bytes_accessed=16 * pack * width, transcendentals=0
        ),
    )(
        place,
        queries,
        all_keys,
        all_values,
        grads,
        attended,
        totals,
        near,
        own_turned,
        all_turned,
        parts,
    )


def last_kernel(
    groups,
    seqs,
    halves,
    grad_q_any,
    grad_k_any,
    grad_v_any,
    first_any,
    grad_hidden_any,
    rows_any,
    tokens_ref,
    gains_ref,
    sums_ref,
    starts_ref,
    backs_ref,
    query_ref,
    key_ref,
    value_ref,
    inner_ref,
    cross_key_ref,
    cross_value_ref,
    query_sums_ref,
    key_sums_ref,
    value_sums_ref,
    inner_sums_ref,
    out_sums_ref,
    outer_sums_ref,
    grad_tokens_ref,
    vectors_ref,
    grad_self_value_ref,
    grad_self_out_ref,
    grad_cross_query_ref,
    grad_cross_key_ref,
    grad_cross_value_ref,
    grad_cross_out_ref,
    grad_second_inner_ref,
    grad_second_outer_ref,
    grad_pooler_ref,
    query_out,
    key_out,
    value_out,
    inner_out,
    attention_out,
    outer_out,
    pieces,
    grad_q_ref,
    grad_k_ref,
    grad_v_ref,
    first_ref,
    grad_hidden_ref,
    rows_ref,
    copy_sem,
):
    rows, width = tokens_ref.shape
    part = query_ref.shape[0]
    feeds = inner_ref.shape[1] // width
    number = groups * seqs
    every = 2 * HEAD_ROWS
    group = lax.axis_index("batch")
    copies = [
        pltpu.make_async_copy(source, target, copy_sem.at[i])
        for i, (source, target) in enumerate(
            (
                (rows_any, rows_ref),
                (grad_q_any, grad_q_ref),
                (grad_k_any, grad_k_ref),
                (grad_v_any, grad_v_ref),
                (first_any, first_ref),
                (grad_hidden_any, grad_hidden_ref),
            )
        )
    ]
    for copy in copies:
        copy.start()
    for source, target in (
        (query_sums_ref, query_out),
        (key_sums_ref, key_out),
        (value_sums_ref, value_out),
        (inner_sums_ref, inner_out),
        (out_sums_ref, attention_out),
        (outer_sums_ref, outer_out),
    ):
        target[...] = source[...]
    copies[0].wait()

    def chooser(count, first):
        row = lax.broadcasted_iota(jnp.int32, (count, width), 0)
        column = lax.broadcasted_iota(jnp.int32, (count, width), 1)
        return column == first + row

    chosen = chooser(part, group * part)
    choose = chosen.astype(wide).astype(low)
    tiles = width // LANES
    for i in range(tiles):
        pieces[i] = (
            rows_ref[:, :, LANES * i : LANES * (i + 1)].reshape(number * every, LANES).astype(wide)
        )

    def piece(at):
        return jnp.concatenate(
            [pieces[i, pl.ds(at, number, stride=every), :] for i in range(tiles)], axis=1
        ).astype(low)

    def own(values, which=None):
        which = choose if which is None else which
        return lax.dot_general(
            which, values, (((1,), (1,)), ((), ())), preferred_element_type=wide
        ).astype(low)

    def pair(left, right):
        return product(left, right)

    grad_cross_out_ref[...] = pair(own(piece(0)), piece(7))
    second_in = own(piece(1))
    grad_second_inner = [pair(second_in, piece(8 + j)) for j in range(feeds)]
    share = grad_second_outer_ref.shape[0]
    half = share // halves
    per = width // half
    grad_out = piece(12)
    for i in range(halves):
        chunk = group // per
        at = lax.rem(group, per) * half
        which = chooser(half, at).astype(wide).astype(low)
        found = jnp.zeros((half, number), wide)
        for j in range(feeds // halves):
            here = own(piece(2 + feeds // halves * i + j), which).astype(wide)
            found = jnp.where(chunk == j, here, found)
        grad_second_outer_ref[half * i : half * (i + 1), :] = pair(found.astype(low), grad_out)
    for j in range(feeds):
        grad_second_inner_ref[:, width * j : width * (j + 1)] = grad_second_inner[j]
    grad_pooler_ref[...] = pair(own(piece(6)), piece(13))

    mixed = rows_ref[:, HEAD_ROWS:, :].reshape(number * HEAD_ROWS, width)
    repeat = (
        lax.broadcasted_iota(jnp.int32, (number * HEAD_ROWS, number), 0) // HEAD_ROWS
        == lax.broadcasted_iota(jnp.int32, (number * HEAD_ROWS, number), 1)
    )
    heads = product(repeat.astype(wide).astype(low), piece(14))
    head = lax.broadcasted_iota(jnp.int32, heads.shape, 0) % HEAD_ROWS
    head_column = lax.broadcasted_iota(jnp.int32, heads.shape, 1) // HEAD
    heads = jnp.where(head == head_column, heads, 0.0).astype(low)
    grad_cross_value = pair(own(mixed), heads)
    grad_cross_value_ref[...] = grad_cross_value

    def exact(left, right):
        return lax.dot_general(
            left,
            right,
            (((1,), (1,)), ((), ())),
            precision=highest,
            preferred_element_type=wide,
        )

    chosen = chosen.astype(wide)
    key_rows = exact(chosen, sums_ref[:HEAD_ROWS, :])
    head_row = lax.broadcasted_iota(jnp.int32, (HEAD_ROWS, width), 0)
    head_mask = head_row == lax.broadcasted_iota(jnp.int32, (HEAD_ROWS, width), 1) // HEAD
    query_row = starts_ref[5:6, :].astype(low).astype(wide)
    query_heads = jnp.where(head_mask, jnp.broadcast_to(query_row, (HEAD_ROWS, width)), 0.0)
    grad_cross_key = jnp.dot(
        key_rows, query_heads, precision=highest, preferred_element_type=wide
    )
    grad_cross_key_ref[...] = grad_cross_key
    starts = exact(chosen, starts_ref[...])
    grad_self_value_ref[...] = starts[:, 1:2] * backs_ref[5:6, :]
    grad_self_out_ref[...] = starts[:, 2:3] * backs_ref[4:5, :]
    grad_cross_query_ref[...] = starts[:, 4:5] * backs_ref[3:4, :]

    def gain_sum(weight, grads):
        ones = jnp.ones((8, grads.shape[1]), wide)
        return exact(ones, weight.astype(wide) * grads)[:1]

    attention = (
        gain_sum(query_ref[...], query_sums_ref[...])
        + gain_sum(key_ref[...], key_sums_ref[...])
        + gain_sum(value_ref[...], value_sums_ref[...])
    )
    feed = gain_sum(inner_ref[...], inner_sums_ref[...])
    encoder = gain_sum(cross_key_ref[...], grad_cross_key) + gain_sum(
        cross_value_ref[...], grad_cross_value
    )
    gains = exact(gains_ref[:8, :], chosen)
    backs = exact(backs_ref[...], chosen)
    others = exact(sums_ref[HEAD_ROWS:, :], chosen)
    for i, row in enumerate(
        (
            attention / gains[0:1],
            feed / gains[1:2],
            encoder / gains[2:3],
            backs[0:1],
            backs[1:2],
            backs[2:3],
            others[2:3],
            others[1:2],
        )
    ):
        vectors_ref[i] = row

    for copy in copies[1:]:
        copy.wait()
    grad_normed = (
        back_product(grad_q_ref[...], first_ref[0])
        + back_product(grad_k_ref[...], first_ref[1])
        + back_product(grad_v_ref[...], first_ref[2])
    )
    grad_tokens, _ = rms_back(tokens_ref[...].astype(wide), gains_ref[:1, :], grad_normed)
    grad_tokens_ref[...] = grad_tokens + grad_hidden_ref[...]


def last_step(groups, seqs, halves, tokens, part, share, feeds, *arrays):
    rows, width = tokens.shape
    whole = pl.BlockSpec(memory_space=pltpu.VMEM)
    square = jax.ShapeDtypeStruct((part, width), wide)
    return pl.pallas_call(
        functools.partial(last_kernel, groups, seqs, halves),
        name="last",
        in_specs=[pl.BlockSpec(memory_space=pltpu.HBM)] * 6 + [whole] * (len(arrays) - 6),
        out_specs=[whole] * 17,
        out_shape=[
            jax.ShapeDtypeStruct((rows, width), wide),
            jax.ShapeDtypeStruct((8, 1, part), wide),
            square,
            square,
            square,
            square,
            square,
            square,
            jax.ShapeDtypeStruct((part, feeds * width), wide),
            jax.ShapeDtypeStruct((share, width), wide),
            square,
            square,
            square,
            square,
            jax.ShapeDtypeStruct((part, feeds * width), wide),
            square,
            jax.ShapeDtypeStruct((share, width), wide),
        ],
        scratch_shapes=[
            pltpu.VMEM((width // LANES, groups * seqs * 2 * HEAD_ROWS, LANES), wide),
            pltpu.VMEM((rows, width), low),
            pltpu.VMEM((rows, width), low),
            pltpu.VMEM((rows, width), low),
            pltpu.VMEM((3, width, width), low),
            pltpu.VMEM((rows, width), wide),
            pltpu.VMEM((groups * seqs, 2 * HEAD_ROWS, width), low),
            pltpu.SemaphoreType.DMA((6,)),
        ],
        compiler_params=pltpu.CompilerParams(vmem_limit_bytes=50 * 2**20),
    )(*arrays)


def in_blocks(gathered, sizes):
    count, _, width = gathered.shape
    join = 16 // math.gcd(16, sizes[0])
    if join == 1:
        return gathered
    pieces, at = [], 0
    for size in sizes:
        piece = gathered[:, at : at + size].reshape(count // join, join * size, width)
        pieces.append(piece)
        at += size
    return jnp.concatenate(pieces, axis=1)


def column_blocks(weight, model_width):
    rows, columns = weight.shape
    blocks = columns // model_width
    return jnp.transpose(weight.reshape(rows, blocks, model_width), (1, 0, 2)).reshape(
        blocks * rows, model_width
    )


def shards(
    tokens,
    lengths,
    labels,
    attention_gain,
    query_weight,
    key_weight,
    value_weight,
    attention_out,
    position_bias,
    feed_gain,
    feed_inner,
    feed_outer,
    encoder_gain,
    start_token,
    self_gain,
    self_value,
    self_out,
    cross_gain,
    cross_query,
    cross_key,
    cross_value,
    cross_out,
    second_gain,
    second_inner,
    second_outer,
    final_gain,
    pooler_weight,
):
    rows, width = tokens.shape
    part = query_weight.shape[0]
    share = feed_outer.shape[0]
    groups = lax.axis_size("batch")
    members = lax.axis_size("seq")
    blocks = feed_inner.shape[1] // width
    pack = rows * members
    seqs = lengths.shape[1]
    group = lax.axis_index("batch")
    member = lax.axis_index("seq")
    own_first = member * rows
    ends = jnp.cumsum(lengths[0])
    place = jnp.stack(
        [ends[0], ends[1], own_first, own_first % LANES]
    ).astype(jnp.int32)

    vectors = jnp.stack(
        [
            attention_gain,
            feed_gain,
            encoder_gain,
            start_token,
            self_gain,
            cross_gain,
            second_gain,
            final_gain,
        ],
        axis=0,
    )
    bias_part = position_bias.reshape(1, -1)
    bias_size = bias_part.shape[1]
    extra = jnp.zeros((16, width), low)
    extra = lax.dynamic_update_slice(extra, vectors, (0, group * part))
    extra = lax.dynamic_update_slice(extra, bias_part, (8, group * bias_size))
    queries, all_keys, all_values, normed_all, gains, first_full = project(
        tokens, extra, [query_weight, key_weight, value_weight], groups, members
    )
    table = gains[8, : BUCKETS * HEADS].reshape(BUCKETS, HEADS).astype(low)
    second_part = jnp.concatenate(
        [
            attention_out[None],
            column_blocks(feed_inner, width).reshape(blocks, part, width),
            feed_outer.reshape(blocks, part, width),
        ],
        axis=0,
    )
    halves = 2 if members == 2 else 1
    half_share = share // halves
    half_inner = lax.dynamic_slice_in_dim(
        second_inner.reshape(part, groups, share), member % halves * half_share, half_share, 2
    ).reshape(part, groups * half_share)
    half_outer = lax.dynamic_slice_in_dim(second_outer, member % halves * half_share, half_share)
    rest_part = jnp.concatenate(
        [
            second_part.reshape(-1, width),
            self_value,
            self_out,
            cross_query,
            cross_key,
            cross_value,
            cross_out,
            pooler_weight,
            column_blocks(half_inner, width),
            half_outer,
        ],
        axis=0,
    )
    rest = lax.all_gather(rest_part, "batch", axis=0, tiled=False)

    near = offset_biases(table, block_rows(rows), pack, place[3])
    attended, totals = attend(queries, all_keys, all_values, near, place)
    rest_blocks = in_blocks(
        rest,
        [part] * (1 + blocks) + [share] + [part] * (7 + blocks // halves) + [half_share],
    )
    base = (1 + 2 * blocks) * (width // rest_blocks.shape[0])
    hidden, inner_pre, encoded, context = feed_forward(
        attended, tokens, rest_blocks, gains, blocks
    )

    embedded, loss, grad_context, decoder_rows, starts, decoder_totals = decoder_step(
        context, rest_blocks, base, gains, labels, place, groups, members, seqs
    )
    contrastive_loss = loss[0, :1]
    embedded = embedded[:seqs]
    decoder_rows = lax.all_gather(
        decoder_rows.reshape(seqs * 2 * HEAD_ROWS, width), "batch", axis=0, tiled=False
    )

    second_grads, grad_hidden, grad_attended, sums, backs = feed_back(
        grad_context,
        encoded,
        hidden,
        inner_pre,
        attended,
        rest_blocks,
        base,
        gains,
        decoder_totals,
        starts,
        groups,
        members,
        part,
    )
    normed = lax.dynamic_slice_in_dim(normed_all, own_first, rows)
    (
        grad_query_rows,
        grad_key_rows,
        grad_value_rows,
        table_sums,
        out_sums,
        inner_sums,
        outer_sums,
        query_sums,
        key_sums,
        value_sums,
    ) = attend_back(
        queries,
        all_keys,
        all_values,
        grad_attended,
        attended,
        totals,
        near,
        place,
        normed.T,
        normed_all.T,
        second_grads,
    )
    (
        grad_tokens,
        vectors,
        grad_self_value,
        grad_self_out,
        grad_cross_query,
        grad_cross_key,
        grad_cross_value,
        grad_cross_out,
        grad_second_inner,
        grad_second_outer,
        grad_pooler,
        query_sums,
        key_sums,
        value_sums,
        inner_sums,
        out_sums,
        outer_sums,
    ) = last_step(
        groups,
        seqs,
        halves,
        tokens,
        part,
        share,
        blocks,
        grad_query_rows,
        grad_key_rows,
        grad_value_rows,
        first_full,
        grad_hidden,
        decoder_rows.reshape(groups * seqs, 2 * HEAD_ROWS, width),
        tokens,
        gains,
        sums,
        starts,
        backs,
        query_weight,
        key_weight,
        value_weight,
        feed_inner,
        cross_key,
        cross_value,
        query_sums,
        key_sums,
        value_sums,
        inner_sums,
        out_sums,
        outer_sums,
    )
    half_share = share // halves
    grad_second_inner = jnp.transpose(
        grad_second_inner.reshape(part, halves, groups, half_share), (0, 2, 1, 3)
    ).reshape(part, blocks * width)
    vectors = vectors.reshape(8, part)
    own_buckets = BUCKETS // groups
    grad_table = lax.dynamic_slice_in_dim(table_sums, group * own_buckets, own_buckets, 1)[:HEADS].T
    return (
        contrastive_loss,
        embedded,
        grad_tokens,
        vectors[0],
        query_sums,
        key_sums,
        value_sums,
        out_sums,
        grad_table,
        vectors[1],
        inner_sums,
        outer_sums,
        vectors[2],
        vectors[3],
        vectors[4],
        grad_self_value,
        grad_self_out,
        vectors[5],
        grad_cross_query,
        grad_cross_key,
        grad_cross_value,
        grad_cross_out,
        vectors[6],
        grad_second_inner,
        grad_second_outer,
        vectors[7],
        grad_pooler,
    )


def solution(mesh):
    placed = (
        P(("batch", "seq"), None),
        P("batch", None),
        P(),
        P("batch"),
        P("batch", None),
        P("batch", None),
        P("batch", None),
        P("batch", None),
        P("batch", None),
        P("batch"),
        P("batch", None),
        P("batch", None),
        P("batch"),
        P("batch"),
        P("batch"),
        P("batch", None),
        P("batch", None),
        P("batch"),
        P("batch", None),
        P("batch", None),
        P("batch", None),
        P("batch", None),
        P("batch"),
        P("batch", None),
        P("batch", None),
        P("batch"),
        P("batch", None),
    )
    return jax.shard_map(
        shards,
        mesh=mesh,
        in_specs=placed,
        out_specs=(
            P(),
            P("batch", None),
            P(("batch", "seq"), None),
            P("batch"),
            P("batch", None),
            P("batch", None),
            P("batch", None),
            P("batch", None),
            P("batch", None),
            P("batch"),
            P("batch", None),
            P("batch", None),
            P("batch"),
            P("batch"),
            P("batch"),
            P("batch", None),
            P("batch", None),
            P("batch"),
            P("batch", None),
            P("batch", None),
            P("batch", None),
            P("batch", None),
            P("batch"),
            P("batch", None),
            P("batch", None),
            P("batch"),
            P("batch", None),
        ),
        check_vma=False,
    )
```

```python
import functools
import math

import jax
import jax.numpy as jnp
from jax import lax
from jax.experimental import pallas as pl
from jax.experimental.pallas import tpu as pltpu
from jax.sharding import PartitionSpec as P

HEADS = 12
HEAD = 64
BUCKETS = 32
LANES = 128
far_apart = float(2**30)

eps_norm = 1e-06
masked_score = -1000000000.0
logit_scale = 20.0
bucket_limits = (12, 16, 23, 32, 46, 64, 91)
highest = lax.Precision.HIGHEST
low = jnp.bfloat16
wide = jnp.float32
MESH = pl.DeviceIdType.MESH


def rms_factor(values):
    return lax.rsqrt(jnp.mean(values * values, axis=-1, keepdims=True) + eps_norm)


def rms_norm(values, gain_vector):
    return (
        values
        * lax.rsqrt(jnp.mean(values * values, axis=-1, keepdims=True) + eps_norm)
        * gain_vector
    )


def unit_length(values):
    return values * lax.rsqrt(jnp.sum(values * values, axis=-1, keepdims=True) + eps_norm)


def bucket_of(offsets):
    upper_half = jnp.where(offsets > 0, 16, 0).astype(jnp.int32)
    distance = jnp.abs(offsets)
    far_bucket = 8 + sum(((distance >= threshold).astype(jnp.int32) for threshold in bucket_limits))
    return upper_half + jnp.where(distance < 8, distance, far_bucket)


def product(left_side, right_side):
    return jnp.dot(left_side, right_side, preferred_element_type=wide)


def back_product(left_side, right_side):
    return lax.dot_general(
        left_side, right_side, (((1,), (1,)), ((), ())), preferred_element_type=wide
    )


def weight_grad(left_side, right_side):
    return lax.dot_general(
        left_side, right_side, (((0,), (0,)), ((), ())), preferred_element_type=wide
    )


def norm_back(values, gain_vector, grad_rows):
    _, pullback = jax.vjp(rms_norm, values, gain_vector)
    return pullback(grad_rows)


def gelu_back(values, grad_rows):
    _, pullback = jax.vjp(jax.nn.gelu, values)
    return pullback(grad_rows)[0]


def segment_of(places, ends):
    return (places >= ends[0]).astype(jnp.int32) + (places >= ends[1]).astype(jnp.int32)


def block_rows(rows):
    return 256 if rows % 256 == 0 else rows


def table_sizes(size, pack):
    slack = LANES if size % LANES else 0
    reach = -(-(size + slack + 91) // LANES) * LANES
    lead = -(-(size + slack) // LANES) * LANES
    middle = -(-(pack - size) // LANES) * LANES
    return middle, reach, lead, middle + max(pack, reach)


def offset_biases(table, size, pack, shift):
    _, reach, lead, _ = table_sizes(size, pack)
    offsets = jnp.arange(lead + reach + LANES, dtype=jnp.int32) - (lead + LANES) - shift
    onehot = (
        bucket_of(offsets)[None, :] == jnp.arange(BUCKETS, dtype=jnp.int32)[:, None]
    ).astype(low)
    return weight_grad(table, onehot)[:, None, :]


def turned_biases(row, size, lead):
    spread = jnp.broadcast_to(row, (size, row.shape[1]))
    return pltpu.roll(spread, 0, 1, stride=1, stride_axis=0)[:, lead:]


class Gathering:
    def __init__(self, groups, members, sems):
        self.groups = groups
        self.members = members
        self.lines = groups // 4
        self.group = lax.axis_index("batch")
        self.member = lax.axis_index("seq")
        self.z = self.group // 4
        self.y = lax.rem(self.group // 2, 2)
        self.core = lax.rem(self.group, 2)
        self.line_send, self.line_recv, self.pair_sems, self.chip_sems, self.share_sems = sems

    def batch_id(self, offset):
        return {"batch": self.group + offset}

    def neighbours(self):
        found = [
            (None, self.batch_id(1 - 2 * self.core)),
            (None, self.batch_id(2 - 4 * self.y)),
            (self.z > 0, self.batch_id(-4)),
            (self.z < self.lines - 1, self.batch_id(4)),
        ]
        for step in range(1, self.members):
            found.append((None, {"seq": lax.rem(self.member + step, self.members)}))
        return found

    def greet(self, barrier):
        for condition, device in self.neighbours():
            if condition is None:
                pl.semaphore_signal(barrier, inc=1, device_id=device, device_id_type=MESH)
            else:

                @pl.when(condition)
                def _():
                    pl.semaphore_signal(barrier, inc=1, device_id=device, device_id_type=MESH)

    def greeted(self, barrier):
        ends = (self.z > 0).astype(jnp.int32) + (self.z < self.lines - 1).astype(jnp.int32)
        pl.semaphore_wait(barrier, 2 + self.members - 1 + ends)

    def copy(self, source, target, send, recv, device):
        return pltpu.make_async_remote_copy(
            src_ref=source,
            dst_ref=target,
            send_sem=send,
            recv_sem=recv,
            device_id=device,
            device_id_type=MESH,
        )

    def line_copy(self, item, source, full, way, step):
        place = self.z + step if way else self.z - step
        block = full.at[place, self.y, self.core]
        return self.copy(
            source if step == 0 else block,
            block,
            self.line_send.at[item, way, step],
            self.line_recv.at[item, way, step],
            self.batch_id(-4 if way else 4),
        )

    def line_sends(self, way, step):
        if way:
            return (self.z > 0) & (self.z + step < self.lines)
        return (self.z < self.lines - 1) & (self.z - step >= 0)

    def line_arrives(self, way, step):
        return self.z + step < self.lines if way else self.z - step >= 0

    def send_line(self, item, source, full, step):
        for way in range(2):

            @pl.when(self.line_sends(way, step))
            def _():
                self.line_copy(item, source, full, way, step).start()

    def pair_copy(self, item, full):
        span = full.at[:, self.y, self.core]
        return self.copy(
            span,
            span,
            self.pair_sems.at[item, 0],
            self.pair_sems.at[item, 1],
            self.batch_id(2 - 4 * self.y),
        )

    def share_copy(self, item, full):
        span = full.at[:, :, self.core]
        return self.copy(
            span,
            span,
            self.share_sems.at[item, 0],
            self.share_sems.at[item, 1],
            {"seq": 1 - self.member},
        )

    def chip_copy(self, item, which, full):
        span = full.at[:, :, self.core]
        return self.copy(
            span,
            span,
            self.chip_sems.at[item, which, 0],
            self.chip_sems.at[item, which, 1],
            self.batch_id(1 - 2 * self.core),
        )

    def stages(self, split):
        return self.lines + (3 if split else 2)

    def stage(self, number, item, source, full, other=None):
        lines = self.lines
        if number == 0:
            own = pltpu.make_async_copy(
                source, full.at[self.z, self.y, self.core], self.chip_sems.at[item, 0, 0]
            )
            own.start()
            self.send_line(item, source, full, 0)
            own.wait()
        elif number < lines:
            for way in range(2):

                @pl.when(self.line_arrives(way, number))
                def _():
                    self.line_copy(item, source, full, way, number - 1).wait_recv()

            if number < lines - 1:
                self.send_line(item, source, full, number)
            else:
                self.pair_copy(item, full).start()
        elif number == lines:
            self.pair_copy(item, full).wait()
            if other is not None:
                self.share_copy(item, full).start()
            self.chip_copy(item, 0, full).start()
        elif number == lines + 1 and other is not None:
            self.share_copy(item, full).wait()
            self.chip_copy(item, 1, other).start()
        else:
            self.chip_copy(item, 0, full).wait()
            if other is not None:
                self.chip_copy(item, 1, other).wait()
            for way in range(2):
                for step in range(lines - 1):

                    @pl.when(self.line_sends(way, step))
                    def _():
                        self.line_copy(item, source, full, way, step).wait_send()


def gathering_sems(groups, items):
    lines = groups // 4
    return [
        pltpu.SemaphoreType.DMA((items, 2, lines)),
        pltpu.SemaphoreType.DMA((items, 2, lines)),
        pltpu.SemaphoreType.DMA((items, 2)),
        pltpu.SemaphoreType.DMA((items, 2, 2)),
        pltpu.SemaphoreType.DMA((items, 2)),
    ]


def joined_rows(blocks):
    size, width = blocks.shape[-2:]
    rows = size * math.prod(blocks.shape[:-2])
    if size % 16:
        return blocks.astype(wide).reshape(rows, width).astype(low)
    return blocks.reshape(rows, width)


def first_kernel(
    groups,
    members,
    tokens_ref,
    extra_ref,
    query_ref,
    key_ref,
    value_ref,
    queries_ref,
    keys_ref,
    values_ref,
    normed_ref,
    gains_ref,
    weights_ref,
    all_tokens,
    all_extra,
    all_query,
    all_key,
    all_value,
    token_send,
    token_recv,
    *sems,
):
    parts = (extra_ref, query_ref, key_ref, value_ref)
    fulls = (all_extra, all_query, all_key, all_value)
    gathering = Gathering(groups, members, sems)
    member = gathering.member
    rows, width = tokens_ref.shape
    barrier = pltpu.get_barrier_semaphore()
    gathering.greet(barrier)
    gathering.greeted(barrier)
    copies = []
    for step in range(1, members):
        copies.append(
            pltpu.make_async_remote_copy(
                src_ref=tokens_ref,
                dst_ref=all_tokens.at[member],
                send_sem=token_send.at[step - 1],
                recv_sem=token_recv.at[step - 1],
                device_id={"seq": lax.rem(member + step, members)},
                device_id_type=MESH,
            )
        )
        copies[-1].start()
    all_tokens[member] = tokens_ref[...]

    def normed(values):
        values = values.astype(wide)
        return (values * rms_factor(values) * gains_ref[:1, :]).astype(low)

    def finished(item):
        if item == 0:
            total = jnp.zeros((16, width), wide)
            for z in range(groups // 4):
                for y in range(2):
                    for core in range(2):
                        total = total + all_extra[z, y, core].astype(wide)
            gains_ref[...] = total
        elif item == 1:
            weights_ref[0] = joined_rows(all_query[...])
            queries_ref[...] = product(normed(tokens_ref[...]), weights_ref[0]).astype(low)
        elif item == 2:
            for copy in copies:
                copy.wait()
            weights_ref[1] = joined_rows(all_key[...])
            for part in range(members):
                span = slice(rows * part, rows * (part + 1))
                normed_ref[span, :] = normed(all_tokens[part])
                keys_ref[span, :] = product(normed_ref[span, :], weights_ref[1]).astype(low)
        else:
            weights_ref[2] = joined_rows(all_value[...])
            for part in range(members):
                span = slice(rows * part, rows * (part + 1))
                values_ref[span, :] = product(normed_ref[span, :], weights_ref[2]).astype(low)

    stages = gathering.stages(False)
    for step in range(len(parts) + stages - 1):
        for stage in reversed(range(stages)):
            if 0 <= step - stage < len(parts):
                item = step - stage
                gathering.stage(stage, item, parts[item], fulls[item])
        if step - (stages - 1) >= 0:
            finished(step - (stages - 1))


def project(tokens, extra, parts, groups, members):
    rows, width = tokens.shape
    whole = pl.BlockSpec(memory_space=pltpu.VMEM)
    lines = groups // 4
    items = [extra] + list(parts)
    pack = members * rows
    return pl.pallas_call(
        functools.partial(first_kernel, groups, members),
        name="project",
        in_specs=[whole] * 5,
        out_specs=[whole] * 6,
        out_shape=[
            jax.ShapeDtypeStruct((rows, width), low),
            jax.ShapeDtypeStruct((pack, width), low),
            jax.ShapeDtypeStruct((pack, width), low),
            jax.ShapeDtypeStruct((pack, width), low),
            jax.ShapeDtypeStruct((16, width), wide),
            jax.ShapeDtypeStruct((3, width, width), low),
        ],
        scratch_shapes=[pltpu.VMEM((members,) + tokens.shape, low)]
        + [pltpu.VMEM((lines, 2, 2) + item.shape, low) for item in items]
        + [
            pltpu.SemaphoreType.DMA((max(members - 1, 1),)),
            pltpu.SemaphoreType.DMA((max(members - 1, 1),)),
        ]
        + gathering_sems(groups, len(items)),
        compiler_params=pltpu.CompilerParams(
            collective_id=3, has_side_effects=True, vmem_limit_bytes=48 * 2**20
        ),
        cost_estimate=pl.CostEstimate(
            flops=2**31, bytes_accessed=32 * pack * width, transcendentals=0
        ),
    )(tokens, extra, *parts)


FAR_LANE = 3


def key_lanes(places, lane, ends, near, begins, reach):
    blocks = len(begins)
    values = jnp.where((segment_of(places, ends) == lane) & (lane < 3), 1.0, 0.0)
    for half in range(2):
        row = near[half]
        for i, begin in enumerate(begins):
            far = jnp.where(
                places < begin - LANES,
                row[:, :1],
                jnp.where(places >= begin + reach, row[:, -1:], 0.0),
            )
            values = jnp.where(lane == FAR_LANE + half * blocks + i, far, values)
    return values.astype(low)


def attend_kernel(
    place, q_ref, k_ref, v_ref, near_ref, attended_ref, total_ref, key_side, value_side, scores_ref
):
    pair = pl.program_id(0)
    pack = k_ref.shape[0]
    rows = q_ref.shape[0]
    size = block_rows(rows)
    blocks = rows // size
    _, reach, lead, _ = table_sizes(size, pack)
    ends = (place[0], place[1])
    shift = place[3]
    begins = [place[2] - shift + size * i for i in range(blocks)]
    near = [near_ref[half] for half in range(2)]
    places = lax.broadcasted_iota(jnp.int32, (pack, LANES), 0)
    lane = lax.broadcasted_iota(jnp.int32, (pack, LANES), 1)
    key_side[:, :LANES] = k_ref[...]
    key_side[:, LANES:] = key_lanes(places, lane, ends, near, begins, reach)
    value_side[:, :LANES] = v_ref[...]
    value_side[:, LANES:] = jnp.ones((pack, LANES), low)

    lane = lax.broadcasted_iota(jnp.int32, (rows, LANES), 1)
    row = lax.broadcasted_iota(jnp.int32, (rows, LANES), 0)
    apart = jnp.where(
        (segment_of(place[2] + row, ends) != lane) & (lane < 3), -far_apart, 0.0
    )
    queries = q_ref[...]
    outputs = []
    totals = total_ref[...]
    for half in range(2):
        mine = (lane >= HEAD) if half else (lane < HEAD)
        side = jnp.where(lane == FAR_LANE + half * blocks + row // size, 1.0, apart).astype(low)
        query_side = jnp.concatenate(
            [jnp.where(mine, queries, jnp.zeros_like(queries)), side], axis=1
        )
        scores_ref[half, :, LANES : LANES + pack] = back_product(query_side, key_side[...])
        band = turned_biases(near[half], size, lead)
        for i in range(blocks):
            span = slice(size * i, size * (i + 1))
            columns = pl.ds(pl.multiple_of(begins[i], LANES), LANES + reach)
            scores_ref[half, span, columns] += band
        scores = scores_ref[half, :, LANES : LANES + pack]
        top = jnp.max(scores, axis=1, keepdims=True)
        weights = jnp.exp(scores - top).astype(low)
        output = product(weights, value_side[...])
        total = output[:, LANES:]
        outputs.append(output[:, :LANES] / total)
        totals = jnp.where(lane == 2 * pair + half, top + jnp.log(total), totals)
    attended_ref[...] = jnp.where(lane < HEAD, outputs[0], outputs[1])
    total_ref[...] = totals


def attend(queries, all_keys, all_values, near, place):
    rows, width = queries.shape
    pack = all_keys.shape[0]
    size = block_rows(rows)
    _, reach, _, _ = table_sizes(size, pack)
    pairs = width // LANES
    return pl.pallas_call(
        attend_kernel,
        name="attend",
        grid=(pairs,),
        in_specs=[
            pl.BlockSpec(memory_space=pltpu.SMEM),
            pl.BlockSpec((rows, LANES), lambda p: (0, p)),
            pl.BlockSpec((pack, LANES), lambda p: (0, p)),
            pl.BlockSpec((pack, LANES), lambda p: (0, p)),
            pl.BlockSpec((2, 1, near.shape[2]), lambda p: (p, 0, 0)),
        ],
        out_specs=[
            pl.BlockSpec((rows, LANES), lambda p: (0, p)),
            pl.BlockSpec((rows, LANES), lambda p: (0, 0)),
        ],
        out_shape=[
            jax.ShapeDtypeStruct((rows, width), wide),
            jax.ShapeDtypeStruct((rows, LANES), wide),
        ],
        scratch_shapes=[
            pltpu.VMEM((pack, 2 * LANES), low),
            pltpu.VMEM((pack, 2 * LANES), low),
            pltpu.VMEM((2, rows, LANES + pack + reach), wide),
        ],
        compiler_params=pltpu.CompilerParams(vmem_limit_bytes=56 * 2**20),
        cost_estimate=pl.CostEstimate(
            flops=8 * rows * pack * width * 2, bytes_accessed=16 * pack * width, transcendentals=0
        ),
    )(place, queries, all_keys, all_values, near)


SEQ_ROWS = 8
HEAD_ROWS = 16


def rms_back(values, gain_row, grad_rows):
    factor = rms_factor(values)
    scaled = gain_row * grad_rows
    inner = jnp.mean(scaled * values, axis=-1, keepdims=True)
    return (
        factor * scaled - values * (factor * factor * factor) * inner,
        jnp.sum(grad_rows * values * factor, axis=0, keepdims=True),
    )


gelu_scale = 0.7978845608028654


def gelu_value(values):
    return 0.5 * values * (
        1.0 + jnp.tanh(gelu_scale * (values + 0.044715 * values * values * values))
    )


def gelu_slope(values):
    square = values * values
    bent = jnp.tanh(gelu_scale * (values + 0.044715 * square * values))
    return 0.5 * (1.0 + bent) + 0.5 * values * (1.0 - bent * bent) * gelu_scale * (
        1.0 + 0.134145 * square
    )


def decoder_kernel(
    base,
    groups,
    members,
    seqs,
    place,
    context_ref,
    third_ref,
    gains_ref,
    target_ref,
    embedded_ref,
    loss_ref,
    grad_context_ref,
    pieces_ref,
    starts_ref,
    totals_ref,
    weights,
    everyone,
    unpacked,
    shared,
    similar_ref,
    halves_sent,
    halves_got,
    piece_rows,
    weight_sem,
    every_send,
    every_recv,
    share_send,
    share_recv,
    half_send,
    half_recv,
):
    rows, width = context_ref.shape
    count, _, _ = third_ref.shape
    unit = width // count
    halves = 2 if members == 2 else 1
    feeds = 4 // halves
    blocks = feeds * unit
    group = lax.axis_index("batch")
    member = lax.axis_index("seq")
    seq_total = groups * seqs

    barrier = pltpu.get_barrier_semaphore()
    for step in range(1, groups):
        pl.semaphore_signal(
            barrier,
            inc=1,
            device_id={"batch": lax.rem(group + step, groups)},
            device_id_type=MESH,
        )
    for step in range(1, members):
        pl.semaphore_signal(
            barrier,
            inc=1,
            device_id={"seq": lax.rem(member + step, members)},
            device_id_type=MESH,
        )

    sizes = [unit] * 7 + [unit] * feeds + [blocks]
    firsts = [sum(sizes[:i]) for i in range(len(sizes))]
    copies = [
        pltpu.make_async_copy(
            third_ref.at[:, base + first : base + first + size, :],
            weights.at[:, first : first + size, :],
            weight_sem.at[i],
        )
        for i, (first, size) in enumerate(zip(firsts, sizes))
    ]
    for copy in copies:
        copy.start()

    def weight(i):
        return weights[:, firsts[i] : firsts[i] + unit, :].reshape(width, width)

    def outer_weight(j):
        per = count // feeds
        return weights[per * j : per * (j + 1), firsts[-1] : firsts[-1] + blocks, :].reshape(
            width, width
        )

    def half_copy(which, first, number):
        span = pl.ds(first, number)
        return pltpu.make_async_remote_copy(
            src_ref=halves_sent.at[span],
            dst_ref=halves_got.at[span],
            send_sem=half_send.at[which],
            recv_sem=half_recv.at[which],
            device_id={"seq": 1 - member},
            device_id_type=MESH,
        )

    def joined(which, part):
        if halves == 1:
            return part
        halves_sent[which] = part
        copy = half_copy(which, which, 1)
        copy.start()
        copy.wait()
        return part + halves_got[which]

    gain = {
        name: gains_ref[i : i + 1, :]
        for i, name in enumerate(
            ("attention", "feed", "encoder", "start", "own", "cross", "second", "final")
        )
    }
    context = context_ref[...]

    start = jnp.broadcast_to(gain["start"], (SEQ_ROWS, width))
    self_in = (start * rms_factor(start) * gain["own"]).astype(low)
    copies[0].wait()
    self_vals = product(self_in, weight(0)).astype(low)
    copies[1].wait()
    after_self = start + product(self_vals, weight(1))
    cross_in = (after_self * rms_factor(after_self) * gain["cross"]).astype(low)
    copies[2].wait()
    cross_query = product(cross_in, weight(2))
    head_row = lax.broadcasted_iota(jnp.int32, (HEAD_ROWS, width), 0)
    head_mask = head_row == lax.broadcasted_iota(jnp.int32, (HEAD_ROWS, width), 1) // HEAD
    query_heads = jnp.where(
        head_mask, jnp.broadcast_to(cross_query[:1], (HEAD_ROWS, width)), 0.0
    ).astype(low)
    copies[3].wait()
    key_rows = back_product(query_heads, weight(3)).astype(low)

    many = seqs * HEAD_ROWS
    scores = back_product(key_rows, context)
    scores = jnp.concatenate([scores] * seqs, axis=0)
    places = member * rows + lax.broadcasted_iota(jnp.int32, (many, rows), 1)
    row_seq = lax.broadcasted_iota(jnp.int32, (many, rows), 0) // HEAD_ROWS
    inside = segment_of(places, (place[0], place[1])) == row_seq
    scores = jnp.where(inside, scores, masked_score)
    part_top = jnp.max(scores, axis=1, keepdims=True)
    part_weights = jnp.where(inside, jnp.exp(scores - part_top), 0.0).astype(low)
    part_total = jnp.sum(part_weights.astype(wide), axis=1, keepdims=True)
    lane = lax.broadcasted_iota(jnp.int32, (many, LANES), 1)
    shared[0, :, :width] = product(part_weights, context)
    shared[0, :, width:] = jnp.where(lane == 0, part_top, part_total)

    pl.semaphore_wait(barrier, groups - 1 + members - 1)
    for step in range(1, members):
        pltpu.make_async_remote_copy(
            src_ref=shared.at[0],
            dst_ref=shared.at[step],
            send_sem=share_send.at[step - 1],
            recv_sem=share_recv.at[step - 1],
            device_id={"seq": lax.rem(member + step, members)},
            device_id_type=MESH,
        ).start()
    for step in range(1, members):
        pltpu.make_async_remote_copy(
            src_ref=shared.at[0],
            dst_ref=shared.at[step],
            send_sem=share_send.at[step - 1],
            recv_sem=share_recv.at[step - 1],
            device_id={"seq": lax.rem(member + step, members)},
            device_id_type=MESH,
        ).wait()
    top = shared[0, :, width : width + 1]
    for step in range(1, members):
        top = jnp.maximum(top, shared[step, :, width : width + 1])
    total = jnp.zeros((many, 1), wide)
    mixed = jnp.zeros((many, width), wide)
    for step in range(members):
        scale = jnp.exp(shared[step, :, width : width + 1] - top)
        total = total + shared[step, :, width + 1 : width + 2] * scale
        mixed = mixed + shared[step, :, :width] * scale
    mixed = (mixed / total).astype(low)
    log_total = top + jnp.log(total)

    def by_seq(parts):
        row = lax.broadcasted_iota(jnp.int32, (SEQ_ROWS, width), 0)
        joined = jnp.zeros((SEQ_ROWS, width), wide)
        for i, part in enumerate(parts):
            joined = jnp.where(row == i, part, joined)
        return joined

    copies[4].wait()
    spread = product(mixed, weight(4))
    cross_attended = by_seq(
        [
            jnp.sum(
                jnp.where(head_mask, spread[HEAD_ROWS * i : HEAD_ROWS * (i + 1)], 0.0),
                axis=0,
                keepdims=True,
            )
            for i in range(seqs)
        ]
    )
    cross_low = cross_attended.astype(low)
    copies[5].wait()
    after_cross = after_self + product(cross_low, weight(5))
    second_in = (after_cross * rms_factor(after_cross) * gain["second"]).astype(low)
    for copy in copies[7:]:
        copy.wait()
    second_pre = [product(second_in, weight(7 + j)) for j in range(feeds)]
    second_act = [gelu_value(second_pre[j]).astype(low) for j in range(feeds)]
    second_out = product(second_act[0], outer_weight(0))
    for j in range(1, feeds):
        second_out = second_out + product(second_act[j], outer_weight(j))
    decoded = after_cross + joined(0, second_out)
    pooled_in = (decoded * rms_factor(decoded) * gain["final"]).astype(low)
    copies[6].wait()
    pooled = product(pooled_in, weight(6))
    size = lax.rsqrt(jnp.sum(pooled * pooled, axis=-1, keepdims=True) + eps_norm)
    embedded = pooled * size
    embedded_ref[...] = embedded

    tiles = width // LANES
    for i in range(tiles):
        everyone[0, 4 * i : 4 * (i + 1), :] = embedded[:4, LANES * i : LANES * (i + 1)]
    sends = []
    for step in range(1, groups):
        sends.append(
            pltpu.make_async_remote_copy(
                src_ref=everyone.at[0],
                dst_ref=everyone.at[step],
                send_sem=every_send,
                recv_sem=every_recv,
                device_id={"batch": lax.rem(group + step, groups)},
                device_id_type=MESH,
            )
        )
        sends[-1].start()
    arrival = pltpu.make_async_remote_copy(
        src_ref=everyone.at[pl.ds(1, groups - 1)],
        dst_ref=everyone.at[pl.ds(1, groups - 1)],
        send_sem=every_send,
        recv_sem=every_recv,
        device_id={"batch": lax.rem(group + 1, groups)},
        device_id_type=MESH,
    )
    arrival.wait_recv()
    arrival.wait_send()
    unpacked[...] = jnp.zeros_like(unpacked)
    for i in range(tiles):
        unpacked[:, :4, LANES * i : LANES * (i + 1)] = everyone[:, 4 * i : 4 * (i + 1), :]
    all_rows = unpacked[...].reshape(groups * SEQ_ROWS, width)
    number = groups * SEQ_ROWS
    row = lax.broadcasted_iota(jnp.int32, (number, number), 0)
    column = lax.broadcasted_iota(jnp.int32, (number, number), 1)
    row_valid = row % SEQ_ROWS < seqs
    valid = row_valid & (column % SEQ_ROWS < seqs)
    similar = logit_scale * lax.dot_general(
        all_rows,
        all_rows,
        (((1,), (1,)), ((), ())),
        precision=highest,
        preferred_element_type=wide,
    )
    similar = jnp.where(valid & (row != column), similar, masked_score)
    best = jnp.max(similar, axis=1, keepdims=True)
    log_norm = best + jnp.log(jnp.sum(jnp.exp(similar - best), axis=1, keepdims=True))
    row_group = lax.rem(group - row // SEQ_ROWS + groups, groups)
    column_group = lax.rem(group - column // SEQ_ROWS + groups, groups)
    row_number = row_group * seqs + row % SEQ_ROWS
    column_number = column_group * seqs + column % SEQ_ROWS
    label = jnp.max(
        jnp.where(
            lax.broadcasted_iota(jnp.int32, (number, target_ref.shape[1]), 1)
            == row_number[:, : target_ref.shape[1]],
            target_ref[:1, :],
            -1.0,
        ),
        axis=1,
        keepdims=True,
    )
    target = (column_number.astype(wide) == label) & valid
    picked = jnp.sum(jnp.where(target, similar, 0.0), axis=1, keepdims=True)
    losses = jnp.where(row_valid[:, :1], log_norm - picked, 0.0)
    loss_ref[...] = jnp.broadcast_to(
        jnp.sum(losses, axis=0, keepdims=True) / seq_total, loss_ref.shape
    )
    grad_similar = jnp.where(
        valid, (jnp.exp(similar - log_norm) - target.astype(wide)) / seq_total, 0.0
    )
    similar_ref[...] = grad_similar + grad_similar.T
    grad_embedded = logit_scale * jnp.dot(
        similar_ref[:SEQ_ROWS, :], all_rows, precision=highest, preferred_element_type=wide
    )

    grad_pooled = (
        size
        * (grad_embedded - embedded * jnp.sum(embedded * grad_embedded, axis=-1, keepdims=True))
    ).astype(low)
    grad_decoded, grad_final_gain = rms_back(
        decoded, gain["final"], back_product(grad_pooled, weight(6))
    )
    grad_second_out = grad_decoded.astype(low)
    grad_second_pre = [
        (gelu_slope(second_pre[j]) * back_product(grad_second_out, outer_weight(j))).astype(low)
        for j in range(feeds)
    ]
    if halves == 2:
        for j in range(feeds):
            halves_sent[2 + j] = second_act[j].astype(wide)
            halves_sent[2 + feeds + j] = grad_second_pre[j].astype(wide)
        half_copy(2, 2, 2 * feeds).start()
    grad_second_in = back_product(grad_second_pre[0], weight(7))
    for j in range(1, feeds):
        grad_second_in = grad_second_in + back_product(grad_second_pre[j], weight(7 + j))
    grad_second_in = joined(1, grad_second_in)
    grad_after_cross, grad_second_gain = rms_back(after_cross, gain["second"], grad_second_in)
    grad_after_cross = grad_after_cross + grad_decoded
    grad_cross_branch = grad_after_cross.astype(low)
    grad_cross_att = back_product(grad_cross_branch, weight(5)).astype(low)
    grad_cross_wide = grad_cross_att.astype(wide)
    grad_heads = jnp.concatenate(
        [
            jnp.where(
                head_mask,
                jnp.broadcast_to(grad_cross_wide[i : i + 1], (HEAD_ROWS, width)),
                0.0,
            )
            for i in range(seqs)
        ],
        axis=0,
    )
    attended_heads = jnp.concatenate(
        [
            jnp.broadcast_to(cross_attended[i : i + 1], (HEAD_ROWS, width))
            for i in range(seqs)
        ],
        axis=0,
    )
    row_terms = jnp.sum(grad_heads * attended_heads, axis=1, keepdims=True)
    value_rows = back_product(grad_heads.astype(low), weight(4)).astype(low)
    probs = jnp.where(inside, jnp.exp(scores - log_total), 0.0)
    grad_scores = (probs * (back_product(value_rows, context) - row_terms)).astype(low)
    grad_context_ref[...] = weight_grad(
        jnp.concatenate([grad_scores, probs.astype(low)], axis=0),
        jnp.concatenate([key_rows] * seqs + [value_rows], axis=0),
    )
    key_sums = product(grad_scores, context)
    sums = key_sums[:HEAD_ROWS]
    for i in range(1, seqs):
        sums = sums + key_sums[HEAD_ROWS * i : HEAD_ROWS * (i + 1)]
    first_member = jnp.where(member == 0, 1.0, 0.0)
    totals_ref[:HEAD_ROWS, :] = sums
    totals_ref[HEAD_ROWS:, :] = first_member * by_seq(
        [jnp.sum(grad_after_cross, axis=0, keepdims=True), grad_final_gain, grad_second_gain]
    )
    def put(at, values):
        for i in range(seqs):
            piece_rows[i, pl.ds(at, 1), :] = values[i : i + 1].astype(wide)

    piece_rows[...] = jnp.zeros_like(piece_rows)
    for i, piece in zip(
        (0, 1, 6, 7, 12, 13, 14),
        (
            cross_low,
            second_in,
            pooled_in,
            grad_cross_branch,
            grad_second_out,
            grad_pooled,
            grad_cross_att,
        ),
    ):
        put(i, piece)
    if halves == 2:
        half_copy(2, 2, 2 * feeds).wait()
    for first, values, got in ((2, second_act, 2), (8, grad_second_pre, 2 + feeds)):
        for j in range(feeds):
            if halves == 1:
                put(first + j, values[j])
            else:
                put(first + feeds * member + j, values[j])
                put(first + feeds * (1 - member) + j, halves_got[got + j])
    for i in range(seqs):
        piece_rows[i, HEAD_ROWS:, :] = mixed[HEAD_ROWS * i : HEAD_ROWS * (i + 1)].astype(wide)
    pieces_ref[...] = piece_rows[...].astype(low)
    for i, piece in enumerate([start, self_in, self_vals, after_self, cross_in, cross_query]):
        starts_ref[i : i + 1, :] = piece[:1].astype(wide)
    starts_ref[6:, :] = jnp.zeros((2, width), wide)


def decoder_step(context, third, base, gains, labels, place, groups, members, seqs):
    rows, width = context.shape
    everything = pl.BlockSpec(memory_space=pltpu.VMEM)
    labels = jnp.pad(labels.astype(wide)[None], ((0, 7), (0, LANES - labels.shape[0])))
    number = groups * SEQ_ROWS
    return pl.pallas_call(
        functools.partial(decoder_kernel, base, groups, members, seqs),
        name="decoder",
        in_specs=[
            pl.BlockSpec(memory_space=pltpu.SMEM),
            everything,
            pl.BlockSpec(memory_space=pl.ANY),
            everything,
            everything,
        ],
        out_specs=[everything] * 6,
        out_shape=[
            jax.ShapeDtypeStruct((SEQ_ROWS, width), wide),
            jax.ShapeDtypeStruct((8, LANES), wide),
            jax.ShapeDtypeStruct((rows, width), wide),
            jax.ShapeDtypeStruct((seqs, 2 * HEAD_ROWS, width), low),
            jax.ShapeDtypeStruct((8, width), wide),
            jax.ShapeDtypeStruct((HEAD_ROWS + SEQ_ROWS, width), wide),
        ],
        scratch_shapes=[
            pltpu.VMEM((third.shape[0], third.shape[1] - base, width), low),
            pltpu.VMEM((groups, 4 * width // LANES, LANES), wide),
            pltpu.VMEM((groups, SEQ_ROWS, width), wide),
            pltpu.VMEM((members, seqs * HEAD_ROWS, width + LANES), wide),
            pltpu.VMEM((number, number), wide),
            pltpu.VMEM((10, SEQ_ROWS, width), wide),
            pltpu.VMEM((10, SEQ_ROWS, width), wide),
            pltpu.VMEM((seqs, 2 * HEAD_ROWS, width), wide),
            pltpu.SemaphoreType.DMA((12,)),
            pltpu.SemaphoreType.DMA,
            pltpu.SemaphoreType.DMA,
            pltpu.SemaphoreType.DMA((max(members - 1, 1),)),
            pltpu.SemaphoreType.DMA((max(members - 1, 1),)),
            pltpu.SemaphoreType.DMA((3,)),
            pltpu.SemaphoreType.DMA((3,)),
        ],
        compiler_params=pltpu.CompilerParams(
            collective_id=0, has_side_effects=True, vmem_limit_bytes=56 * 2**20
        ),
        cost_estimate=pl.CostEstimate(
            flops=2 * rows * width * 300, bytes_accessed=2 * third.size, transcendentals=0
        ),
    )(place, context, third, gains, labels)


class Summing:
    def __init__(self, groups, members, buffers):
        self.groups = groups
        self.members = members
        self.lines = groups // 4
        self.group = lax.axis_index("batch")
        self.member = lax.axis_index("seq")
        self.z = self.group // 4
        self.y = lax.rem(self.group // 2, 2)
        self.core = lax.rem(self.group, 2)
        (
            self.chip,
            self.pairs,
            self.line,
            self.shares,
            self.chip_send,
            self.chip_recv,
            self.pair_send,
            self.pair_recv,
            self.line_send,
            self.line_recv,
            self.share_send,
            self.share_recv,
        ) = buffers
        self.stages = 3 + self.lines

    def batch_id(self, offset):
        return {"batch": self.group + offset}

    def neighbours(self):
        found = [
            (None, self.batch_id(1 - 2 * self.core)),
            (None, self.batch_id(2 - 4 * self.y)),
            (self.z > 0, self.batch_id(-4)),
            (self.z < self.lines - 1, self.batch_id(4)),
        ]
        for step in range(1, self.members):
            found.append((None, {"seq": lax.rem(self.member + step, self.members)}))
        return found

    def greet(self, barrier):
        for condition, device in self.neighbours():
            if condition is None:
                pl.semaphore_signal(barrier, inc=1, device_id=device, device_id_type=MESH)
            else:

                @pl.when(condition)
                def _():
                    pl.semaphore_signal(barrier, inc=1, device_id=device, device_id_type=MESH)

    def greeted(self, barrier):
        ends = (self.z > 0).astype(jnp.int32) + (self.z < self.lines - 1).astype(jnp.int32)
        pl.semaphore_wait(barrier, 2 + self.members - 1 + ends)

    def copy(self, source, target, send, recv, device):
        return pltpu.make_async_remote_copy(
            src_ref=source,
            dst_ref=target,
            send_sem=send,
            recv_sem=recv,
            device_id=device,
            device_id_type=MESH,
        )

    def chip_copy(self, chunk, source):
        return self.copy(
            source,
            self.chip.at[chunk],
            self.chip_send.at[chunk],
            self.chip_recv.at[chunk],
            self.batch_id(1 - 2 * self.core),
        )

    def pair_copy(self, chunk):
        return self.copy(
            self.chip.at[chunk, :, 1 - self.y],
            self.pairs.at[chunk],
            self.pair_send.at[chunk],
            self.pair_recv.at[chunk],
            self.batch_id(2 - 4 * self.y),
        )

    def line_copy(self, chunk, way, first, last, source):
        return self.copy(
            source.at[chunk, pl.ds(first, last - first)]
            if source is self.pairs
            else source.at[chunk, way, pl.ds(first, last - first)],
            self.line.at[chunk, way, pl.ds(first, last - first)],
            self.line_send.at[chunk, way],
            self.line_recv.at[chunk, way],
            self.batch_id(-4 if way else 4),
        )

    def share_copy(self, chunk, step):
        return self.copy(
            self.shares.at[chunk, self.member],
            self.shares.at[chunk, self.member],
            self.share_send.at[chunk, step - 1],
            self.share_recv.at[chunk, step - 1],
            {"seq": lax.rem(self.member + step, self.members)},
        )

    def start(self, chunk, source):
        self.chip_copy(chunk, source).start()

    def to_pair(self, chunk, source, own):
        self.chip_copy(chunk, source).wait()
        self.chip[chunk] = self.chip[chunk] + own
        self.pair_copy(chunk).start()

    def to_line(self, chunk, step):
        lines = self.lines
        if step == 0:
            self.pair_copy(chunk).wait()
            self.pairs[chunk] = self.pairs[chunk] + self.chip[chunk, :, self.y]
        for way in range(2):
            at = lines - 1 - step if way else step
            first, last = (0, at) if way else (at + 1, lines)

            @pl.when(self.z == at)
            def _():
                if step > 0:
                    kept = (0, at + 1) if way else (at, lines)
                    self.line_copy(chunk, way, kept[0], kept[1], self.line).wait_recv()
                    span = pl.ds(first, last - first)
                    self.line[chunk, way, span] = (
                        self.line[chunk, way, span] + self.pairs[chunk, span]
                    )
                self.line_copy(
                    chunk, way, first, last, self.line if step > 0 else self.pairs
                ).start()

    def to_members(self, chunk, held):
        lines = self.lines
        for way in range(2):
            end = 0 if way else lines - 1

            @pl.when(self.z == end)
            def _():
                kept = (0, 1) if way else (lines - 1, lines)
                self.line_copy(chunk, way, kept[0], kept[1], self.line).wait_recv()

            for step in range(lines - 1):
                at = lines - 1 - step if way else step
                first, last = (0, at) if way else (at + 1, lines)

                @pl.when(self.z == at)
                def _():
                    self.line_copy(chunk, way, first, last, self.line).wait_send()

        held[...] = self.pairs[chunk, self.z].astype(wide)

        @pl.when(self.z > 0)
        def _():
            held[...] += self.line[chunk, 0, self.z].astype(wide)

        @pl.when(self.z < lines - 1)
        def _():
            held[...] += self.line[chunk, 1, self.z].astype(wide)

        self.shares[chunk, self.member] = held[...].astype(low)
        for step in range(1, self.members):
            self.share_copy(chunk, step).start()

    def result(self, chunk):
        for step in range(1, self.members):
            self.share_copy(chunk, step).wait()
        total = self.shares[chunk, 0].astype(wide)
        for member in range(1, self.members):
            total = total + self.shares[chunk, member].astype(wide)
        return total


def summing_scratch(groups, members, chunks, rows, columns):
    lines = groups // 4
    return [
        pltpu.VMEM((chunks, lines, 2, rows, columns), low),
        pltpu.VMEM((chunks, lines, rows, columns), low),
        pltpu.VMEM((chunks, 2, lines, rows, columns), low),
        pltpu.VMEM((chunks, members, rows, columns), low),
        pltpu.SemaphoreType.DMA((chunks,)),
        pltpu.SemaphoreType.DMA((chunks,)),
        pltpu.SemaphoreType.DMA((chunks,)),
        pltpu.SemaphoreType.DMA((chunks,)),
        pltpu.SemaphoreType.DMA((chunks, 2)),
        pltpu.SemaphoreType.DMA((chunks, 2)),
        pltpu.SemaphoreType.DMA((chunks, max(members - 1, 1))),
        pltpu.SemaphoreType.DMA((chunks, max(members - 1, 1))),
    ]


def stage_delays(lines):
    return [1, 4] + [6 + 2 * step for step in range(lines - 2)] + [2 * lines + 2, 2 * lines + 6]


def feed_weights(rest_ref, out, inner, outer, sem):
    count, _, width = rest_ref.shape
    unit = width // count
    feeds = inner.shape[0]
    per = count // feeds
    copies = [pltpu.make_async_copy(rest_ref.at[:, :unit, :], out, sem.at[0])]
    for j in range(feeds):
        first = unit * (1 + j)
        copies.append(
            pltpu.make_async_copy(
                rest_ref.at[:, first : first + unit, :], inner.at[j], sem.at[1 + j]
            )
        )
    first = unit * (1 + feeds)
    for j in range(feeds):
        copies.append(
            pltpu.make_async_copy(
                rest_ref.at[per * j : per * (j + 1), first : first + feeds * unit, :],
                outer.at[j],
                sem.at[1 + feeds + j],
            )
        )
    return copies


def feed_arrival(rest_ref, inner, outer, sem, j):
    feeds = inner.shape[0]
    unit = inner.shape[2]
    pltpu.make_async_copy(rest_ref.at[:, :unit, :], inner.at[j], sem.at[1 + j]).wait()
    pltpu.make_async_copy(
        rest_ref.at[: outer.shape[1], : outer.shape[2], :], outer.at[j], sem.at[1 + feeds + j]
    ).wait()


def feed_buffers(rest, feeds):
    count, _, width = rest.shape
    unit = width // count
    return [
        pltpu.VMEM((count, unit, width), low),
        pltpu.VMEM((feeds, count, unit, width), low),
        pltpu.VMEM((feeds, count // feeds, feeds * unit, width), low),
        pltpu.SemaphoreType.DMA((1 + 2 * feeds,)),
    ]


def feed_kernel(
    attended_ref,
    tokens_ref,
    rest_ref,
    gains_ref,
    hidden_ref,
    pre_ref,
    encoded_ref,
    context_ref,
    out,
    inner,
    outer,
    sem,
    inner_in,
):
    width = tokens_ref.shape[1]
    feeds = pre_ref.shape[0]
    copies = feed_weights(rest_ref, out, inner, outer, sem)
    copies[0].start()
    for j in range(feeds):
        copies[1 + j].start()
        copies[1 + feeds + j].start()
    copies[0].wait()
    hidden = tokens_ref[...].astype(wide) + product(
        attended_ref[...].astype(low), out[...].reshape(width, width)
    )
    hidden_ref[...] = hidden
    inner_in[...] = (hidden * rms_factor(hidden) * gains_ref[1:2, :]).astype(low)
    encoded_ref[...] = hidden

    def step(j, carry):
        feed_arrival(rest_ref, inner, outer, sem, j)
        pre = product(inner_in[...], inner[j].reshape(width, width))
        pre_ref[j] = pre.astype(low)
        encoded_ref[...] += product(
            gelu_value(pre).astype(low), outer[j].reshape(width, width)
        )
        return carry

    lax.fori_loop(0, feeds, step, 0)
    encoded = encoded_ref[...]
    context_ref[...] = (encoded * rms_factor(encoded) * gains_ref[2:3, :]).astype(low)


def feed_forward(attended, tokens, rest, gains, feeds):
    rows, width = tokens.shape
    whole = pl.BlockSpec(memory_space=pltpu.VMEM)
    return pl.pallas_call(
        feed_kernel,
        name="feed_forward",
        in_specs=[whole, whole, pl.BlockSpec(memory_space=pl.ANY), whole],
        out_specs=[whole] * 4,
        out_shape=[
            jax.ShapeDtypeStruct((rows, width), wide),
            jax.ShapeDtypeStruct((feeds, rows, width), low),
            jax.ShapeDtypeStruct((rows, width), wide),
            jax.ShapeDtypeStruct((rows, width), low),
        ],
        scratch_shapes=feed_buffers(rest, feeds) + [pltpu.VMEM((rows, width), low)],
        compiler_params=pltpu.CompilerParams(vmem_limit_bytes=50 * 2**20),
        cost_estimate=pl.CostEstimate(
            flops=18 * rows * width * width, bytes_accessed=40 * width * width, transcendentals=0
        ),
    )(attended, tokens, rest, gains)


def feed_back_kernel(
    base,
    groups,
    members,
    grad_context_ref,
    encoded_ref,
    hidden_ref,
    pre_ref,
    attended_ref,
    rest_ref,
    gains_ref,
    rows_ref,
    starts_ref,
    parts_ref,
    grad_hidden_ref,
    grad_attended_ref,
    sums_ref,
    backs_ref,
    out,
    inner,
    outer,
    sem,
    inner_in,
    grad_branch,
    grad_inner_in,
    outer_grad,
    inner_grad,
    grad_sem,
    weights,
    sides,
    weight_sem,
    send_sem,
    recv_sem,
):
    rows, width = encoded_ref.shape
    feeds = pre_ref.shape[0]
    count = rest_ref.shape[0]
    unit = width // count
    lines = groups // 4
    group = lax.axis_index("batch")
    member = lax.axis_index("seq")

    partners = []
    for axis, place, number in (("batch", group, groups), ("seq", member, members)):
        span = 1
        while span < number:
            bit = lax.rem(place // span, 2)
            partners.append({axis: place + span * (1 - 2 * bit)})
            span *= 2
    barrier = pltpu.get_barrier_semaphore()
    for partner in partners:
        pl.semaphore_signal(barrier, inc=1, device_id=partner, device_id_type=MESH)

    def swap(i):
        return pltpu.make_async_remote_copy(
            src_ref=sides.at[2 * i],
            dst_ref=sides.at[2 * i + 1],
            send_sem=send_sem.at[i],
            recv_sem=recv_sem.at[i],
            device_id=partners[i],
            device_id_type=MESH,
        )

    def swapped(i):
        swap(i).wait()
        sides[2 * i + 2] = sides[2 * i] + sides[2 * i + 1]
        if i + 1 < len(partners):
            swap(i + 1).start()

    copies = feed_weights(rest_ref, out, inner, outer, sem)
    for j in range(feeds):
        copies[1 + feeds + j].start()
        copies[1 + j].start()
    copies[0].start()
    start_copies = [
        pltpu.make_async_copy(
            rest_ref.at[:, base + unit * i : base + unit * (i + 1), :],
            weights.at[i],
            weight_sem.at[i],
        )
        for i in range(4)
    ]
    for copy in start_copies:
        copy.start()
    sides[0] = rows_ref[...]
    hidden = hidden_ref[...]
    inner_in[...] = (hidden * rms_factor(hidden) * gains_ref[1:2, :]).astype(low).T
    grad_encoded, _ = rms_back(encoded_ref[...], gains_ref[2:3, :], grad_context_ref[...])
    grad_hidden_ref[...] = grad_encoded
    grad_branch[...] = grad_encoded.astype(low)
    grad_inner_in[...] = jnp.zeros_like(grad_inner_in)
    pl.semaphore_wait(barrier, len(partners))
    swap(0).start()

    def outer_put(j, slot):
        per = lines // feeds
        return pltpu.make_async_copy(
            outer_grad.at[slot],
            parts_ref.at[pl.ds(j * per, per), :, :, 1 + feeds :],
            grad_sem.at[0, slot],
        )

    def inner_put(j, slot):
        return pltpu.make_async_copy(
            inner_grad.at[slot], parts_ref.at[:, :, :, 1 + j], grad_sem.at[1, slot]
        )

    def step(j, carry):
        slot = lax.rem(j, 2)
        feed_arrival(rest_ref, inner, outer, sem, j)
        pre = pre_ref[j].astype(wide)
        grad_act = back_product(grad_branch[...], outer[j].reshape(width, width))
        grad_pre = (gelu_slope(pre) * grad_act).astype(low)
        grad_inner_in[...] += back_product(grad_pre, inner[j].reshape(width, width))
        act = gelu_value(pre).astype(low)

        @pl.when(j >= 2)
        def _():
            outer_put(j - 2, slot).wait()
            inner_put(j - 2, slot).wait()

        outer_grad[slot] = (
            weight_grad(act, grad_branch[...]).reshape(outer_grad.shape[1:]).astype(low)
        )
        outer_put(j, slot).start()
        inner_grad[slot] = (
            product(inner_in[...], grad_pre).reshape(inner_grad.shape[1:]).astype(low)
        )
        inner_put(j, slot).start()
        for i in range(min(feeds, len(partners))):

            @pl.when(j == i)
            def _():
                swapped(i)

        return carry

    lax.fori_loop(0, feeds, step, 0)
    grad_hidden, _ = rms_back(hidden_ref[...], gains_ref[1:2, :], grad_inner_in[...])
    grad_hidden = grad_hidden + grad_hidden_ref[...]
    grad_hidden_ref[...] = grad_hidden
    grad_branch[...] = grad_hidden.astype(low)
    copies[0].wait()
    grad_attended_ref[...] = back_product(
        grad_branch[...], out[...].reshape(width, width)
    ).astype(low)
    for j in range(feeds - 2, feeds):
        outer_put(j, j % 2).wait()
        inner_put(j, j % 2).wait()
    inner_grad[0] = (
        weight_grad(attended_ref[...].astype(low), grad_branch[...])
        .reshape(inner_grad.shape[1:])
        .astype(low)
    )
    out_put = pltpu.make_async_copy(
        inner_grad.at[0], parts_ref.at[:, :, :, 0], grad_sem.at[1, 0]
    )
    out_put.start()

    for i in range(feeds, len(partners)):
        swapped(i)
    sums = sides[2 * len(partners)]
    sums_ref[...] = sums
    for copy in start_copies:
        copy.wait()

    def weight(i):
        return weights[i].reshape(width, width)

    head_row = lax.broadcasted_iota(jnp.int32, (HEAD_ROWS, width), 0)
    head_mask = head_row == lax.broadcasted_iota(jnp.int32, (HEAD_ROWS, width), 1) // HEAD
    spread = product(sums[:HEAD_ROWS].astype(low), weight(3))
    grad_cross_query = jnp.sum(jnp.where(head_mask, spread, 0.0), axis=0, keepdims=True)
    grad_cross_query = grad_cross_query.astype(low)

    def widened(row):
        return jnp.broadcast_to(row.astype(wide), (SEQ_ROWS, width))

    start = widened(starts_ref[0:1, :])
    after_self = widened(starts_ref[3:4, :])
    grad_rows = back_product(widened(grad_cross_query).astype(low), weight(2))
    grad_after_self, _ = rms_back(after_self, gains_ref[5:6, :], grad_rows)
    cross_gain = grad_rows * after_self * rms_factor(after_self)
    grad_after_self = grad_after_self + widened(sums[HEAD_ROWS : HEAD_ROWS + 1])
    grad_self_branch = grad_after_self.astype(low)
    grad_self_vals = back_product(grad_self_branch, weight(1)).astype(low)
    grad_rows = back_product(grad_self_vals, weight(0))
    grad_start, _ = rms_back(start, gains_ref[4:5, :], grad_rows)
    self_gain = grad_rows * start * rms_factor(start)
    for i, row in enumerate(
        (
            grad_start + grad_after_self,
            self_gain,
            cross_gain,
            grad_cross_query,
            grad_self_branch,
            grad_self_vals,
        )
    ):
        backs_ref[i : i + 1, :] = row[:1].astype(wide)
    backs_ref[6:, :] = jnp.zeros((2, width), wide)
    out_put.wait()


def feed_back(
    grad_context, encoded, hidden, pre, attended, rest, base, gains, sum_rows, starts, groups, members, part
):
    rows, width = encoded.shape
    feeds = pre.shape[0]
    lines = groups // 4
    count = rest.shape[0]
    many = sum_rows.shape[0]
    partners = (groups.bit_length() - 1) + (members.bit_length() - 1)
    whole = pl.BlockSpec(memory_space=pltpu.VMEM)
    anywhere = pl.BlockSpec(memory_space=pl.ANY)
    return pl.pallas_call(
        functools.partial(feed_back_kernel, base, groups, members),
        name="feed_back",
        in_specs=[whole] * 5 + [anywhere] + [whole] * 3,
        out_specs=[anywhere] + [whole] * 4,
        out_shape=[
            jax.ShapeDtypeStruct((lines, 2, 2, 1 + 2 * feeds, part, width), low),
            jax.ShapeDtypeStruct((rows, width), wide),
            jax.ShapeDtypeStruct((rows, width), low),
            jax.ShapeDtypeStruct((many, width), wide),
            jax.ShapeDtypeStruct((8, width), wide),
        ],
        scratch_shapes=feed_buffers(rest, feeds)
        + [
            pltpu.VMEM((width, rows), low),
            pltpu.VMEM((rows, width), low),
            pltpu.VMEM((rows, width), wide),
            pltpu.VMEM((2, lines // feeds, 2, 2, feeds, part, width), low),
            pltpu.VMEM((2, lines, 2, 2, part, width), low),
            pltpu.SemaphoreType.DMA((2, 2)),
            pltpu.VMEM((4, count, width // count, width), low),
            pltpu.VMEM((2 * partners + 1, many, width), wide),
            pltpu.SemaphoreType.DMA((4,)),
            pltpu.SemaphoreType.DMA((partners,)),
            pltpu.SemaphoreType.DMA((partners,)),
        ],
        compiler_params=pltpu.CompilerParams(
            collective_id=2, has_side_effects=True, vmem_limit_bytes=60 * 2**20
        ),
        cost_estimate=pl.CostEstimate(
            flops=36 * rows * width * width, bytes_accessed=80 * width * width, transcendentals=0
        ),
    )(
        grad_context, encoded, hidden, pre, attended, rest, gains, sum_rows, starts
    )


def attend_back_kernel(
    groups,
    members,
    place,
    q_ref,
    k_ref,
    v_ref,
    grad_ref,
    attended_ref,
    total_ref,
    near_ref,
    own_turned_ref,
    all_turned_ref,
    parts_ref,
    grad_q_ref,
    grad_k_ref,
    grad_v_ref,
    table_ref,
    out_sums_ref,
    inner_sums_ref,
    outer_sums_ref,
    query_sums_ref,
    key_sums_ref,
    value_sums_ref,
    bias,
    key_side,
    value_side,
    keys_turned,
    grad_scores,
    grad_k_sum,
    grad_v_sum,
    band_sum,
    grad_q_sum,
    pair_grads,
    fetched,
    held,
    fetch_sem,
    bands,
    kept,
    sent,
    got,
    keep_send,
    keep_recv,
    tables,
    table_send,
    table_recv,
    *buffers,
):
    pair = pl.program_id(0)
    block = pl.program_id(1)
    blocks = pl.num_programs(1)
    pairs = pl.num_programs(0)
    now = pair * blocks + block
    pack = k_ref.shape[0]
    size = q_ref.shape[0]
    middle, reach, lead, width = table_sizes(size, pack)
    ends = (place[0], place[1])
    rows_here = size * blocks
    summing = Summing(groups, members, buffers)
    first = summing.member * rows_here + block * size
    shift = lax.rem(summing.member * rows_here, LANES) if size % LANES else 0
    barrier = pltpu.get_barrier_semaphore()
    feed_chunks = 2 * parts_ref.shape[3]
    feeds = (parts_ref.shape[3] - 1) // 2
    half_width = fetched.shape[-1]
    part = fetched.shape[-2]
    lines = groups // 4
    delays = stage_delays(lines)

    def feed_part(chunk, core):
        return parts_ref.at[
            :, :, core, chunk // 2, :, pl.ds(pl.multiple_of(lax.rem(chunk, 2) * half_width, LANES), half_width)
        ]

    def fetch(chunk):
        slot = lax.rem(chunk, 4)
        return pltpu.make_async_copy(
            feed_part(chunk, summing.core), fetched.at[slot], fetch_sem.at[slot]
        )

    def feed_stage(stage, chunk):
        if stage == 0:
            summing.start(chunk, feed_part(chunk, 1 - summing.core))
            fetch(chunk).start()
        elif stage == 1:
            fetch(chunk).wait()
            summing.to_pair(
                chunk, feed_part(chunk, 1 - summing.core), fetched[lax.rem(chunk, 4)]
            )
        elif stage <= lines:
            summing.to_line(chunk, stage - 2)
        elif stage == lines + 1:
            summing.to_members(chunk, held)
        else:
            total = summing.result(chunk)
            piece = chunk // 2
            column = pl.multiple_of(lax.rem(chunk, 2) * half_width, LANES)

            @pl.when(piece == 0)
            def _():
                out_sums_ref[:, pl.ds(column, half_width)] = total

            @pl.when((piece > 0) & (piece <= feeds))
            def _():
                at = pl.multiple_of((piece - 1) * 2 * half_width + column, LANES)
                inner_sums_ref[:, pl.ds(at, half_width)] = total

            @pl.when(piece > feeds)
            def _():
                at = pl.multiple_of((piece - 1 - feeds) * part, 8)
                outer_sums_ref[pl.ds(at, part), pl.ds(column, half_width)] = total

    def pair_stage(stage, which):
        chunk = feed_chunks + which
        if stage == 0:
            summing.start(chunk, pair_grads.at[which, :, :, 1 - summing.core])
        elif stage == 1:
            summing.to_pair(
                chunk,
                pair_grads.at[which, :, :, 1 - summing.core],
                pair_grads[which, :, :, summing.core],
            )
        elif stage <= lines:
            summing.to_line(chunk, stage - 2)
        elif stage == lines + 1:
            summing.to_members(chunk, held)
        else:
            total = summing.result(chunk)
            span = pl.ds(pl.multiple_of(which * LANES, LANES), LANES)
            for i, sums_ref in enumerate((query_sums_ref, key_sums_ref, value_sums_ref)):
                sums_ref[:, span] = total[:, LANES * i : LANES * (i + 1)]

    def keep_copy(which, step):
        return summing.copy(
            sent.at[which, step - 1],
            got.at[which, step - 1],
            keep_send.at[which, step - 1],
            keep_recv.at[which, step - 1],
            {"seq": lax.rem(summing.member + step, members)},
        )

    def keep_result(which):
        total = [kept[lax.rem(which, 2), i] for i in range(2)]
        for step in range(1, members):
            keep_copy(which, step).wait()
            total = [total[i] + got[which, step - 1, i].astype(wide) for i in range(2)]
        span = pl.ds(pl.multiple_of(which * LANES, LANES), LANES)
        grad_k_ref[:, span] = total[0].astype(low)
        grad_v_ref[:, span] = total[1].astype(low)

    partners = []
    for axis, spot, number in (
        ("batch", summing.group, groups),
        ("seq", summing.member, members),
    ):
        reach_out = 1
        while reach_out < number:
            bit = lax.rem(spot // reach_out, 2)
            partners.append({axis: spot + reach_out * (1 - 2 * bit)})
            reach_out *= 2

    def swap(i):
        return summing.copy(
            tables.at[2 * i],
            tables.at[2 * i + 1],
            table_send.at[i],
            table_recv.at[i],
            partners[i],
        )

    def swapped(i):
        swap(i).wait()
        tables[2 * i + 2] = tables[2 * i] + tables[2 * i + 1]
        if i + 1 < len(partners):
            swap(i + 1).start()

    @pl.when(now == 0)
    def _():
        peers = summing.neighbours()
        for i in range(len(partners)):
            peers.append((None, partners[i]))
        for condition, device in peers:
            if condition is None:
                pl.semaphore_signal(barrier, inc=1, device_id=device, device_id_type=MESH)
            else:

                @pl.when(condition)
                def _():
                    pl.semaphore_signal(barrier, inc=1, device_id=device, device_id_type=MESH)

        edges = (summing.z > 0).astype(jnp.int32) + (summing.z < lines - 1).astype(jnp.int32)
        pl.semaphore_wait(barrier, 2 + members - 1 + edges + len(partners))

    stages = 3 + lines
    starts = [0] + delays
    total_steps = pairs * blocks

    def run_stages(step):
        for stage in reversed(range(stages)):
            chunk = step - starts[stage]

            @pl.when((chunk >= 0) & (chunk < feed_chunks))
            def _():
                feed_stage(stage, chunk)

            late = step - (blocks - 1) - starts[stage]

            @pl.when((late >= 0) & (lax.rem(late + 64 * blocks, blocks) == 0) & (late < total_steps))
            def _():
                pair_stage(stage, late // blocks)

    @pl.when(now == 0)
    def _():
        tables[0] = jnp.zeros_like(tables[0])
        bands[...] = jnp.zeros_like(bands)

    @pl.when(block == 0)
    def _():
        places = lax.broadcasted_iota(jnp.int32, (pack, LANES), 0)
        lane = lax.broadcasted_iota(jnp.int32, (pack, LANES), 1)
        key_side[:, :LANES] = k_ref[...]
        ones = (segment_of(places, ends) == lane) | ((lane >= 3) & (lane < 9))
        key_side[:, LANES:] = ones.astype(wide).astype(low)
        value_side[:, :LANES] = v_ref[...]
        value_side[:, LANES:] = (lane < 6).astype(wide).astype(low)
        keys_turned[...] = k_ref[...].T
        for half in range(2):
            row = near_ref[half]
            before = middle - LANES
            after = middle + reach
            bias[half, before:after, :] = turned_biases(row, size, lead).T.astype(low)
            if before > 0:
                bias[half, :before, :] = jnp.broadcast_to(row[:, :1], (before, size)).astype(low)
            if after < width:
                bias[half, after:, :] = jnp.broadcast_to(
                    row[:, -1:], (width - after, size)
                ).astype(low)
        grad_scores[...] = jnp.zeros_like(grad_scores)
        grad_k_sum[...] = jnp.zeros_like(grad_k_sum)
        grad_v_sum[...] = jnp.zeros_like(grad_v_sum)
        band_sum[...] = jnp.zeros_like(band_sum)

    lane = lax.broadcasted_iota(jnp.int32, (size, LANES), 1)
    rows = first + lax.broadcasted_iota(jnp.int32, (size, LANES), 0)
    apart = jnp.where((segment_of(rows, ends) != lane) & (lane < 3), -far_apart, 0.0)
    start = pl.multiple_of(middle - (first - shift), LANES)
    near_rows = pl.ds(pl.multiple_of(first - shift, LANES), LANES + reach)
    queries = q_ref[...]
    grads = grad_ref[...]
    products = grads.astype(wide) * attended_ref[...]
    totals = total_ref[...]

    def in_parts(column, at):
        head = column.astype(low).astype(wide)
        body = (column - head).astype(low).astype(wide)
        tail = column - head - body
        return jnp.where(
            lane == at,
            head,
            jnp.where(lane == at + 1, body, jnp.where(lane == at + 2, tail, 0.0)),
        )

    query_grads = []
    for half in range(2):
        mine = (lane >= HEAD) if half else (lane < HEAD)
        row_term = jnp.sum(jnp.where(mine, products, 0.0), axis=1, keepdims=True)
        row_total = jnp.sum(
            jnp.where(lane == 2 * pair + half, totals, 0.0), axis=1, keepdims=True
        )
        query_part = jnp.where(mine, queries, jnp.zeros_like(queries))
        grad_part = jnp.where(mine, grads, jnp.zeros_like(grads))
        query_side = jnp.concatenate(
            [query_part, (apart - in_parts(row_total, 3 + 3 * half)).astype(low)], axis=1
        )
        grad_side = jnp.concatenate(
            [grad_part, (-in_parts(row_term, 3 * half)).astype(low)], axis=1
        )
        weights = jnp.exp(
            back_product(key_side[...], query_side)
            + bias[half, pl.ds(start, pack), :].astype(wide)
        )
        grad_block = (weights * back_product(value_side[...], grad_side)).astype(low)
        grad_scores[LANES : LANES + pack, :] = grad_block
        grad_v_sum[...] += product(weights.astype(low), grad_part)
        block_lane = jnp.where(lane == 8 * half + block, 1.0, 0.0).astype(low)
        grad_k_sum[...] += product(
            grad_block, jnp.concatenate([query_part, block_lane], axis=1)
        )
        query_grads.append(product(keys_turned[HEAD * half : HEAD * (half + 1), :], grad_block))
        band_sum[half] += grad_scores[near_rows, :].astype(wide)
    grad_query = jnp.concatenate(query_grads, axis=0).T.astype(low)
    grad_q_ref[...] = grad_query
    grad_q_sum[pl.ds(pl.multiple_of(block * size, 64), size), :] = grad_query

    @pl.when(block == blocks - 1)
    def _():
        grad_key = grad_k_sum[:, :LANES].astype(low)
        grad_value = grad_v_sum[...].astype(low)

        @pl.when(pair > 0)
        def _():
            keep_result(pair - 1)

        for step in range(1, members):
            other = pl.multiple_of(lax.rem(summing.member + step, members) * rows_here, 64)
            sent[pair, step - 1, 0] = grad_k_sum[pl.ds(other, rows_here), :LANES].astype(low)
            sent[pair, step - 1, 1] = grad_v_sum[pl.ds(other, rows_here), :].astype(low)
            keep_copy(pair, step).start()
        mine_rows = pl.ds(pl.multiple_of(summing.member * rows_here, 64), rows_here)
        kept[lax.rem(pair, 2), 0] = grad_k_sum[mine_rows, :LANES]
        kept[lax.rem(pair, 2), 1] = grad_v_sum[mine_rows, :]
        for i, gradient in enumerate(
            (
                product(own_turned_ref[...], grad_q_sum[...]),
                product(all_turned_ref[...], grad_key),
                product(all_turned_ref[...], grad_value),
            )
        ):
            pair_grads[pair, :, :, :, :, LANES * i : LANES * (i + 1)] = gradient.reshape(
                lines, 2, 2, part, LANES
            ).astype(low)
        key = lax.broadcasted_iota(jnp.int32, (pack, LANES), 0)
        which = lax.broadcasted_iota(jnp.int32, (pack, LANES), 1) % 8
        begin = summing.member * rows_here - shift + size * which
        sums = grad_k_sum[:, LANES:]
        below = jnp.sum(jnp.where(key < begin - LANES, sums, 0.0), axis=0, keepdims=True)
        above = jnp.sum(jnp.where(key >= begin + reach, sums, 0.0), axis=0, keepdims=True)
        columns = bands.shape[1]
        mirror = (
            lax.broadcasted_iota(jnp.int32, (size, size), 0)
            + lax.broadcasted_iota(jnp.int32, (size, size), 1)
            == size - 1
        ).astype(wide).astype(low)
        row_lane = lax.broadcasted_iota(jnp.int32, (1, LANES), 1)
        for half in range(2):
            rest = band_sum[half]
            flipped = jnp.zeros_like(rest)
            for _ in range(3):
                head_part = rest.astype(low)
                flipped = flipped + product(head_part, mirror)
                rest = rest - head_part.astype(wide)
            padded = jnp.concatenate(
                [flipped, jnp.zeros((rest.shape[0], columns - size), wide)], axis=1
            )
            turned = pltpu.roll(padded, 0, 1, stride=1, stride_axis=0)
            head = pl.ds(2 * pair + half, 1)
            bands[head, :] = jnp.sum(turned, axis=0, keepdims=True)
            own_lanes = row_lane // 8 == half
            low_sum = jnp.sum(jnp.where(own_lanes, below, 0.0), axis=1, keepdims=True)
            high_sum = jnp.sum(jnp.where(own_lanes, above, 0.0), axis=1, keepdims=True)
            tables[0, head, :] = jnp.where(row_lane == 15, low_sum, 0.0) + jnp.where(
                row_lane == 31, high_sum, 0.0
            )

    run_stages(now)

    @pl.when(now == total_steps - 1)
    def _():
        columns = bands.shape[1]
        offset = (
            lax.broadcasted_iota(jnp.int32, (columns, LANES), 0) - (size - 1) - LANES - shift
        )
        onehot = (
            bucket_of(offset) == lax.broadcasted_iota(jnp.int32, (columns, LANES), 1)
        ).astype(wide)
        tables[0] += jnp.dot(
            bands[...], onehot, precision=highest, preferred_element_type=wide
        )
        swap(0).start()

        def drain(step, carry):
            run_stages(step)
            for i in range(len(partners)):

                @pl.when(step == total_steps + i)
                def _():
                    swapped(i)

            return carry

        final = max(starts[-1] + 1, len(partners))
        lax.fori_loop(total_steps, total_steps + final, drain, 0)
        keep_result(pairs - 1)
        table_ref[...] = tables[2 * len(partners)]


def attend_back(
    queries, all_keys, all_values, grads, attended, totals, near, place, own_turned, all_turned, parts
):
    rows, width = queries.shape
    pack = all_keys.shape[0]
    size = block_rows(rows)
    _, reach, _, columns = table_sizes(size, pack)
    band = -(-(size + LANES + reach) // LANES) * LANES
    pairs = width // LANES
    members = pack // rows
    pieces = parts.shape[3]
    part = parts.shape[4]
    groups = 4 * parts.shape[0]
    half_width = width // 2
    chunks = 2 * pieces + pairs

    def own(p, i):
        return (i, p)

    def every(p, i):
        return (0, p)

    whole = pl.BlockSpec(memory_space=pltpu.VMEM)
    partners = (groups.bit_length() - 1) + (members.bit_length() - 1)
    feeds = (pieces - 1) // 2
    return pl.pallas_call(
        functools.partial(attend_back_kernel, groups, members),
        name="attend_back",
        grid=(pairs, rows // size),
        in_specs=[
            pl.BlockSpec(memory_space=pltpu.SMEM),
            pl.BlockSpec((size, LANES), own),
            pl.BlockSpec((pack, LANES), every),
            pl.BlockSpec((pack, LANES), every),
            pl.BlockSpec((size, LANES), own),
            pl.BlockSpec((size, LANES), own),
            pl.BlockSpec((size, LANES), lambda p, i: (i, 0)),
            pl.BlockSpec((2, 1, near.shape[2]), lambda p, i: (p, 0, 0)),
            whole,
            whole,
            pl.BlockSpec(memory_space=pl.ANY),
        ],
        out_specs=[
            pl.BlockSpec((size, LANES), own),
        ]
        + [whole] * 9,
        out_shape=[
            jax.ShapeDtypeStruct((rows, width), low),
            jax.ShapeDtypeStruct((rows, width), low),
            jax.ShapeDtypeStruct((rows, width), low),
            jax.ShapeDtypeStruct((16, LANES), wide),
            jax.ShapeDtypeStruct((part, width), wide),
            jax.ShapeDtypeStruct((part, feeds * width), wide),
            jax.ShapeDtypeStruct((feeds * part, width), wide),
            jax.ShapeDtypeStruct((part, width), wide),
            jax.ShapeDtypeStruct((part, width), wide),
            jax.ShapeDtypeStruct((part, width), wide),
        ],
        scratch_shapes=[
            pltpu.VMEM((2, columns, size), low),
            pltpu.VMEM((pack, 2 * LANES), low),
            pltpu.VMEM((pack, 2 * LANES), low),
            pltpu.VMEM((LANES, pack), low),
            pltpu.VMEM((LANES + pack + reach, size), low),
            pltpu.VMEM((pack, 2 * LANES), wide),
            pltpu.VMEM((pack, LANES), wide),
            pltpu.VMEM((2, LANES + reach, size), wide),
            pltpu.VMEM((rows, LANES), low),
            pltpu.VMEM((pairs, groups // 4, 2, 2, part, half_width), low),
            pltpu.VMEM((4, groups // 4, 2, part, half_width), low),
            pltpu.VMEM((part, half_width), wide),
            pltpu.SemaphoreType.DMA((4,)),
            pltpu.VMEM((16, band), wide),
            pltpu.VMEM((2, 2, rows, LANES), wide),
            pltpu.VMEM((pairs, max(members - 1, 1), 2, rows, LANES), low),
            pltpu.VMEM((pairs, max(members - 1, 1), 2, rows, LANES), low),
            pltpu.SemaphoreType.DMA((pairs, max(members - 1, 1))),
            pltpu.SemaphoreType.DMA((pairs, max(members - 1, 1))),
            pltpu.VMEM((2 * partners + 1, 16, LANES), wide),
            pltpu.SemaphoreType.DMA((partners,)),
            pltpu.SemaphoreType.DMA((partners,)),
        ]
        + summing_scratch(groups, members, chunks, part, half_width),
        compiler_params=pltpu.CompilerParams(
            collective_id=1, has_side_effects=True, vmem_limit_bytes=62 * 2**20
        ),
        cost_estimate=pl.CostEstimate(
            flops=20 * rows * pack * width * 2, bytes_accessed=16 * pack * width, transcendentals=0
        ),
    )(
        place,
        queries,
        all_keys,
        all_values,
        grads,
        attended,
        totals,
        near,
        own_turned,
        all_turned,
        parts,
    )


def last_kernel(
    groups,
    seqs,
    halves,
    grad_q_any,
    grad_k_any,
    grad_v_any,
    first_any,
    grad_hidden_any,
    rows_any,
    query_any,
    key_any,
    value_any,
    inner_any,
    attention_any,
    outer_any,
    tokens_ref,
    gains_ref,
    sums_ref,
    starts_ref,
    backs_ref,
    query_ref,
    key_ref,
    value_ref,
    inner_ref,
    cross_key_ref,
    cross_value_ref,
    grad_tokens_ref,
    vectors_ref,
    grad_self_value_ref,
    grad_self_out_ref,
    grad_cross_query_ref,
    grad_cross_key_ref,
    grad_cross_value_ref,
    grad_cross_out_ref,
    grad_second_inner_ref,
    grad_second_outer_ref,
    grad_pooler_ref,
    query_sums_ref,
    key_sums_ref,
    value_sums_ref,
    inner_sums_ref,
    attention_sums_ref,
    outer_sums_ref,
    pieces,
    grad_q_ref,
    grad_k_ref,
    grad_v_ref,
    first_ref,
    grad_hidden_ref,
    rows_ref,
    copy_sem,
):
    rows, width = tokens_ref.shape
    part = query_ref.shape[0]
    feeds = inner_ref.shape[1] // width
    number = groups * seqs
    every = 2 * HEAD_ROWS
    group = lax.axis_index("batch")
    copies = [
        pltpu.make_async_copy(source, target, copy_sem.at[i])
        for i, (source, target) in enumerate(
            (
                (rows_any, rows_ref),
                (grad_q_any, grad_q_ref),
                (grad_k_any, grad_k_ref),
                (grad_v_any, grad_v_ref),
                (first_any, first_ref),
                (grad_hidden_any, grad_hidden_ref),
                (query_any, query_sums_ref),
                (key_any, key_sums_ref),
                (value_any, value_sums_ref),
                (inner_any, inner_sums_ref),
                (attention_any, attention_sums_ref),
                (outer_any, outer_sums_ref),
            )
        )
    ]
    for copy in copies:
        copy.start()
    copies[0].wait()

    def chooser(count, first):
        row = lax.broadcasted_iota(jnp.int32, (count, width), 0)
        column = lax.broadcasted_iota(jnp.int32, (count, width), 1)
        return column == first + row

    chosen = chooser(part, group * part)
    choose = chosen.astype(wide).astype(low)
    tiles = width // LANES
    for i in range(tiles):
        pieces[i] = (
            rows_ref[:, :, LANES * i : LANES * (i + 1)].reshape(number * every, LANES).astype(wide)
        )

    def piece(at):
        return jnp.concatenate(
            [pieces[i, pl.ds(at, number, stride=every), :] for i in range(tiles)], axis=1
        ).astype(low)

    def own(values, which=None):
        which = choose if which is None else which
        return lax.dot_general(
            which, values, (((1,), (1,)), ((), ())), preferred_element_type=wide
        ).astype(low)

    def pair(left, right):
        return product(left, right)

    grad_cross_out_ref[...] = pair(own(piece(0)), piece(7))
    second_in = own(piece(1))
    grad_second_inner = [pair(second_in, piece(8 + j)) for j in range(feeds)]
    share = grad_second_outer_ref.shape[0]
    half = share // halves
    per = width // half
    grad_out = piece(12)
    for i in range(halves):
        chunk = group // per
        at = lax.rem(group, per) * half
        which = chooser(half, at).astype(wide).astype(low)
        found = jnp.zeros((half, number), wide)
        for j in range(feeds // halves):
            here = own(piece(2 + feeds // halves * i + j), which).astype(wide)
            found = jnp.where(chunk == j, here, found)
        grad_second_outer_ref[half * i : half * (i + 1), :] = pair(found.astype(low), grad_out)
    for j in range(feeds):
        grad_second_inner_ref[:, width * j : width * (j + 1)] = grad_second_inner[j]
    grad_pooler_ref[...] = pair(own(piece(6)), piece(13))

    mixed = rows_ref[:, HEAD_ROWS:, :].reshape(number * HEAD_ROWS, width)
    repeat = (
        lax.broadcasted_iota(jnp.int32, (number * HEAD_ROWS, number), 0) // HEAD_ROWS
        == lax.broadcasted_iota(jnp.int32, (number * HEAD_ROWS, number), 1)
    )
    heads = product(repeat.astype(wide).astype(low), piece(14))
    head = lax.broadcasted_iota(jnp.int32, heads.shape, 0) % HEAD_ROWS
    head_column = lax.broadcasted_iota(jnp.int32, heads.shape, 1) // HEAD
    heads = jnp.where(head == head_column, heads, 0.0).astype(low)
    grad_cross_value = pair(own(mixed), heads)
    grad_cross_value_ref[...] = grad_cross_value

    def exact(left, right):
        return lax.dot_general(
            left,
            right,
            (((1,), (1,)), ((), ())),
            precision=highest,
            preferred_element_type=wide,
        )

    chosen = chosen.astype(wide)
    key_rows = exact(chosen, sums_ref[:HEAD_ROWS, :])
    head_row = lax.broadcasted_iota(jnp.int32, (HEAD_ROWS, width), 0)
    head_mask = head_row == lax.broadcasted_iota(jnp.int32, (HEAD_ROWS, width), 1) // HEAD
    query_row = starts_ref[5:6, :].astype(low).astype(wide)
    query_heads = jnp.where(head_mask, jnp.broadcast_to(query_row, (HEAD_ROWS, width)), 0.0)
    grad_cross_key = jnp.dot(
        key_rows, query_heads, precision=highest, preferred_element_type=wide
    )
    grad_cross_key_ref[...] = grad_cross_key
    starts = exact(chosen, starts_ref[...])
    grad_self_value_ref[...] = starts[:, 1:2] * backs_ref[5:6, :]
    grad_self_out_ref[...] = starts[:, 2:3] * backs_ref[4:5, :]
    grad_cross_query_ref[...] = starts[:, 4:5] * backs_ref[3:4, :]

    def gain_sum(weight, grads):
        ones = jnp.ones((8, grads.shape[1]), wide)
        return exact(ones, weight.astype(wide) * grads)[:1]

    for copy in copies[1:]:
        copy.wait()
    attention = (
        gain_sum(query_ref[...], query_sums_ref[...])
        + gain_sum(key_ref[...], key_sums_ref[...])
        + gain_sum(value_ref[...], value_sums_ref[...])
    )
    feed = gain_sum(inner_ref[...], inner_sums_ref[...])
    encoder = gain_sum(cross_key_ref[...], grad_cross_key) + gain_sum(
        cross_value_ref[...], grad_cross_value
    )
    gains = exact(gains_ref[:8, :], chosen)
    backs = exact(backs_ref[...], chosen)
    others = exact(sums_ref[HEAD_ROWS:, :], chosen)
    for i, row in enumerate(
        (
            attention / gains[0:1],
            feed / gains[1:2],
            encoder / gains[2:3],
            backs[0:1],
            backs[1:2],
            backs[2:3],
            others[2:3],
            others[1:2],
        )
    ):
        vectors_ref[i] = row

    grad_normed = (
        back_product(grad_q_ref[...], first_ref[0])
        + back_product(grad_k_ref[...], first_ref[1])
        + back_product(grad_v_ref[...], first_ref[2])
    )
    grad_tokens, _ = rms_back(tokens_ref[...].astype(wide), gains_ref[:1, :], grad_normed)
    grad_tokens_ref[...] = grad_tokens + grad_hidden_ref[...]


def last_step(groups, seqs, halves, tokens, part, share, feeds, *arrays):
    rows, width = tokens.shape
    whole = pl.BlockSpec(memory_space=pltpu.VMEM)
    square = jax.ShapeDtypeStruct((part, width), wide)
    return pl.pallas_call(
        functools.partial(last_kernel, groups, seqs, halves),
        name="last",
        in_specs=[pl.BlockSpec(memory_space=pltpu.HBM)] * 12
        + [whole] * (len(arrays) - 12),
        out_specs=[whole] * 17,
        out_shape=[
            jax.ShapeDtypeStruct((rows, width), wide),
            jax.ShapeDtypeStruct((8, 1, part), wide),
            square,
            square,
            square,
            square,
            square,
            square,
            jax.ShapeDtypeStruct((part, feeds * width), wide),
            jax.ShapeDtypeStruct((share, width), wide),
            square,
            square,
            square,
            square,
            jax.ShapeDtypeStruct((part, feeds * width), wide),
            square,
            jax.ShapeDtypeStruct((share, width), wide),
        ],
        scratch_shapes=[
            pltpu.VMEM((width // LANES, groups * seqs * 2 * HEAD_ROWS, LANES), wide),
            pltpu.VMEM((rows, width), low),
            pltpu.VMEM((rows, width), low),
            pltpu.VMEM((rows, width), low),
            pltpu.VMEM((3, width, width), low),
            pltpu.VMEM((rows, width), wide),
            pltpu.VMEM((groups * seqs, 2 * HEAD_ROWS, width), low),
            pltpu.SemaphoreType.DMA((12,)),
        ],
        compiler_params=pltpu.CompilerParams(vmem_limit_bytes=62 * 2**20),
    )(*arrays)


def in_blocks(gathered, sizes):
    count, _, width = gathered.shape
    join = 16 // math.gcd(16, sizes[0])
    if join == 1:
        return gathered
    pieces, at = [], 0
    for size in sizes:
        piece = gathered[:, at : at + size].reshape(count // join, join * size, width)
        pieces.append(piece)
        at += size
    return jnp.concatenate(pieces, axis=1)


def column_blocks(weight, model_width):
    rows, columns = weight.shape
    blocks = columns // model_width
    return jnp.transpose(weight.reshape(rows, blocks, model_width), (1, 0, 2)).reshape(
        blocks * rows, model_width
    )


def shards(
    tokens,
    lengths,
    labels,
    attention_gain,
    query_weight,
    key_weight,
    value_weight,
    attention_out,
    position_bias,
    feed_gain,
    feed_inner,
    feed_outer,
    encoder_gain,
    start_token,
    self_gain,
    self_value,
    self_out,
    cross_gain,
    cross_query,
    cross_key,
    cross_value,
    cross_out,
    second_gain,
    second_inner,
    second_outer,
    final_gain,
    pooler_weight,
):
    rows, width = tokens.shape
    part = query_weight.shape[0]
    share = feed_outer.shape[0]
    groups = lax.axis_size("batch")
    members = lax.axis_size("seq")
    blocks = feed_inner.shape[1] // width
    pack = rows * members
    seqs = lengths.shape[1]
    group = lax.axis_index("batch")
    member = lax.axis_index("seq")
    own_first = member * rows
    ends = jnp.cumsum(lengths[0])
    place = jnp.stack(
        [ends[0], ends[1], own_first, own_first % LANES]
    ).astype(jnp.int32)

    vectors = jnp.stack(
        [
            attention_gain,
            feed_gain,
            encoder_gain,
            start_token,
            self_gain,
            cross_gain,
            second_gain,
            final_gain,
        ],
        axis=0,
    )
    bias_part = position_bias.reshape(1, -1)
    bias_size = bias_part.shape[1]
    extra = jnp.zeros((16, width), low)
    extra = lax.dynamic_update_slice(extra, vectors, (0, group * part))
    extra = lax.dynamic_update_slice(extra, bias_part, (8, group * bias_size))
    queries, all_keys, all_values, normed_all, gains, first_full = project(
        tokens, extra, [query_weight, key_weight, value_weight], groups, members
    )
    table = gains[8, : BUCKETS * HEADS].reshape(BUCKETS, HEADS).astype(low)
    second_part = jnp.concatenate(
        [
            attention_out[None],
            column_blocks(feed_inner, width).reshape(blocks, part, width),
            feed_outer.reshape(blocks, part, width),
        ],
        axis=0,
    )
    halves = 2 if members == 2 else 1
    half_share = share // halves
    half_inner = lax.dynamic_slice_in_dim(
        second_inner.reshape(part, groups, share), member % halves * half_share, half_share, 2
    ).reshape(part, groups * half_share)
    half_outer = lax.dynamic_slice_in_dim(second_outer, member % halves * half_share, half_share)
    rest_part = jnp.concatenate(
        [
            second_part.reshape(-1, width),
            self_value,
            self_out,
            cross_query,
            cross_key,
            cross_value,
            cross_out,
            pooler_weight,
            column_blocks(half_inner, width),
            half_outer,
        ],
        axis=0,
    )
    rest = lax.all_gather(rest_part, "batch", axis=0, tiled=False)

    near = offset_biases(table, block_rows(rows), pack, place[3])
    attended, totals = attend(queries, all_keys, all_values, near, place)
    rest_blocks = in_blocks(
        rest,
        [part] * (1 + blocks) + [share] + [part] * (7 + blocks // halves) + [half_share],
    )
    base = (1 + 2 * blocks) * (width // rest_blocks.shape[0])
    hidden, inner_pre, encoded, context = feed_forward(
        attended, tokens, rest_blocks, gains, blocks
    )

    embedded, loss, grad_context, decoder_rows, starts, decoder_totals = decoder_step(
        context, rest_blocks, base, gains, labels, place, groups, members, seqs
    )
    contrastive_loss = loss[0, :1]
    embedded = embedded[:seqs]
    decoder_rows = lax.all_gather(
        decoder_rows.reshape(seqs * 2 * HEAD_ROWS, width), "batch", axis=0, tiled=False
    )

    second_grads, grad_hidden, grad_attended, sums, backs = feed_back(
        grad_context,
        encoded,
        hidden,
        inner_pre,
        attended,
        rest_blocks,
        base,
        gains,
        decoder_totals,
        starts,
        groups,
        members,
        part,
    )
    normed = lax.dynamic_slice_in_dim(normed_all, own_first, rows)
    (
        grad_query_rows,
        grad_key_rows,
        grad_value_rows,
        table_sums,
        out_sums,
        inner_sums,
        outer_sums,
        query_sums,
        key_sums,
        value_sums,
    ) = attend_back(
        queries,
        all_keys,
        all_values,
        grad_attended,
        attended,
        totals,
        near,
        place,
        normed.T,
        normed_all.T,
        second_grads,
    )
    (
        grad_tokens,
        vectors,
        grad_self_value,
        grad_self_out,
        grad_cross_query,
        grad_cross_key,
        grad_cross_value,
        grad_cross_out,
        grad_second_inner,
        grad_second_outer,
        grad_pooler,
        query_sums,
        key_sums,
        value_sums,
        inner_sums,
        out_sums,
        outer_sums,
    ) = last_step(
        groups,
        seqs,
        halves,
        tokens,
        part,
        share,
        blocks,
        grad_query_rows,
        grad_key_rows,
        grad_value_rows,
        first_full,
        grad_hidden,
        decoder_rows.reshape(groups * seqs, 2 * HEAD_ROWS, width),
        query_sums,
        key_sums,
        value_sums,
        inner_sums,
        out_sums,
        outer_sums,
        tokens,
        gains,
        sums,
        starts,
        backs,
        query_weight,
        key_weight,
        value_weight,
        feed_inner,
        cross_key,
        cross_value,
    )
    half_share = share // halves
    grad_second_inner = jnp.transpose(
        grad_second_inner.reshape(part, halves, groups, half_share), (0, 2, 1, 3)
    ).reshape(part, blocks * width)
    vectors = vectors.reshape(8, part)
    own_buckets = BUCKETS // groups
    grad_table = lax.dynamic_slice_in_dim(table_sums, group * own_buckets, own_buckets, 1)[:HEADS].T
    return (
        contrastive_loss,
        embedded,
        grad_tokens,
        vectors[0],
        query_sums,
        key_sums,
        value_sums,
        out_sums,
        grad_table,
        vectors[1],
        inner_sums,
        outer_sums,
        vectors[2],
        vectors[3],
        vectors[4],
        grad_self_value,
        grad_self_out,
        vectors[5],
        grad_cross_query,
        grad_cross_key,
        grad_cross_value,
        grad_cross_out,
        vectors[6],
        grad_second_inner,
        grad_second_outer,
        vectors[7],
        grad_pooler,
    )


def solution(mesh):
    placed = (
        P(("batch", "seq"), None),
        P("batch", None),
        P(),
        P("batch"),
        P("batch", None),
        P("batch", None),
        P("batch", None),
        P("batch", None),
        P("batch", None),
        P("batch"),
        P("batch", None),
        P("batch", None),
        P("batch"),
        P("batch"),
        P("batch"),
        P("batch", None),
        P("batch", None),
        P("batch"),
        P("batch", None),
        P("batch", None),
        P("batch", None),
        P("batch", None),
        P("batch"),
        P("batch", None),
        P("batch", None),
        P("batch"),
        P("batch", None),
    )
    return jax.shard_map(
        shards,
        mesh=mesh,
        in_specs=placed,
        out_specs=(
            P(),
            P("batch", None),
            P(("batch", "seq"), None),
            P("batch"),
            P("batch", None),
            P("batch", None),
            P("batch", None),
            P("batch", None),
            P("batch", None),
            P("batch"),
            P("batch", None),
            P("batch", None),
            P("batch"),
            P("batch"),
            P("batch"),
            P("batch", None),
            P("batch", None),
            P("batch"),
            P("batch", None),
            P("batch", None),
            P("batch", None),
            P("batch", None),
            P("batch"),
            P("batch", None),
            P("batch", None),
            P("batch"),
            P("batch", None),
        ),
        check_vma=False,
    )
```

```python
import functools
import math

import jax
import jax.numpy as jnp
from jax import lax
from jax.experimental import pallas as pl
from jax.experimental.pallas import tpu as pltpu
from jax.sharding import PartitionSpec as P

HEADS = 12
HEAD = 64
BUCKETS = 32
LANES = 128
far_apart = float(2**30)

eps_norm = 1e-06
masked_score = -1000000000.0
logit_scale = 20.0
bucket_limits = (12, 16, 23, 32, 46, 64, 91)
highest = lax.Precision.HIGHEST
low = jnp.bfloat16
wide = jnp.float32
MESH = pl.DeviceIdType.MESH


def rms_factor(values):
    return lax.rsqrt(jnp.mean(values * values, axis=-1, keepdims=True) + eps_norm)


def rms_norm(values, gain_vector):
    return (
        values
        * lax.rsqrt(jnp.mean(values * values, axis=-1, keepdims=True) + eps_norm)
        * gain_vector
    )


def unit_length(values):
    return values * lax.rsqrt(jnp.sum(values * values, axis=-1, keepdims=True) + eps_norm)


def bucket_of(offsets):
    upper_half = jnp.where(offsets > 0, 16, 0).astype(jnp.int32)
    distance = jnp.abs(offsets)
    far_bucket = 8 + sum(((distance >= threshold).astype(jnp.int32) for threshold in bucket_limits))
    return upper_half + jnp.where(distance < 8, distance, far_bucket)


def product(left_side, right_side):
    return jnp.dot(left_side, right_side, preferred_element_type=wide)


def back_product(left_side, right_side):
    return lax.dot_general(
        left_side, right_side, (((1,), (1,)), ((), ())), preferred_element_type=wide
    )


def weight_grad(left_side, right_side):
    return lax.dot_general(
        left_side, right_side, (((0,), (0,)), ((), ())), preferred_element_type=wide
    )


def norm_back(values, gain_vector, grad_rows):
    _, pullback = jax.vjp(rms_norm, values, gain_vector)
    return pullback(grad_rows)


def gelu_back(values, grad_rows):
    _, pullback = jax.vjp(jax.nn.gelu, values)
    return pullback(grad_rows)[0]


def segment_of(places, ends):
    return (places >= ends[0]).astype(jnp.int32) + (places >= ends[1]).astype(jnp.int32)


def block_rows(rows):
    return 256 if rows % 256 == 0 else rows


def table_sizes(size, pack):
    slack = LANES if size % LANES else 0
    reach = -(-(size + slack + 91) // LANES) * LANES
    lead = -(-(size + slack) // LANES) * LANES
    middle = -(-(pack - size) // LANES) * LANES
    return middle, reach, lead, middle + max(pack, reach)


def offset_biases(table, size, pack, shift):
    _, reach, lead, _ = table_sizes(size, pack)
    offsets = jnp.arange(lead + reach + LANES, dtype=jnp.int32) - (lead + LANES) - shift
    onehot = (
        bucket_of(offsets)[None, :] == jnp.arange(BUCKETS, dtype=jnp.int32)[:, None]
    ).astype(low)
    return weight_grad(table, onehot)[:, None, :]


def turned_biases(row, size, lead):
    spread = jnp.broadcast_to(row, (size, row.shape[1]))
    return pltpu.roll(spread, 0, 1, stride=1, stride_axis=0)[:, lead:]


class Gathering:
    def __init__(self, groups, members, sems):
        self.groups = groups
        self.members = members
        self.lines = groups // 4
        self.group = lax.axis_index("batch")
        self.member = lax.axis_index("seq")
        self.z = self.group // 4
        self.y = lax.rem(self.group // 2, 2)
        self.core = lax.rem(self.group, 2)
        self.line_send, self.line_recv, self.pair_sems, self.chip_sems, self.share_sems = sems

    def batch_id(self, offset):
        return {"batch": self.group + offset}

    def neighbours(self):
        found = [
            (None, self.batch_id(1 - 2 * self.core)),
            (None, self.batch_id(2 - 4 * self.y)),
            (self.z > 0, self.batch_id(-4)),
            (self.z < self.lines - 1, self.batch_id(4)),
        ]
        for step in range(1, self.members):
            found.append((None, {"seq": lax.rem(self.member + step, self.members)}))
        return found

    def greet(self, barrier):
        for condition, device in self.neighbours():
            if condition is None:
                pl.semaphore_signal(barrier, inc=1, device_id=device, device_id_type=MESH)
            else:

                @pl.when(condition)
                def _():
                    pl.semaphore_signal(barrier, inc=1, device_id=device, device_id_type=MESH)

    def greeted(self, barrier):
        ends = (self.z > 0).astype(jnp.int32) + (self.z < self.lines - 1).astype(jnp.int32)
        pl.semaphore_wait(barrier, 2 + self.members - 1 + ends)

    def copy(self, source, target, send, recv, device):
        return pltpu.make_async_remote_copy(
            src_ref=source,
            dst_ref=target,
            send_sem=send,
            recv_sem=recv,
            device_id=device,
            device_id_type=MESH,
        )

    def line_copy(self, item, source, full, way, step):
        place = self.z + step if way else self.z - step
        block = full.at[place, self.y, self.core]
        return self.copy(
            source if step == 0 else block,
            block,
            self.line_send.at[item, way, step],
            self.line_recv.at[item, way, step],
            self.batch_id(-4 if way else 4),
        )

    def line_sends(self, way, step):
        if way:
            return (self.z > 0) & (self.z + step < self.lines)
        return (self.z < self.lines - 1) & (self.z - step >= 0)

    def line_arrives(self, way, step):
        return self.z + step < self.lines if way else self.z - step >= 0

    def send_line(self, item, source, full, step):
        for way in range(2):

            @pl.when(self.line_sends(way, step))
            def _():
                self.line_copy(item, source, full, way, step).start()

    def pair_copy(self, item, full):
        span = full.at[:, self.y, self.core]
        return self.copy(
            span,
            span,
            self.pair_sems.at[item, 0],
            self.pair_sems.at[item, 1],
            self.batch_id(2 - 4 * self.y),
        )

    def share_copy(self, item, full):
        span = full.at[:, :, self.core]
        return self.copy(
            span,
            span,
            self.share_sems.at[item, 0],
            self.share_sems.at[item, 1],
            {"seq": 1 - self.member},
        )

    def chip_copy(self, item, which, full):
        span = full.at[:, :, self.core]
        return self.copy(
            span,
            span,
            self.chip_sems.at[item, which, 0],
            self.chip_sems.at[item, which, 1],
            self.batch_id(1 - 2 * self.core),
        )

    def stages(self, split):
        return self.lines + (3 if split else 2)

    def stage(self, number, item, source, full, other=None):
        lines = self.lines
        if number == 0:
            own = pltpu.make_async_copy(
                source, full.at[self.z, self.y, self.core], self.chip_sems.at[item, 0, 0]
            )
            own.start()
            self.send_line(item, source, full, 0)
            own.wait()
        elif number < lines:
            for way in range(2):

                @pl.when(self.line_arrives(way, number))
                def _():
                    self.line_copy(item, source, full, way, number - 1).wait_recv()

            if number < lines - 1:
                self.send_line(item, source, full, number)
            else:
                self.pair_copy(item, full).start()
        elif number == lines:
            self.pair_copy(item, full).wait()
            if other is not None:
                self.share_copy(item, full).start()
            self.chip_copy(item, 0, full).start()
        elif number == lines + 1 and other is not None:
            self.share_copy(item, full).wait()
            self.chip_copy(item, 1, other).start()
        else:
            self.chip_copy(item, 0, full).wait()
            if other is not None:
                self.chip_copy(item, 1, other).wait()
            for way in range(2):
                for step in range(lines - 1):

                    @pl.when(self.line_sends(way, step))
                    def _():
                        self.line_copy(item, source, full, way, step).wait_send()


def gathering_sems(groups, items):
    lines = groups // 4
    return [
        pltpu.SemaphoreType.DMA((items, 2, lines)),
        pltpu.SemaphoreType.DMA((items, 2, lines)),
        pltpu.SemaphoreType.DMA((items, 2)),
        pltpu.SemaphoreType.DMA((items, 2, 2)),
        pltpu.SemaphoreType.DMA((items, 2)),
    ]


def joined_rows(blocks):
    size, width = blocks.shape[-2:]
    rows = size * math.prod(blocks.shape[:-2])
    if size % 16:
        return blocks.astype(wide).reshape(rows, width).astype(low)
    return blocks.reshape(rows, width)


def first_kernel(
    groups,
    members,
    tokens_ref,
    extra_ref,
    query_ref,
    key_ref,
    value_ref,
    queries_ref,
    keys_ref,
    values_ref,
    normed_ref,
    gains_ref,
    weights_ref,
    all_tokens,
    all_extra,
    all_query,
    all_key,
    all_value,
    token_send,
    token_recv,
    *sems,
):
    parts = (extra_ref, query_ref, key_ref, value_ref)
    fulls = (all_extra, all_query, all_key, all_value)
    gathering = Gathering(groups, members, sems)
    member = gathering.member
    rows, width = tokens_ref.shape
    barrier = pltpu.get_barrier_semaphore()
    gathering.greet(barrier)
    gathering.greeted(barrier)
    copies = []
    for step in range(1, members):
        copies.append(
            pltpu.make_async_remote_copy(
                src_ref=tokens_ref,
                dst_ref=all_tokens.at[member],
                send_sem=token_send.at[step - 1],
                recv_sem=token_recv.at[step - 1],
                device_id={"seq": lax.rem(member + step, members)},
                device_id_type=MESH,
            )
        )
        copies[-1].start()
    all_tokens[member] = tokens_ref[...]

    def normed(values):
        values = values.astype(wide)
        return (values * rms_factor(values) * gains_ref[:1, :]).astype(low)

    def finished(item):
        if item == 0:
            total = jnp.zeros((16, width), wide)
            for z in range(groups // 4):
                for y in range(2):
                    for core in range(2):
                        total = total + all_extra[z, y, core].astype(wide)
            gains_ref[...] = total
        elif item == 1:
            weights_ref[0] = joined_rows(all_query[...])
            queries_ref[...] = product(normed(tokens_ref[...]), weights_ref[0]).astype(low)
        elif item == 2:
            for copy in copies:
                copy.wait()
            weights_ref[1] = joined_rows(all_key[...])
            for part in range(members):
                span = slice(rows * part, rows * (part + 1))
                normed_ref[span, :] = normed(all_tokens[part])
                keys_ref[span, :] = product(normed_ref[span, :], weights_ref[1]).astype(low)
        else:
            weights_ref[2] = joined_rows(all_value[...])
            for part in range(members):
                span = slice(rows * part, rows * (part + 1))
                values_ref[span, :] = product(normed_ref[span, :], weights_ref[2]).astype(low)

    stages = gathering.stages(False)
    for step in range(len(parts) + stages - 1):
        for stage in reversed(range(stages)):
            if 0 <= step - stage < len(parts):
                item = step - stage
                gathering.stage(stage, item, parts[item], fulls[item])
        if step - (stages - 1) >= 0:
            finished(step - (stages - 1))


def project(tokens, extra, parts, groups, members):
    rows, width = tokens.shape
    whole = pl.BlockSpec(memory_space=pltpu.VMEM)
    lines = groups // 4
    items = [extra] + list(parts)
    pack = members * rows
    return pl.pallas_call(
        functools.partial(first_kernel, groups, members),
        name="project",
        in_specs=[whole] * 5,
        out_specs=[whole] * 6,
        out_shape=[
            jax.ShapeDtypeStruct((rows, width), low),
            jax.ShapeDtypeStruct((pack, width), low),
            jax.ShapeDtypeStruct((pack, width), low),
            jax.ShapeDtypeStruct((pack, width), low),
            jax.ShapeDtypeStruct((16, width), wide),
            jax.ShapeDtypeStruct((3, width, width), low),
        ],
        scratch_shapes=[pltpu.VMEM((members,) + tokens.shape, low)]
        + [pltpu.VMEM((lines, 2, 2) + item.shape, low) for item in items]
        + [
            pltpu.SemaphoreType.DMA((max(members - 1, 1),)),
            pltpu.SemaphoreType.DMA((max(members - 1, 1),)),
        ]
        + gathering_sems(groups, len(items)),
        compiler_params=pltpu.CompilerParams(
            collective_id=3, has_side_effects=True, vmem_limit_bytes=48 * 2**20
        ),
        cost_estimate=pl.CostEstimate(
            flops=2**31, bytes_accessed=32 * pack * width, transcendentals=0
        ),
    )(tokens, extra, *parts)


FAR_LANE = 3


def key_lanes(places, lane, ends, near, begins, reach):
    blocks = len(begins)
    values = jnp.where((segment_of(places, ends) == lane) & (lane < 3), 1.0, 0.0)
    for half in range(2):
        row = near[half]
        for i, begin in enumerate(begins):
            far = jnp.where(
                places < begin - LANES,
                row[:, :1],
                jnp.where(places >= begin + reach, row[:, -1:], 0.0),
            )
            values = jnp.where(lane == FAR_LANE + half * blocks + i, far, values)
    return values.astype(low)


def attend_kernel(
    place, q_ref, k_ref, v_ref, near_ref, attended_ref, total_ref, key_side, value_side, scores_ref
):
    pair = pl.program_id(0)
    pack = k_ref.shape[0]
    rows = q_ref.shape[0]
    size = block_rows(rows)
    blocks = rows // size
    _, reach, lead, _ = table_sizes(size, pack)
    ends = (place[0], place[1])
    shift = place[3]
    begins = [place[2] - shift + size * i for i in range(blocks)]
    near = [near_ref[half] for half in range(2)]
    places = lax.broadcasted_iota(jnp.int32, (pack, LANES), 0)
    lane = lax.broadcasted_iota(jnp.int32, (pack, LANES), 1)
    key_side[:, :LANES] = k_ref[...]
    key_side[:, LANES:] = key_lanes(places, lane, ends, near, begins, reach)
    value_side[:, :LANES] = v_ref[...]
    value_side[:, LANES:] = jnp.ones((pack, LANES), low)

    lane = lax.broadcasted_iota(jnp.int32, (rows, LANES), 1)
    row = lax.broadcasted_iota(jnp.int32, (rows, LANES), 0)
    apart = jnp.where(
        (segment_of(place[2] + row, ends) != lane) & (lane < 3), -far_apart, 0.0
    )
    queries = q_ref[...]
    outputs = []
    totals = total_ref[...]
    for half in range(2):
        mine = (lane >= HEAD) if half else (lane < HEAD)
        side = jnp.where(lane == FAR_LANE + half * blocks + row // size, 1.0, apart).astype(low)
        query_side = jnp.concatenate(
            [jnp.where(mine, queries, jnp.zeros_like(queries)), side], axis=1
        )
        scores_ref[half, :, LANES : LANES + pack] = back_product(query_side, key_side[...])
        band = turned_biases(near[half], size, lead)
        for i in range(blocks):
            span = slice(size * i, size * (i + 1))
            columns = pl.ds(pl.multiple_of(begins[i], LANES), LANES + reach)
            scores_ref[half, span, columns] += band
        scores = scores_ref[half, :, LANES : LANES + pack]
        top = jnp.max(scores, axis=1, keepdims=True)
        weights = jnp.exp(scores - top).astype(low)
        output = product(weights, value_side[...])
        total = output[:, LANES:]
        outputs.append(output[:, :LANES] / total)
        totals = jnp.where(lane == 2 * pair + half, top + jnp.log(total), totals)
    attended_ref[...] = jnp.where(lane < HEAD, outputs[0], outputs[1])
    total_ref[...] = totals


def attend(queries, all_keys, all_values, near, place):
    rows, width = queries.shape
    pack = all_keys.shape[0]
    size = block_rows(rows)
    _, reach, _, _ = table_sizes(size, pack)
    pairs = width // LANES
    return pl.pallas_call(
        attend_kernel,
        name="attend",
        grid=(pairs,),
        in_specs=[
            pl.BlockSpec(memory_space=pltpu.SMEM),
            pl.BlockSpec((rows, LANES), lambda p: (0, p)),
            pl.BlockSpec((pack, LANES), lambda p: (0, p)),
            pl.BlockSpec((pack, LANES), lambda p: (0, p)),
            pl.BlockSpec((2, 1, near.shape[2]), lambda p: (p, 0, 0)),
        ],
        out_specs=[
            pl.BlockSpec((rows, LANES), lambda p: (0, p)),
            pl.BlockSpec((rows, LANES), lambda p: (0, 0)),
        ],
        out_shape=[
            jax.ShapeDtypeStruct((rows, width), wide),
            jax.ShapeDtypeStruct((rows, LANES), wide),
        ],
        scratch_shapes=[
            pltpu.VMEM((pack, 2 * LANES), low),
            pltpu.VMEM((pack, 2 * LANES), low),
            pltpu.VMEM((2, rows, LANES + pack + reach), wide),
        ],
        compiler_params=pltpu.CompilerParams(vmem_limit_bytes=56 * 2**20),
        cost_estimate=pl.CostEstimate(
            flops=8 * rows * pack * width * 2, bytes_accessed=16 * pack * width, transcendentals=0
        ),
    )(place, queries, all_keys, all_values, near)


SEQ_ROWS = 8
HEAD_ROWS = 16


def rms_back(values, gain_row, grad_rows):
    factor = rms_factor(values)
    scaled = gain_row * grad_rows
    inner = jnp.mean(scaled * values, axis=-1, keepdims=True)
    return (
        factor * scaled - values * (factor * factor * factor) * inner,
        jnp.sum(grad_rows * values * factor, axis=0, keepdims=True),
    )


gelu_scale = 0.7978845608028654


def gelu_value(values):
    return 0.5 * values * (
        1.0 + jnp.tanh(gelu_scale * (values + 0.044715 * values * values * values))
    )


def gelu_slope(values):
    square = values * values
    bent = jnp.tanh(gelu_scale * (values + 0.044715 * square * values))
    return 0.5 * (1.0 + bent) + 0.5 * values * (1.0 - bent * bent) * gelu_scale * (
        1.0 + 0.134145 * square
    )


def decoder_kernel(
    base,
    groups,
    members,
    seqs,
    place,
    context_ref,
    third_ref,
    gains_ref,
    target_ref,
    embedded_ref,
    loss_ref,
    grad_context_ref,
    pieces_ref,
    starts_ref,
    totals_ref,
    weights,
    everyone,
    unpacked,
    shared,
    similar_ref,
    halves_sent,
    halves_got,
    piece_rows,
    weight_sem,
    every_send,
    every_recv,
    share_send,
    share_recv,
    half_send,
    half_recv,
):
    rows, width = context_ref.shape
    count, _, _ = third_ref.shape
    unit = width // count
    halves = 2 if members == 2 else 1
    feeds = 4 // halves
    blocks = feeds * unit
    group = lax.axis_index("batch")
    member = lax.axis_index("seq")
    seq_total = groups * seqs

    barrier = pltpu.get_barrier_semaphore()
    for step in range(1, groups):
        pl.semaphore_signal(
            barrier,
            inc=1,
            device_id={"batch": lax.rem(group + step, groups)},
            device_id_type=MESH,
        )
    for step in range(1, members):
        pl.semaphore_signal(
            barrier,
            inc=1,
            device_id={"seq": lax.rem(member + step, members)},
            device_id_type=MESH,
        )

    sizes = [unit] * 7 + [unit] * feeds + [blocks]
    firsts = [sum(sizes[:i]) for i in range(len(sizes))]
    copies = [
        pltpu.make_async_copy(
            third_ref.at[:, base + first : base + first + size, :],
            weights.at[:, first : first + size, :],
            weight_sem.at[i],
        )
        for i, (first, size) in enumerate(zip(firsts, sizes))
    ]
    for copy in copies:
        copy.start()

    def weight(i):
        return weights[:, firsts[i] : firsts[i] + unit, :].reshape(width, width)

    def outer_weight(j):
        per = count // feeds
        return weights[per * j : per * (j + 1), firsts[-1] : firsts[-1] + blocks, :].reshape(
            width, width
        )

    def half_copy(which, first, number):
        span = pl.ds(first, number)
        return pltpu.make_async_remote_copy(
            src_ref=halves_sent.at[span],
            dst_ref=halves_got.at[span],
            send_sem=half_send.at[which],
            recv_sem=half_recv.at[which],
            device_id={"seq": 1 - member},
            device_id_type=MESH,
        )

    def joined(which, part):
        if halves == 1:
            return part
        halves_sent[which] = part
        copy = half_copy(which, which, 1)
        copy.start()
        copy.wait()
        return part + halves_got[which]

    gain = {
        name: gains_ref[i : i + 1, :]
        for i, name in enumerate(
            ("attention", "feed", "encoder", "start", "own", "cross", "second", "final")
        )
    }
    context = context_ref[...]

    start = jnp.broadcast_to(gain["start"], (SEQ_ROWS, width))
    self_in = (start * rms_factor(start) * gain["own"]).astype(low)
    copies[0].wait()
    self_vals = product(self_in, weight(0)).astype(low)
    copies[1].wait()
    after_self = start + product(self_vals, weight(1))
    cross_in = (after_self * rms_factor(after_self) * gain["cross"]).astype(low)
    copies[2].wait()
    cross_query = product(cross_in, weight(2))
    head_row = lax.broadcasted_iota(jnp.int32, (HEAD_ROWS, width), 0)
    head_mask = head_row == lax.broadcasted_iota(jnp.int32, (HEAD_ROWS, width), 1) // HEAD
    query_heads = jnp.where(
        head_mask, jnp.broadcast_to(cross_query[:1], (HEAD_ROWS, width)), 0.0
    ).astype(low)
    copies[3].wait()
    key_rows = back_product(query_heads, weight(3)).astype(low)

    many = seqs * HEAD_ROWS
    scores = back_product(key_rows, context)
    scores = jnp.concatenate([scores] * seqs, axis=0)
    places = member * rows + lax.broadcasted_iota(jnp.int32, (many, rows), 1)
    row_seq = lax.broadcasted_iota(jnp.int32, (many, rows), 0) // HEAD_ROWS
    inside = segment_of(places, (place[0], place[1])) == row_seq
    scores = jnp.where(inside, scores, masked_score)
    part_top = jnp.max(scores, axis=1, keepdims=True)
    part_weights = jnp.where(inside, jnp.exp(scores - part_top), 0.0).astype(low)
    part_total = jnp.sum(part_weights.astype(wide), axis=1, keepdims=True)
    lane = lax.broadcasted_iota(jnp.int32, (many, LANES), 1)
    shared[0, :, :width] = product(part_weights, context)
    shared[0, :, width:] = jnp.where(lane == 0, part_top, part_total)

    pl.semaphore_wait(barrier, groups - 1 + members - 1)
    for step in range(1, members):
        pltpu.make_async_remote_copy(
            src_ref=shared.at[0],
            dst_ref=shared.at[step],
            send_sem=share_send.at[step - 1],
            recv_sem=share_recv.at[step - 1],
            device_id={"seq": lax.rem(member + step, members)},
            device_id_type=MESH,
        ).start()
    for step in range(1, members):
        pltpu.make_async_remote_copy(
            src_ref=shared.at[0],
            dst_ref=shared.at[step],
            send_sem=share_send.at[step - 1],
            recv_sem=share_recv.at[step - 1],
            device_id={"seq": lax.rem(member + step, members)},
            device_id_type=MESH,
        ).wait()
    top = shared[0, :, width : width + 1]
    for step in range(1, members):
        top = jnp.maximum(top, shared[step, :, width : width + 1])
    total = jnp.zeros((many, 1), wide)
    mixed = jnp.zeros((many, width), wide)
    for step in range(members):
        scale = jnp.exp(shared[step, :, width : width + 1] - top)
        total = total + shared[step, :, width + 1 : width + 2] * scale
        mixed = mixed + shared[step, :, :width] * scale
    mixed = (mixed / total).astype(low)
    log_total = top + jnp.log(total)

    def by_seq(parts):
        row = lax.broadcasted_iota(jnp.int32, (SEQ_ROWS, width), 0)
        joined = jnp.zeros((SEQ_ROWS, width), wide)
        for i, part in enumerate(parts):
            joined = jnp.where(row == i, part, joined)
        return joined

    copies[4].wait()
    spread = product(mixed, weight(4))
    cross_attended = by_seq(
        [
            jnp.sum(
                jnp.where(head_mask, spread[HEAD_ROWS * i : HEAD_ROWS * (i + 1)], 0.0),
                axis=0,
                keepdims=True,
            )
            for i in range(seqs)
        ]
    )
    cross_low = cross_attended.astype(low)
    copies[5].wait()
    after_cross = after_self + product(cross_low, weight(5))
    second_in = (after_cross * rms_factor(after_cross) * gain["second"]).astype(low)
    for copy in copies[7:]:
        copy.wait()
    second_pre = [product(second_in, weight(7 + j)) for j in range(feeds)]
    second_act = [gelu_value(second_pre[j]).astype(low) for j in range(feeds)]
    second_out = product(second_act[0], outer_weight(0))
    for j in range(1, feeds):
        second_out = second_out + product(second_act[j], outer_weight(j))
    decoded = after_cross + joined(0, second_out)
    pooled_in = (decoded * rms_factor(decoded) * gain["final"]).astype(low)
    copies[6].wait()
    pooled = product(pooled_in, weight(6))
    size = lax.rsqrt(jnp.sum(pooled * pooled, axis=-1, keepdims=True) + eps_norm)
    embedded = pooled * size
    embedded_ref[...] = embedded

    tiles = width // LANES
    for i in range(tiles):
        everyone[0, 4 * i : 4 * (i + 1), :] = embedded[:4, LANES * i : LANES * (i + 1)]
    sends = []
    for step in range(1, groups):
        sends.append(
            pltpu.make_async_remote_copy(
                src_ref=everyone.at[0],
                dst_ref=everyone.at[step],
                send_sem=every_send,
                recv_sem=every_recv,
                device_id={"batch": lax.rem(group + step, groups)},
                device_id_type=MESH,
            )
        )
        sends[-1].start()
    arrival = pltpu.make_async_remote_copy(
        src_ref=everyone.at[pl.ds(1, groups - 1)],
        dst_ref=everyone.at[pl.ds(1, groups - 1)],
        send_sem=every_send,
        recv_sem=every_recv,
        device_id={"batch": lax.rem(group + 1, groups)},
        device_id_type=MESH,
    )
    arrival.wait_recv()
    arrival.wait_send()
    unpacked[...] = jnp.zeros_like(unpacked)
    for i in range(tiles):
        unpacked[:, :4, LANES * i : LANES * (i + 1)] = everyone[:, 4 * i : 4 * (i + 1), :]
    all_rows = unpacked[...].reshape(groups * SEQ_ROWS, width)
    number = groups * SEQ_ROWS
    row = lax.broadcasted_iota(jnp.int32, (number, number), 0)
    column = lax.broadcasted_iota(jnp.int32, (number, number), 1)
    row_valid = row % SEQ_ROWS < seqs
    valid = row_valid & (column % SEQ_ROWS < seqs)
    similar = logit_scale * lax.dot_general(
        all_rows,
        all_rows,
        (((1,), (1,)), ((), ())),
        precision=highest,
        preferred_element_type=wide,
    )
    similar = jnp.where(valid & (row != column), similar, masked_score)
    best = jnp.max(similar, axis=1, keepdims=True)
    log_norm = best + jnp.log(jnp.sum(jnp.exp(similar - best), axis=1, keepdims=True))
    row_group = lax.rem(group - row // SEQ_ROWS + groups, groups)
    column_group = lax.rem(group - column // SEQ_ROWS + groups, groups)
    row_number = row_group * seqs + row % SEQ_ROWS
    column_number = column_group * seqs + column % SEQ_ROWS
    label = jnp.max(
        jnp.where(
            lax.broadcasted_iota(jnp.int32, (number, target_ref.shape[1]), 1)
            == row_number[:, : target_ref.shape[1]],
            target_ref[:1, :],
            -1.0,
        ),
        axis=1,
        keepdims=True,
    )
    target = (column_number.astype(wide) == label) & valid
    picked = jnp.sum(jnp.where(target, similar, 0.0), axis=1, keepdims=True)
    losses = jnp.where(row_valid[:, :1], log_norm - picked, 0.0)
    loss_ref[...] = jnp.broadcast_to(
        jnp.sum(losses, axis=0, keepdims=True) / seq_total, loss_ref.shape
    )
    grad_similar = jnp.where(
        valid, (jnp.exp(similar - log_norm) - target.astype(wide)) / seq_total, 0.0
    )
    similar_ref[...] = grad_similar + grad_similar.T
    grad_embedded = logit_scale * jnp.dot(
        similar_ref[:SEQ_ROWS, :], all_rows, precision=highest, preferred_element_type=wide
    )

    grad_pooled = (
        size
        * (grad_embedded - embedded * jnp.sum(embedded * grad_embedded, axis=-1, keepdims=True))
    ).astype(low)
    grad_decoded, grad_final_gain = rms_back(
        decoded, gain["final"], back_product(grad_pooled, weight(6))
    )
    grad_second_out = grad_decoded.astype(low)
    grad_second_pre = [
        (gelu_slope(second_pre[j]) * back_product(grad_second_out, outer_weight(j))).astype(low)
        for j in range(feeds)
    ]
    if halves == 2:
        for j in range(feeds):
            halves_sent[2 + j] = second_act[j].astype(wide)
            halves_sent[2 + feeds + j] = grad_second_pre[j].astype(wide)
        half_copy(2, 2, 2 * feeds).start()
    grad_second_in = back_product(grad_second_pre[0], weight(7))
    for j in range(1, feeds):
        grad_second_in = grad_second_in + back_product(grad_second_pre[j], weight(7 + j))
    grad_second_in = joined(1, grad_second_in)
    grad_after_cross, grad_second_gain = rms_back(after_cross, gain["second"], grad_second_in)
    grad_after_cross = grad_after_cross + grad_decoded
    grad_cross_branch = grad_after_cross.astype(low)
    grad_cross_att = back_product(grad_cross_branch, weight(5)).astype(low)
    grad_cross_wide = grad_cross_att.astype(wide)
    grad_heads = jnp.concatenate(
        [
            jnp.where(
                head_mask,
                jnp.broadcast_to(grad_cross_wide[i : i + 1], (HEAD_ROWS, width)),
                0.0,
            )
            for i in range(seqs)
        ],
        axis=0,
    )
    attended_heads = jnp.concatenate(
        [
            jnp.broadcast_to(cross_attended[i : i + 1], (HEAD_ROWS, width))
            for i in range(seqs)
        ],
        axis=0,
    )
    row_terms = jnp.sum(grad_heads * attended_heads, axis=1, keepdims=True)
    value_rows = back_product(grad_heads.astype(low), weight(4)).astype(low)
    probs = jnp.where(inside, jnp.exp(scores - log_total), 0.0)
    grad_scores = (probs * (back_product(value_rows, context) - row_terms)).astype(low)
    grad_context_ref[...] = weight_grad(
        jnp.concatenate([grad_scores, probs.astype(low)], axis=0),
        jnp.concatenate([key_rows] * seqs + [value_rows], axis=0),
    )
    key_sums = product(grad_scores, context)
    sums = key_sums[:HEAD_ROWS]
    for i in range(1, seqs):
        sums = sums + key_sums[HEAD_ROWS * i : HEAD_ROWS * (i + 1)]
    first_member = jnp.where(member == 0, 1.0, 0.0)
    totals_ref[:HEAD_ROWS, :] = sums
    totals_ref[HEAD_ROWS:, :] = first_member * by_seq(
        [jnp.sum(grad_after_cross, axis=0, keepdims=True), grad_final_gain, grad_second_gain]
    )
    def put(at, values):
        for i in range(seqs):
            piece_rows[i, pl.ds(at, 1), :] = values[i : i + 1].astype(wide)

    piece_rows[...] = jnp.zeros_like(piece_rows)
    for i, piece in zip(
        (0, 1, 6, 7, 12, 13, 14),
        (
            cross_low,
            second_in,
            pooled_in,
            grad_cross_branch,
            grad_second_out,
            grad_pooled,
            grad_cross_att,
        ),
    ):
        put(i, piece)
    if halves == 2:
        half_copy(2, 2, 2 * feeds).wait()
    for first, values, got in ((2, second_act, 2), (8, grad_second_pre, 2 + feeds)):
        for j in range(feeds):
            if halves == 1:
                put(first + j, values[j])
            else:
                put(first + feeds * member + j, values[j])
                put(first + feeds * (1 - member) + j, halves_got[got + j])
    for i in range(seqs):
        piece_rows[i, HEAD_ROWS:, :] = mixed[HEAD_ROWS * i : HEAD_ROWS * (i + 1)].astype(wide)
    pieces_ref[...] = piece_rows[...].astype(low)
    for i, piece in enumerate([start, self_in, self_vals, after_self, cross_in, cross_query]):
        starts_ref[i : i + 1, :] = piece[:1].astype(wide)
    starts_ref[6:, :] = jnp.zeros((2, width), wide)


def decoder_step(context, third, base, gains, labels, place, groups, members, seqs):
    rows, width = context.shape
    everything = pl.BlockSpec(memory_space=pltpu.VMEM)
    labels = jnp.pad(labels.astype(wide)[None], ((0, 7), (0, LANES - labels.shape[0])))
    number = groups * SEQ_ROWS
    return pl.pallas_call(
        functools.partial(decoder_kernel, base, groups, members, seqs),
        name="decoder",
        in_specs=[
            pl.BlockSpec(memory_space=pltpu.SMEM),
            everything,
            pl.BlockSpec(memory_space=pl.ANY),
            everything,
            everything,
        ],
        out_specs=[everything] * 6,
        out_shape=[
            jax.ShapeDtypeStruct((SEQ_ROWS, width), wide),
            jax.ShapeDtypeStruct((8, LANES), wide),
            jax.ShapeDtypeStruct((rows, width), wide),
            jax.ShapeDtypeStruct((seqs, 2 * HEAD_ROWS, width), low),
            jax.ShapeDtypeStruct((8, width), wide),
            jax.ShapeDtypeStruct((HEAD_ROWS + SEQ_ROWS, width), wide),
        ],
        scratch_shapes=[
            pltpu.VMEM((third.shape[0], third.shape[1] - base, width), low),
            pltpu.VMEM((groups, 4 * width // LANES, LANES), wide),
            pltpu.VMEM((groups, SEQ_ROWS, width), wide),
            pltpu.VMEM((members, seqs * HEAD_ROWS, width + LANES), wide),
            pltpu.VMEM((number, number), wide),
            pltpu.VMEM((10, SEQ_ROWS, width), wide),
            pltpu.VMEM((10, SEQ_ROWS, width), wide),
            pltpu.VMEM((seqs, 2 * HEAD_ROWS, width), wide),
            pltpu.SemaphoreType.DMA((12,)),
            pltpu.SemaphoreType.DMA,
            pltpu.SemaphoreType.DMA,
            pltpu.SemaphoreType.DMA((max(members - 1, 1),)),
            pltpu.SemaphoreType.DMA((max(members - 1, 1),)),
            pltpu.SemaphoreType.DMA((3,)),
            pltpu.SemaphoreType.DMA((3,)),
        ],
        compiler_params=pltpu.CompilerParams(
            collective_id=0, has_side_effects=True, vmem_limit_bytes=56 * 2**20
        ),
        cost_estimate=pl.CostEstimate(
            flops=2 * rows * width * 300, bytes_accessed=2 * third.size, transcendentals=0
        ),
    )(place, context, third, gains, labels)


class Summing:
    def __init__(self, groups, members, buffers):
        self.groups = groups
        self.members = members
        self.lines = groups // 4
        self.group = lax.axis_index("batch")
        self.member = lax.axis_index("seq")
        self.z = self.group // 4
        self.y = lax.rem(self.group // 2, 2)
        self.core = lax.rem(self.group, 2)
        (
            self.chip,
            self.pairs,
            self.line,
            self.shares,
            self.chip_send,
            self.chip_recv,
            self.pair_send,
            self.pair_recv,
            self.line_send,
            self.line_recv,
            self.share_send,
            self.share_recv,
        ) = buffers
        self.stages = 3 + self.lines

    def batch_id(self, offset):
        return {"batch": self.group + offset}

    def neighbours(self):
        found = [
            (None, self.batch_id(1 - 2 * self.core)),
            (None, self.batch_id(2 - 4 * self.y)),
            (self.z > 0, self.batch_id(-4)),
            (self.z < self.lines - 1, self.batch_id(4)),
        ]
        for step in range(1, self.members):
            found.append((None, {"seq": lax.rem(self.member + step, self.members)}))
        return found

    def greet(self, barrier):
        for condition, device in self.neighbours():
            if condition is None:
                pl.semaphore_signal(barrier, inc=1, device_id=device, device_id_type=MESH)
            else:

                @pl.when(condition)
                def _():
                    pl.semaphore_signal(barrier, inc=1, device_id=device, device_id_type=MESH)

    def greeted(self, barrier):
        ends = (self.z > 0).astype(jnp.int32) + (self.z < self.lines - 1).astype(jnp.int32)
        pl.semaphore_wait(barrier, 2 + self.members - 1 + ends)

    def copy(self, source, target, send, recv, device):
        return pltpu.make_async_remote_copy(
            src_ref=source,
            dst_ref=target,
            send_sem=send,
            recv_sem=recv,
            device_id=device,
            device_id_type=MESH,
        )

    def chip_copy(self, chunk, source):
        return self.copy(
            source,
            self.chip.at[chunk],
            self.chip_send.at[chunk],
            self.chip_recv.at[chunk],
            self.batch_id(1 - 2 * self.core),
        )

    def pair_copy(self, chunk):
        return self.copy(
            self.chip.at[chunk, :, 1 - self.y],
            self.pairs.at[chunk],
            self.pair_send.at[chunk],
            self.pair_recv.at[chunk],
            self.batch_id(2 - 4 * self.y),
        )

    def line_copy(self, chunk, way, first, last, source):
        return self.copy(
            source.at[chunk, pl.ds(first, last - first)]
            if source is self.pairs
            else source.at[chunk, way, pl.ds(first, last - first)],
            self.line.at[chunk, way, pl.ds(first, last - first)],
            self.line_send.at[chunk, way],
            self.line_recv.at[chunk, way],
            self.batch_id(-4 if way else 4),
        )

    def share_copy(self, chunk, step):
        return self.copy(
            self.shares.at[chunk, self.member],
            self.shares.at[chunk, self.member],
            self.share_send.at[chunk, step - 1],
            self.share_recv.at[chunk, step - 1],
            {"seq": lax.rem(self.member + step, self.members)},
        )

    def start(self, chunk, source):
        self.chip_copy(chunk, source).start()

    def to_pair(self, chunk, source, own):
        self.chip_copy(chunk, source).wait()
        self.chip[chunk] = self.chip[chunk] + own
        self.pair_copy(chunk).start()

    def to_line(self, chunk, step):
        lines = self.lines
        if step == 0:
            self.pair_copy(chunk).wait()
            self.pairs[chunk] = self.pairs[chunk] + self.chip[chunk, :, self.y]
        for way in range(2):
            at = lines - 1 - step if way else step
            first, last = (0, at) if way else (at + 1, lines)

            @pl.when(self.z == at)
            def _():
                if step > 0:
                    kept = (0, at + 1) if way else (at, lines)
                    self.line_copy(chunk, way, kept[0], kept[1], self.line).wait_recv()
                    span = pl.ds(first, last - first)
                    self.line[chunk, way, span] = (
                        self.line[chunk, way, span] + self.pairs[chunk, span]
                    )
                self.line_copy(
                    chunk, way, first, last, self.line if step > 0 else self.pairs
                ).start()

    def to_members(self, chunk, held):
        lines = self.lines
        for way in range(2):
            end = 0 if way else lines - 1

            @pl.when(self.z == end)
            def _():
                kept = (0, 1) if way else (lines - 1, lines)
                self.line_copy(chunk, way, kept[0], kept[1], self.line).wait_recv()

            for step in range(lines - 1):
                at = lines - 1 - step if way else step
                first, last = (0, at) if way else (at + 1, lines)

                @pl.when(self.z == at)
                def _():
                    self.line_copy(chunk, way, first, last, self.line).wait_send()

        held[...] = self.pairs[chunk, self.z].astype(wide)

        @pl.when(self.z > 0)
        def _():
            held[...] += self.line[chunk, 0, self.z].astype(wide)

        @pl.when(self.z < lines - 1)
        def _():
            held[...] += self.line[chunk, 1, self.z].astype(wide)

        self.shares[chunk, self.member] = held[...].astype(low)
        for step in range(1, self.members):
            self.share_copy(chunk, step).start()

    def result(self, chunk):
        for step in range(1, self.members):
            self.share_copy(chunk, step).wait()
        total = self.shares[chunk, 0].astype(wide)
        for member in range(1, self.members):
            total = total + self.shares[chunk, member].astype(wide)
        return total


def summing_scratch(groups, members, chunks, rows, columns):
    lines = groups // 4
    return [
        pltpu.VMEM((chunks, lines, 2, rows, columns), low),
        pltpu.VMEM((chunks, lines, rows, columns), low),
        pltpu.VMEM((chunks, 2, lines, rows, columns), low),
        pltpu.VMEM((chunks, members, rows, columns), low),
        pltpu.SemaphoreType.DMA((chunks,)),
        pltpu.SemaphoreType.DMA((chunks,)),
        pltpu.SemaphoreType.DMA((chunks,)),
        pltpu.SemaphoreType.DMA((chunks,)),
        pltpu.SemaphoreType.DMA((chunks, 2)),
        pltpu.SemaphoreType.DMA((chunks, 2)),
        pltpu.SemaphoreType.DMA((chunks, max(members - 1, 1))),
        pltpu.SemaphoreType.DMA((chunks, max(members - 1, 1))),
    ]


def stage_delays(lines):
    return [1, 4] + [6 + 2 * step for step in range(lines - 2)] + [2 * lines + 2, 2 * lines + 6]


def feed_weights(rest_ref, out, inner, outer, sem):
    count, _, width = rest_ref.shape
    unit = width // count
    feeds = inner.shape[0]
    per = count // feeds
    copies = [pltpu.make_async_copy(rest_ref.at[:, :unit, :], out, sem.at[0])]
    for j in range(feeds):
        first = unit * (1 + j)
        copies.append(
            pltpu.make_async_copy(
                rest_ref.at[:, first : first + unit, :], inner.at[j], sem.at[1 + j]
            )
        )
    first = unit * (1 + feeds)
    for j in range(feeds):
        copies.append(
            pltpu.make_async_copy(
                rest_ref.at[per * j : per * (j + 1), first : first + feeds * unit, :],
                outer.at[j],
                sem.at[1 + feeds + j],
            )
        )
    return copies


def feed_arrival(rest_ref, inner, outer, sem, j):
    feeds = inner.shape[0]
    unit = inner.shape[2]
    pltpu.make_async_copy(rest_ref.at[:, :unit, :], inner.at[j], sem.at[1 + j]).wait()
    pltpu.make_async_copy(
        rest_ref.at[: outer.shape[1], : outer.shape[2], :], outer.at[j], sem.at[1 + feeds + j]
    ).wait()


def feed_buffers(rest, feeds):
    count, _, width = rest.shape
    unit = width // count
    return [
        pltpu.VMEM((count, unit, width), low),
        pltpu.VMEM((feeds, count, unit, width), low),
        pltpu.VMEM((feeds, count // feeds, feeds * unit, width), low),
        pltpu.SemaphoreType.DMA((1 + 2 * feeds,)),
    ]


def feed_kernel(
    attended_ref,
    tokens_ref,
    rest_ref,
    gains_ref,
    hidden_ref,
    pre_ref,
    encoded_ref,
    context_ref,
    out,
    inner,
    outer,
    sem,
    inner_in,
):
    width = tokens_ref.shape[1]
    feeds = pre_ref.shape[0]
    copies = feed_weights(rest_ref, out, inner, outer, sem)
    copies[0].start()
    for j in range(feeds):
        copies[1 + j].start()
        copies[1 + feeds + j].start()
    copies[0].wait()
    hidden = tokens_ref[...].astype(wide) + product(
        attended_ref[...].astype(low), out[...].reshape(width, width)
    )
    hidden_ref[...] = hidden
    inner_in[...] = (hidden * rms_factor(hidden) * gains_ref[1:2, :]).astype(low)
    encoded_ref[...] = hidden

    def step(j, carry):
        feed_arrival(rest_ref, inner, outer, sem, j)
        pre = product(inner_in[...], inner[j].reshape(width, width))
        pre_ref[j] = pre.astype(low)
        encoded_ref[...] += product(
            gelu_value(pre).astype(low), outer[j].reshape(width, width)
        )
        return carry

    lax.fori_loop(0, feeds, step, 0)
    encoded = encoded_ref[...]
    context_ref[...] = (encoded * rms_factor(encoded) * gains_ref[2:3, :]).astype(low)


def feed_forward(attended, tokens, rest, gains, feeds):
    rows, width = tokens.shape
    whole = pl.BlockSpec(memory_space=pltpu.VMEM)
    return pl.pallas_call(
        feed_kernel,
        name="feed_forward",
        in_specs=[whole, whole, pl.BlockSpec(memory_space=pl.ANY), whole],
        out_specs=[whole] * 4,
        out_shape=[
            jax.ShapeDtypeStruct((rows, width), wide),
            jax.ShapeDtypeStruct((feeds, rows, width), low),
            jax.ShapeDtypeStruct((rows, width), wide),
            jax.ShapeDtypeStruct((rows, width), low),
        ],
        scratch_shapes=feed_buffers(rest, feeds) + [pltpu.VMEM((rows, width), low)],
        compiler_params=pltpu.CompilerParams(vmem_limit_bytes=50 * 2**20),
        cost_estimate=pl.CostEstimate(
            flops=18 * rows * width * width, bytes_accessed=40 * width * width, transcendentals=0
        ),
    )(attended, tokens, rest, gains)


def feed_back_kernel(
    base,
    groups,
    members,
    grad_context_ref,
    encoded_ref,
    hidden_ref,
    pre_ref,
    attended_ref,
    rest_ref,
    gains_ref,
    rows_ref,
    starts_ref,
    parts_ref,
    grad_hidden_ref,
    grad_attended_ref,
    sums_ref,
    backs_ref,
    out,
    inner,
    outer,
    sem,
    inner_in,
    grad_branch,
    grad_inner_in,
    outer_grad,
    inner_grad,
    grad_sem,
    weights,
    sides,
    weight_sem,
    send_sem,
    recv_sem,
):
    rows, width = encoded_ref.shape
    feeds = pre_ref.shape[0]
    count = rest_ref.shape[0]
    unit = width // count
    lines = groups // 4
    group = lax.axis_index("batch")
    member = lax.axis_index("seq")

    partners = []
    for axis, place, number in (("batch", group, groups), ("seq", member, members)):
        span = 1
        while span < number:
            bit = lax.rem(place // span, 2)
            partners.append({axis: place + span * (1 - 2 * bit)})
            span *= 2
    barrier = pltpu.get_barrier_semaphore()
    for partner in partners:
        pl.semaphore_signal(barrier, inc=1, device_id=partner, device_id_type=MESH)

    def swap(i):
        return pltpu.make_async_remote_copy(
            src_ref=sides.at[2 * i],
            dst_ref=sides.at[2 * i + 1],
            send_sem=send_sem.at[i],
            recv_sem=recv_sem.at[i],
            device_id=partners[i],
            device_id_type=MESH,
        )

    def swapped(i):
        swap(i).wait()
        sides[2 * i + 2] = sides[2 * i] + sides[2 * i + 1]
        if i + 1 < len(partners):
            swap(i + 1).start()

    copies = feed_weights(rest_ref, out, inner, outer, sem)
    for j in range(feeds):
        copies[1 + feeds + j].start()
        copies[1 + j].start()
    copies[0].start()
    start_copies = [
        pltpu.make_async_copy(
            rest_ref.at[:, base + unit * i : base + unit * (i + 1), :],
            weights.at[i],
            weight_sem.at[i],
        )
        for i in range(4)
    ]
    for copy in start_copies:
        copy.start()
    sides[0] = rows_ref[...]
    hidden = hidden_ref[...]
    inner_in[...] = (hidden * rms_factor(hidden) * gains_ref[1:2, :]).astype(low).T
    grad_encoded, _ = rms_back(encoded_ref[...], gains_ref[2:3, :], grad_context_ref[...])
    grad_hidden_ref[...] = grad_encoded
    grad_branch[...] = grad_encoded.astype(low)
    grad_inner_in[...] = jnp.zeros_like(grad_inner_in)
    pl.semaphore_wait(barrier, len(partners))
    swap(0).start()

    def outer_put(j, slot):
        per = lines // feeds
        return pltpu.make_async_copy(
            outer_grad.at[slot],
            parts_ref.at[pl.ds(j * per, per), :, :, 1 + feeds :],
            grad_sem.at[0, slot],
        )

    def inner_put(j, slot):
        return pltpu.make_async_copy(
            inner_grad.at[slot], parts_ref.at[:, :, :, 1 + j], grad_sem.at[1, slot]
        )

    def step(j, carry):
        slot = lax.rem(j, 2)
        feed_arrival(rest_ref, inner, outer, sem, j)
        pre = pre_ref[j].astype(wide)
        grad_act = back_product(grad_branch[...], outer[j].reshape(width, width))
        grad_pre = (gelu_slope(pre) * grad_act).astype(low)
        grad_inner_in[...] += back_product(grad_pre, inner[j].reshape(width, width))
        act = gelu_value(pre).astype(low)

        @pl.when(j >= 2)
        def _():
            outer_put(j - 2, slot).wait()
            inner_put(j - 2, slot).wait()

        outer_grad[slot] = (
            weight_grad(act, grad_branch[...]).reshape(outer_grad.shape[1:]).astype(low)
        )
        outer_put(j, slot).start()
        inner_grad[slot] = (
            product(inner_in[...], grad_pre).reshape(inner_grad.shape[1:]).astype(low)
        )
        inner_put(j, slot).start()
        for i in range(min(feeds, len(partners))):

            @pl.when(j == i)
            def _():
                swapped(i)

        return carry

    lax.fori_loop(0, feeds, step, 0)
    grad_hidden, _ = rms_back(hidden_ref[...], gains_ref[1:2, :], grad_inner_in[...])
    grad_hidden = grad_hidden + grad_hidden_ref[...]
    grad_hidden_ref[...] = grad_hidden
    grad_branch[...] = grad_hidden.astype(low)
    copies[0].wait()
    grad_attended_ref[...] = back_product(
        grad_branch[...], out[...].reshape(width, width)
    ).astype(low)
    for j in range(feeds - 2, feeds):
        outer_put(j, j % 2).wait()
        inner_put(j, j % 2).wait()
    inner_grad[0] = (
        weight_grad(attended_ref[...].astype(low), grad_branch[...])
        .reshape(inner_grad.shape[1:])
        .astype(low)
    )
    out_put = pltpu.make_async_copy(
        inner_grad.at[0], parts_ref.at[:, :, :, 0], grad_sem.at[1, 0]
    )
    out_put.start()

    for i in range(feeds, len(partners)):
        swapped(i)
    sums = sides[2 * len(partners)]
    sums_ref[...] = sums
    for copy in start_copies:
        copy.wait()

    def weight(i):
        return weights[i].reshape(width, width)

    head_row = lax.broadcasted_iota(jnp.int32, (HEAD_ROWS, width), 0)
    head_mask = head_row == lax.broadcasted_iota(jnp.int32, (HEAD_ROWS, width), 1) // HEAD
    spread = product(sums[:HEAD_ROWS].astype(low), weight(3))
    grad_cross_query = jnp.sum(jnp.where(head_mask, spread, 0.0), axis=0, keepdims=True)
    grad_cross_query = grad_cross_query.astype(low)

    def widened(row):
        return jnp.broadcast_to(row.astype(wide), (SEQ_ROWS, width))

    start = widened(starts_ref[0:1, :])
    after_self = widened(starts_ref[3:4, :])
    grad_rows = back_product(widened(grad_cross_query).astype(low), weight(2))
    grad_after_self, _ = rms_back(after_self, gains_ref[5:6, :], grad_rows)
    cross_gain = grad_rows * after_self * rms_factor(after_self)
    grad_after_self = grad_after_self + widened(sums[HEAD_ROWS : HEAD_ROWS + 1])
    grad_self_branch = grad_after_self.astype(low)
    grad_self_vals = back_product(grad_self_branch, weight(1)).astype(low)
    grad_rows = back_product(grad_self_vals, weight(0))
    grad_start, _ = rms_back(start, gains_ref[4:5, :], grad_rows)
    self_gain = grad_rows * start * rms_factor(start)
    for i, row in enumerate(
        (
            grad_start + grad_after_self,
            self_gain,
            cross_gain,
            grad_cross_query,
            grad_self_branch,
            grad_self_vals,
        )
    ):
        backs_ref[i : i + 1, :] = row[:1].astype(wide)
    backs_ref[6:, :] = jnp.zeros((2, width), wide)
    out_put.wait()


def feed_back(
    grad_context, encoded, hidden, pre, attended, rest, base, gains, sum_rows, starts, groups, members, part
):
    rows, width = encoded.shape
    feeds = pre.shape[0]
    lines = groups // 4
    count = rest.shape[0]
    many = sum_rows.shape[0]
    partners = (groups.bit_length() - 1) + (members.bit_length() - 1)
    whole = pl.BlockSpec(memory_space=pltpu.VMEM)
    anywhere = pl.BlockSpec(memory_space=pl.ANY)
    return pl.pallas_call(
        functools.partial(feed_back_kernel, base, groups, members),
        name="feed_back",
        in_specs=[whole] * 5 + [anywhere] + [whole] * 3,
        out_specs=[anywhere] + [whole] * 4,
        out_shape=[
            jax.ShapeDtypeStruct((lines, 2, 2, 1 + 2 * feeds, part, width), low),
            jax.ShapeDtypeStruct((rows, width), wide),
            jax.ShapeDtypeStruct((rows, width), low),
            jax.ShapeDtypeStruct((many, width), wide),
            jax.ShapeDtypeStruct((8, width), wide),
        ],
        scratch_shapes=feed_buffers(rest, feeds)
        + [
            pltpu.VMEM((width, rows), low),
            pltpu.VMEM((rows, width), low),
            pltpu.VMEM((rows, width), wide),
            pltpu.VMEM((2, lines // feeds, 2, 2, feeds, part, width), low),
            pltpu.VMEM((2, lines, 2, 2, part, width), low),
            pltpu.SemaphoreType.DMA((2, 2)),
            pltpu.VMEM((4, count, width // count, width), low),
            pltpu.VMEM((2 * partners + 1, many, width), wide),
            pltpu.SemaphoreType.DMA((4,)),
            pltpu.SemaphoreType.DMA((partners,)),
            pltpu.SemaphoreType.DMA((partners,)),
        ],
        compiler_params=pltpu.CompilerParams(
            collective_id=2, has_side_effects=True, vmem_limit_bytes=60 * 2**20
        ),
        cost_estimate=pl.CostEstimate(
            flops=36 * rows * width * width, bytes_accessed=80 * width * width, transcendentals=0
        ),
    )(
        grad_context, encoded, hidden, pre, attended, rest, gains, sum_rows, starts
    )


def attend_back_kernel(
    groups,
    members,
    place,
    q_ref,
    k_ref,
    v_ref,
    grad_ref,
    attended_ref,
    total_ref,
    near_ref,
    own_turned_ref,
    all_turned_ref,
    parts_ref,
    grad_q_ref,
    grad_k_ref,
    grad_v_ref,
    table_ref,
    out_sums_ref,
    inner_sums_ref,
    outer_sums_ref,
    query_sums_ref,
    key_sums_ref,
    value_sums_ref,
    bias,
    key_side,
    value_side,
    keys_turned,
    grad_scores,
    grad_k_sum,
    grad_v_sum,
    band_sum,
    grad_q_sum,
    pair_grads,
    fetched,
    held,
    fetch_sem,
    bands,
    kept,
    sent,
    got,
    keep_send,
    keep_recv,
    tables,
    table_send,
    table_recv,
    *buffers,
):
    pair = pl.program_id(0)
    block = pl.program_id(1)
    blocks = pl.num_programs(1)
    pairs = pl.num_programs(0)
    now = pair * blocks + block
    pack = k_ref.shape[0]
    size = q_ref.shape[0]
    middle, reach, lead, width = table_sizes(size, pack)
    ends = (place[0], place[1])
    rows_here = size * blocks
    summing = Summing(groups, members, buffers)
    first = summing.member * rows_here + block * size
    shift = lax.rem(summing.member * rows_here, LANES) if size % LANES else 0
    barrier = pltpu.get_barrier_semaphore()
    feed_chunks = 2 * parts_ref.shape[3]
    feeds = (parts_ref.shape[3] - 1) // 2
    half_width = fetched.shape[-1]
    part = fetched.shape[-2]
    lines = groups // 4
    delays = stage_delays(lines)

    def feed_part(chunk, core):
        return parts_ref.at[
            :, :, core, chunk // 2, :, pl.ds(pl.multiple_of(lax.rem(chunk, 2) * half_width, LANES), half_width)
        ]

    def fetch(chunk):
        slot = lax.rem(chunk, 4)
        return pltpu.make_async_copy(
            feed_part(chunk, summing.core), fetched.at[slot], fetch_sem.at[slot]
        )

    def feed_stage(stage, chunk):
        if stage == 0:
            summing.start(chunk, feed_part(chunk, 1 - summing.core))
            fetch(chunk).start()
        elif stage == 1:
            fetch(chunk).wait()
            summing.to_pair(
                chunk, feed_part(chunk, 1 - summing.core), fetched[lax.rem(chunk, 4)]
            )
        elif stage <= lines:
            summing.to_line(chunk, stage - 2)
        elif stage == lines + 1:
            summing.to_members(chunk, held)
        else:
            total = summing.result(chunk)
            piece = chunk // 2
            column = pl.multiple_of(lax.rem(chunk, 2) * half_width, LANES)

            @pl.when(piece == 0)
            def _():
                out_sums_ref[:, pl.ds(column, half_width)] = total

            @pl.when((piece > 0) & (piece <= feeds))
            def _():
                at = pl.multiple_of((piece - 1) * 2 * half_width + column, LANES)
                inner_sums_ref[:, pl.ds(at, half_width)] = total

            @pl.when(piece > feeds)
            def _():
                at = pl.multiple_of((piece - 1 - feeds) * part, 8)
                outer_sums_ref[pl.ds(at, part), pl.ds(column, half_width)] = total

    def pair_stage(stage, which):
        chunk = feed_chunks + which
        if stage == 0:
            summing.start(chunk, pair_grads.at[which, :, :, 1 - summing.core])
        elif stage == 1:
            summing.to_pair(
                chunk,
                pair_grads.at[which, :, :, 1 - summing.core],
                pair_grads[which, :, :, summing.core],
            )
        elif stage <= lines:
            summing.to_line(chunk, stage - 2)
        elif stage == lines + 1:
            summing.to_members(chunk, held)
        else:
            total = summing.result(chunk)
            span = pl.ds(pl.multiple_of(which * LANES, LANES), LANES)
            for i, sums_ref in enumerate((query_sums_ref, key_sums_ref, value_sums_ref)):
                sums_ref[:, span] = total[:, LANES * i : LANES * (i + 1)]

    def keep_copy(which, step):
        return summing.copy(
            sent.at[which, step - 1],
            got.at[which, step - 1],
            keep_send.at[which, step - 1],
            keep_recv.at[which, step - 1],
            {"seq": lax.rem(summing.member + step, members)},
        )

    def keep_result(which):
        total = [kept[lax.rem(which, 2), i] for i in range(2)]
        for step in range(1, members):
            keep_copy(which, step).wait()
            total = [total[i] + got[which, step - 1, i].astype(wide) for i in range(2)]
        span = pl.ds(pl.multiple_of(which * LANES, LANES), LANES)
        grad_k_ref[:, span] = total[0].astype(low)
        grad_v_ref[:, span] = total[1].astype(low)

    partners = []
    for axis, spot, number in (
        ("batch", summing.group, groups),
        ("seq", summing.member, members),
    ):
        reach_out = 1
        while reach_out < number:
            bit = lax.rem(spot // reach_out, 2)
            partners.append({axis: spot + reach_out * (1 - 2 * bit)})
            reach_out *= 2

    def swap(i):
        return summing.copy(
            tables.at[2 * i],
            tables.at[2 * i + 1],
            table_send.at[i],
            table_recv.at[i],
            partners[i],
        )

    def swapped(i):
        swap(i).wait()
        tables[2 * i + 2] = tables[2 * i] + tables[2 * i + 1]
        if i + 1 < len(partners):
            swap(i + 1).start()

    @pl.when(now == 0)
    def _():
        peers = summing.neighbours()
        for i in range(len(partners)):
            peers.append((None, partners[i]))
        for condition, device in peers:
            if condition is None:
                pl.semaphore_signal(barrier, inc=1, device_id=device, device_id_type=MESH)
            else:

                @pl.when(condition)
                def _():
                    pl.semaphore_signal(barrier, inc=1, device_id=device, device_id_type=MESH)

        edges = (summing.z > 0).astype(jnp.int32) + (summing.z < lines - 1).astype(jnp.int32)
        pl.semaphore_wait(barrier, 2 + members - 1 + edges + len(partners))

    stages = 3 + lines
    starts = [0] + delays
    total_steps = pairs * blocks

    def run_stages(step):
        for stage in reversed(range(stages)):
            chunk = step - starts[stage]

            @pl.when((chunk >= 0) & (chunk < feed_chunks))
            def _():
                feed_stage(stage, chunk)

            late = step - (blocks - 1) - starts[stage]

            @pl.when((late >= 0) & (lax.rem(late + 64 * blocks, blocks) == 0) & (late < total_steps))
            def _():
                pair_stage(stage, late // blocks)

    @pl.when(now == 0)
    def _():
        tables[0] = jnp.zeros_like(tables[0])
        bands[...] = jnp.zeros_like(bands)

    @pl.when(block == 0)
    def _():
        places = lax.broadcasted_iota(jnp.int32, (pack, LANES), 0)
        lane = lax.broadcasted_iota(jnp.int32, (pack, LANES), 1)
        key_side[:, :LANES] = k_ref[...]
        ones = (segment_of(places, ends) == lane) | ((lane >= 3) & (lane < 9))
        key_side[:, LANES:] = ones.astype(wide).astype(low)
        value_side[:, :LANES] = v_ref[...]
        value_side[:, LANES:] = (lane < 6).astype(wide).astype(low)
        keys_turned[...] = k_ref[...].T
        for half in range(2):
            row = near_ref[half]
            before = middle - LANES
            after = middle + reach
            bias[half, before:after, :] = turned_biases(row, size, lead).T.astype(low)
            if before > 0:
                bias[half, :before, :] = jnp.broadcast_to(row[:, :1], (before, size)).astype(low)
            if after < width:
                bias[half, after:, :] = jnp.broadcast_to(
                    row[:, -1:], (width - after, size)
                ).astype(low)
        grad_scores[...] = jnp.zeros_like(grad_scores)
        grad_k_sum[...] = jnp.zeros_like(grad_k_sum)
        grad_v_sum[...] = jnp.zeros_like(grad_v_sum)
        band_sum[...] = jnp.zeros_like(band_sum)

    lane = lax.broadcasted_iota(jnp.int32, (size, LANES), 1)
    rows = first + lax.broadcasted_iota(jnp.int32, (size, LANES), 0)
    apart = jnp.where((segment_of(rows, ends) != lane) & (lane < 3), -far_apart, 0.0)
    start = pl.multiple_of(middle - (first - shift), LANES)
    near_rows = pl.ds(pl.multiple_of(first - shift, LANES), LANES + reach)
    queries = q_ref[...]
    grads = grad_ref[...]
    products = grads.astype(wide) * attended_ref[...]
    totals = total_ref[...]

    def in_parts(column, at):
        head = column.astype(low).astype(wide)
        body = (column - head).astype(low).astype(wide)
        tail = column - head - body
        return jnp.where(
            lane == at,
            head,
            jnp.where(lane == at + 1, body, jnp.where(lane == at + 2, tail, 0.0)),
        )

    query_grads = []
    for half in range(2):
        mine = (lane >= HEAD) if half else (lane < HEAD)
        row_term = jnp.sum(jnp.where(mine, products, 0.0), axis=1, keepdims=True)
        row_total = jnp.sum(
            jnp.where(lane == 2 * pair + half, totals, 0.0), axis=1, keepdims=True
        )
        query_part = jnp.where(mine, queries, jnp.zeros_like(queries))
        grad_part = jnp.where(mine, grads, jnp.zeros_like(grads))
        query_side = jnp.concatenate(
            [query_part, (apart - in_parts(row_total, 3 + 3 * half)).astype(low)], axis=1
        )
        grad_side = jnp.concatenate(
            [grad_part, (-in_parts(row_term, 3 * half)).astype(low)], axis=1
        )
        weights = jnp.exp(
            back_product(key_side[...], query_side)
            + bias[half, pl.ds(start, pack), :].astype(wide)
        )
        grad_block = (weights * back_product(value_side[...], grad_side)).astype(low)
        grad_scores[LANES : LANES + pack, :] = grad_block
        grad_v_sum[...] += product(weights.astype(low), grad_part)
        block_lane = jnp.where(lane == 8 * half + block, 1.0, 0.0).astype(low)
        grad_k_sum[...] += product(
            grad_block, jnp.concatenate([query_part, block_lane], axis=1)
        )
        query_grads.append(product(keys_turned[HEAD * half : HEAD * (half + 1), :], grad_block))
        band_sum[half] += grad_scores[near_rows, :].astype(wide)
    grad_query = jnp.concatenate(query_grads, axis=0).T.astype(low)
    grad_q_ref[...] = grad_query
    grad_q_sum[pl.ds(pl.multiple_of(block * size, 64), size), :] = grad_query

    @pl.when(block == blocks - 1)
    def _():
        grad_key = grad_k_sum[:, :LANES].astype(low)
        grad_value = grad_v_sum[...].astype(low)

        @pl.when(pair > 0)
        def _():
            keep_result(pair - 1)

        for step in range(1, members):
            other = pl.multiple_of(lax.rem(summing.member + step, members) * rows_here, 64)
            sent[pair, step - 1, 0] = grad_k_sum[pl.ds(other, rows_here), :LANES].astype(low)
            sent[pair, step - 1, 1] = grad_v_sum[pl.ds(other, rows_here), :].astype(low)
            keep_copy(pair, step).start()
        mine_rows = pl.ds(pl.multiple_of(summing.member * rows_here, 64), rows_here)
        kept[lax.rem(pair, 2), 0] = grad_k_sum[mine_rows, :LANES]
        kept[lax.rem(pair, 2), 1] = grad_v_sum[mine_rows, :]
        for i, gradient in enumerate(
            (
                product(own_turned_ref[...], grad_q_sum[...]),
                product(all_turned_ref[...], grad_key),
                product(all_turned_ref[...], grad_value),
            )
        ):
            pair_grads[pair, :, :, :, :, LANES * i : LANES * (i + 1)] = gradient.reshape(
                lines, 2, 2, part, LANES
            ).astype(low)
        key = lax.broadcasted_iota(jnp.int32, (pack, LANES), 0)
        which = lax.broadcasted_iota(jnp.int32, (pack, LANES), 1) % 8
        begin = summing.member * rows_here - shift + size * which
        sums = grad_k_sum[:, LANES:]
        below = jnp.sum(jnp.where(key < begin - LANES, sums, 0.0), axis=0, keepdims=True)
        above = jnp.sum(jnp.where(key >= begin + reach, sums, 0.0), axis=0, keepdims=True)
        columns = bands.shape[1]
        mirror = (
            lax.broadcasted_iota(jnp.int32, (size, size), 0)
            + lax.broadcasted_iota(jnp.int32, (size, size), 1)
            == size - 1
        ).astype(wide).astype(low)
        row_lane = lax.broadcasted_iota(jnp.int32, (1, LANES), 1)
        for half in range(2):
            rest = band_sum[half]
            flipped = jnp.zeros_like(rest)
            for _ in range(3):
                head_part = rest.astype(low)
                flipped = flipped + product(head_part, mirror)
                rest = rest - head_part.astype(wide)
            padded = jnp.concatenate(
                [flipped, jnp.zeros((rest.shape[0], columns - size), wide)], axis=1
            )
            turned = pltpu.roll(padded, 0, 1, stride=1, stride_axis=0)
            head = pl.ds(2 * pair + half, 1)
            bands[head, :] = jnp.sum(turned, axis=0, keepdims=True)
            own_lanes = row_lane // 8 == half
            low_sum = jnp.sum(jnp.where(own_lanes, below, 0.0), axis=1, keepdims=True)
            high_sum = jnp.sum(jnp.where(own_lanes, above, 0.0), axis=1, keepdims=True)
            tables[0, head, :] = jnp.where(row_lane == 15, low_sum, 0.0) + jnp.where(
                row_lane == 31, high_sum, 0.0
            )

    run_stages(now)

    @pl.when(now == total_steps - 1)
    def _():
        columns = bands.shape[1]
        offset = (
            lax.broadcasted_iota(jnp.int32, (columns, LANES), 0) - (size - 1) - LANES - shift
        )
        onehot = (
            bucket_of(offset) == lax.broadcasted_iota(jnp.int32, (columns, LANES), 1)
        ).astype(wide)
        tables[0] += jnp.dot(
            bands[...], onehot, precision=highest, preferred_element_type=wide
        )
        swap(0).start()

        def drain(step, carry):
            run_stages(step)
            for i in range(len(partners)):

                @pl.when(step == total_steps + i)
                def _():
                    swapped(i)

            return carry

        final = max(starts[-1] + 1, len(partners))
        lax.fori_loop(total_steps, total_steps + final, drain, 0)
        keep_result(pairs - 1)
        table_ref[...] = tables[2 * len(partners)]


def attend_back(
    queries, all_keys, all_values, grads, attended, totals, near, place, own_turned, all_turned, parts
):
    rows, width = queries.shape
    pack = all_keys.shape[0]
    size = block_rows(rows)
    _, reach, _, columns = table_sizes(size, pack)
    band = -(-(size + LANES + reach) // LANES) * LANES
    pairs = width // LANES
    members = pack // rows
    pieces = parts.shape[3]
    part = parts.shape[4]
    groups = 4 * parts.shape[0]
    half_width = width // 2
    chunks = 2 * pieces + pairs

    def own(p, i):
        return (i, p)

    def every(p, i):
        return (0, p)

    whole = pl.BlockSpec(memory_space=pltpu.VMEM)
    partners = (groups.bit_length() - 1) + (members.bit_length() - 1)
    feeds = (pieces - 1) // 2
    return pl.pallas_call(
        functools.partial(attend_back_kernel, groups, members),
        name="attend_back",
        grid=(pairs, rows // size),
        in_specs=[
            pl.BlockSpec(memory_space=pltpu.SMEM),
            pl.BlockSpec((size, LANES), own),
            pl.BlockSpec((pack, LANES), every),
            pl.BlockSpec((pack, LANES), every),
            pl.BlockSpec((size, LANES), own),
            pl.BlockSpec((size, LANES), own),
            pl.BlockSpec((size, LANES), lambda p, i: (i, 0)),
            pl.BlockSpec((2, 1, near.shape[2]), lambda p, i: (p, 0, 0)),
            whole,
            whole,
            pl.BlockSpec(memory_space=pl.ANY),
        ],
        out_specs=[
            pl.BlockSpec((size, LANES), own),
        ]
        + [whole] * 9,
        out_shape=[
            jax.ShapeDtypeStruct((rows, width), low),
            jax.ShapeDtypeStruct((rows, width), low),
            jax.ShapeDtypeStruct((rows, width), low),
            jax.ShapeDtypeStruct((16, LANES), wide),
            jax.ShapeDtypeStruct((part, width), wide),
            jax.ShapeDtypeStruct((part, feeds * width), wide),
            jax.ShapeDtypeStruct((feeds * part, width), wide),
            jax.ShapeDtypeStruct((part, width), wide),
            jax.ShapeDtypeStruct((part, width), wide),
            jax.ShapeDtypeStruct((part, width), wide),
        ],
        scratch_shapes=[
            pltpu.VMEM((2, columns, size), low),
            pltpu.VMEM((pack, 2 * LANES), low),
            pltpu.VMEM((pack, 2 * LANES), low),
            pltpu.VMEM((LANES, pack), low),
            pltpu.VMEM((LANES + pack + reach, size), low),
            pltpu.VMEM((pack, 2 * LANES), wide),
            pltpu.VMEM((pack, LANES), wide),
            pltpu.VMEM((2, LANES + reach, size), wide),
            pltpu.VMEM((rows, LANES), low),
            pltpu.VMEM((pairs, groups // 4, 2, 2, part, half_width), low),
            pltpu.VMEM((4, groups // 4, 2, part, half_width), low),
            pltpu.VMEM((part, half_width), wide),
            pltpu.SemaphoreType.DMA((4,)),
            pltpu.VMEM((16, band), wide),
            pltpu.VMEM((2, 2, rows, LANES), wide),
            pltpu.VMEM((pairs, max(members - 1, 1), 2, rows, LANES), low),
            pltpu.VMEM((pairs, max(members - 1, 1), 2, rows, LANES), low),
            pltpu.SemaphoreType.DMA((pairs, max(members - 1, 1))),
            pltpu.SemaphoreType.DMA((pairs, max(members - 1, 1))),
            pltpu.VMEM((2 * partners + 1, 16, LANES), wide),
            pltpu.SemaphoreType.DMA((partners,)),
            pltpu.SemaphoreType.DMA((partners,)),
        ]
        + summing_scratch(groups, members, chunks, part, half_width),
        compiler_params=pltpu.CompilerParams(
            collective_id=1, has_side_effects=True, vmem_limit_bytes=62 * 2**20
        ),
        cost_estimate=pl.CostEstimate(
            flops=20 * rows * pack * width * 2, bytes_accessed=16 * pack * width, transcendentals=0
        ),
    )(
        place,
        queries,
        all_keys,
        all_values,
        grads,
        attended,
        totals,
        near,
        own_turned,
        all_turned,
        parts,
    )


def last_kernel(
    groups,
    seqs,
    halves,
    grad_q_any,
    grad_k_any,
    grad_v_any,
    first_any,
    grad_hidden_any,
    rows_any,
    query_any,
    key_any,
    value_any,
    inner_any,
    attention_any,
    outer_any,
    tokens_ref,
    gains_ref,
    sums_ref,
    starts_ref,
    backs_ref,
    query_ref,
    key_ref,
    value_ref,
    inner_ref,
    cross_key_ref,
    cross_value_ref,
    embedded_ref,
    loss_ref,
    table_ref,
    grad_tokens_ref,
    vectors_ref,
    grad_self_value_ref,
    grad_self_out_ref,
    grad_cross_query_ref,
    grad_cross_key_ref,
    grad_cross_value_ref,
    grad_cross_out_ref,
    grad_second_inner_ref,
    grad_second_outer_ref,
    grad_pooler_ref,
    query_sums_ref,
    key_sums_ref,
    value_sums_ref,
    inner_sums_ref,
    attention_sums_ref,
    outer_sums_ref,
    embedded_out,
    loss_out,
    table_out,
    pieces,
    grad_q_ref,
    grad_k_ref,
    grad_v_ref,
    first_ref,
    grad_hidden_ref,
    rows_ref,
    copy_sem,
):
    rows, width = tokens_ref.shape
    part = query_ref.shape[0]
    feeds = inner_ref.shape[1] // width
    number = groups * seqs
    every = 2 * HEAD_ROWS
    group = lax.axis_index("batch")
    copies = [
        pltpu.make_async_copy(source, target, copy_sem.at[i])
        for i, (source, target) in enumerate(
            (
                (rows_any, rows_ref),
                (grad_q_any, grad_q_ref),
                (grad_k_any, grad_k_ref),
                (grad_v_any, grad_v_ref),
                (first_any, first_ref),
                (grad_hidden_any, grad_hidden_ref),
                (query_any, query_sums_ref),
                (key_any, key_sums_ref),
                (value_any, value_sums_ref),
                (inner_any, inner_sums_ref),
                (attention_any, attention_sums_ref),
                (outer_any, outer_sums_ref),
            )
        )
    ]
    for copy in copies:
        copy.start()
    embedded_out[...] = embedded_ref[:seqs, :]
    loss_out[...] = loss_ref[:1, :1]
    buckets = table_out.shape[0]
    bucket_row = lax.broadcasted_iota(jnp.int32, (8, LANES), 0)
    bucket_column = lax.broadcasted_iota(jnp.int32, (8, LANES), 1)
    own_buckets = (bucket_column == group * buckets + bucket_row).astype(wide)
    table_out[...] = lax.dot_general(
        own_buckets,
        table_ref[...],
        (((1,), (1,)), ((), ())),
        precision=highest,
        preferred_element_type=wide,
    )[:buckets, :HEADS]
    copies[0].wait()

    def chooser(count, first):
        row = lax.broadcasted_iota(jnp.int32, (count, width), 0)
        column = lax.broadcasted_iota(jnp.int32, (count, width), 1)
        return column == first + row

    chosen = chooser(part, group * part)
    choose = chosen.astype(wide).astype(low)
    tiles = width // LANES
    for i in range(tiles):
        pieces[i] = (
            rows_ref[:, :, LANES * i : LANES * (i + 1)].reshape(number * every, LANES).astype(wide)
        )

    def piece(at):
        return jnp.concatenate(
            [pieces[i, pl.ds(at, number, stride=every), :] for i in range(tiles)], axis=1
        ).astype(low)

    def own(values, which=None):
        which = choose if which is None else which
        return lax.dot_general(
            which, values, (((1,), (1,)), ((), ())), preferred_element_type=wide
        ).astype(low)

    def pair(left, right):
        return product(left, right)

    grad_cross_out_ref[...] = pair(own(piece(0)), piece(7))
    second_in = own(piece(1))
    grad_second_inner = [pair(second_in, piece(8 + j)) for j in range(feeds)]
    share = grad_second_outer_ref.shape[0]
    half = share // halves
    per = width // half
    grad_out = piece(12)
    for i in range(halves):
        chunk = group // per
        at = lax.rem(group, per) * half
        which = chooser(half, at).astype(wide).astype(low)
        found = jnp.zeros((half, number), wide)
        for j in range(feeds // halves):
            here = own(piece(2 + feeds // halves * i + j), which).astype(wide)
            found = jnp.where(chunk == j, here, found)
        grad_second_outer_ref[half * i : half * (i + 1), :] = pair(found.astype(low), grad_out)
    for j in range(feeds):
        grad_second_inner_ref[:, width * j : width * (j + 1)] = grad_second_inner[j]
    grad_pooler_ref[...] = pair(own(piece(6)), piece(13))

    mixed = rows_ref[:, HEAD_ROWS:, :].reshape(number * HEAD_ROWS, width)
    repeat = (
        lax.broadcasted_iota(jnp.int32, (number * HEAD_ROWS, number), 0) // HEAD_ROWS
        == lax.broadcasted_iota(jnp.int32, (number * HEAD_ROWS, number), 1)
    )
    heads = product(repeat.astype(wide).astype(low), piece(14))
    head = lax.broadcasted_iota(jnp.int32, heads.shape, 0) % HEAD_ROWS
    head_column = lax.broadcasted_iota(jnp.int32, heads.shape, 1) // HEAD
    heads = jnp.where(head == head_column, heads, 0.0).astype(low)
    grad_cross_value = pair(own(mixed), heads)
    grad_cross_value_ref[...] = grad_cross_value

    def exact(left, right):
        return lax.dot_general(
            left,
            right,
            (((1,), (1,)), ((), ())),
            precision=highest,
            preferred_element_type=wide,
        )

    chosen = chosen.astype(wide)
    key_rows = exact(chosen, sums_ref[:HEAD_ROWS, :])
    head_row = lax.broadcasted_iota(jnp.int32, (HEAD_ROWS, width), 0)
    head_mask = head_row == lax.broadcasted_iota(jnp.int32, (HEAD_ROWS, width), 1) // HEAD
    query_row = starts_ref[5:6, :].astype(low).astype(wide)
    query_heads = jnp.where(head_mask, jnp.broadcast_to(query_row, (HEAD_ROWS, width)), 0.0)
    grad_cross_key = jnp.dot(
        key_rows, query_heads, precision=highest, preferred_element_type=wide
    )
    grad_cross_key_ref[...] = grad_cross_key
    starts = exact(chosen, starts_ref[...])
    grad_self_value_ref[...] = starts[:, 1:2] * backs_ref[5:6, :]
    grad_self_out_ref[...] = starts[:, 2:3] * backs_ref[4:5, :]
    grad_cross_query_ref[...] = starts[:, 4:5] * backs_ref[3:4, :]

    def gain_sum(weight, grads):
        ones = jnp.ones((8, grads.shape[1]), wide)
        return exact(ones, weight.astype(wide) * grads)[:1]

    for copy in copies[1:]:
        copy.wait()
    attention = (
        gain_sum(query_ref[...], query_sums_ref[...])
        + gain_sum(key_ref[...], key_sums_ref[...])
        + gain_sum(value_ref[...], value_sums_ref[...])
    )
    feed = gain_sum(inner_ref[...], inner_sums_ref[...])
    encoder = gain_sum(cross_key_ref[...], grad_cross_key) + gain_sum(
        cross_value_ref[...], grad_cross_value
    )
    gains = exact(gains_ref[:8, :], chosen)
    backs = exact(backs_ref[...], chosen)
    others = exact(sums_ref[HEAD_ROWS:, :], chosen)
    for i, row in enumerate(
        (
            attention / gains[0:1],
            feed / gains[1:2],
            encoder / gains[2:3],
            backs[0:1],
            backs[1:2],
            backs[2:3],
            others[2:3],
            others[1:2],
        )
    ):
        vectors_ref[i] = row

    grad_normed = (
        back_product(grad_q_ref[...], first_ref[0])
        + back_product(grad_k_ref[...], first_ref[1])
        + back_product(grad_v_ref[...], first_ref[2])
    )
    grad_tokens, _ = rms_back(tokens_ref[...].astype(wide), gains_ref[:1, :], grad_normed)
    grad_tokens_ref[...] = grad_tokens + grad_hidden_ref[...]


def last_step(groups, seqs, halves, tokens, part, share, feeds, *arrays):
    rows, width = tokens.shape
    whole = pl.BlockSpec(memory_space=pltpu.VMEM)
    square = jax.ShapeDtypeStruct((part, width), wide)
    return pl.pallas_call(
        functools.partial(last_kernel, groups, seqs, halves),
        name="last",
        in_specs=[pl.BlockSpec(memory_space=pltpu.HBM)] * 12
        + [whole] * (len(arrays) - 12),
        out_specs=[whole] * 20,
        out_shape=[
            jax.ShapeDtypeStruct((rows, width), wide),
            jax.ShapeDtypeStruct((8, 1, part), wide),
            square,
            square,
            square,
            square,
            square,
            square,
            jax.ShapeDtypeStruct((part, feeds * width), wide),
            jax.ShapeDtypeStruct((share, width), wide),
            square,
            square,
            square,
            square,
            jax.ShapeDtypeStruct((part, feeds * width), wide),
            square,
            jax.ShapeDtypeStruct((share, width), wide),
            jax.ShapeDtypeStruct((seqs, width), wide),
            jax.ShapeDtypeStruct((1, 1), wide),
            jax.ShapeDtypeStruct((BUCKETS // groups, HEADS), wide),
        ],
        scratch_shapes=[
            pltpu.VMEM((width // LANES, groups * seqs * 2 * HEAD_ROWS, LANES), wide),
            pltpu.VMEM((rows, width), low),
            pltpu.VMEM((rows, width), low),
            pltpu.VMEM((rows, width), low),
            pltpu.VMEM((3, width, width), low),
            pltpu.VMEM((rows, width), wide),
            pltpu.VMEM((groups * seqs, 2 * HEAD_ROWS, width), low),
            pltpu.SemaphoreType.DMA((12,)),
        ],
        compiler_params=pltpu.CompilerParams(vmem_limit_bytes=62 * 2**20),
    )(*arrays)


def in_blocks(gathered, sizes):
    count, _, width = gathered.shape
    join = 16 // math.gcd(16, sizes[0])
    if join == 1:
        return gathered
    pieces, at = [], 0
    for size in sizes:
        piece = gathered[:, at : at + size].reshape(count // join, join * size, width)
        pieces.append(piece)
        at += size
    return jnp.concatenate(pieces, axis=1)


def column_blocks(weight, model_width):
    rows, columns = weight.shape
    blocks = columns // model_width
    return jnp.transpose(weight.reshape(rows, blocks, model_width), (1, 0, 2)).reshape(
        blocks * rows, model_width
    )


def shards(
    tokens,
    lengths,
    labels,
    attention_gain,
    query_weight,
    key_weight,
    value_weight,
    attention_out,
    position_bias,
    feed_gain,
    feed_inner,
    feed_outer,
    encoder_gain,
    start_token,
    self_gain,
    self_value,
    self_out,
    cross_gain,
    cross_query,
    cross_key,
    cross_value,
    cross_out,
    second_gain,
    second_inner,
    second_outer,
    final_gain,
    pooler_weight,
):
    rows, width = tokens.shape
    part = query_weight.shape[0]
    share = feed_outer.shape[0]
    groups = lax.axis_size("batch")
    members = lax.axis_size("seq")
    blocks = feed_inner.shape[1] // width
    pack = rows * members
    seqs = lengths.shape[1]
    group = lax.axis_index("batch")
    member = lax.axis_index("seq")
    own_first = member * rows
    ends = jnp.cumsum(lengths[0])
    place = jnp.stack(
        [ends[0], ends[1], own_first, own_first % LANES]
    ).astype(jnp.int32)

    vectors = jnp.stack(
        [
            attention_gain,
            feed_gain,
            encoder_gain,
            start_token,
            self_gain,
            cross_gain,
            second_gain,
            final_gain,
        ],
        axis=0,
    )
    bias_part = position_bias.reshape(1, -1)
    bias_size = bias_part.shape[1]
    extra = jnp.zeros((16, width), low)
    extra = lax.dynamic_update_slice(extra, vectors, (0, group * part))
    extra = lax.dynamic_update_slice(extra, bias_part, (8, group * bias_size))
    queries, all_keys, all_values, normed_all, gains, first_full = project(
        tokens, extra, [query_weight, key_weight, value_weight], groups, members
    )
    table = gains[8, : BUCKETS * HEADS].reshape(BUCKETS, HEADS).astype(low)
    second_part = jnp.concatenate(
        [
            attention_out[None],
            column_blocks(feed_inner, width).reshape(blocks, part, width),
            feed_outer.reshape(blocks, part, width),
        ],
        axis=0,
    )
    halves = 2 if members == 2 else 1
    half_share = share // halves
    half_inner = lax.dynamic_slice_in_dim(
        second_inner.reshape(part, groups, share), member % halves * half_share, half_share, 2
    ).reshape(part, groups * half_share)
    half_outer = lax.dynamic_slice_in_dim(second_outer, member % halves * half_share, half_share)
    rest_part = jnp.concatenate(
        [
            second_part.reshape(-1, width),
            self_value,
            self_out,
            cross_query,
            cross_key,
            cross_value,
            cross_out,
            pooler_weight,
            column_blocks(half_inner, width),
            half_outer,
        ],
        axis=0,
    )
    rest = lax.all_gather(rest_part, "batch", axis=0, tiled=False)

    near = offset_biases(table, block_rows(rows), pack, place[3])
    attended, totals = attend(queries, all_keys, all_values, near, place)
    rest_blocks = in_blocks(
        rest,
        [part] * (1 + blocks) + [share] + [part] * (7 + blocks // halves) + [half_share],
    )
    base = (1 + 2 * blocks) * (width // rest_blocks.shape[0])
    hidden, inner_pre, encoded, context = feed_forward(
        attended, tokens, rest_blocks, gains, blocks
    )

    embedded, loss, grad_context, decoder_rows, starts, decoder_totals = decoder_step(
        context, rest_blocks, base, gains, labels, place, groups, members, seqs
    )
    decoder_rows = lax.all_gather(
        decoder_rows.reshape(seqs * 2 * HEAD_ROWS, width), "batch", axis=0, tiled=False
    )

    second_grads, grad_hidden, grad_attended, sums, backs = feed_back(
        grad_context,
        encoded,
        hidden,
        inner_pre,
        attended,
        rest_blocks,
        base,
        gains,
        decoder_totals,
        starts,
        groups,
        members,
        part,
    )
    normed = lax.dynamic_slice_in_dim(normed_all, own_first, rows)
    (
        grad_query_rows,
        grad_key_rows,
        grad_value_rows,
        table_sums,
        out_sums,
        inner_sums,
        outer_sums,
        query_sums,
        key_sums,
        value_sums,
    ) = attend_back(
        queries,
        all_keys,
        all_values,
        grad_attended,
        attended,
        totals,
        near,
        place,
        normed.T,
        normed_all.T,
        second_grads,
    )
    (
        grad_tokens,
        vectors,
        grad_self_value,
        grad_self_out,
        grad_cross_query,
        grad_cross_key,
        grad_cross_value,
        grad_cross_out,
        grad_second_inner,
        grad_second_outer,
        grad_pooler,
        query_sums,
        key_sums,
        value_sums,
        inner_sums,
        out_sums,
        outer_sums,
        embedded,
        loss,
        grad_table,
    ) = last_step(
        groups,
        seqs,
        halves,
        tokens,
        part,
        share,
        blocks,
        grad_query_rows,
        grad_key_rows,
        grad_value_rows,
        first_full,
        grad_hidden,
        decoder_rows.reshape(groups * seqs, 2 * HEAD_ROWS, width),
        query_sums,
        key_sums,
        value_sums,
        inner_sums,
        out_sums,
        outer_sums,
        tokens,
        gains,
        sums,
        starts,
        backs,
        query_weight,
        key_weight,
        value_weight,
        feed_inner,
        cross_key,
        cross_value,
        embedded,
        loss,
        table_sums,
    )
    half_share = share // halves
    grad_second_inner = jnp.transpose(
        grad_second_inner.reshape(part, halves, groups, half_share), (0, 2, 1, 3)
    ).reshape(part, blocks * width)
    vectors = vectors.reshape(8, part)
    return (
        loss.reshape(1),
        embedded,
        grad_tokens,
        vectors[0],
        query_sums,
        key_sums,
        value_sums,
        out_sums,
        grad_table,
        vectors[1],
        inner_sums,
        outer_sums,
        vectors[2],
        vectors[3],
        vectors[4],
        grad_self_value,
        grad_self_out,
        vectors[5],
        grad_cross_query,
        grad_cross_key,
        grad_cross_value,
        grad_cross_out,
        vectors[6],
        grad_second_inner,
        grad_second_outer,
        vectors[7],
        grad_pooler,
    )


def solution(mesh):
    placed = (
        P(("batch", "seq"), None),
        P("batch", None),
        P(),
        P("batch"),
        P("batch", None),
        P("batch", None),
        P("batch", None),
        P("batch", None),
        P("batch", None),
        P("batch"),
        P("batch", None),
        P("batch", None),
        P("batch"),
        P("batch"),
        P("batch"),
        P("batch", None),
        P("batch", None),
        P("batch"),
        P("batch", None),
        P("batch", None),
        P("batch", None),
        P("batch", None),
        P("batch"),
        P("batch", None),
        P("batch", None),
        P("batch"),
        P("batch", None),
    )
    return jax.shard_map(
        shards,
        mesh=mesh,
        in_specs=placed,
        out_specs=(
            P(),
            P("batch", None),
            P(("batch", "seq"), None),
            P("batch"),
            P("batch", None),
            P("batch", None),
            P("batch", None),
            P("batch", None),
            P("batch", None),
            P("batch"),
            P("batch", None),
            P("batch", None),
            P("batch"),
            P("batch"),
            P("batch"),
            P("batch", None),
            P("batch", None),
            P("batch"),
            P("batch", None),
            P("batch", None),
            P("batch", None),
            P("batch", None),
            P("batch"),
            P("batch", None),
            P("batch", None),
            P("batch"),
            P("batch", None),
        ),
        check_vma=False,
    )
```
